32 devices in a mesh: seq: 16 (over z, y, core), head: 2 (over x).
Axes of the slice: x: 2, y: 2, z: 4, core: 2. Of those that a mesh axis runs over, the one named last changes fastest.
Arguments:
- queries: bfloat16 [2048, 4096], P(('seq', 'head')), may hold values from -16 to 16
- keys: bfloat16 [2048, 4096], P(('seq', 'head')), may hold values from -16 to 16
- values: bfloat16 [2048, 4096], P(('seq', 'head')), may hold values from -6 to 6
- out_grad: bfloat16 [2048, 4096], P(('seq', 'head')), may hold values from -6 to 6
Outputs:
- attended: bfloat16 [2048, 4096], P(('seq', 'head'))
- query_grad: bfloat16 [2048, 4096], P(('seq', 'head'))
- key_grad: bfloat16 [2048, 4096], P(('seq', 'head'))
- value_gradient_array: bfloat16 [2048, 4096], P(('seq', 'head'))
The draws below stay inside these ranges and needn't reach their ends.
All inputs are finite; a program needn't handle non-finite values.
Results may differ from the reference program's by a relative error of at most 0.034.
The reference program's roundings to bfloat16 on the way count: a program that leaves them out, or rounds other values in their place, can miss the bound.
Values may be sent and summed in bfloat16 or wider, within the bound.
No kernel may reach another device: no remote copies, remote signals or barrier semaphores. Data moves between devices by JAX's collectives and lax.ppermute only.
A program may use at most 128 MiB of HBM per device.

```python
import jax
import jax.numpy as jnp
from jax import lax

H = 32
HD = 128
D = 4096
M = 256
PINV_ITERS = 6
TOKENS = 2048
SEG = 8


def base_field(key):
    noise_key, common_key = jax.random.split(jax.random.fold_in(key, 1), 2)
    noise = jax.random.normal(noise_key, (TOKENS, D), jnp.float32)
    common = jax.random.normal(common_key, (M, D), jnp.float32)
    return noise + jnp.repeat(common, SEG, axis=0)


def draw_queries(key, part):
    key = jax.random.fold_in(key, 11)
    field = base_field(key)
    return jnp.clip(field, -16.0, 16.0).astype(jnp.bfloat16)


def draw_keys(key, part):
    key = jax.random.fold_in(key, 23)
    field = base_field(key)
    return jnp.clip(field, -16.0, 16.0).astype(jnp.bfloat16)


def shard_levels(stream_key, dims, shards, least, high):
    gain, own = 1.0, jax.random.fold_in(stream_key, 6)
    for position, parts in shards:
        heights = jnp.exp(jax.random.uniform(jax.random.fold_in(own, position), (parts,), jnp.float32, least / len(shards), high / len(shards)))
        gain = gain * jnp.repeat(heights, dims[position] // parts).reshape([-1 if axis == position else 1 for axis in range(len(dims))])
    return gain


def normal_values(key, dims, scale, reach, shards=(), held_as=jnp.bfloat16):
    level = shard_levels(key, dims, shards, -0.22, 0.18) if shards else 1.0
    values = jax.random.normal(key, dims, jnp.float32) * scale * level
    return jnp.minimum(jnp.maximum(values, -reach), reach).astype(held_as)


def setup_inputs(seed: int = 0) -> dict:
    splits = jax.random.split(jax.random.key(seed), 5)
    return {
        "queries": draw_queries(jax.random.fold_in(splits[4], 71), 0),
        "keys": draw_keys(jax.random.fold_in(splits[4], 71), 0),
        "values": normal_values(splits[2], (TOKENS, D), 1.0, 6.0, ((0, 32),)),
        "out_grad": normal_values(splits[3], (TOKENS, D), 1.0, 6.0, ((0, 32),)),
    }


def exact_dot(left, right):
    return jnp.matmul(left, right, precision=lax.Precision.HIGHEST)

def newton_inverse(matrix):
    identity = jnp.eye(matrix.shape[0], dtype=matrix.dtype)
    factor = lax.stop_gradient(1.0 / jnp.max(lax.optimization_barrier(jnp.sum(matrix, axis=0))))
    iterate = matrix.T * factor
    for sweep_index in range(PINV_ITERS):
        product = exact_dot(matrix, iterate)
        inner_term = exact_dot(product, 7.0 * identity - product)
        inner_term = exact_dot(product, 15.0 * identity - inner_term)
        iterate = 0.25 * exact_dot(iterate, 13.0 * identity - inner_term)
    return iterate

def one_head(operands):
    query_cols, key_cols, value_cols, grad_cols = operands
    score_scale = HD ** (-0.5)
    landmark_q = (lax.optimization_barrier(jnp.sum(query_cols.reshape(M, SEG, HD), axis=1, dtype=jnp.float32)) / SEG).astype(jnp.bfloat16)
    landmark_k = (lax.optimization_barrier(jnp.sum(key_cols.reshape(M, SEG, HD), axis=1, dtype=jnp.float32)) / SEG).astype(jnp.bfloat16)
    token_prob = jax.nn.softmax(jnp.dot(query_cols, landmark_k.T, preferred_element_type=jnp.float32) * score_scale, axis=-1)
    token_probability_lowered = token_prob.astype(jnp.bfloat16)
    mark_prob = jax.nn.softmax(jnp.dot(landmark_q, landmark_k.T, preferred_element_type=jnp.float32) * score_scale, axis=-1)
    pseudo_inverse_matrix, pull_back = jax.vjp(newton_inverse, mark_prob)
    key_score = jnp.dot(landmark_q, key_cols.T, preferred_element_type=jnp.float32) * score_scale
    key_exp = jnp.exp(key_score - lax.optimization_barrier(jnp.max(key_score, axis=1, keepdims=True)))
    key_total = lax.optimization_barrier(jnp.sum(key_exp, axis=1))
    numerator = jnp.dot(key_exp.astype(jnp.bfloat16), value_cols, preferred_element_type=jnp.float32)
    landmark_value_rows = numerator / key_total[:, None]
    mixing_matrix = exact_dot(pseudo_inverse_matrix, landmark_value_rows)
    mixing_matrix_lowered = mixing_matrix.astype(jnp.bfloat16)
    attended = jnp.dot(token_probability_lowered, mixing_matrix_lowered, preferred_element_type=jnp.float32).astype(jnp.bfloat16)
    token_grad = jnp.dot(grad_cols, mixing_matrix_lowered.T, preferred_element_type=jnp.float32)
    mixing_matrix_gradient = jnp.dot(token_probability_lowered.T, grad_cols, preferred_element_type=jnp.float32)
    token_score_gradient = (token_prob * (token_grad - lax.optimization_barrier(jnp.sum(token_grad * token_prob, axis=1, keepdims=True)))).astype(jnp.bfloat16)
    direct_qgrad = jnp.dot(token_score_gradient, landmark_k, preferred_element_type=jnp.float32) * score_scale
    mark_kgrad_f = jnp.dot(token_score_gradient.T, query_cols, preferred_element_type=jnp.float32) * score_scale
    pseudo_inverse_gradient = exact_dot(mixing_matrix_gradient, landmark_value_rows.T)
    landmark_value_gradient = exact_dot(pseudo_inverse_matrix.T, mixing_matrix_gradient)
    mark_grad, = pull_back(pseudo_inverse_gradient)
    mark_sgrad = mark_prob * (mark_grad - lax.optimization_barrier(jnp.sum(mark_grad * mark_prob, axis=1, keepdims=True)))
    mark_qgrad_a = exact_dot(mark_sgrad, landmark_k.astype(jnp.float32)) * score_scale
    mark_kgrad_a = exact_dot(mark_sgrad.T, landmark_q.astype(jnp.float32)) * score_scale
    landmark_value_lowered = landmark_value_gradient.astype(jnp.bfloat16)
    key_prob = key_exp / key_total[:, None]
    key_probability_lowered = key_prob.astype(jnp.bfloat16)
    value_gradient_array = jnp.dot(key_probability_lowered.T, landmark_value_lowered, preferred_element_type=jnp.float32)
    key_direct_gradient = jnp.dot(landmark_value_lowered, value_cols.T, preferred_element_type=jnp.float32)
    row_total = lax.optimization_barrier(jnp.sum(key_prob * key_direct_gradient, axis=1, keepdims=True))
    key_score_gradient = (key_prob * (key_direct_gradient - row_total)).astype(jnp.bfloat16)
    direct_kgrad = jnp.dot(key_score_gradient.T, landmark_q, preferred_element_type=jnp.float32) * score_scale
    mark_qgrad_b = jnp.dot(key_score_gradient, key_cols, preferred_element_type=jnp.float32) * score_scale
    query_grad = direct_qgrad + jnp.repeat((mark_qgrad_a + mark_qgrad_b) / SEG, SEG, axis=0)
    key_grad = direct_kgrad + jnp.repeat((mark_kgrad_a + mark_kgrad_f) / SEG, SEG, axis=0)
    return (attended, query_grad.astype(jnp.bfloat16), key_grad.astype(jnp.bfloat16), value_gradient_array.astype(jnp.bfloat16))

def split_heads(matrix):
    return jnp.transpose(matrix.reshape(TOKENS, H, HD), (1, 0, 2))

def join_heads(stacked):
    return jnp.transpose(stacked, (1, 0, 2)).reshape(TOKENS, D)

def reference(queries, keys, values, out_grad):
    results = lax.map(one_head, (split_heads(queries), split_heads(keys), split_heads(values), split_heads(out_grad)))
    return (join_heads(results[0]), join_heads(results[1]), join_heads(results[2]), join_heads(results[3]))
```

```python
import jax
import jax.numpy as jnp
from jax import lax
from jax.sharding import PartitionSpec as P

HD = 128
M = 256
PINV_ITERS = 6


precise_setting = lax.Precision.HIGHEST


def newton_inverse(matrix):
    identity = jnp.eye(matrix.shape[0], dtype=matrix.dtype)
    factor = lax.stop_gradient(1.0 / jnp.max(jnp.sum(matrix, axis=0)))
    iterate = matrix.T * factor
    for sweep_index in range(PINV_ITERS):
        product = jnp.matmul(matrix, iterate, precision=precise_setting)
        inner_term = jnp.matmul(product, 7.0 * identity - product, precision=precise_setting)
        inner_term = jnp.matmul(product, 15.0 * identity - inner_term, precision=precise_setting)
        iterate = 0.25 * jnp.matmul(
            iterate, 13.0 * identity - inner_term, precision=precise_setting
        )
    return iterate


def share_heads(own_matrix, head_count):
    seq_index = lax.axis_index("seq")
    slot_mask = (jnp.arange(head_count, dtype=jnp.int32) == seq_index).astype(jnp.float32)
    return lax.psum(slot_mask[:, None, None] * own_matrix[None], "seq")


def shared_body(queries, keys, values, out_grad):
    query_rows, key_rows, value_rows, grad_rows = (
        lax.all_to_all(queries, "head", split_axis=1, concat_axis=0, tiled=True),
        lax.all_to_all(keys, "head", split_axis=1, concat_axis=0, tiled=True),
        lax.all_to_all(values, "head", split_axis=1, concat_axis=0, tiled=True),
        lax.all_to_all(out_grad, "head", split_axis=1, concat_axis=0, tiled=True),
    )
    tok_rows = query_rows.shape[0]
    head_count = query_rows.shape[1] // HD
    local_marks = M // lax.axis_size("seq")
    segment_len = tok_rows // local_marks
    score_scale = HD ** (-0.5)
    seq_index = lax.axis_index("seq")

    def landmark(matrix):
        summed = jnp.sum(
            matrix.reshape(local_marks, segment_len, matrix.shape[1]), axis=1, dtype=jnp.float32
        )
        return (summed / segment_len).astype(jnp.bfloat16)

    mark_queries, mark_keys = (
        lax.all_gather(landmark(query_rows), "seq", axis=0, tiled=True),
        lax.all_gather(landmark(key_rows), "seq", axis=0, tiled=True),
    )
    query_per_head = query_rows.reshape(tok_rows, head_count, HD)
    key_per_head = key_rows.reshape(tok_rows, head_count, HD)
    value_per_head = value_rows.reshape(tok_rows, head_count, HD)
    gradient_per_head = grad_rows.reshape(tok_rows, head_count, HD)
    landmark_query_heads = mark_queries.reshape(M, head_count, HD)
    landmark_key_heads = mark_keys.reshape(M, head_count, HD)
    key_score = (
        jnp.einsum(
            "pcv,gcv->cpg", landmark_query_heads, key_per_head, preferred_element_type=jnp.float32
        )
        * score_scale
    )
    key_max = lax.pmax(jnp.max(key_score, axis=-1), "seq")
    key_exp = jnp.exp(key_score - key_max[..., None])
    partial_num = jnp.einsum(
        "akq,qay->aky",
        key_exp.astype(jnp.bfloat16),
        value_per_head,
        preferred_element_type=jnp.float32,
    )
    key_total, numerator = lax.psum((jnp.sum(key_exp, axis=-1), partial_num), "seq")
    landmark_value_rows = numerator / key_total[..., None]
    token_prob = jax.nn.softmax(
        jnp.einsum(
            "jti,cti->tjc", query_per_head, landmark_key_heads, preferred_element_type=jnp.float32
        )
        * score_scale,
        axis=-1,
    )
    token_probability_lowered = token_prob.astype(jnp.bfloat16)
    mark_prob = jax.nn.softmax(
        jnp.einsum(
            "jou,iou->oji",
            landmark_query_heads,
            landmark_key_heads,
            preferred_element_type=jnp.float32,
        )
        * score_scale,
        axis=-1,
    )
    own_head = seq_index % head_count
    own_mark = lax.dynamic_index_in_dim(mark_prob, own_head, 0, keepdims=False)
    own_inverse, pull_back = jax.vjp(newton_inverse, own_mark)
    pseudo_inverse_matrix = share_heads(own_inverse, head_count)
    mixing_matrix = jnp.einsum(
        "jvy,jys->jvs", pseudo_inverse_matrix, landmark_value_rows, precision=precise_setting
    )
    mixing_matrix_lowered = mixing_matrix.astype(jnp.bfloat16)
    attended = jnp.einsum(
        "yvo,yor->vyr",
        token_probability_lowered,
        mixing_matrix_lowered,
        preferred_element_type=jnp.float32,
    ).astype(jnp.bfloat16)
    token_grad = jnp.einsum(
        "fag,aog->afo", gradient_per_head, mixing_matrix_lowered, preferred_element_type=jnp.float32
    )
    partial_mix = jnp.einsum(
        "klz,lkr->kzr",
        token_probability_lowered,
        gradient_per_head,
        preferred_element_type=jnp.float32,
    )
    mixing_matrix_gradient = lax.psum(partial_mix, "seq")
    token_score_gradient = (
        token_prob * (token_grad - jnp.sum(token_grad * token_prob, axis=-1, keepdims=True))
    ).astype(jnp.bfloat16)
    direct_qgrad = (
        jnp.einsum(
            "ufg,guc->fuc",
            token_score_gradient,
            landmark_key_heads,
            preferred_element_type=jnp.float32,
        )
        * score_scale
    )
    mark_kgrad_f = (
        jnp.einsum(
            "xgi,gxy->ixy", token_score_gradient, query_per_head, preferred_element_type=jnp.float32
        )
        * score_scale
    )
    pseudo_inverse_gradient = jnp.einsum(
        "ktu,kyu->kty", mixing_matrix_gradient, landmark_value_rows, precision=precise_setting
    )
    landmark_value_gradient = jnp.einsum(
        "lrb,lrz->lbz", pseudo_inverse_matrix, mixing_matrix_gradient, precision=precise_setting
    )
    own_igrad = lax.dynamic_index_in_dim(pseudo_inverse_gradient, own_head, 0, keepdims=False)
    (own_mgrad,) = pull_back(own_igrad)
    mark_grad = share_heads(own_mgrad, head_count)
    mark_sgrad = mark_prob * (mark_grad - jnp.sum(mark_grad * mark_prob, axis=-1, keepdims=True))
    first_mark = seq_index * local_marks
    score_gradient_rows = lax.dynamic_slice_in_dim(mark_sgrad, first_mark, local_marks, 1)
    score_gradient_columns = lax.dynamic_slice_in_dim(mark_sgrad, first_mark, local_marks, 2)
    own_qgrad_a = (
        jnp.einsum(
            "txs,ste->xte",
            score_gradient_rows,
            landmark_key_heads.astype(jnp.float32),
            precision=precise_setting,
        )
        * score_scale
    )
    own_kgrad_a = (
        jnp.einsum(
            "eaj,aev->jev",
            score_gradient_columns,
            landmark_query_heads.astype(jnp.float32),
            precision=precise_setting,
        )
        * score_scale
    )
    landmark_value_lowered = landmark_value_gradient.astype(jnp.bfloat16)
    key_prob = key_exp / key_total[..., None]
    key_probability_lowered = key_prob.astype(jnp.bfloat16)
    value_gradient_array = jnp.einsum(
        "zct,zcj->tzj",
        key_probability_lowered,
        landmark_value_lowered,
        preferred_element_type=jnp.float32,
    )
    key_direct_gradient = jnp.einsum(
        "exb,geb->exg", landmark_value_lowered, value_per_head, preferred_element_type=jnp.float32
    )
    row_total = lax.psum(jnp.sum(key_prob * key_direct_gradient, axis=-1), "seq")
    key_score_gradient = (key_prob * (key_direct_gradient - row_total[..., None])).astype(
        jnp.bfloat16
    )
    direct_kgrad = (
        jnp.einsum(
            "pbo,bpx->opx",
            key_score_gradient,
            landmark_query_heads,
            preferred_element_type=jnp.float32,
        )
        * score_scale
    )
    mark_qgrad_b = (
        jnp.einsum(
            "cbj,jcp->bcp", key_score_gradient, key_per_head, preferred_element_type=jnp.float32
        )
        * score_scale
    )
    own_kgrad_f, own_qgrad_b = (
        lax.psum_scatter(mark_kgrad_f, "seq", scatter_dimension=0, tiled=True),
        lax.psum_scatter(mark_qgrad_b, "seq", scatter_dimension=0, tiled=True),
    )
    mark_qtotal = (own_qgrad_a + own_qgrad_b) / segment_len
    mark_ktotal = (own_kgrad_a + own_kgrad_f) / segment_len
    query_grad = (
        direct_qgrad.reshape(local_marks, segment_len, head_count, HD) + mark_qtotal[:, None]
    )
    key_grad = direct_kgrad.reshape(local_marks, segment_len, head_count, HD) + mark_ktotal[:, None]
    width = head_count * HD
    results = (
        attended.reshape(tok_rows, width),
        query_grad.astype(jnp.bfloat16).reshape(tok_rows, width),
        key_grad.astype(jnp.bfloat16).reshape(tok_rows, width),
        value_gradient_array.astype(jnp.bfloat16).reshape(tok_rows, width),
    )
    attended_out, query_out, key_out, value_out = (
        lax.all_to_all(results[0], "head", split_axis=0, concat_axis=1, tiled=True),
        lax.all_to_all(results[1], "head", split_axis=0, concat_axis=1, tiled=True),
        lax.all_to_all(results[2], "head", split_axis=0, concat_axis=1, tiled=True),
        lax.all_to_all(results[3], "head", split_axis=0, concat_axis=1, tiled=True),
    )
    return (attended_out, query_out, key_out, value_out)


def precise_dot(left, right):
    return jnp.matmul(left, right, precision=precise_setting)


def body(queries, keys, values, out_grad):
    axes = ("seq", "head")
    query_cols, key_cols, value_cols, grad_cols = (
        lax.all_to_all(rows, axes, split_axis=1, concat_axis=0, tiled=True)
        for rows in (queries, keys, values, out_grad)
    )
    tokens = query_cols.shape[0]
    segment_len = tokens // M
    score_scale = HD ** (-0.5)

    def landmark(matrix):
        summed = jnp.sum(matrix.reshape(M, segment_len, HD), axis=1, dtype=jnp.float32)
        return (summed / segment_len).astype(jnp.bfloat16)

    def wide_dot(left, right):
        return jnp.dot(left, right, preferred_element_type=jnp.float32)

    landmark_q, landmark_k = landmark(query_cols), landmark(key_cols)
    token_prob = jax.nn.softmax(wide_dot(query_cols, landmark_k.T) * score_scale, axis=-1)
    token_low = token_prob.astype(jnp.bfloat16)
    mark_prob = jax.nn.softmax(wide_dot(landmark_q, landmark_k.T) * score_scale, axis=-1)
    inverse, pull_back = jax.vjp(newton_inverse, mark_prob)
    key_score = wide_dot(landmark_q, key_cols.T) * score_scale
    key_exp = jnp.exp(key_score - jnp.max(key_score, axis=1, keepdims=True))
    key_total = jnp.sum(key_exp, axis=1, keepdims=True)
    landmark_values = wide_dot(key_exp.astype(jnp.bfloat16), value_cols) / key_total
    mixing_low = precise_dot(inverse, landmark_values).astype(jnp.bfloat16)
    attended = wide_dot(token_low, mixing_low).astype(jnp.bfloat16)
    token_grad = wide_dot(grad_cols, mixing_low.T)
    mixing_grad = wide_dot(token_low.T, grad_cols)
    token_sgrad = (
        token_prob * (token_grad - jnp.sum(token_grad * token_prob, axis=1, keepdims=True))
    ).astype(jnp.bfloat16)
    direct_qgrad = wide_dot(token_sgrad, landmark_k) * score_scale
    mark_kgrad_f = wide_dot(token_sgrad.T, query_cols) * score_scale
    inverse_grad = precise_dot(mixing_grad, landmark_values.T)
    lv_low = precise_dot(inverse.T, mixing_grad).astype(jnp.bfloat16)
    (mark_grad,) = pull_back(inverse_grad)
    mark_sgrad = mark_prob * (mark_grad - jnp.sum(mark_grad * mark_prob, axis=1, keepdims=True))
    mark_qgrad_a = precise_dot(mark_sgrad, landmark_k.astype(jnp.float32)) * score_scale
    mark_kgrad_a = precise_dot(mark_sgrad.T, landmark_q.astype(jnp.float32)) * score_scale
    key_prob = key_exp / key_total
    value_gradient_array = wide_dot(key_prob.astype(jnp.bfloat16).T, lv_low).astype(jnp.bfloat16)
    key_dgrad = wide_dot(lv_low, value_cols.T)
    row_total = jnp.sum(key_prob * key_dgrad, axis=1, keepdims=True)
    key_sgrad = (key_prob * (key_dgrad - row_total)).astype(jnp.bfloat16)
    direct_kgrad = wide_dot(key_sgrad.T, landmark_q) * score_scale
    mark_qgrad_b = wide_dot(key_sgrad, key_cols) * score_scale

    def spread(direct, marks):
        return (
            (direct.reshape(M, segment_len, HD) + (marks / segment_len)[:, None])
            .reshape(tokens, HD)
            .astype(jnp.bfloat16)
        )

    query_grad = spread(direct_qgrad, mark_qgrad_a + mark_qgrad_b)
    key_grad = spread(direct_kgrad, mark_kgrad_a + mark_kgrad_f)
    return tuple(
        lax.all_to_all(cols, axes, split_axis=0, concat_axis=1, tiled=True)
        for cols in (attended, query_grad, key_grad, value_gradient_array)
    )


def solution(mesh):
    placement = P(("seq", "head"), None)

    def layer(queries, keys, values, out_grad):
        one_head_each = queries.shape[1] // HD == mesh.size
        return jax.shard_map(
            body if one_head_each else shared_body,
            mesh=mesh,
            in_specs=(placement,) * 4,
            out_specs=(placement,) * 4,
            check_vma=False,
        )(queries, keys, values, out_grad)

    return layer
```

```python
import jax
import jax.numpy as jnp
from jax import lax
from jax.experimental import pallas as pl
from jax.experimental.pallas import tpu as pltpu
from jax.sharding import PartitionSpec as P

HD = 128
M = 256
PINV_ITERS = 6
CHUNK = 256
VMEM_LIMIT = 40 * 2**20
FORWARD_FLOPS = 10 * 10**9
MIXING_FLOPS = 2 * 10**9
GRADIENT_FLOPS = 14 * 10**9


precise_setting = lax.Precision.HIGHEST


def newton_inverse(matrix):
    identity = jnp.eye(matrix.shape[0], dtype=matrix.dtype)
    factor = lax.stop_gradient(1.0 / jnp.max(jnp.sum(matrix, axis=0)))
    iterate = matrix.T * factor
    for sweep_index in range(PINV_ITERS):
        product = jnp.matmul(matrix, iterate, precision=precise_setting)
        inner_term = jnp.matmul(product, 7.0 * identity - product, precision=precise_setting)
        inner_term = jnp.matmul(product, 15.0 * identity - inner_term, precision=precise_setting)
        iterate = 0.25 * jnp.matmul(
            iterate, 13.0 * identity - inner_term, precision=precise_setting
        )
    return iterate


def share_heads(own_matrix, head_count):
    seq_index = lax.axis_index("seq")
    slot_mask = (jnp.arange(head_count, dtype=jnp.int32) == seq_index).astype(jnp.float32)
    return lax.psum(slot_mask[:, None, None] * own_matrix[None], "seq")


def shared_body(queries, keys, values, out_grad):
    query_rows, key_rows, value_rows, grad_rows = (
        lax.all_to_all(queries, "head", split_axis=1, concat_axis=0, tiled=True),
        lax.all_to_all(keys, "head", split_axis=1, concat_axis=0, tiled=True),
        lax.all_to_all(values, "head", split_axis=1, concat_axis=0, tiled=True),
        lax.all_to_all(out_grad, "head", split_axis=1, concat_axis=0, tiled=True),
    )
    tok_rows = query_rows.shape[0]
    head_count = query_rows.shape[1] // HD
    local_marks = M // lax.axis_size("seq")
    segment_len = tok_rows // local_marks
    score_scale = HD ** (-0.5)
    seq_index = lax.axis_index("seq")

    def landmark(matrix):
        summed = jnp.sum(
            matrix.reshape(local_marks, segment_len, matrix.shape[1]), axis=1, dtype=jnp.float32
        )
        return (summed / segment_len).astype(jnp.bfloat16)

    mark_queries, mark_keys = (
        lax.all_gather(landmark(query_rows), "seq", axis=0, tiled=True),
        lax.all_gather(landmark(key_rows), "seq", axis=0, tiled=True),
    )
    query_per_head = query_rows.reshape(tok_rows, head_count, HD)
    key_per_head = key_rows.reshape(tok_rows, head_count, HD)
    value_per_head = value_rows.reshape(tok_rows, head_count, HD)
    gradient_per_head = grad_rows.reshape(tok_rows, head_count, HD)
    landmark_query_heads = mark_queries.reshape(M, head_count, HD)
    landmark_key_heads = mark_keys.reshape(M, head_count, HD)
    key_score = (
        jnp.einsum(
            "pcv,gcv->cpg", landmark_query_heads, key_per_head, preferred_element_type=jnp.float32
        )
        * score_scale
    )
    key_max = lax.pmax(jnp.max(key_score, axis=-1), "seq")
    key_exp = jnp.exp(key_score - key_max[..., None])
    partial_num = jnp.einsum(
        "akq,qay->aky",
        key_exp.astype(jnp.bfloat16),
        value_per_head,
        preferred_element_type=jnp.float32,
    )
    key_total, numerator = lax.psum((jnp.sum(key_exp, axis=-1), partial_num), "seq")
    landmark_value_rows = numerator / key_total[..., None]
    token_prob = jax.nn.softmax(
        jnp.einsum(
            "jti,cti->tjc", query_per_head, landmark_key_heads, preferred_element_type=jnp.float32
        )
        * score_scale,
        axis=-1,
    )
    token_probability_lowered = token_prob.astype(jnp.bfloat16)
    mark_prob = jax.nn.softmax(
        jnp.einsum(
            "jou,iou->oji",
            landmark_query_heads,
            landmark_key_heads,
            preferred_element_type=jnp.float32,
        )
        * score_scale,
        axis=-1,
    )
    own_head = seq_index % head_count
    own_mark = lax.dynamic_index_in_dim(mark_prob, own_head, 0, keepdims=False)
    own_inverse, pull_back = jax.vjp(newton_inverse, own_mark)
    pseudo_inverse_matrix = share_heads(own_inverse, head_count)
    mixing_matrix = jnp.einsum(
        "jvy,jys->jvs", pseudo_inverse_matrix, landmark_value_rows, precision=precise_setting
    )
    mixing_matrix_lowered = mixing_matrix.astype(jnp.bfloat16)
    attended = jnp.einsum(
        "yvo,yor->vyr",
        token_probability_lowered,
        mixing_matrix_lowered,
        preferred_element_type=jnp.float32,
    ).astype(jnp.bfloat16)
    token_grad = jnp.einsum(
        "fag,aog->afo", gradient_per_head, mixing_matrix_lowered, preferred_element_type=jnp.float32
    )
    partial_mix = jnp.einsum(
        "klz,lkr->kzr",
        token_probability_lowered,
        gradient_per_head,
        preferred_element_type=jnp.float32,
    )
    mixing_matrix_gradient = lax.psum(partial_mix, "seq")
    token_score_gradient = (
        token_prob * (token_grad - jnp.sum(token_grad * token_prob, axis=-1, keepdims=True))
    ).astype(jnp.bfloat16)
    direct_qgrad = (
        jnp.einsum(
            "ufg,guc->fuc",
            token_score_gradient,
            landmark_key_heads,
            preferred_element_type=jnp.float32,
        )
        * score_scale
    )
    mark_kgrad_f = (
        jnp.einsum(
            "xgi,gxy->ixy", token_score_gradient, query_per_head, preferred_element_type=jnp.float32
        )
        * score_scale
    )
    pseudo_inverse_gradient = jnp.einsum(
        "ktu,kyu->kty", mixing_matrix_gradient, landmark_value_rows, precision=precise_setting
    )
    landmark_value_gradient = jnp.einsum(
        "lrb,lrz->lbz", pseudo_inverse_matrix, mixing_matrix_gradient, precision=precise_setting
    )
    own_igrad = lax.dynamic_index_in_dim(pseudo_inverse_gradient, own_head, 0, keepdims=False)
    (own_mgrad,) = pull_back(own_igrad)
    mark_grad = share_heads(own_mgrad, head_count)
    mark_sgrad = mark_prob * (mark_grad - jnp.sum(mark_grad * mark_prob, axis=-1, keepdims=True))
    first_mark = seq_index * local_marks
    score_gradient_rows = lax.dynamic_slice_in_dim(mark_sgrad, first_mark, local_marks, 1)
    score_gradient_columns = lax.dynamic_slice_in_dim(mark_sgrad, first_mark, local_marks, 2)
    own_qgrad_a = (
        jnp.einsum(
            "txs,ste->xte",
            score_gradient_rows,
            landmark_key_heads.astype(jnp.float32),
            precision=precise_setting,
        )
        * score_scale
    )
    own_kgrad_a = (
        jnp.einsum(
            "eaj,aev->jev",
            score_gradient_columns,
            landmark_query_heads.astype(jnp.float32),
            precision=precise_setting,
        )
        * score_scale
    )
    landmark_value_lowered = landmark_value_gradient.astype(jnp.bfloat16)
    key_prob = key_exp / key_total[..., None]
    key_probability_lowered = key_prob.astype(jnp.bfloat16)
    value_gradient_array = jnp.einsum(
        "zct,zcj->tzj",
        key_probability_lowered,
        landmark_value_lowered,
        preferred_element_type=jnp.float32,
    )
    key_direct_gradient = jnp.einsum(
        "exb,geb->exg", landmark_value_lowered, value_per_head, preferred_element_type=jnp.float32
    )
    row_total = lax.psum(jnp.sum(key_prob * key_direct_gradient, axis=-1), "seq")
    key_score_gradient = (key_prob * (key_direct_gradient - row_total[..., None])).astype(
        jnp.bfloat16
    )
    direct_kgrad = (
        jnp.einsum(
            "pbo,bpx->opx",
            key_score_gradient,
            landmark_query_heads,
            preferred_element_type=jnp.float32,
        )
        * score_scale
    )
    mark_qgrad_b = (
        jnp.einsum(
            "cbj,jcp->bcp", key_score_gradient, key_per_head, preferred_element_type=jnp.float32
        )
        * score_scale
    )
    own_kgrad_f, own_qgrad_b = (
        lax.psum_scatter(mark_kgrad_f, "seq", scatter_dimension=0, tiled=True),
        lax.psum_scatter(mark_qgrad_b, "seq", scatter_dimension=0, tiled=True),
    )
    mark_qtotal = (own_qgrad_a + own_qgrad_b) / segment_len
    mark_ktotal = (own_kgrad_a + own_kgrad_f) / segment_len
    query_grad = (
        direct_qgrad.reshape(local_marks, segment_len, head_count, HD) + mark_qtotal[:, None]
    )
    key_grad = direct_kgrad.reshape(local_marks, segment_len, head_count, HD) + mark_ktotal[:, None]
    width = head_count * HD
    results = (
        attended.reshape(tok_rows, width),
        query_grad.astype(jnp.bfloat16).reshape(tok_rows, width),
        key_grad.astype(jnp.bfloat16).reshape(tok_rows, width),
        value_gradient_array.astype(jnp.bfloat16).reshape(tok_rows, width),
    )
    attended_out, query_out, key_out, value_out = (
        lax.all_to_all(results[0], "head", split_axis=0, concat_axis=1, tiled=True),
        lax.all_to_all(results[1], "head", split_axis=0, concat_axis=1, tiled=True),
        lax.all_to_all(results[2], "head", split_axis=0, concat_axis=1, tiled=True),
        lax.all_to_all(results[3], "head", split_axis=0, concat_axis=1, tiled=True),
    )
    return (attended_out, query_out, key_out, value_out)


def dims_of(rows):
    tokens = rows.shape[0] * rows.shape[2]
    return tokens, rows.shape[2], tokens // CHUNK


def halves(matrix):
    high = matrix.astype(jnp.bfloat16)
    return high, (matrix - high.astype(jnp.float32)).astype(jnp.bfloat16)


def wide_dot(left, right):
    return jnp.dot(left, right, preferred_element_type=jnp.float32)


def wide_dot_nt(left, right):
    return lax.dot_general(
        left, right, (((1,), (1,)), ((), ())), preferred_element_type=jnp.float32
    )


def split_dot(left, right):
    left_high, left_low = left
    right_high, right_low = right
    return wide_dot(
        jnp.concatenate([left_high, left_high, left_low], axis=1),
        jnp.concatenate([right_high, right_low, right_high], axis=0),
    )


def split_dot_nt(left, right):
    left_high, left_low = left
    right_high, right_low = right
    return wide_dot_nt(
        jnp.concatenate([left_high, left_high, left_low], axis=1),
        jnp.concatenate([right_high, right_low, right_high], axis=1),
    )


def identity_matrix():
    return (
        lax.broadcasted_iota(jnp.int32, (M, M), 0) == lax.broadcasted_iota(jnp.int32, (M, M), 1)
    ).astype(jnp.float32)


def chunk_of(ref, slot, index):
    rows = ref.shape[2]
    per = CHUNK // rows
    return ref[pl.ds(index * per, per), slot].reshape(CHUNK, HD)


def store_chunk(ref, slot, index, value):
    rows = ref.shape[2]
    per = CHUNK // rows
    ref[pl.ds(index * per, per), slot] = value.reshape(per, rows, HD)


def columns(index):
    return pl.ds(pl.multiple_of(index * CHUNK, CHUNK), CHUNK)


def pack_kernel(first_ref, second_ref, out_ref):
    for head in range(out_ref.shape[0]):
        out_ref[head, 0] = first_ref[:, head * HD : (head + 1) * HD]
        out_ref[head, 1] = second_ref[:, head * HD : (head + 1) * HD]


def unpack_kernel(packed_ref, first_ref, second_ref):
    for head in range(packed_ref.shape[0]):
        first_ref[:, head * HD : (head + 1) * HD] = packed_ref[head, 0]
        second_ref[:, head * HD : (head + 1) * HD] = packed_ref[head, 1]


def forward_kernel(
    qk_ref,
    mark_q_ref,
    mark_k_ref,
    mark_prob_ref,
    factor_ref,
    token_prob_ref,
    token_low_ref,
    token_turned_ref,
    key_prob_ref,
    key_plow_ref,
    key_turned_ref,
    total_inverse_ref,
    columns_turned_ref,
    pair_ref,
    weight_ref,
    growth_ref,
    inverse_ref,
    inverse_turned_ref,
    last_growth_ref,
    power_s,
    iterate_s,
):
    tokens, rows, chunks = dims_of(qk_ref)
    segment_len = tokens // M
    marks_per = CHUNK // segment_len
    score_scale = HD ** (-0.5)
    member = (
        lax.broadcasted_iota(jnp.int32, (marks_per, CHUNK), 1) // segment_len
        == lax.broadcasted_iota(jnp.int32, (marks_per, CHUNK), 0)
    ).astype(jnp.bfloat16)
    for index in range(chunks):
        both = jnp.concatenate([chunk_of(qk_ref, 0, index), chunk_of(qk_ref, 1, index)], axis=1)
        mean = (wide_dot(member, both) / segment_len).astype(jnp.bfloat16)
        mark_q_ref[index * marks_per : (index + 1) * marks_per] = mean[:, :HD]
        mark_k_ref[index * marks_per : (index + 1) * marks_per] = mean[:, HD:]
    landmark_q, landmark_k = mark_q_ref[...], mark_k_ref[...]

    mark_score = wide_dot_nt(landmark_q, landmark_k) * score_scale
    mark_exp = jnp.exp(mark_score - jnp.max(mark_score, axis=1, keepdims=True))
    mark_prob = mark_exp / jnp.sum(mark_exp, axis=1, keepdims=True)
    mark_prob_ref[...] = mark_prob
    factor = 1.0 / jnp.max(jnp.sum(mark_prob, axis=0, keepdims=True), axis=1, keepdims=True)
    factor_ref[...] = jnp.broadcast_to(factor, factor_ref.shape)
    mark_halves = halves(mark_prob)
    power_s[...] = split_dot_nt(mark_halves, mark_halves) * factor
    iterate_s[0:M] = mark_prob.T * factor
    iterate_s[M:] = identity_matrix()

    def newton(sweep, carry):
        power = power_s[...]
        power_high, power_low = halves(power)
        square = split_dot((power_high, power_low), (power_high, power_low))
        square_halves = halves(square)
        pair = (
            jnp.concatenate([power_high, square_halves[0]], axis=0),
            jnp.concatenate([power_low, square_halves[1]], axis=0),
        )
        pair_ref[sweep, 0], pair_ref[sweep, 1] = pair
        higher = split_dot(pair, square_halves)
        cube, fourth = higher[:M], higher[M:]
        weight = halves(
            0.25 * (13.0 * identity_matrix() - 15.0 * power + 7.0 * square - cube)
        )
        power_s[...] = 0.25 * (13.0 * power - 15.0 * square + 7.0 * cube - fourth)
        weight_ref[sweep, 0], weight_ref[sweep, 1] = weight
        iterate = halves(iterate_s[...])
        growth_ref[sweep, 0], growth_ref[sweep, 1] = iterate[0][M:], iterate[1][M:]
        iterate_s[...] = split_dot(iterate, weight)
        return carry

    lax.fori_loop(0, PINV_ITERS, newton, 0)
    inverse = iterate_s[0:M]
    inverse_ref[0], inverse_ref[1] = halves(inverse)
    inverse_turned_ref[0], inverse_turned_ref[1] = halves(inverse.T)
    last_growth_ref[0], last_growth_ref[1] = halves(iterate_s[M:])

    def scores(index, key_max):
        query_chunk, key_chunk = chunk_of(qk_ref, 0, index), chunk_of(qk_ref, 1, index)
        place = columns(index)
        columns_turned_ref[0, :, place] = query_chunk.T
        columns_turned_ref[1, :, place] = key_chunk.T
        score = wide_dot_nt(query_chunk, landmark_k) * score_scale
        grown = jnp.exp(score - jnp.max(score, axis=1, keepdims=True))
        prob = grown / jnp.sum(grown, axis=1, keepdims=True)
        token_prob_ref[place] = prob
        low = prob.astype(jnp.bfloat16)
        token_low_ref[place] = low
        token_turned_ref[:, place] = low.T
        key_score = wide_dot_nt(key_chunk, landmark_q) * score_scale
        key_prob_ref[place] = key_score
        return jnp.maximum(key_max, jnp.max(key_score, axis=0, keepdims=True))

    key_max = lax.fori_loop(0, chunks, scores, jnp.full((1, M), -jnp.inf, jnp.float32))

    def grow(index, key_total):
        place = columns(index)
        grown = jnp.exp(key_prob_ref[place] - key_max)
        key_prob_ref[place] = grown
        key_turned_ref[:, place] = grown.astype(jnp.bfloat16).T
        return key_total + jnp.sum(grown, axis=0, keepdims=True)

    key_total = lax.fori_loop(0, chunks, grow, jnp.zeros((1, M), jnp.float32))
    total_inverse = 1.0 / key_total
    total_inverse_ref[...] = jnp.broadcast_to(total_inverse, (HD, M)).T

    def normalise(index, carry):
        place = columns(index)
        prob = key_prob_ref[place] * total_inverse
        key_prob_ref[place] = prob
        key_plow_ref[place] = prob.astype(jnp.bfloat16)
        return carry

    lax.fori_loop(0, chunks, normalise, 0)


def mixing_kernel(
    vg_ref,
    token_low_ref,
    token_turned_ref,
    key_plow_ref,
    key_turned_ref,
    total_inverse_ref,
    inverse_ref,
    inverse_turned_ref,
    out_ref,
    mixing_low_ref,
    mixing_grad_ref,
    mark_values_ref,
    values_low_ref,
):
    tokens, rows, chunks = dims_of(vg_ref)
    values = vg_ref[:, 0].reshape(tokens, HD)
    out_grad = vg_ref[:, 1].reshape(tokens, HD)
    landmark_values = wide_dot(key_turned_ref[...], values) * total_inverse_ref[...]
    mixing_grad = wide_dot(token_turned_ref[...], out_grad)
    mark_values_ref[...] = landmark_values
    mixing_grad_ref[...] = mixing_grad
    mixing_low = split_dot(
        (inverse_ref[0], inverse_ref[1]), halves(landmark_values)
    ).astype(jnp.bfloat16)
    values_low = split_dot(
        (inverse_turned_ref[0], inverse_turned_ref[1]), halves(mixing_grad)
    ).astype(jnp.bfloat16)
    mixing_low_ref[...] = mixing_low
    values_low_ref[...] = values_low

    def emit(index, carry):
        place = columns(index)
        store_chunk(
            out_ref, 0, index, wide_dot(token_low_ref[place], mixing_low).astype(jnp.bfloat16)
        )
        store_chunk(
            out_ref, 1, index, wide_dot(key_plow_ref[place], values_low).astype(jnp.bfloat16)
        )
        return carry

    lax.fori_loop(0, chunks, emit, 0)


def gradient_kernel(
    vg_ref,
    mark_q_ref,
    mark_k_ref,
    mark_prob_ref,
    factor_ref,
    token_prob_ref,
    key_prob_ref,
    columns_turned_ref,
    pair_ref,
    weight_ref,
    growth_ref,
    last_growth_ref,
    mixing_low_ref,
    mixing_grad_ref,
    mark_values_ref,
    values_low_ref,
    out_ref,
    power_s,
    growth_s,
    direct_s,
    kept_s,
):
    tokens, rows, chunks = dims_of(vg_ref)
    segment_len = tokens // M
    marks_per = CHUNK // segment_len
    score_scale = HD ** (-0.5)
    landmark_q, landmark_k = mark_q_ref[...], mark_k_ref[...]
    mark_prob = mark_prob_ref[...]
    mark_halves = halves(mark_prob)
    factor = factor_ref[0:1, 0:1]
    inverse_grad = split_dot_nt(halves(mixing_grad_ref[...]), halves(mark_values_ref[...]))
    inverse_grad_halves = halves(inverse_grad)
    toward = split_dot(mark_halves, inverse_grad_halves) * factor
    power_s[...] = 0.5 * (toward + toward.T)
    growth_s[...] = jnp.zeros((M, M), jnp.float32)

    def newton(sweep, carry):
        power = power_s[...]
        pair = (pair_ref[sweep, 0], pair_ref[sweep, 1])
        first = split_dot(pair, halves(power))
        square = first[:M] + first[:M].T
        second = split_dot(pair, halves(square))
        cube = first[M:].T + second[:M]
        fourth = second[M:] + second[M:].T
        weight = halves(0.25 * (7.0 * square - 15.0 * power - cube))
        power_s[...] = 0.25 * (13.0 * power - 15.0 * square + 7.0 * cube - fourth)
        grown_high, grown_low = halves(growth_s[...])
        held_high, held_low = growth_ref[sweep, 0], growth_ref[sweep, 1]
        held_weight_high, held_weight_low = weight_ref[sweep, 0], weight_ref[sweep, 1]
        growth_s[...] = wide_dot(
            jnp.concatenate(
                [grown_high, grown_high, grown_low, held_high, held_high, held_low], axis=1
            ),
            jnp.concatenate(
                [
                    held_weight_high,
                    held_weight_low,
                    held_weight_high,
                    weight[0],
                    weight[1],
                    weight[0],
                ],
                axis=0,
            ),
        )
        return carry

    lax.fori_loop(0, PINV_ITERS, newton, 0)
    growth = growth_s[...]
    mark_grad = factor * (
        split_dot_nt((last_growth_ref[0], last_growth_ref[1]), inverse_grad_halves)
        + split_dot(halves(growth + growth.T), mark_halves)
    )
    mark_sgrad = mark_prob * (mark_grad - jnp.sum(mark_grad * mark_prob, axis=1, keepdims=True))

    def marks_dot(left, right):
        high, low = halves(left)
        return wide_dot(
            jnp.concatenate([high, low], axis=1), jnp.concatenate([right, right], axis=0)
        )

    mark_qgrad_a = marks_dot(mark_sgrad, landmark_k)
    mark_kgrad_a = marks_dot(mark_sgrad.T, landmark_q)

    values_low = values_low_ref[...]

    def key_rows(index, row_total):
        place = columns(index)
        key_dgrad = wide_dot_nt(chunk_of(vg_ref, 0, index), values_low)
        kept_s[place] = key_dgrad
        return row_total + jnp.sum(key_prob_ref[place] * key_dgrad, axis=0, keepdims=True)

    row_total = lax.fori_loop(0, chunks, key_rows, jnp.zeros((1, M), jnp.float32))

    def key_side(index, total):
        place = columns(index)
        key_sgrad = (key_prob_ref[place] * (kept_s[place] - row_total)).astype(jnp.bfloat16)
        direct_s[place] = wide_dot(key_sgrad, landmark_q) * score_scale
        return total + wide_dot(columns_turned_ref[1, :, place], key_sgrad)

    mark_qgrad_b = lax.fori_loop(0, chunks, key_side, jnp.zeros((HD, M), jnp.float32))
    mark_qtotal = (mark_qgrad_a + mark_qgrad_b.T) * (score_scale / segment_len)
    mixing_low = mixing_low_ref[...]

    def spread(direct, marks):
        wide = jnp.broadcast_to(marks[:, None], (marks_per, segment_len, HD))
        return (direct + wide.reshape(CHUNK, HD)).astype(jnp.bfloat16)

    kept_s[0:M, 0:HD] = mark_qtotal

    def token_side(index, total):
        place = columns(index)
        prob = token_prob_ref[place]
        token_grad = wide_dot_nt(chunk_of(vg_ref, 1, index), mixing_low)
        token_sgrad = (
            prob * (token_grad - jnp.sum(token_grad * prob, axis=1, keepdims=True))
        ).astype(jnp.bfloat16)
        direct = wide_dot(token_sgrad, landmark_k) * score_scale
        marks = kept_s[pl.ds(pl.multiple_of(index * marks_per, marks_per), marks_per), 0:HD]
        store_chunk(out_ref, 0, index, spread(direct, marks))
        return total + wide_dot(columns_turned_ref[0, :, place], token_sgrad)

    mark_kgrad_f = lax.fori_loop(0, chunks, token_side, jnp.zeros((HD, M), jnp.float32))
    kept_s[0:M, 0:HD] = (mark_kgrad_a + mark_kgrad_f.T) * (score_scale / segment_len)

    def finish(index, carry):
        marks = kept_s[pl.ds(pl.multiple_of(index * marks_per, marks_per), marks_per), 0:HD]
        store_chunk(out_ref, 1, index, spread(direct_s[columns(index)], marks))
        return carry

    lax.fori_loop(0, chunks, finish, 0)


def kernel_call(kernel, out_shape, scratch, flops, operands):
    moved = sum(x.size * x.dtype.itemsize for x in operands)
    in_vmem = pl.BlockSpec(memory_space=pltpu.VMEM)
    return pl.pallas_call(
        kernel,
        out_shape=out_shape,
        in_specs=[in_vmem] * len(operands),
        out_specs=jax.tree.map(lambda _: in_vmem, out_shape),
        scratch_shapes=scratch,
        compiler_params=pltpu.CompilerParams(vmem_limit_bytes=VMEM_LIMIT),
        cost_estimate=pl.CostEstimate(flops=flops, bytes_accessed=moved, transcendentals=0),
    )(*operands)


def pack(first, second):
    rows, width = first.shape
    shape = jax.ShapeDtypeStruct((width // HD, 2, rows, HD), first.dtype)
    return kernel_call(pack_kernel, shape, [], 0, (first, second))


def unpack(packed):
    heads, _, rows, _ = packed.shape
    shape = jax.ShapeDtypeStruct((rows, heads * HD), packed.dtype)
    return kernel_call(unpack_kernel, (shape, shape), [], 0, (packed,))


def forward_part(qk):
    tokens = qk.shape[0] * qk.shape[2]

    def low(*shape):
        return jax.ShapeDtypeStruct(shape, jnp.bfloat16)

    def wide(*shape):
        return jax.ShapeDtypeStruct(shape, jnp.float32)

    shapes = dict(
        mark_q=low(M, HD),
        mark_k=low(M, HD),
        mark_prob=wide(M, M),
        factor=wide(8, HD),
        token_prob=wide(tokens, M),
        token_low=low(tokens, M),
        token_turned=low(M, tokens),
        key_prob=wide(tokens, M),
        key_plow=low(tokens, M),
        key_turned=low(M, tokens),
        total_inverse=wide(M, HD),
        columns_turned=low(2, HD, tokens),
        pair=low(PINV_ITERS, 2, 2 * M, M),
        weight=low(PINV_ITERS, 2, M, M),
        growth=low(PINV_ITERS, 2, M, M),
        inverse=low(2, M, M),
        inverse_turned=low(2, M, M),
        last_growth=low(2, M, M),
    )
    scratch = [pltpu.VMEM((M, M), jnp.float32), pltpu.VMEM((2 * M, M), jnp.float32)]
    results = kernel_call(
        forward_kernel, tuple(shapes.values()), scratch, FORWARD_FLOPS, (qk,)
    )
    return dict(zip(shapes, results))


def mixing_part(vg, kept):
    names = (
        "token_low",
        "token_turned",
        "key_plow",
        "key_turned",
        "total_inverse",
        "inverse",
        "inverse_turned",
    )
    shapes = (
        jax.ShapeDtypeStruct(vg.shape, jnp.bfloat16),
        jax.ShapeDtypeStruct((M, HD), jnp.bfloat16),
        jax.ShapeDtypeStruct((M, HD), jnp.float32),
        jax.ShapeDtypeStruct((M, HD), jnp.float32),
        jax.ShapeDtypeStruct((M, HD), jnp.bfloat16),
    )
    return kernel_call(
        mixing_kernel, shapes, [], MIXING_FLOPS, (vg, *(kept[name] for name in names))
    )


def gradient_part(vg, kept, mixed):
    names = (
        "mark_q",
        "mark_k",
        "mark_prob",
        "factor",
        "token_prob",
        "key_prob",
        "columns_turned",
        "pair",
        "weight",
        "growth",
        "last_growth",
    )
    tokens = vg.shape[0] * vg.shape[2]
    scratch = [
        pltpu.VMEM((M, M), jnp.float32),
        pltpu.VMEM((M, M), jnp.float32),
        pltpu.VMEM((tokens, HD), jnp.float32),
        pltpu.VMEM((tokens, M), jnp.float32),
    ]
    return kernel_call(
        gradient_kernel,
        jax.ShapeDtypeStruct(vg.shape, jnp.bfloat16),
        scratch,
        GRADIENT_FLOPS,
        (vg, *(kept[name] for name in names), *mixed),
    )


def exchange(packed):
    return lax.all_to_all(packed, ("seq", "head"), split_axis=0, concat_axis=0, tiled=True)


def body(queries, keys, values, out_grad):
    qk = exchange(pack(queries, keys))
    vg = exchange(pack(values, out_grad))
    kept = forward_part(qk)
    first_results, *mixed = mixing_part(vg, kept)
    second_results = gradient_part(vg, kept, mixed)
    attended, value_gradient_array = unpack(exchange(first_results))
    query_grad, key_grad = unpack(exchange(second_results))
    return attended, query_grad, key_grad, value_gradient_array


def solution(mesh):
    placement = P(("seq", "head"), None)

    def layer(queries, keys, values, out_grad):
        one_head_each = queries.shape[1] // HD == mesh.size and queries.shape[0] % CHUNK == 0
        return jax.shard_map(
            body if one_head_each else shared_body,
            mesh=mesh,
            in_specs=(placement,) * 4,
            out_specs=(placement,) * 4,
            check_vma=False,
        )(queries, keys, values, out_grad)

    return layer
```

```python
import functools

import jax
import jax.numpy as jnp
from jax import lax
from jax.experimental import pallas as pl
from jax.experimental.pallas import tpu as pltpu
from jax.sharding import PartitionSpec as P

HD = 128
M = 256
PINV_ITERS = 6
CHUNK = 256
PACK_GROUPS = 4
VMEM_LIMIT = 60 * 2**20
FORWARD_FLOPS = 10 * 10**9
MIXING_FLOPS = 2 * 10**9
GRADIENT_FLOPS = 14 * 10**9
MIXING_NAMES = (
    "key_turned",
    "token_turned",
    "total_inverse",
    "inverse",
    "inverse_turned",
    "token_low",
    "key_plow",
)
GRADIENT_NAMES = (
    "mark_q",
    "mark_k",
    "key_prob",
    "columns_turned",
    "token_prob",
    "mark_prob",
    "factor",
    "pair",
    "weight",
    "growth",
    "last_growth",
)
EARLY_NAMES = (
    "mark_q",
    "mark_k",
    "mark_prob",
    "factor",
    "token_prob",
    "token_low",
    "token_turned",
    "key_prob",
    "key_plow",
    "key_turned",
    "total_inverse",
    "columns_turned",
)


precise_setting = lax.Precision.HIGHEST


def newton_inverse(matrix):
    identity = jnp.eye(matrix.shape[0], dtype=matrix.dtype)
    factor = lax.stop_gradient(1.0 / jnp.max(jnp.sum(matrix, axis=0)))
    iterate = matrix.T * factor
    for sweep_index in range(PINV_ITERS):
        product = jnp.matmul(matrix, iterate, precision=precise_setting)
        inner_term = jnp.matmul(product, 7.0 * identity - product, precision=precise_setting)
        inner_term = jnp.matmul(product, 15.0 * identity - inner_term, precision=precise_setting)
        iterate = 0.25 * jnp.matmul(
            iterate, 13.0 * identity - inner_term, precision=precise_setting
        )
    return iterate


def share_heads(own_matrix, head_count):
    seq_index = lax.axis_index("seq")
    slot_mask = (jnp.arange(head_count, dtype=jnp.int32) == seq_index).astype(jnp.float32)
    return lax.psum(slot_mask[:, None, None] * own_matrix[None], "seq")


def shared_body(queries, keys, values, out_grad):
    query_rows, key_rows, value_rows, grad_rows = (
        lax.all_to_all(queries, "head", split_axis=1, concat_axis=0, tiled=True),
        lax.all_to_all(keys, "head", split_axis=1, concat_axis=0, tiled=True),
        lax.all_to_all(values, "head", split_axis=1, concat_axis=0, tiled=True),
        lax.all_to_all(out_grad, "head", split_axis=1, concat_axis=0, tiled=True),
    )
    tok_rows = query_rows.shape[0]
    head_count = query_rows.shape[1] // HD
    local_marks = M // lax.axis_size("seq")
    segment_len = tok_rows // local_marks
    score_scale = HD ** (-0.5)
    seq_index = lax.axis_index("seq")

    def landmark(matrix):
        summed = jnp.sum(
            matrix.reshape(local_marks, segment_len, matrix.shape[1]), axis=1, dtype=jnp.float32
        )
        return (summed / segment_len).astype(jnp.bfloat16)

    mark_queries, mark_keys = (
        lax.all_gather(landmark(query_rows), "seq", axis=0, tiled=True),
        lax.all_gather(landmark(key_rows), "seq", axis=0, tiled=True),
    )
    query_per_head = query_rows.reshape(tok_rows, head_count, HD)
    key_per_head = key_rows.reshape(tok_rows, head_count, HD)
    value_per_head = value_rows.reshape(tok_rows, head_count, HD)
    gradient_per_head = grad_rows.reshape(tok_rows, head_count, HD)
    landmark_query_heads = mark_queries.reshape(M, head_count, HD)
    landmark_key_heads = mark_keys.reshape(M, head_count, HD)
    key_score = (
        jnp.einsum(
            "pcv,gcv->cpg", landmark_query_heads, key_per_head, preferred_element_type=jnp.float32
        )
        * score_scale
    )
    key_max = lax.pmax(jnp.max(key_score, axis=-1), "seq")
    key_exp = jnp.exp(key_score - key_max[..., None])
    partial_num = jnp.einsum(
        "akq,qay->aky",
        key_exp.astype(jnp.bfloat16),
        value_per_head,
        preferred_element_type=jnp.float32,
    )
    key_total, numerator = lax.psum((jnp.sum(key_exp, axis=-1), partial_num), "seq")
    landmark_value_rows = numerator / key_total[..., None]
    token_prob = jax.nn.softmax(
        jnp.einsum(
            "jti,cti->tjc", query_per_head, landmark_key_heads, preferred_element_type=jnp.float32
        )
        * score_scale,
        axis=-1,
    )
    token_probability_lowered = token_prob.astype(jnp.bfloat16)
    mark_prob = jax.nn.softmax(
        jnp.einsum(
            "jou,iou->oji",
            landmark_query_heads,
            landmark_key_heads,
            preferred_element_type=jnp.float32,
        )
        * score_scale,
        axis=-1,
    )
    own_head = seq_index % head_count
    own_mark = lax.dynamic_index_in_dim(mark_prob, own_head, 0, keepdims=False)
    own_inverse, pull_back = jax.vjp(newton_inverse, own_mark)
    pseudo_inverse_matrix = share_heads(own_inverse, head_count)
    mixing_matrix = jnp.einsum(
        "jvy,jys->jvs", pseudo_inverse_matrix, landmark_value_rows, precision=precise_setting
    )
    mixing_matrix_lowered = mixing_matrix.astype(jnp.bfloat16)
    attended = jnp.einsum(
        "yvo,yor->vyr",
        token_probability_lowered,
        mixing_matrix_lowered,
        preferred_element_type=jnp.float32,
    ).astype(jnp.bfloat16)
    token_grad = jnp.einsum(
        "fag,aog->afo", gradient_per_head, mixing_matrix_lowered, preferred_element_type=jnp.float32
    )
    partial_mix = jnp.einsum(
        "klz,lkr->kzr",
        token_probability_lowered,
        gradient_per_head,
        preferred_element_type=jnp.float32,
    )
    mixing_matrix_gradient = lax.psum(partial_mix, "seq")
    token_score_gradient = (
        token_prob * (token_grad - jnp.sum(token_grad * token_prob, axis=-1, keepdims=True))
    ).astype(jnp.bfloat16)
    direct_qgrad = (
        jnp.einsum(
            "ufg,guc->fuc",
            token_score_gradient,
            landmark_key_heads,
            preferred_element_type=jnp.float32,
        )
        * score_scale
    )
    mark_kgrad_f = (
        jnp.einsum(
            "xgi,gxy->ixy", token_score_gradient, query_per_head, preferred_element_type=jnp.float32
        )
        * score_scale
    )
    pseudo_inverse_gradient = jnp.einsum(
        "ktu,kyu->kty", mixing_matrix_gradient, landmark_value_rows, precision=precise_setting
    )
    landmark_value_gradient = jnp.einsum(
        "lrb,lrz->lbz", pseudo_inverse_matrix, mixing_matrix_gradient, precision=precise_setting
    )
    own_igrad = lax.dynamic_index_in_dim(pseudo_inverse_gradient, own_head, 0, keepdims=False)
    (own_mgrad,) = pull_back(own_igrad)
    mark_grad = share_heads(own_mgrad, head_count)
    mark_sgrad = mark_prob * (mark_grad - jnp.sum(mark_grad * mark_prob, axis=-1, keepdims=True))
    first_mark = seq_index * local_marks
    score_gradient_rows = lax.dynamic_slice_in_dim(mark_sgrad, first_mark, local_marks, 1)
    score_gradient_columns = lax.dynamic_slice_in_dim(mark_sgrad, first_mark, local_marks, 2)
    own_qgrad_a = (
        jnp.einsum(
            "txs,ste->xte",
            score_gradient_rows,
            landmark_key_heads.astype(jnp.float32),
            precision=precise_setting,
        )
        * score_scale
    )
    own_kgrad_a = (
        jnp.einsum(
            "eaj,aev->jev",
            score_gradient_columns,
            landmark_query_heads.astype(jnp.float32),
            precision=precise_setting,
        )
        * score_scale
    )
    landmark_value_lowered = landmark_value_gradient.astype(jnp.bfloat16)
    key_prob = key_exp / key_total[..., None]
    key_probability_lowered = key_prob.astype(jnp.bfloat16)
    value_gradient_array = jnp.einsum(
        "zct,zcj->tzj",
        key_probability_lowered,
        landmark_value_lowered,
        preferred_element_type=jnp.float32,
    )
    key_direct_gradient = jnp.einsum(
        "exb,geb->exg", landmark_value_lowered, value_per_head, preferred_element_type=jnp.float32
    )
    row_total = lax.psum(jnp.sum(key_prob * key_direct_gradient, axis=-1), "seq")
    key_score_gradient = (key_prob * (key_direct_gradient - row_total[..., None])).astype(
        jnp.bfloat16
    )
    direct_kgrad = (
        jnp.einsum(
            "pbo,bpx->opx",
            key_score_gradient,
            landmark_query_heads,
            preferred_element_type=jnp.float32,
        )
        * score_scale
    )
    mark_qgrad_b = (
        jnp.einsum(
            "cbj,jcp->bcp", key_score_gradient, key_per_head, preferred_element_type=jnp.float32
        )
        * score_scale
    )
    own_kgrad_f, own_qgrad_b = (
        lax.psum_scatter(mark_kgrad_f, "seq", scatter_dimension=0, tiled=True),
        lax.psum_scatter(mark_qgrad_b, "seq", scatter_dimension=0, tiled=True),
    )
    mark_qtotal = (own_qgrad_a + own_qgrad_b) / segment_len
    mark_ktotal = (own_kgrad_a + own_kgrad_f) / segment_len
    query_grad = (
        direct_qgrad.reshape(local_marks, segment_len, head_count, HD) + mark_qtotal[:, None]
    )
    key_grad = direct_kgrad.reshape(local_marks, segment_len, head_count, HD) + mark_ktotal[:, None]
    width = head_count * HD
    results = (
        attended.reshape(tok_rows, width),
        query_grad.astype(jnp.bfloat16).reshape(tok_rows, width),
        key_grad.astype(jnp.bfloat16).reshape(tok_rows, width),
        value_gradient_array.astype(jnp.bfloat16).reshape(tok_rows, width),
    )
    attended_out, query_out, key_out, value_out = (
        lax.all_to_all(results[0], "head", split_axis=0, concat_axis=1, tiled=True),
        lax.all_to_all(results[1], "head", split_axis=0, concat_axis=1, tiled=True),
        lax.all_to_all(results[2], "head", split_axis=0, concat_axis=1, tiled=True),
        lax.all_to_all(results[3], "head", split_axis=0, concat_axis=1, tiled=True),
    )
    return (attended_out, query_out, key_out, value_out)


def dims_of(rows):
    tokens = rows.shape[0] * rows.shape[2]
    return tokens, rows.shape[2], tokens // CHUNK


def halves(matrix):
    high = matrix.astype(jnp.bfloat16)
    return high, (matrix - high.astype(jnp.float32)).astype(jnp.bfloat16)


def wide_dot(left, right):
    return jnp.dot(left, right, preferred_element_type=jnp.float32)


def wide_dot_nt(left, right):
    return lax.dot_general(
        left, right, (((1,), (1,)), ((), ())), preferred_element_type=jnp.float32
    )


def split_dot(left, right):
    left_high, left_low = left
    right_high, right_low = right
    return wide_dot(
        jnp.concatenate([left_high, left_high, left_low], axis=1),
        jnp.concatenate([right_high, right_low, right_high], axis=0),
    )


def split_dot_nt(left, right):
    left_high, left_low = left
    right_high, right_low = right
    return wide_dot_nt(
        jnp.concatenate([left_high, left_high, left_low], axis=1),
        jnp.concatenate([right_high, right_low, right_high], axis=1),
    )


def identity_matrix():
    return (
        lax.broadcasted_iota(jnp.int32, (M, M), 0) == lax.broadcasted_iota(jnp.int32, (M, M), 1)
    ).astype(jnp.float32)


def chunk_of(ref, slot, index):
    rows = ref.shape[2]
    per = CHUNK // rows
    return ref[pl.ds(index * per, per), slot].reshape(CHUNK, HD)


def store_chunk(ref, slot, index, value):
    rows = ref.shape[2]
    per = CHUNK // rows
    ref[pl.ds(index * per, per), slot] = value.reshape(per, rows, HD)


def columns(index):
    return pl.ds(pl.multiple_of(index * CHUNK, CHUNK), CHUNK)


def pack_kernel(first_ref, second_ref, out_ref, rows_s, packed_s, in_done, out_done):
    heads = out_ref.shape[0]
    group = heads // PACK_GROUPS
    reads, writes = [], []
    for index in range(PACK_GROUPS):
        for slot, ref in enumerate((first_ref, second_ref)):
            place = pl.ds(index * group * HD, group * HD)
            reads.append(
                pltpu.make_async_copy(
                    ref.at[:, place], rows_s.at[slot, :, place], in_done.at[slot, index]
                )
            )
        place = pl.ds(index * group, group)
        writes.append(
            pltpu.make_async_copy(packed_s.at[place], out_ref.at[place], out_done.at[index])
        )
    for copy in reads:
        copy.start()
    for index in range(PACK_GROUPS):
        for slot in range(2):
            reads[2 * index + slot].wait()
            for head in range(index * group, (index + 1) * group):
                packed_s[head, slot] = rows_s[slot, :, head * HD : (head + 1) * HD]
        writes[index].start()
    for copy in writes:
        copy.wait()


def unpack_kernel(packed_ref, first_ref, second_ref, packed_s, rows_s, in_done, out_done):
    heads = packed_ref.shape[0]
    group = heads // PACK_GROUPS
    reads, writes = [], []
    for index in range(PACK_GROUPS):
        place = pl.ds(index * group, group)
        reads.append(
            pltpu.make_async_copy(packed_ref.at[place], packed_s.at[place], in_done.at[index])
        )
        for slot, ref in enumerate((first_ref, second_ref)):
            place = pl.ds(index * group * HD, group * HD)
            writes.append(
                pltpu.make_async_copy(
                    rows_s.at[slot, :, place], ref.at[:, place], out_done.at[slot, index]
                )
            )
    for copy in reads:
        copy.start()
    for index in range(PACK_GROUPS):
        reads[index].wait()
        for slot in range(2):
            for head in range(index * group, (index + 1) * group):
                rows_s[slot, :, head * HD : (head + 1) * HD] = packed_s[head, slot]
            writes[2 * index + slot].start()
    for copy in writes:
        copy.wait()


def forward_kernel(
    names,
    qk_hbm,
    *refs,
):
    count = len(names)
    homes = dict(zip(names, refs[:count]))
    held = dict(zip(names, refs[count : 2 * count]))
    qk_ref, power_s, iterate_s, in_done, out_done = refs[2 * count :]
    copies = {
        name: pltpu.make_async_copy(held[name], homes[name], out_done.at[index])
        for index, name in enumerate(names)
    }
    arrive = pltpu.make_async_copy(qk_hbm, qk_ref, in_done)
    arrive.start()
    arrive.wait()
    (
        mark_q_ref,
        mark_k_ref,
        mark_prob_ref,
        factor_ref,
        token_prob_ref,
        token_low_ref,
        token_turned_ref,
        key_prob_ref,
        key_plow_ref,
        key_turned_ref,
        total_inverse_ref,
        columns_turned_ref,
        pair_ref,
        weight_ref,
        growth_ref,
        inverse_ref,
        inverse_turned_ref,
        last_growth_ref,
    ) = (held[name] for name in names)
    tokens, rows, chunks = dims_of(qk_ref)
    segment_len = tokens // M
    marks_per = CHUNK // segment_len
    score_scale = HD ** (-0.5)
    member = (
        lax.broadcasted_iota(jnp.int32, (marks_per, CHUNK), 1) // segment_len
        == lax.broadcasted_iota(jnp.int32, (marks_per, CHUNK), 0)
    ).astype(jnp.bfloat16)
    for index in range(chunks):
        both = jnp.concatenate([chunk_of(qk_ref, 0, index), chunk_of(qk_ref, 1, index)], axis=1)
        mean = (wide_dot(member, both) / segment_len).astype(jnp.bfloat16)
        mark_q_ref[index * marks_per : (index + 1) * marks_per] = mean[:, :HD]
        mark_k_ref[index * marks_per : (index + 1) * marks_per] = mean[:, HD:]
    landmark_q, landmark_k = mark_q_ref[...], mark_k_ref[...]

    mark_score = wide_dot_nt(landmark_q, landmark_k) * score_scale
    mark_exp = jnp.exp(mark_score - jnp.max(mark_score, axis=1, keepdims=True))
    mark_prob = mark_exp / jnp.sum(mark_exp, axis=1, keepdims=True)
    mark_prob_ref[...] = mark_prob
    factor = 1.0 / jnp.max(jnp.sum(mark_prob, axis=0, keepdims=True), axis=1, keepdims=True)
    factor_ref[...] = jnp.broadcast_to(factor, factor_ref.shape)
    mark_halves = halves(mark_prob)
    power_s[...] = split_dot_nt(mark_halves, mark_halves) * factor
    iterate_s[0:M] = mark_prob.T * factor
    iterate_s[M:] = identity_matrix()

    def scores(index, key_max):
        query_chunk, key_chunk = chunk_of(qk_ref, 0, index), chunk_of(qk_ref, 1, index)
        place = columns(index)
        columns_turned_ref[0, :, place] = query_chunk.T
        columns_turned_ref[1, :, place] = key_chunk.T
        score = wide_dot_nt(query_chunk, landmark_k) * score_scale
        grown = jnp.exp(score - jnp.max(score, axis=1, keepdims=True))
        prob = grown / jnp.sum(grown, axis=1, keepdims=True)
        token_prob_ref[place] = prob
        low = prob.astype(jnp.bfloat16)
        token_low_ref[place] = low
        token_turned_ref[:, place] = low.T
        key_score = wide_dot_nt(key_chunk, landmark_q) * score_scale
        key_prob_ref[place] = key_score
        return jnp.maximum(key_max, jnp.max(key_score, axis=0, keepdims=True))

    key_max = lax.fori_loop(0, chunks, scores, jnp.full((1, M), -jnp.inf, jnp.float32))

    def grow(index, key_total):
        place = columns(index)
        grown = jnp.exp(key_prob_ref[place] - key_max)
        key_prob_ref[place] = grown
        key_turned_ref[:, place] = grown.astype(jnp.bfloat16).T
        return key_total + jnp.sum(grown, axis=0, keepdims=True)

    key_total = lax.fori_loop(0, chunks, grow, jnp.zeros((1, M), jnp.float32))
    total_inverse = 1.0 / key_total
    total_inverse_ref[...] = jnp.broadcast_to(total_inverse, (HD, M)).T

    def normalise(index, carry):
        place = columns(index)
        prob = key_prob_ref[place] * total_inverse
        key_prob_ref[place] = prob
        key_plow_ref[place] = prob.astype(jnp.bfloat16)
        return carry

    lax.fori_loop(0, chunks, normalise, 0)
    for name in EARLY_NAMES:
        copies[name].start()

    def newton(sweep, carry):
        power = power_s[...]
        power_high, power_low = halves(power)
        square = split_dot((power_high, power_low), (power_high, power_low))
        square_halves = halves(square)
        pair = (
            jnp.concatenate([power_high, square_halves[0]], axis=0),
            jnp.concatenate([power_low, square_halves[1]], axis=0),
        )
        pair_ref[sweep, 0], pair_ref[sweep, 1] = pair
        higher = split_dot(pair, square_halves)
        cube, fourth = higher[:M], higher[M:]
        weight = halves(
            0.25 * (13.0 * identity_matrix() - 15.0 * power + 7.0 * square - cube)
        )
        power_s[...] = 0.25 * (13.0 * power - 15.0 * square + 7.0 * cube - fourth)
        weight_ref[sweep, 0], weight_ref[sweep, 1] = weight
        iterate = halves(iterate_s[...])
        growth_ref[sweep, 0], growth_ref[sweep, 1] = iterate[0][M:], iterate[1][M:]
        iterate_s[...] = split_dot(iterate, weight)
        return carry

    lax.fori_loop(0, PINV_ITERS, newton, 0)
    inverse = iterate_s[0:M]
    inverse_ref[0], inverse_ref[1] = halves(inverse)
    inverse_turned_ref[0], inverse_turned_ref[1] = halves(inverse.T)
    last_growth_ref[0], last_growth_ref[1] = halves(iterate_s[M:])
    for name in names:
        if name not in EARLY_NAMES:
            copies[name].start()
    for name in names:
        copies[name].wait()


def start_reads(sources, held, done):
    reads = [
        pltpu.make_async_copy(source, ref, done.at[index])
        for index, (source, ref) in enumerate(zip(sources, held))
    ]
    for read in reads:
        read.start()
    return reads


def mixing_kernel(*refs):
    count = len(MIXING_NAMES) + 1
    sources, homes, held = refs[:count], refs[count : count + 5], refs[count + 5 : 2 * count + 5]
    results, (in_done, out_done) = refs[2 * count + 5 : 2 * count + 10], refs[2 * count + 10 :]
    reads = start_reads(sources, held, in_done)
    (
        vg_ref,
        key_turned_ref,
        token_turned_ref,
        total_inverse_ref,
        inverse_ref,
        inverse_turned_ref,
        token_low_ref,
        key_plow_ref,
    ) = held
    out_ref, mixing_low_ref, mixing_grad_ref, mark_values_ref, values_low_ref = results
    writes = [
        pltpu.make_async_copy(result, home, out_done.at[index])
        for index, (result, home) in enumerate(zip(results, homes))
    ]
    tokens, rows, chunks = dims_of(vg_ref)
    for read in reads[:6]:
        read.wait()
    values = vg_ref[:, 0].reshape(tokens, HD)
    out_grad = vg_ref[:, 1].reshape(tokens, HD)
    landmark_values = wide_dot(key_turned_ref[...], values) * total_inverse_ref[...]
    mixing_grad = wide_dot(token_turned_ref[...], out_grad)
    mark_values_ref[...] = landmark_values
    mixing_grad_ref[...] = mixing_grad
    mixing_low = split_dot(
        (inverse_ref[0], inverse_ref[1]), halves(landmark_values)
    ).astype(jnp.bfloat16)
    values_low = split_dot(
        (inverse_turned_ref[0], inverse_turned_ref[1]), halves(mixing_grad)
    ).astype(jnp.bfloat16)
    mixing_low_ref[...] = mixing_low
    values_low_ref[...] = values_low
    for write in writes[1:]:
        write.start()
    for read in reads[6:]:
        read.wait()

    def emit(index, carry):
        place = columns(index)
        store_chunk(
            out_ref, 0, index, wide_dot(token_low_ref[place], mixing_low).astype(jnp.bfloat16)
        )
        store_chunk(
            out_ref, 1, index, wide_dot(key_plow_ref[place], values_low).astype(jnp.bfloat16)
        )
        return carry

    lax.fori_loop(0, chunks, emit, 0)
    writes[0].start()
    for write in writes:
        write.wait()


def gradient_kernel(*refs):
    count = len(GRADIENT_NAMES) + 5
    sources, home, held = refs[:count], refs[count], refs[count + 1 : 2 * count + 1]
    out_ref, power_s, growth_s, query_s, direct_s, kept_s, in_done, out_done = refs[2 * count + 1 :]
    reads = start_reads(sources, held, in_done)
    (
        values_low_ref,
        mixing_low_ref,
        vg_ref,
        mark_q_ref,
        mark_k_ref,
        key_prob_ref,
        columns_turned_ref,
        token_prob_ref,
        mark_prob_ref,
        factor_ref,
        pair_ref,
        weight_ref,
        growth_ref,
        last_growth_ref,
        mixing_grad_ref,
        mark_values_ref,
    ) = held
    tokens, rows, chunks = dims_of(vg_ref)
    segment_len = tokens // M
    marks_per = CHUNK // segment_len
    score_scale = HD ** (-0.5)
    for read in reads[:8]:
        read.wait()
    landmark_q, landmark_k = mark_q_ref[...], mark_k_ref[...]

    values_low = values_low_ref[...]

    def key_rows(index, row_total):
        place = columns(index)
        key_dgrad = wide_dot_nt(chunk_of(vg_ref, 0, index), values_low)
        kept_s[place] = key_dgrad
        return row_total + jnp.sum(key_prob_ref[place] * key_dgrad, axis=0, keepdims=True)

    row_total = lax.fori_loop(0, chunks, key_rows, jnp.zeros((1, M), jnp.float32))

    def key_side(index, total):
        place = columns(index)
        key_sgrad = (key_prob_ref[place] * (kept_s[place] - row_total)).astype(jnp.bfloat16)
        direct_s[place] = wide_dot(key_sgrad, landmark_q) * score_scale
        return total + wide_dot(columns_turned_ref[1, :, place], key_sgrad)

    mark_qgrad_b = lax.fori_loop(0, chunks, key_side, jnp.zeros((HD, M), jnp.float32))
    mixing_low = mixing_low_ref[...]

    def token_side(index, total):
        place = columns(index)
        prob = token_prob_ref[place]
        token_grad = wide_dot_nt(chunk_of(vg_ref, 1, index), mixing_low)
        token_sgrad = (
            prob * (token_grad - jnp.sum(token_grad * prob, axis=1, keepdims=True))
        ).astype(jnp.bfloat16)
        query_s[place] = wide_dot(token_sgrad, landmark_k) * score_scale
        return total + wide_dot(columns_turned_ref[0, :, place], token_sgrad)

    mark_kgrad_f = lax.fori_loop(0, chunks, token_side, jnp.zeros((HD, M), jnp.float32))

    for read in reads[8:]:
        read.wait()
    mark_prob = mark_prob_ref[...]
    mark_halves = halves(mark_prob)
    factor = factor_ref[0:1, 0:1]
    inverse_grad = split_dot_nt(halves(mixing_grad_ref[...]), halves(mark_values_ref[...]))
    inverse_grad_halves = halves(inverse_grad)
    toward = split_dot(mark_halves, inverse_grad_halves) * factor
    power_s[...] = 0.5 * (toward + toward.T)
    growth_s[...] = jnp.zeros((M, M), jnp.float32)

    def newton(sweep, carry):
        power = power_s[...]
        pair = (pair_ref[sweep, 0], pair_ref[sweep, 1])
        first = split_dot(pair, halves(power))
        square = first[:M] + first[:M].T
        second = split_dot(pair, halves(square))
        cube = first[M:].T + second[:M]
        fourth = second[M:] + second[M:].T
        weight = halves(0.25 * (7.0 * square - 15.0 * power - cube))
        power_s[...] = 0.25 * (13.0 * power - 15.0 * square + 7.0 * cube - fourth)
        grown_high, grown_low = halves(growth_s[...])
        held_high, held_low = growth_ref[sweep, 0], growth_ref[sweep, 1]
        held_weight_high, held_weight_low = weight_ref[sweep, 0], weight_ref[sweep, 1]
        growth_s[...] = wide_dot(
            jnp.concatenate(
                [grown_high, grown_high, grown_low, held_high, held_high, held_low], axis=1
            ),
            jnp.concatenate(
                [
                    held_weight_high,
                    held_weight_low,
                    held_weight_high,
                    weight[0],
                    weight[1],
                    weight[0],
                ],
                axis=0,
            ),
        )
        return carry

    lax.fori_loop(0, PINV_ITERS, newton, 0)
    growth = growth_s[...]
    mark_grad = factor * (
        split_dot_nt((last_growth_ref[0], last_growth_ref[1]), inverse_grad_halves)
        + split_dot(halves(growth + growth.T), mark_halves)
    )
    mark_sgrad = mark_prob * (mark_grad - jnp.sum(mark_grad * mark_prob, axis=1, keepdims=True))

    def marks_dot(left, right):
        high, low = halves(left)
        return wide_dot(
            jnp.concatenate([high, low], axis=1), jnp.concatenate([right, right], axis=0)
        )

    mark_qgrad_a = marks_dot(mark_sgrad, landmark_k)
    mark_kgrad_a = marks_dot(mark_sgrad.T, landmark_q)
    kept_s[0:M, 0:HD] = (mark_qgrad_a + mark_qgrad_b.T) * (score_scale / segment_len)
    kept_s[0:M, HD:] = (mark_kgrad_a + mark_kgrad_f.T) * (score_scale / segment_len)

    def spread(direct, marks):
        wide = jnp.broadcast_to(marks[:, None], (marks_per, segment_len, HD))
        return (direct + wide.reshape(CHUNK, HD)).astype(jnp.bfloat16)

    def finish(index, carry):
        marks = kept_s[pl.ds(pl.multiple_of(index * marks_per, marks_per), marks_per)]
        place = columns(index)
        store_chunk(out_ref, 0, index, spread(query_s[place], marks[:, :HD]))
        store_chunk(out_ref, 1, index, spread(direct_s[place], marks[:, HD:]))
        return carry

    lax.fori_loop(0, chunks, finish, 0)
    write = pltpu.make_async_copy(out_ref, home, out_done)
    write.start()
    write.wait()


def kernel_call(kernel, out_shape, scratch, flops, operands):
    moved = sum(x.size * x.dtype.itemsize for x in operands)
    in_place = pl.BlockSpec(memory_space=pl.ANY)
    return pl.pallas_call(
        kernel,
        out_shape=out_shape,
        in_specs=[in_place] * len(operands),
        out_specs=jax.tree.map(lambda _: in_place, out_shape),
        scratch_shapes=scratch,
        compiler_params=pltpu.CompilerParams(vmem_limit_bytes=VMEM_LIMIT),
        cost_estimate=pl.CostEstimate(flops=flops, bytes_accessed=moved, transcendentals=0),
    )(*operands)


def in_vmem(array):
    return pltpu.VMEM(array.shape, array.dtype)


def pack(first, second):
    rows, width = first.shape
    heads = width // HD
    shape = jax.ShapeDtypeStruct((heads, 2, rows, HD), first.dtype)
    scratch = [
        pltpu.VMEM((2, rows, width), first.dtype),
        pltpu.VMEM((heads, 2, rows, HD), first.dtype),
        pltpu.SemaphoreType.DMA((2, PACK_GROUPS)),
        pltpu.SemaphoreType.DMA((PACK_GROUPS,)),
    ]
    return kernel_call(pack_kernel, shape, scratch, 0, (first, second))


def unpack(packed):
    heads, _, rows, _ = packed.shape
    shape = jax.ShapeDtypeStruct((rows, heads * HD), packed.dtype)
    scratch = [
        pltpu.VMEM((heads, 2, rows, HD), packed.dtype),
        pltpu.VMEM((2, rows, heads * HD), packed.dtype),
        pltpu.SemaphoreType.DMA((PACK_GROUPS,)),
        pltpu.SemaphoreType.DMA((2, PACK_GROUPS)),
    ]
    return kernel_call(unpack_kernel, (shape, shape), scratch, 0, (packed,))


def forward_part(qk):
    tokens = qk.shape[0] * qk.shape[2]

    def low(*shape):
        return jax.ShapeDtypeStruct(shape, jnp.bfloat16)

    def wide(*shape):
        return jax.ShapeDtypeStruct(shape, jnp.float32)

    shapes = dict(
        mark_q=low(M, HD),
        mark_k=low(M, HD),
        mark_prob=wide(M, M),
        factor=wide(8, HD),
        token_prob=wide(tokens, M),
        token_low=low(tokens, M),
        token_turned=low(M, tokens),
        key_prob=wide(tokens, M),
        key_plow=low(tokens, M),
        key_turned=low(M, tokens),
        total_inverse=wide(M, HD),
        columns_turned=low(2, HD, tokens),
        pair=low(PINV_ITERS, 2, 2 * M, M),
        weight=low(PINV_ITERS, 2, M, M),
        growth=low(PINV_ITERS, 2, M, M),
        inverse=low(2, M, M),
        inverse_turned=low(2, M, M),
        last_growth=low(2, M, M),
    )
    scratch = [
        *(in_vmem(shape) for shape in shapes.values()),
        in_vmem(qk),
        pltpu.VMEM((M, M), jnp.float32),
        pltpu.VMEM((2 * M, M), jnp.float32),
        pltpu.SemaphoreType.DMA,
        pltpu.SemaphoreType.DMA((len(shapes),)),
    ]
    results = kernel_call(
        functools.partial(forward_kernel, tuple(shapes)),
        tuple(shapes.values()),
        scratch,
        FORWARD_FLOPS,
        (qk,),
    )
    return dict(zip(shapes, results))


def mixing_part(vg, kept):
    shapes = (
        jax.ShapeDtypeStruct(vg.shape, jnp.bfloat16),
        jax.ShapeDtypeStruct((M, HD), jnp.bfloat16),
        jax.ShapeDtypeStruct((M, HD), jnp.float32),
        jax.ShapeDtypeStruct((M, HD), jnp.float32),
        jax.ShapeDtypeStruct((M, HD), jnp.bfloat16),
    )
    operands = (vg, *(kept[name] for name in MIXING_NAMES))
    scratch = [
        *(in_vmem(array) for array in (*operands, *shapes)),
        pltpu.SemaphoreType.DMA((len(operands),)),
        pltpu.SemaphoreType.DMA((len(shapes),)),
    ]
    return kernel_call(mixing_kernel, shapes, scratch, MIXING_FLOPS, operands)


def gradient_part(vg, kept, mixed):
    mixing_low, mixing_grad, mark_values, values_low = mixed
    operands = (
        values_low,
        mixing_low,
        vg,
        *(kept[name] for name in GRADIENT_NAMES),
        mixing_grad,
        mark_values,
    )
    tokens = vg.shape[0] * vg.shape[2]
    scratch = [
        *(in_vmem(array) for array in (*operands, vg)),
        pltpu.VMEM((M, M), jnp.float32),
        pltpu.VMEM((M, M), jnp.float32),
        pltpu.VMEM((tokens, HD), jnp.float32),
        pltpu.VMEM((tokens, HD), jnp.float32),
        pltpu.VMEM((tokens, M), jnp.float32),
        pltpu.SemaphoreType.DMA((len(operands),)),
        pltpu.SemaphoreType.DMA,
    ]
    shape = jax.ShapeDtypeStruct(vg.shape, jnp.bfloat16)
    return kernel_call(gradient_kernel, shape, scratch, GRADIENT_FLOPS, operands)


def exchange(packed):
    return lax.all_to_all(packed, ("seq", "head"), split_axis=0, concat_axis=0, tiled=True)


def body(queries, keys, values, out_grad):
    qk = exchange(pack(queries, keys))
    vg = exchange(pack(values, out_grad))
    kept = forward_part(qk)
    first_results, *mixed = mixing_part(vg, kept)
    second_results = gradient_part(vg, kept, mixed)
    attended, value_gradient_array = unpack(exchange(first_results))
    query_grad, key_grad = unpack(exchange(second_results))
    return attended, query_grad, key_grad, value_gradient_array


def solution(mesh):
    placement = P(("seq", "head"), None)

    def layer(queries, keys, values, out_grad):
        one_head_each = queries.shape[1] // HD == mesh.size and queries.shape[0] % CHUNK == 0
        return jax.shard_map(
            body if one_head_each else shared_body,
            mesh=mesh,
            in_specs=(placement,) * 4,
            out_specs=(placement,) * 4,
            check_vma=False,
        )(queries, keys, values, out_grad)

    return layer
```

```python
import functools
from types import SimpleNamespace

import jax
import jax.numpy as jnp
from jax import lax
from jax.experimental import pallas as pl
from jax.experimental.pallas import tpu as pltpu
from jax.sharding import PartitionSpec as P

HD = 128
M = 256
PINV_ITERS = 6
CHUNK = 256
PACK_GROUPS = 4
HALF = M // 2
SWAP = ((0, 1), (1, 0))
VMEM_LIMIT = 60 * 2**20


precise_setting = lax.Precision.HIGHEST


def newton_inverse(matrix):
    identity = jnp.eye(matrix.shape[0], dtype=matrix.dtype)
    factor = lax.stop_gradient(1.0 / jnp.max(jnp.sum(matrix, axis=0)))
    iterate = matrix.T * factor
    for sweep_index in range(PINV_ITERS):
        product = jnp.matmul(matrix, iterate, precision=precise_setting)
        inner_term = jnp.matmul(product, 7.0 * identity - product, precision=precise_setting)
        inner_term = jnp.matmul(product, 15.0 * identity - inner_term, precision=precise_setting)
        iterate = 0.25 * jnp.matmul(
            iterate, 13.0 * identity - inner_term, precision=precise_setting
        )
    return iterate


def share_heads(own_matrix, head_count):
    seq_index = lax.axis_index("seq")
    slot_mask = (jnp.arange(head_count, dtype=jnp.int32) == seq_index).astype(jnp.float32)
    return lax.psum(slot_mask[:, None, None] * own_matrix[None], "seq")


def shared_body(queries, keys, values, out_grad):
    query_rows, key_rows, value_rows, grad_rows = (
        lax.all_to_all(queries, "head", split_axis=1, concat_axis=0, tiled=True),
        lax.all_to_all(keys, "head", split_axis=1, concat_axis=0, tiled=True),
        lax.all_to_all(values, "head", split_axis=1, concat_axis=0, tiled=True),
        lax.all_to_all(out_grad, "head", split_axis=1, concat_axis=0, tiled=True),
    )
    tok_rows = query_rows.shape[0]
    head_count = query_rows.shape[1] // HD
    local_marks = M // lax.axis_size("seq")
    segment_len = tok_rows // local_marks
    score_scale = HD ** (-0.5)
    seq_index = lax.axis_index("seq")

    def landmark(matrix):
        summed = jnp.sum(
            matrix.reshape(local_marks, segment_len, matrix.shape[1]), axis=1, dtype=jnp.float32
        )
        return (summed / segment_len).astype(jnp.bfloat16)

    mark_queries, mark_keys = (
        lax.all_gather(landmark(query_rows), "seq", axis=0, tiled=True),
        lax.all_gather(landmark(key_rows), "seq", axis=0, tiled=True),
    )
    query_per_head = query_rows.reshape(tok_rows, head_count, HD)
    key_per_head = key_rows.reshape(tok_rows, head_count, HD)
    value_per_head = value_rows.reshape(tok_rows, head_count, HD)
    gradient_per_head = grad_rows.reshape(tok_rows, head_count, HD)
    landmark_query_heads = mark_queries.reshape(M, head_count, HD)
    landmark_key_heads = mark_keys.reshape(M, head_count, HD)
    key_score = (
        jnp.einsum(
            "pcv,gcv->cpg", landmark_query_heads, key_per_head, preferred_element_type=jnp.float32
        )
        * score_scale
    )
    key_max = lax.pmax(jnp.max(key_score, axis=-1), "seq")
    key_exp = jnp.exp(key_score - key_max[..., None])
    partial_num = jnp.einsum(
        "akq,qay->aky",
        key_exp.astype(jnp.bfloat16),
        value_per_head,
        preferred_element_type=jnp.float32,
    )
    key_total, numerator = lax.psum((jnp.sum(key_exp, axis=-1), partial_num), "seq")
    landmark_value_rows = numerator / key_total[..., None]
    token_prob = jax.nn.softmax(
        jnp.einsum(
            "jti,cti->tjc", query_per_head, landmark_key_heads, preferred_element_type=jnp.float32
        )
        * score_scale,
        axis=-1,
    )
    token_probability_lowered = token_prob.astype(jnp.bfloat16)
    mark_prob = jax.nn.softmax(
        jnp.einsum(
            "jou,iou->oji",
            landmark_query_heads,
            landmark_key_heads,
            preferred_element_type=jnp.float32,
        )
        * score_scale,
        axis=-1,
    )
    own_head = seq_index % head_count
    own_mark = lax.dynamic_index_in_dim(mark_prob, own_head, 0, keepdims=False)
    own_inverse, pull_back = jax.vjp(newton_inverse, own_mark)
    pseudo_inverse_matrix = share_heads(own_inverse, head_count)
    mixing_matrix = jnp.einsum(
        "jvy,jys->jvs", pseudo_inverse_matrix, landmark_value_rows, precision=precise_setting
    )
    mixing_matrix_lowered = mixing_matrix.astype(jnp.bfloat16)
    attended = jnp.einsum(
        "yvo,yor->vyr",
        token_probability_lowered,
        mixing_matrix_lowered,
        preferred_element_type=jnp.float32,
    ).astype(jnp.bfloat16)
    token_grad = jnp.einsum(
        "fag,aog->afo", gradient_per_head, mixing_matrix_lowered, preferred_element_type=jnp.float32
    )
    partial_mix = jnp.einsum(
        "klz,lkr->kzr",
        token_probability_lowered,
        gradient_per_head,
        preferred_element_type=jnp.float32,
    )
    mixing_matrix_gradient = lax.psum(partial_mix, "seq")
    token_score_gradient = (
        token_prob * (token_grad - jnp.sum(token_grad * token_prob, axis=-1, keepdims=True))
    ).astype(jnp.bfloat16)
    direct_qgrad = (
        jnp.einsum(
            "ufg,guc->fuc",
            token_score_gradient,
            landmark_key_heads,
            preferred_element_type=jnp.float32,
        )
        * score_scale
    )
    mark_kgrad_f = (
        jnp.einsum(
            "xgi,gxy->ixy", token_score_gradient, query_per_head, preferred_element_type=jnp.float32
        )
        * score_scale
    )
    pseudo_inverse_gradient = jnp.einsum(
        "ktu,kyu->kty", mixing_matrix_gradient, landmark_value_rows, precision=precise_setting
    )
    landmark_value_gradient = jnp.einsum(
        "lrb,lrz->lbz", pseudo_inverse_matrix, mixing_matrix_gradient, precision=precise_setting
    )
    own_igrad = lax.dynamic_index_in_dim(pseudo_inverse_gradient, own_head, 0, keepdims=False)
    (own_mgrad,) = pull_back(own_igrad)
    mark_grad = share_heads(own_mgrad, head_count)
    mark_sgrad = mark_prob * (mark_grad - jnp.sum(mark_grad * mark_prob, axis=-1, keepdims=True))
    first_mark = seq_index * local_marks
    score_gradient_rows = lax.dynamic_slice_in_dim(mark_sgrad, first_mark, local_marks, 1)
    score_gradient_columns = lax.dynamic_slice_in_dim(mark_sgrad, first_mark, local_marks, 2)
    own_qgrad_a = (
        jnp.einsum(
            "txs,ste->xte",
            score_gradient_rows,
            landmark_key_heads.astype(jnp.float32),
            precision=precise_setting,
        )
        * score_scale
    )
    own_kgrad_a = (
        jnp.einsum(
            "eaj,aev->jev",
            score_gradient_columns,
            landmark_query_heads.astype(jnp.float32),
            precision=precise_setting,
        )
        * score_scale
    )
    landmark_value_lowered = landmark_value_gradient.astype(jnp.bfloat16)
    key_prob = key_exp / key_total[..., None]
    key_probability_lowered = key_prob.astype(jnp.bfloat16)
    value_gradient_array = jnp.einsum(
        "zct,zcj->tzj",
        key_probability_lowered,
        landmark_value_lowered,
        preferred_element_type=jnp.float32,
    )
    key_direct_gradient = jnp.einsum(
        "exb,geb->exg", landmark_value_lowered, value_per_head, preferred_element_type=jnp.float32
    )
    row_total = lax.psum(jnp.sum(key_prob * key_direct_gradient, axis=-1), "seq")
    key_score_gradient = (key_prob * (key_direct_gradient - row_total[..., None])).astype(
        jnp.bfloat16
    )
    direct_kgrad = (
        jnp.einsum(
            "pbo,bpx->opx",
            key_score_gradient,
            landmark_query_heads,
            preferred_element_type=jnp.float32,
        )
        * score_scale
    )
    mark_qgrad_b = (
        jnp.einsum(
            "cbj,jcp->bcp", key_score_gradient, key_per_head, preferred_element_type=jnp.float32
        )
        * score_scale
    )
    own_kgrad_f, own_qgrad_b = (
        lax.psum_scatter(mark_kgrad_f, "seq", scatter_dimension=0, tiled=True),
        lax.psum_scatter(mark_qgrad_b, "seq", scatter_dimension=0, tiled=True),
    )
    mark_qtotal = (own_qgrad_a + own_qgrad_b) / segment_len
    mark_ktotal = (own_kgrad_a + own_kgrad_f) / segment_len
    query_grad = (
        direct_qgrad.reshape(local_marks, segment_len, head_count, HD) + mark_qtotal[:, None]
    )
    key_grad = direct_kgrad.reshape(local_marks, segment_len, head_count, HD) + mark_ktotal[:, None]
    width = head_count * HD
    results = (
        attended.reshape(tok_rows, width),
        query_grad.astype(jnp.bfloat16).reshape(tok_rows, width),
        key_grad.astype(jnp.bfloat16).reshape(tok_rows, width),
        value_gradient_array.astype(jnp.bfloat16).reshape(tok_rows, width),
    )
    attended_out, query_out, key_out, value_out = (
        lax.all_to_all(results[0], "head", split_axis=0, concat_axis=1, tiled=True),
        lax.all_to_all(results[1], "head", split_axis=0, concat_axis=1, tiled=True),
        lax.all_to_all(results[2], "head", split_axis=0, concat_axis=1, tiled=True),
        lax.all_to_all(results[3], "head", split_axis=0, concat_axis=1, tiled=True),
    )
    return (attended_out, query_out, key_out, value_out)


def halves(matrix):
    high = matrix.astype(jnp.bfloat16)
    return high, (matrix - high.astype(jnp.float32)).astype(jnp.bfloat16)


def wide_dot(left, right):
    return jnp.dot(left, right, preferred_element_type=jnp.float32)


def wide_dot_nt(left, right):
    return lax.dot_general(
        left, right, (((1,), (1,)), ((), ())), preferred_element_type=jnp.float32
    )


def split_dot(left, right):
    left_high, left_low = left
    right_high, right_low = right
    return wide_dot(
        jnp.concatenate([left_high, left_high, left_low], axis=1),
        jnp.concatenate([right_high, right_low, right_high], axis=0),
    )


def split_dot_nt(left, right):
    left_high, left_low = left
    right_high, right_low = right
    return wide_dot_nt(
        jnp.concatenate([left_high, left_high, left_low], axis=1),
        jnp.concatenate([right_high, right_low, right_high], axis=1),
    )


def identity_matrix():
    return (
        lax.broadcasted_iota(jnp.int32, (M, M), 0) == lax.broadcasted_iota(jnp.int32, (M, M), 1)
    ).astype(jnp.float32)


def chunk_of(ref, array, slot, index):
    rows = ref.shape[3]
    per = CHUNK // rows
    return ref[pl.ds(index * per, per), array, slot].reshape(CHUNK, HD)


def store_chunk(ref, array, slot, index, value):
    rows = ref.shape[3]
    per = CHUNK // rows
    ref[pl.ds(index * per, per), array, slot] = value.reshape(per, rows, HD)


def all_tokens(ref, array, slot):
    return ref[:, array, slot].reshape(ref.shape[0] * ref.shape[3], HD)


def tokens_of(ref):
    return ref.shape[0] * ref.shape[3]


def columns(index):
    return pl.ds(pl.multiple_of(index * CHUNK, CHUNK), CHUNK)


def swap_marks(matrix):
    return jnp.concatenate([matrix[HALF:], matrix[:HALF]], axis=0)


def as_rows(row):
    return [row[:, :HD], row[:, HD:]]


def as_columns(row):
    return jnp.broadcast_to(row, (HD, M)).T


def own_stat(stats, slot, kind):
    place = 4 * slot + 2 * kind
    return jnp.concatenate([stats[place : place + 1], stats[place + 1 : place + 2]], axis=1)


def other_stat(stats, slot, kind):
    place = 4 * (1 - slot) + 2 * kind
    return jnp.concatenate([stats[place + 1 : place + 2], stats[place : place + 1]], axis=1)


def key_scales(own_stats, other_stats, slot):
    own_max, other_max = own_stat(own_stats, slot, 0), other_stat(other_stats, slot, 0)
    key_max = jnp.maximum(own_max, other_max)
    own_factor, other_factor = jnp.exp(own_max - key_max), jnp.exp(other_max - key_max)
    key_total = own_stat(own_stats, slot, 1) * own_factor + (
        other_stat(other_stats, slot, 1) * other_factor
    )
    return own_factor / key_total, other_factor / key_total


def staged_kernel(compute, in_names, out_names, *refs):
    n_in, n_out = len(in_names), len(out_names)
    sources, homes = refs[:n_in], refs[n_in : n_in + n_out]
    held_in, held_out = refs[n_in + n_out : 2 * n_in + n_out], refs[2 * n_in + n_out :][:n_out]
    *extra, in_done, out_done = refs[2 * (n_in + n_out) :]
    reads = [
        pltpu.make_async_copy(source, ref, in_done.at[index])
        for index, (source, ref) in enumerate(zip(sources, held_in))
    ]
    writes = [
        pltpu.make_async_copy(ref, home, out_done.at[index])
        for index, (ref, home) in enumerate(zip(held_out, homes))
    ]
    for read in reads:
        read.start()
    arrived, written = [], []

    def place_of(wanted, held):
        return next(index for index, ref in enumerate(held) if ref is wanted)

    def need(*wanted):
        places = [place_of(ref, held_in) for ref in wanted] or range(n_in)
        for place in places:
            if place not in arrived:
                reads[place].wait()
                arrived.append(place)

    def put(ref):
        place = place_of(ref, held_out)
        writes[place].start()
        written.append(place)

    compute(
        SimpleNamespace(**dict(zip(in_names, held_in))),
        SimpleNamespace(**dict(zip(out_names, held_out))),
        need,
        put,
        *extra,
    )
    need()
    for place in range(n_out):
        if place not in written:
            writes[place].start()
    for write in writes:
        write.wait()


def staged_call(compute, inputs, outputs, flops, extra=(), after=(), scalar=None):
    operands = tuple(inputs.values())
    n_in, n_after = len(operands), len(after)
    moved = sum(x.size * x.dtype.itemsize for x in (*operands, *outputs.values()))
    in_place = pl.BlockSpec(memory_space=pl.ANY)

    scalars = () if scalar is None else (scalar,)
    first = len(scalars)

    def kernel(*refs):
        staged_kernel(
            functools.partial(compute, *refs[:first]),
            tuple(inputs),
            tuple(outputs),
            *refs[first : first + n_in],
            *refs[first + n_in + n_after :],
        )

    results = pl.pallas_call(
        kernel,
        out_shape=tuple(outputs.values()),
        in_specs=[pl.BlockSpec(memory_space=pltpu.SMEM)] * first + [in_place] * (n_in + n_after),
        out_specs=(in_place,) * len(outputs),
        scratch_shapes=[
            *(pltpu.VMEM(x.shape, x.dtype) for x in (*operands, *outputs.values())),
            *extra,
            pltpu.SemaphoreType.DMA((n_in,)),
            pltpu.SemaphoreType.DMA((len(outputs),)),
        ],
        compiler_params=pltpu.CompilerParams(vmem_limit_bytes=VMEM_LIMIT),
        cost_estimate=pl.CostEstimate(
            flops=int(flops * 10**9), bytes_accessed=moved, transcendentals=0
        ),
    )(*scalars, *operands, *after)
    return SimpleNamespace(**dict(zip(outputs, results)))


def low(*shape):
    return jax.ShapeDtypeStruct(shape, jnp.bfloat16)


def wide(*shape):
    return jax.ShapeDtypeStruct(shape, jnp.float32)


def pack_kernel(half_ref, first_ref, second_ref, out_ref, rows_s, packed_s, in_done, out_done):
    half = half_ref[0]
    pairs = out_ref.shape[0]
    group = pairs // PACK_GROUPS
    span = 2 * HD
    reads, writes = [], []
    for index in range(PACK_GROUPS):
        for array, ref in enumerate((first_ref, second_ref)):
            place = pl.ds(index * group * span, group * span)
            reads.append(
                pltpu.make_async_copy(
                    ref.at[:, place], rows_s.at[array, :, place], in_done.at[array, index]
                )
            )
        place = pl.ds(index * group, group)
        writes.append(
            pltpu.make_async_copy(packed_s.at[place], out_ref.at[place], out_done.at[index])
        )
    for copy in reads:
        copy.start()
    for index in range(PACK_GROUPS):
        for array in range(2):
            reads[2 * index + array].wait()
            for pair in range(index * group, (index + 1) * group):
                start = pair * span
                packed_s[pair, array, half] = rows_s[array, :, start : start + HD]
                packed_s[pair, array, 1 - half] = rows_s[array, :, start + HD : start + span]
        writes[index].start()
    for copy in writes:
        copy.wait()


def unpack_kernel(half_ref, packed_ref, *refs):
    half = half_ref[0]
    pairs, arrays = packed_ref.shape[:2]
    homes, (packed_s, rows_s, in_done, out_done) = refs[:arrays], refs[arrays:]
    group = pairs // PACK_GROUPS
    span = 2 * HD
    reads, writes = [], []
    for index in range(PACK_GROUPS):
        place = pl.ds(index * group, group)
        reads.append(
            pltpu.make_async_copy(packed_ref.at[place], packed_s.at[place], in_done.at[index])
        )
        for array, ref in enumerate(homes):
            place = pl.ds(index * group * span, group * span)
            writes.append(
                pltpu.make_async_copy(
                    rows_s.at[array, :, place], ref.at[:, place], out_done.at[array, index]
                )
            )
    for copy in reads:
        copy.start()
    for index in range(PACK_GROUPS):
        reads[index].wait()
        for array in range(arrays):
            for pair in range(index * group, (index + 1) * group):
                start = pair * span
                rows_s[array, :, start : start + HD] = packed_s[pair, array, half]
                rows_s[array, :, start + HD : start + span] = packed_s[pair, array, 1 - half]
            writes[arrays * index + array].start()
    for copy in writes:
        copy.wait()


def landmark_kernel(first_ref, second_ref, out_ref, rows_s, packed_s, in_done, out_done, segment_len):
    pairs = out_ref.shape[0] // 2
    rows = first_ref.shape[0]
    span = 2 * HD
    reads = [
        pltpu.make_async_copy(ref, rows_s.at[array], in_done.at[array])
        for array, ref in enumerate((first_ref, second_ref))
    ]
    for copy in reads:
        copy.start()
    count = rows // segment_len
    member = (
        lax.broadcasted_iota(jnp.int32, (count, rows), 1) // segment_len
        == lax.broadcasted_iota(jnp.int32, (count, rows), 0)
    ).astype(jnp.bfloat16)
    for copy in reads:
        copy.wait()
    group = pairs // PACK_GROUPS
    for index in range(PACK_GROUPS):
        place = slice(index * group * span, (index + 1) * group * span)
        means = [wide_dot(member, rows_s[array, :, place]) / segment_len for array in range(2)]
        both = jnp.concatenate(means, axis=0).astype(jnp.bfloat16)
        for pair in range(group):
            for head in range(2):
                start = pair * span + head * HD
                packed_s[index * group + pair, head] = both[:, start : start + HD]
    writes = [
        pltpu.make_async_copy(packed_s, out_ref.at[pl.ds(side * pairs, pairs)], out_done.at[side])
        for side in range(2)
    ]
    for copy in writes:
        copy.start()
    for copy in writes:
        copy.wait()


def layout_call(kernel, scalars, operands, out_shape, scratch):
    in_place = pl.BlockSpec(memory_space=pl.ANY)
    moved = 2 * sum(x.size * x.dtype.itemsize for x in operands)
    return pl.pallas_call(
        kernel,
        out_shape=out_shape,
        in_specs=[pl.BlockSpec(memory_space=pltpu.SMEM)] * len(scalars)
        + [in_place] * len(operands),
        out_specs=jax.tree.map(lambda _: in_place, out_shape),
        scratch_shapes=scratch,
        compiler_params=pltpu.CompilerParams(vmem_limit_bytes=VMEM_LIMIT),
        cost_estimate=pl.CostEstimate(flops=0, bytes_accessed=moved, transcendentals=0),
    )(*scalars, *operands)


def pack(half, first, second):
    rows, width = first.shape
    shape = low(width // (2 * HD), 2, 2, rows, HD)
    scratch = [
        pltpu.VMEM((2, rows, width), jnp.bfloat16),
        pltpu.VMEM(shape.shape, jnp.bfloat16),
        pltpu.SemaphoreType.DMA((2, PACK_GROUPS)),
        pltpu.SemaphoreType.DMA((PACK_GROUPS,)),
    ]
    return layout_call(pack_kernel, (half,), (first, second), shape, scratch)


def unpack(half, packed):
    pairs, arrays, _, rows, _ = packed.shape
    shape = low(rows, pairs * 2 * HD)
    scratch = [
        pltpu.VMEM(packed.shape, jnp.bfloat16),
        pltpu.VMEM((arrays, *shape.shape), jnp.bfloat16),
        pltpu.SemaphoreType.DMA((PACK_GROUPS,)),
        pltpu.SemaphoreType.DMA((arrays, PACK_GROUPS)),
    ]
    return layout_call(unpack_kernel, (half,), (packed,), (shape,) * arrays, scratch)


def local_landmarks(first, second, segment_len):
    rows, width = first.shape
    pairs = width // (2 * HD)
    shape = low(2 * pairs, 2, 2 * rows // segment_len, HD)
    scratch = [
        pltpu.VMEM((2, rows, width), jnp.bfloat16),
        pltpu.VMEM((pairs, *shape.shape[1:]), jnp.bfloat16),
        pltpu.SemaphoreType.DMA((2,)),
        pltpu.SemaphoreType.DMA((2,)),
    ]
    kernel = functools.partial(landmark_kernel, segment_len=segment_len)
    return layout_call(kernel, (), (first, second), shape, scratch)


def inverse_compute(half_ref, ins, outs, need, put, power_s, iterate_s):
    need()
    half = half_ref[0]
    score_scale = HD ** (-0.5)
    sources = ins.gathered.shape[0] // 2
    count = ins.gathered.shape[2] // 2
    for slot, head in ((0, half), (1, 1 - half)):
        sides = [
            ins.gathered[pl.ds(side * sources, sources), head].astype(jnp.float32)
            for side in (half, 1 - half)
        ]
        for array in range(2):
            parts = [
                side[:, array * count : (array + 1) * count].reshape(HALF, HD) for side in sides
            ]
            outs.marks[slot, array] = jnp.concatenate(parts, axis=0).astype(jnp.bfloat16)
    put(outs.marks)
    landmark_q, landmark_k = outs.marks[0, 0], outs.marks[0, 1]
    mark_score = wide_dot_nt(landmark_q, landmark_k) * score_scale
    mark_exp = jnp.exp(mark_score - jnp.max(mark_score, axis=1, keepdims=True))
    mark_prob = mark_exp / jnp.sum(mark_exp, axis=1, keepdims=True)
    outs.mark_prob[...] = mark_prob
    factor = 1.0 / jnp.max(jnp.sum(mark_prob, axis=0, keepdims=True), axis=1, keepdims=True)
    outs.factor[...] = jnp.broadcast_to(factor, outs.factor.shape)
    mark_halves = halves(mark_prob)
    power_s[...] = split_dot_nt(mark_halves, mark_halves) * factor
    iterate_s[0:M] = mark_prob.T * factor
    iterate_s[M:] = identity_matrix()

    def newton(pair_ref, weight_ref, growth_ref, sweep, carry):
        power = power_s[...]
        power_high, power_low = halves(power)
        square = split_dot((power_high, power_low), (power_high, power_low))
        square_halves = halves(square)
        pair = (
            jnp.concatenate([power_high, square_halves[0]], axis=0),
            jnp.concatenate([power_low, square_halves[1]], axis=0),
        )
        pair_ref[sweep, 0], pair_ref[sweep, 1] = pair
        higher = split_dot(pair, square_halves)
        cube, fourth = higher[:M], higher[M:]
        weight = halves(
            0.25 * (13.0 * identity_matrix() - 15.0 * power + 7.0 * square - cube)
        )
        power_s[...] = 0.25 * (13.0 * power - 15.0 * square + 7.0 * cube - fourth)
        weight_ref[sweep, 0], weight_ref[sweep, 1] = weight
        iterate = halves(iterate_s[...])
        growth_ref[sweep, 0], growth_ref[sweep, 1] = iterate[0][M:], iterate[1][M:]
        iterate_s[...] = split_dot(iterate, weight)
        return carry

    for saved in ((outs.pair_a, outs.weight_a, outs.growth_a), (outs.pair_b, outs.weight_b, outs.growth_b)):
        lax.fori_loop(0, PINV_ITERS // 2, functools.partial(newton, *saved), 0)
        for ref in saved:
            put(ref)
    inverse = iterate_s[0:M]
    outs.inverse[0], outs.inverse[1] = halves(inverse)
    outs.inverse_turned[0], outs.inverse_turned[1] = halves(inverse.T)
    outs.last_growth[0], outs.last_growth[1] = halves(iterate_s[M:])


def key_probability_compute(ins, outs, need, put, low_s):
    need()
    kv_ref, key_exp_ref = ins.kv, outs.key_exp
    chunks = tokens_of(kv_ref) // CHUNK
    score_scale = HD ** (-0.5)
    stats = []
    for slot in (1, 0):
        landmark_q = ins.marks[slot, 0]

        def scores(index, key_max):
            key_chunk = chunk_of(kv_ref, 0, slot, index)
            place = columns(index)
            outs.turned[slot, :, place] = key_chunk.T
            key_score = wide_dot_nt(key_chunk, landmark_q) * score_scale
            key_exp_ref[slot, place] = key_score
            return jnp.maximum(key_max, jnp.max(key_score, axis=0, keepdims=True))

        key_max = lax.fori_loop(0, chunks, scores, jnp.full((1, M), -jnp.inf, jnp.float32))

        def grow(index, key_total):
            place = columns(index)
            grown = jnp.exp(key_exp_ref[slot, place] - key_max)
            key_exp_ref[slot, place] = grown
            low_s[:, place] = grown.astype(jnp.bfloat16).T
            return key_total + jnp.sum(grown, axis=0, keepdims=True)

        key_total = lax.fori_loop(0, chunks, grow, jnp.zeros((1, M), jnp.float32))
        stats = as_rows(key_max) + as_rows(key_total) + stats
        home = outs.send if slot == 1 else outs.keep
        home[0:M] = wide_dot(low_s[...], all_tokens(kv_ref, 1, slot))
    outs.stats[...] = jnp.concatenate(stats, axis=0)
    outs.send[M:] = jnp.concatenate(stats, axis=0)


def mixing_compute(ins, outs, need, put):
    need()
    own_scale, other_scale = key_scales(ins.stats[...], ins.got[M:], 0)
    landmark_values = ins.keep[...] * as_columns(own_scale) + (
        swap_marks(ins.got[0:M]) * as_columns(other_scale)
    )
    outs.share[...] = split_dot(
        (ins.inverse[0], ins.inverse[1]), halves(landmark_values)
    ).astype(jnp.bfloat16)
    outs.mark_values[...] = landmark_values


def token_probability_compute(ins, outs, need, put, low_s):
    need()
    qg_ref = ins.qg
    chunks = tokens_of(qg_ref) // CHUNK
    score_scale = HD ** (-0.5)
    for slot in (1, 0):
        landmark_k = ins.marks[slot, 1]

        def one_chunk(index, carry):
            query_chunk = chunk_of(qg_ref, 0, slot, index)
            place = columns(index)
            outs.turned[slot, :, place] = query_chunk.T
            score = wide_dot_nt(query_chunk, landmark_k) * score_scale
            grown = jnp.exp(score - jnp.max(score, axis=1, keepdims=True))
            prob = grown / jnp.sum(grown, axis=1, keepdims=True)
            outs.token_prob[slot, place] = prob
            low_s[:, place] = prob.astype(jnp.bfloat16).T
            return carry

        lax.fori_loop(0, chunks, one_chunk, 0)
        home = outs.send if slot == 1 else outs.keep
        home[...] = wide_dot(low_s[...], all_tokens(qg_ref, 1, slot))
        put(home)


def values_compute(ins, outs, need, put):
    need()
    mixing_grad = ins.keep[...] + swap_marks(ins.got[...])
    values_low = split_dot(
        (ins.inverse_turned[0], ins.inverse_turned[1]), halves(mixing_grad)
    ).astype(jnp.bfloat16)
    outs.share[0:M] = values_low
    product = (values_low.astype(jnp.float32) * ins.mark_values[...]).T
    row_total = jnp.sum(product, axis=0, keepdims=True)
    first = row_total.astype(jnp.bfloat16).astype(jnp.float32)
    second = (row_total - first).astype(jnp.bfloat16).astype(jnp.float32)
    third = row_total - first - second
    rows = as_rows(first) + as_rows(second) + as_rows(third)
    rows.append(jnp.zeros((10, HD), jnp.float32))
    outs.share[M:] = jnp.concatenate(rows, axis=0).astype(jnp.bfloat16)
    outs.mixing_grad[...] = mixing_grad


def newton_gradient_sweeps(power, growth, pair_ref, weight_ref, growth_ref):
    for sweep in range(PINV_ITERS // 2):
        pair = (pair_ref[sweep, 0], pair_ref[sweep, 1])
        first = split_dot(pair, halves(power))
        square = first[:M] + first[:M].T
        second = split_dot(pair, halves(square))
        cube = first[M:].T + second[:M]
        fourth = second[M:] + second[M:].T
        weight = halves(0.25 * (7.0 * square - 15.0 * power - cube))
        power = 0.25 * (13.0 * power - 15.0 * square + 7.0 * cube - fourth)
        held = (growth_ref[sweep, 0], growth_ref[sweep, 1])
        held_weight = (weight_ref[sweep, 0], weight_ref[sweep, 1])
        left, right = [held[0], held[0], held[1]], [weight[0], weight[1], weight[0]]
        if growth is not None:
            grown_high, grown_low = halves(growth)
            left += [grown_high, grown_high, grown_low]
            right += [held_weight[0], held_weight[1], held_weight[0]]
        growth = wide_dot(jnp.concatenate(left, axis=1), jnp.concatenate(right, axis=0))
    return power, growth


def first_gradient_compute(ins, outs, need, put):
    need(ins.mark_prob, ins.factor, ins.mixing_grad, ins.mark_values)
    factor = ins.factor[0:1, 0:1]
    inverse_grad = split_dot_nt(halves(ins.mixing_grad[...]), halves(ins.mark_values[...]))
    inverse_grad_halves = halves(inverse_grad)
    outs.inverse_grad[0], outs.inverse_grad[1] = inverse_grad_halves
    toward = split_dot(halves(ins.mark_prob[...]), inverse_grad_halves) * factor
    need()
    outs.state[0], outs.state[1] = newton_gradient_sweeps(
        0.5 * (toward + toward.T), None, ins.pair, ins.weight, ins.growth
    )


def second_gradient_compute(ins, outs, need, put):
    need()
    _, growth = newton_gradient_sweeps(
        ins.state[0], ins.state[1], ins.pair, ins.weight, ins.growth
    )
    mark_prob = ins.mark_prob[...]
    mark_grad = ins.factor[0:1, 0:1] * (
        split_dot_nt(
            (ins.last_growth[0], ins.last_growth[1]), (ins.inverse_grad[0], ins.inverse_grad[1])
        )
        + split_dot(halves(growth + growth.T), halves(mark_prob))
    )
    mark_sgrad = mark_prob * (mark_grad - jnp.sum(mark_grad * mark_prob, axis=1, keepdims=True))

    def marks_dot(left, right):
        left_high, left_low = halves(left)
        return wide_dot(
            jnp.concatenate([left_high, left_low], axis=1), jnp.concatenate([right, right], axis=0)
        )

    totals = (
        (ins.query_marks, marks_dot(mark_sgrad, ins.marks[0, 1])),
        (ins.key_marks, marks_dot(mark_sgrad.T, ins.marks[0, 0])),
    )
    for kind, (sums_ref, own) in enumerate(totals):
        for slot in range(2):
            total = sums_ref[slot].T
            if slot == 0:
                total = total + own
            total = total * ins.scale[0:1, 0:1]
            outs.far[kind, slot] = total[HALF:].astype(jnp.bfloat16)
            outs.near[kind, slot] = total[:HALF]
    put(outs.far)


def shared(own_ref, other_ref, slot):
    if slot == 0:
        return own_ref[0:M]
    return swap_marks(other_ref[0:M])


def token_gradient_compute(ins, outs, need, put):
    need()
    chunks = tokens_of(ins.qg) // CHUNK
    score_scale = HD ** (-0.5)
    for slot in range(2):
        mixing_low = shared(ins.share, ins.got_share, slot)
        landmark_k = ins.marks[slot, 1]

        def one_chunk(index, total):
            place = columns(index)
            prob = ins.token_prob[slot, place]
            attended = wide_dot(prob.astype(jnp.bfloat16), mixing_low)
            store_chunk(outs.out, 0, slot, index, attended.astype(jnp.bfloat16))
            token_grad = wide_dot_nt(chunk_of(ins.qg, 1, slot, index), mixing_low)
            token_sgrad = (
                prob * (token_grad - jnp.sum(token_grad * prob, axis=1, keepdims=True))
            ).astype(jnp.bfloat16)
            outs.direct[slot, place] = wide_dot(token_sgrad, landmark_k) * score_scale
            return total + wide_dot(ins.turned[slot, :, place], token_sgrad)

        zeros = jnp.zeros((HD, M), jnp.float32)
        outs.marks_sum[slot] = lax.fori_loop(0, chunks, one_chunk, zeros)


def key_gradient_compute(ins, outs, need, put):
    need()
    chunks = tokens_of(ins.kv) // CHUNK
    score_scale = HD ** (-0.5)
    for slot in range(2):
        scale, _ = key_scales(ins.stats[...], ins.got[M:], slot)
        values_low = shared(ins.share, ins.got_share, slot)
        landmark_q = ins.marks[slot, 0]
        tail = (ins.share if slot == 0 else ins.got_share)[M:].astype(jnp.float32)
        rows = [tail[place : place + 1] for place in range(6)]
        near = rows[0] + (rows[2] + rows[4])
        far = rows[1] + (rows[3] + rows[5])
        row_total = jnp.concatenate([near, far] if slot == 0 else [far, near], axis=1)

        def one_chunk(index, total):
            place = columns(index)
            key_prob = ins.key_exp[slot, place] * scale
            value_gradient = wide_dot(key_prob.astype(jnp.bfloat16), values_low)
            store_chunk(outs.out, 0, slot, index, value_gradient.astype(jnp.bfloat16))
            key_dgrad = wide_dot_nt(chunk_of(ins.kv, 1, slot, index), values_low)
            key_sgrad = (key_prob * (key_dgrad - row_total)).astype(jnp.bfloat16)
            outs.direct[slot, place] = wide_dot(key_sgrad, landmark_q) * score_scale
            return total + wide_dot(ins.turned[slot, :, place], key_sgrad)

        zeros = jnp.zeros((HD, M), jnp.float32)
        outs.marks_sum[slot] = lax.fori_loop(0, chunks, one_chunk, zeros)


def finish_compute(ins, outs, need, put):
    need()
    out_ref = outs.out
    segment_len = tokens_of(out_ref) // HALF
    directs = (ins.query_direct, ins.key_direct)
    per = CHUNK // segment_len
    for kind in range(2):
        for slot in range(2):
            for index in range(tokens_of(out_ref) // CHUNK):
                place = slice(index * per, (index + 1) * per)
                marks = ins.near[kind, slot, place] + ins.got_far[
                    kind, 1 - slot, place
                ].astype(jnp.float32)
                spread = jnp.broadcast_to(marks[:, None], (per, segment_len, HD))
                direct = directs[kind][slot, index * CHUNK : (index + 1) * CHUNK]
                store_chunk(
                    out_ref,
                    kind,
                    slot,
                    index,
                    (direct + spread.reshape(CHUNK, HD)).astype(jnp.bfloat16),
                )


def exchange(packed):
    return lax.all_to_all(packed, "cube", split_axis=0, concat_axis=0, tiled=True)


def partner(array):
    return lax.ppermute(array, "half", SWAP)


def spread_landmarks(queries, keys):
    segment_len = queries.shape[0] * lax.axis_size("seq") * lax.axis_size("head") // M
    return lax.all_to_all(
        local_landmarks(queries, keys, segment_len),
        ("seq", "head"),
        split_axis=0,
        concat_axis=0,
        tiled=True,
    )


def body(gathered, queries, keys, values, out_grad):
    half = lax.axis_index("half").reshape(1)
    rows = queries.shape[0]
    devices = lax.axis_size("half") * lax.axis_size("cube")
    segment_len = rows * devices // M
    tokens = rows * devices // 2
    kv = exchange(pack(half, keys, values))
    qg = exchange(pack(half, queries, out_grad))
    square = pltpu.VMEM((M, M), jnp.float32)
    turned_s = pltpu.VMEM((M, tokens), jnp.bfloat16)
    sweeps = PINV_ITERS // 2
    one_array = low(qg.shape[0], 1, *qg.shape[2:])

    newton = staged_call(
        inverse_compute,
        dict(gathered=gathered),
        dict(
            marks=low(2, 2, M, HD),
            mark_prob=wide(M, M),
            factor=wide(8, HD),
            pair_a=low(sweeps, 2, 2 * M, M),
            weight_a=low(sweeps, 2, M, M),
            growth_a=low(sweeps, 2, M, M),
            pair_b=low(sweeps, 2, 2 * M, M),
            weight_b=low(sweeps, 2, M, M),
            growth_b=low(sweeps, 2, M, M),
            inverse=low(2, M, M),
            inverse_turned=low(2, M, M),
            last_growth=low(2, M, M),
        ),
        8,
        extra=(square, pltpu.VMEM((2 * M, M), jnp.float32)),
        scalar=half,
    )
    marks = newton.marks
    key_side = staged_call(
        key_probability_compute,
        dict(kv=kv, marks=marks),
        dict(
            send=wide(M + 8, HD),
            keep=wide(M, HD),
            stats=wide(8, HD),
            key_exp=wide(2, tokens, M),
            turned=low(2, HD, tokens),
        ),
        4,
        extra=(turned_s,),
    )
    got = partner(key_side.send)
    mixed = staged_call(
        mixing_compute,
        dict(got=got, keep=key_side.keep, stats=key_side.stats, inverse=newton.inverse),
        dict(share=low(M, HD), mark_values=wide(M, HD)),
        0.2,
    )
    got_mixing = partner(mixed.share)
    token_side = staged_call(
        token_probability_compute,
        dict(qg=qg, marks=marks),
        dict(
            send=wide(M, HD),
            keep=wide(M, HD),
            token_prob=wide(2, tokens, M),
            turned=low(2, HD, tokens),
        ),
        4,
        extra=(turned_s,),
        after=(mixed.share,),
    )
    got_grad = partner(token_side.send)
    token_grads = staged_call(
        token_gradient_compute,
        dict(
            qg=qg,
            marks=marks,
            token_prob=token_side.token_prob,
            turned=token_side.turned,
            share=mixed.share,
            got_share=got_mixing,
        ),
        dict(out=one_array, direct=wide(2, tokens, HD), marks_sum=wide(2, HD, M)),
        4,
    )
    (attended,) = unpack(half, exchange(token_grads.out))
    lowered = staged_call(
        values_compute,
        dict(
            got=got_grad,
            keep=token_side.keep,
            inverse_turned=newton.inverse_turned,
            mark_values=mixed.mark_values,
        ),
        dict(share=low(M + 16, HD), mixing_grad=wide(M, HD)),
        0.2,
        after=(token_grads.marks_sum,),
    )
    got_values = partner(lowered.share)
    first = staged_call(
        first_gradient_compute,
        dict(
            mark_prob=newton.mark_prob,
            factor=newton.factor,
            mixing_grad=lowered.mixing_grad,
            mark_values=mixed.mark_values,
            pair=newton.pair_a,
            weight=newton.weight_a,
            growth=newton.growth_a,
        ),
        dict(state=wide(2, M, M), inverse_grad=low(2, M, M)),
        6,
    )
    key_grads = staged_call(
        key_gradient_compute,
        dict(
            kv=kv,
            marks=marks,
            key_exp=key_side.key_exp,
            turned=key_side.turned,
            stats=key_side.stats,
            got=got,
            share=lowered.share,
            got_share=got_values,
        ),
        dict(out=one_array, direct=wide(2, tokens, HD), marks_sum=wide(2, HD, M)),
        4,
        after=(first.state,),
    )
    (value_gradient_array,) = unpack(half, exchange(key_grads.out))
    second = staged_call(
        second_gradient_compute,
        dict(
            state=first.state,
            inverse_grad=first.inverse_grad,
            mark_prob=newton.mark_prob,
            factor=newton.factor,
            pair=newton.pair_b,
            weight=newton.weight_b,
            growth=newton.growth_b,
            last_growth=newton.last_growth,
            marks=marks,
            query_marks=key_grads.marks_sum,
            key_marks=token_grads.marks_sum,
            scale=jnp.full((8, HD), HD ** (-0.5) / segment_len, jnp.float32),
        ),
        dict(far=low(2, 2, HALF, HD), near=wide(2, 2, HALF, HD)),
        6,
    )
    results = staged_call(
        finish_compute,
        dict(
            got_far=partner(second.far),
            near=second.near,
            query_direct=token_grads.direct,
            key_direct=key_grads.direct,
        ),
        dict(out=low(*qg.shape)),
        0.5,
    ).out
    query_grad, key_grad = unpack(half, exchange(results))
    return attended, query_grad, key_grad, value_gradient_array


def solution(mesh):
    whole = P(("seq", "head"), None)
    blocks = P(("seq", "head"))
    halved = P(("half", "cube"), None)

    def layer(queries, keys, values, out_grad):
        arrays = (queries, keys, values, out_grad)
        tokens, width = queries.shape
        if width // HD != mesh.size or tokens % (2 * CHUNK):
            return jax.shard_map(
                shared_body,
                mesh=mesh,
                in_specs=(whole,) * 4,
                out_specs=(whole,) * 4,
                check_vma=False,
            )(*arrays)
        gathered = jax.shard_map(
            spread_landmarks, mesh=mesh, in_specs=(whole,) * 2, out_specs=blocks, check_vma=False
        )(queries, keys)
        split = jax.sharding.Mesh(mesh.devices.reshape(2, mesh.size // 2), ("half", "cube"))
        return jax.shard_map(
            body,
            mesh=split,
            in_specs=(P(("half", "cube")), *(halved,) * 4),
            out_specs=(halved,) * 4,
            check_vma=False,
        )(gathered, *arrays)

    return layer
```

```python
import functools

import jax
import jax.numpy as jnp
from jax import lax
from jax.experimental import pallas as pl
from jax.experimental.pallas import tpu as pltpu
from jax.sharding import PartitionSpec as P

HD = 128
M = 256
PINV_ITERS = 6
CHUNK = 256
PACK_GROUPS = 4
MIXING_PARTS = 4
VMEM_LIMIT = 60 * 2**20
SMALL_LIMIT = 16 * 2**20
FORWARD_FLOPS = 10 * 10**9
MIXING_FLOPS = 2 * 10**9
GRADIENT_FLOPS = 14 * 10**9
MIXING_NAMES = (
    "key_low",
    "total_inverse",
    "inverse",
    "token_low",
    "key_plow",
)
GRADIENT_NAMES = (
    "mark_q",
    "mark_k",
    "key_prob",
    "columns_turned",
    "token_prob",
    "mark_prob",
    "factor",
    "pair",
    "weight",
    "growth",
    "last_growth",
)
EARLY_NAMES = (
    "mark_q",
    "mark_k",
    "mark_prob",
    "factor",
    "token_prob",
    "token_low",
    "key_prob",
    "key_plow",
    "key_low",
    "total_inverse",
    "columns_turned",
)


precise_setting = lax.Precision.HIGHEST


def newton_inverse(matrix):
    identity = jnp.eye(matrix.shape[0], dtype=matrix.dtype)
    factor = lax.stop_gradient(1.0 / jnp.max(jnp.sum(matrix, axis=0)))
    iterate = matrix.T * factor
    for sweep_index in range(PINV_ITERS):
        product = jnp.matmul(matrix, iterate, precision=precise_setting)
        inner_term = jnp.matmul(product, 7.0 * identity - product, precision=precise_setting)
        inner_term = jnp.matmul(product, 15.0 * identity - inner_term, precision=precise_setting)
        iterate = 0.25 * jnp.matmul(
            iterate, 13.0 * identity - inner_term, precision=precise_setting
        )
    return iterate


def share_heads(own_matrix, head_count):
    seq_index = lax.axis_index("seq")
    slot_mask = (jnp.arange(head_count, dtype=jnp.int32) == seq_index).astype(jnp.float32)
    return lax.psum(slot_mask[:, None, None] * own_matrix[None], "seq")


def shared_body(queries, keys, values, out_grad):
    query_rows, key_rows, value_rows, grad_rows = (
        lax.all_to_all(queries, "head", split_axis=1, concat_axis=0, tiled=True),
        lax.all_to_all(keys, "head", split_axis=1, concat_axis=0, tiled=True),
        lax.all_to_all(values, "head", split_axis=1, concat_axis=0, tiled=True),
        lax.all_to_all(out_grad, "head", split_axis=1, concat_axis=0, tiled=True),
    )
    tok_rows = query_rows.shape[0]
    head_count = query_rows.shape[1] // HD
    local_marks = M // lax.axis_size("seq")
    segment_len = tok_rows // local_marks
    score_scale = HD ** (-0.5)
    seq_index = lax.axis_index("seq")

    def landmark(matrix):
        summed = jnp.sum(
            matrix.reshape(local_marks, segment_len, matrix.shape[1]), axis=1, dtype=jnp.float32
        )
        return (summed / segment_len).astype(jnp.bfloat16)

    mark_queries, mark_keys = (
        lax.all_gather(landmark(query_rows), "seq", axis=0, tiled=True),
        lax.all_gather(landmark(key_rows), "seq", axis=0, tiled=True),
    )
    query_per_head = query_rows.reshape(tok_rows, head_count, HD)
    key_per_head = key_rows.reshape(tok_rows, head_count, HD)
    value_per_head = value_rows.reshape(tok_rows, head_count, HD)
    gradient_per_head = grad_rows.reshape(tok_rows, head_count, HD)
    landmark_query_heads = mark_queries.reshape(M, head_count, HD)
    landmark_key_heads = mark_keys.reshape(M, head_count, HD)
    key_score = (
        jnp.einsum(
            "pcv,gcv->cpg", landmark_query_heads, key_per_head, preferred_element_type=jnp.float32
        )
        * score_scale
    )
    key_max = lax.pmax(jnp.max(key_score, axis=-1), "seq")
    key_exp = jnp.exp(key_score - key_max[..., None])
    partial_num = jnp.einsum(
        "akq,qay->aky",
        key_exp.astype(jnp.bfloat16),
        value_per_head,
        preferred_element_type=jnp.float32,
    )
    key_total, numerator = lax.psum((jnp.sum(key_exp, axis=-1), partial_num), "seq")
    landmark_value_rows = numerator / key_total[..., None]
    token_prob = jax.nn.softmax(
        jnp.einsum(
            "jti,cti->tjc", query_per_head, landmark_key_heads, preferred_element_type=jnp.float32
        )
        * score_scale,
        axis=-1,
    )
    token_probability_lowered = token_prob.astype(jnp.bfloat16)
    mark_prob = jax.nn.softmax(
        jnp.einsum(
            "jou,iou->oji",
            landmark_query_heads,
            landmark_key_heads,
            preferred_element_type=jnp.float32,
        )
        * score_scale,
        axis=-1,
    )
    own_head = seq_index % head_count
    own_mark = lax.dynamic_index_in_dim(mark_prob, own_head, 0, keepdims=False)
    own_inverse, pull_back = jax.vjp(newton_inverse, own_mark)
    pseudo_inverse_matrix = share_heads(own_inverse, head_count)
    mixing_matrix = jnp.einsum(
        "jvy,jys->jvs", pseudo_inverse_matrix, landmark_value_rows, precision=precise_setting
    )
    mixing_matrix_lowered = mixing_matrix.astype(jnp.bfloat16)
    attended = jnp.einsum(
        "yvo,yor->vyr",
        token_probability_lowered,
        mixing_matrix_lowered,
        preferred_element_type=jnp.float32,
    ).astype(jnp.bfloat16)
    token_grad = jnp.einsum(
        "fag,aog->afo", gradient_per_head, mixing_matrix_lowered, preferred_element_type=jnp.float32
    )
    partial_mix = jnp.einsum(
        "klz,lkr->kzr",
        token_probability_lowered,
        gradient_per_head,
        preferred_element_type=jnp.float32,
    )
    mixing_matrix_gradient = lax.psum(partial_mix, "seq")
    token_score_gradient = (
        token_prob * (token_grad - jnp.sum(token_grad * token_prob, axis=-1, keepdims=True))
    ).astype(jnp.bfloat16)
    direct_qgrad = (
        jnp.einsum(
            "ufg,guc->fuc",
            token_score_gradient,
            landmark_key_heads,
            preferred_element_type=jnp.float32,
        )
        * score_scale
    )
    mark_kgrad_f = (
        jnp.einsum(
            "xgi,gxy->ixy", token_score_gradient, query_per_head, preferred_element_type=jnp.float32
        )
        * score_scale
    )
    pseudo_inverse_gradient = jnp.einsum(
        "ktu,kyu->kty", mixing_matrix_gradient, landmark_value_rows, precision=precise_setting
    )
    landmark_value_gradient = jnp.einsum(
        "lrb,lrz->lbz", pseudo_inverse_matrix, mixing_matrix_gradient, precision=precise_setting
    )
    own_igrad = lax.dynamic_index_in_dim(pseudo_inverse_gradient, own_head, 0, keepdims=False)
    (own_mgrad,) = pull_back(own_igrad)
    mark_grad = share_heads(own_mgrad, head_count)
    mark_sgrad = mark_prob * (mark_grad - jnp.sum(mark_grad * mark_prob, axis=-1, keepdims=True))
    first_mark = seq_index * local_marks
    score_gradient_rows = lax.dynamic_slice_in_dim(mark_sgrad, first_mark, local_marks, 1)
    score_gradient_columns = lax.dynamic_slice_in_dim(mark_sgrad, first_mark, local_marks, 2)
    own_qgrad_a = (
        jnp.einsum(
            "txs,ste->xte",
            score_gradient_rows,
            landmark_key_heads.astype(jnp.float32),
            precision=precise_setting,
        )
        * score_scale
    )
    own_kgrad_a = (
        jnp.einsum(
            "eaj,aev->jev",
            score_gradient_columns,
            landmark_query_heads.astype(jnp.float32),
            precision=precise_setting,
        )
        * score_scale
    )
    landmark_value_lowered = landmark_value_gradient.astype(jnp.bfloat16)
    key_prob = key_exp / key_total[..., None]
    key_probability_lowered = key_prob.astype(jnp.bfloat16)
    value_gradient_array = jnp.einsum(
        "zct,zcj->tzj",
        key_probability_lowered,
        landmark_value_lowered,
        preferred_element_type=jnp.float32,
    )
    key_direct_gradient = jnp.einsum(
        "exb,geb->exg", landmark_value_lowered, value_per_head, preferred_element_type=jnp.float32
    )
    row_total = lax.psum(jnp.sum(key_prob * key_direct_gradient, axis=-1), "seq")
    key_score_gradient = (key_prob * (key_direct_gradient - row_total[..., None])).astype(
        jnp.bfloat16
    )
    direct_kgrad = (
        jnp.einsum(
            "pbo,bpx->opx",
            key_score_gradient,
            landmark_query_heads,
            preferred_element_type=jnp.float32,
        )
        * score_scale
    )
    mark_qgrad_b = (
        jnp.einsum(
            "cbj,jcp->bcp", key_score_gradient, key_per_head, preferred_element_type=jnp.float32
        )
        * score_scale
    )
    own_kgrad_f, own_qgrad_b = (
        lax.psum_scatter(mark_kgrad_f, "seq", scatter_dimension=0, tiled=True),
        lax.psum_scatter(mark_qgrad_b, "seq", scatter_dimension=0, tiled=True),
    )
    mark_qtotal = (own_qgrad_a + own_qgrad_b) / segment_len
    mark_ktotal = (own_kgrad_a + own_kgrad_f) / segment_len
    query_grad = (
        direct_qgrad.reshape(local_marks, segment_len, head_count, HD) + mark_qtotal[:, None]
    )
    key_grad = direct_kgrad.reshape(local_marks, segment_len, head_count, HD) + mark_ktotal[:, None]
    width = head_count * HD
    results = (
        attended.reshape(tok_rows, width),
        query_grad.astype(jnp.bfloat16).reshape(tok_rows, width),
        key_grad.astype(jnp.bfloat16).reshape(tok_rows, width),
        value_gradient_array.astype(jnp.bfloat16).reshape(tok_rows, width),
    )
    attended_out, query_out, key_out, value_out = (
        lax.all_to_all(results[0], "head", split_axis=0, concat_axis=1, tiled=True),
        lax.all_to_all(results[1], "head", split_axis=0, concat_axis=1, tiled=True),
        lax.all_to_all(results[2], "head", split_axis=0, concat_axis=1, tiled=True),
        lax.all_to_all(results[3], "head", split_axis=0, concat_axis=1, tiled=True),
    )
    return (attended_out, query_out, key_out, value_out)


def dims_of(rows):
    tokens = rows.shape[0] * rows.shape[2]
    return tokens, rows.shape[2], tokens // CHUNK


def halves(matrix):
    high = matrix.astype(jnp.bfloat16)
    return high, (matrix - high.astype(jnp.float32)).astype(jnp.bfloat16)


def wide_dot(left, right):
    return jnp.dot(left, right, preferred_element_type=jnp.float32)


def wide_dot_nt(left, right):
    return lax.dot_general(
        left, right, (((1,), (1,)), ((), ())), preferred_element_type=jnp.float32
    )


def split_dot(left, right):
    left_high, left_low = left
    right_high, right_low = right
    return wide_dot(
        jnp.concatenate([left_high, left_high, left_low], axis=1),
        jnp.concatenate([right_high, right_low, right_high], axis=0),
    )


def split_dot_nt(left, right):
    left_high, left_low = left
    right_high, right_low = right
    return wide_dot_nt(
        jnp.concatenate([left_high, left_high, left_low], axis=1),
        jnp.concatenate([right_high, right_low, right_high], axis=1),
    )


def identity_matrix():
    return (
        lax.broadcasted_iota(jnp.int32, (M, M), 0) == lax.broadcasted_iota(jnp.int32, (M, M), 1)
    ).astype(jnp.float32)


def chunk_of(ref, slot, index):
    rows = ref.shape[2]
    per = CHUNK // rows
    return ref[pl.ds(index * per, per), slot].reshape(CHUNK, HD)


def store_chunk(ref, slot, index, value):
    rows = ref.shape[2]
    per = CHUNK // rows
    ref[pl.ds(index * per, per), slot] = value.reshape(per, rows, HD)


def columns(index):
    return pl.ds(pl.multiple_of(index * CHUNK, CHUNK), CHUNK)


def pack_kernel(first_ref, second_ref, out_ref, rows_s, packed_s, in_done, out_done):
    heads = out_ref.shape[0]
    group = heads // PACK_GROUPS
    reads, writes = [], []
    for index in range(PACK_GROUPS):
        for slot, ref in enumerate((first_ref, second_ref)):
            place = pl.ds(index * group * HD, group * HD)
            reads.append(
                pltpu.make_async_copy(
                    ref.at[:, place], rows_s.at[slot, :, place], in_done.at[slot, index]
                )
            )
        place = pl.ds(index * group, group)
        writes.append(
            pltpu.make_async_copy(packed_s.at[place], out_ref.at[place], out_done.at[index])
        )
    for copy in reads:
        copy.start()
    for index in range(PACK_GROUPS):
        for slot in range(2):
            reads[2 * index + slot].wait()
            for head in range(index * group, (index + 1) * group):
                packed_s[head, slot] = rows_s[slot, :, head * HD : (head + 1) * HD]
        writes[index].start()
    for copy in writes:
        copy.wait()


def unpack_kernel(packed_ref, first_ref, second_ref, rows_s, out_done):
    heads = packed_ref.shape[0]
    group = heads // PACK_GROUPS
    writes = []
    for index in range(PACK_GROUPS):
        for slot, ref in enumerate((first_ref, second_ref)):
            for head in range(index * group, (index + 1) * group):
                rows_s[slot, :, head * HD : (head + 1) * HD] = packed_ref[head, slot]
            place = pl.ds(index * group * HD, group * HD)
            write = pltpu.make_async_copy(
                rows_s.at[slot, :, place], ref.at[:, place], out_done.at[slot, index]
            )
            write.start()
            writes.append(write)
    for copy in writes:
        copy.wait()


def forward_kernel(
    names,
    qk_hbm,
    *refs,
):
    count = len(names)
    homes = dict(zip(names, refs[:count]))
    held = dict(zip(names, refs[count : 2 * count]))
    qk_ref, power_s, iterate_s, in_done, out_done = refs[2 * count :]
    copies = {
        name: pltpu.make_async_copy(held[name], homes[name], out_done.at[index])
        for index, name in enumerate(names)
    }
    arrive = pltpu.make_async_copy(qk_hbm, qk_ref, in_done)
    arrive.start()
    arrive.wait()
    (
        mark_q_ref,
        mark_k_ref,
        mark_prob_ref,
        factor_ref,
        token_prob_ref,
        token_low_ref,
        key_prob_ref,
        key_plow_ref,
        key_low_ref,
        total_inverse_ref,
        columns_turned_ref,
        pair_ref,
        weight_ref,
        growth_ref,
        inverse_ref,
        last_growth_ref,
    ) = (held[name] for name in names)
    tokens, rows, chunks = dims_of(qk_ref)
    segment_len = tokens // M
    marks_per = CHUNK // segment_len
    score_scale = HD ** (-0.5)
    member = (
        lax.broadcasted_iota(jnp.int32, (marks_per, CHUNK), 1) // segment_len
        == lax.broadcasted_iota(jnp.int32, (marks_per, CHUNK), 0)
    ).astype(jnp.bfloat16)
    for index in range(chunks):
        both = jnp.concatenate([chunk_of(qk_ref, 0, index), chunk_of(qk_ref, 1, index)], axis=1)
        mean = (wide_dot(member, both) / segment_len).astype(jnp.bfloat16)
        mark_q_ref[index * marks_per : (index + 1) * marks_per] = mean[:, :HD]
        mark_k_ref[index * marks_per : (index + 1) * marks_per] = mean[:, HD:]
    landmark_q, landmark_k = mark_q_ref[...], mark_k_ref[...]

    mark_score = wide_dot_nt(landmark_q, landmark_k) * score_scale
    mark_exp = jnp.exp(mark_score - jnp.max(mark_score, axis=1, keepdims=True))
    mark_prob = mark_exp / jnp.sum(mark_exp, axis=1, keepdims=True)
    mark_prob_ref[...] = mark_prob
    factor = 1.0 / jnp.max(jnp.sum(mark_prob, axis=0, keepdims=True), axis=1, keepdims=True)
    factor_ref[...] = jnp.broadcast_to(factor, factor_ref.shape)
    mark_halves = halves(mark_prob)
    power_s[...] = split_dot_nt(mark_halves, mark_halves) * factor
    iterate_s[0:M] = mark_prob.T * factor
    iterate_s[M:] = identity_matrix()

    def scores(index, key_max):
        query_chunk, key_chunk = chunk_of(qk_ref, 0, index), chunk_of(qk_ref, 1, index)
        place = columns(index)
        columns_turned_ref[0, :, place] = query_chunk.T
        columns_turned_ref[1, :, place] = key_chunk.T
        score = wide_dot_nt(query_chunk, landmark_k) * score_scale
        grown = jnp.exp(score - jnp.max(score, axis=1, keepdims=True))
        prob = grown * (1.0 / jnp.sum(grown, axis=1, keepdims=True))
        token_prob_ref[place] = prob
        token_low_ref[place] = prob.astype(jnp.bfloat16)
        key_score = wide_dot_nt(key_chunk, landmark_q) * score_scale
        key_prob_ref[place] = key_score
        return jnp.maximum(key_max, jnp.max(key_score, axis=0, keepdims=True))

    key_max = lax.fori_loop(0, chunks, scores, jnp.full((1, M), -jnp.inf, jnp.float32))

    def grow(index, key_total):
        place = columns(index)
        grown = jnp.exp(key_prob_ref[place] - key_max)
        key_prob_ref[place] = grown
        key_low_ref[place] = grown.astype(jnp.bfloat16)
        return key_total + jnp.sum(grown, axis=0, keepdims=True)

    key_total = lax.fori_loop(0, chunks, grow, jnp.zeros((1, M), jnp.float32))
    total_inverse = 1.0 / key_total
    total_inverse_ref[...] = jnp.broadcast_to(total_inverse, total_inverse_ref.shape)

    def normalise(index, carry):
        place = columns(index)
        prob = key_prob_ref[place] * total_inverse
        key_prob_ref[place] = prob
        key_plow_ref[place] = prob.astype(jnp.bfloat16)
        return carry

    lax.fori_loop(0, chunks, normalise, 0)
    for name in EARLY_NAMES:
        copies[name].start()

    def newton(sweep, carry):
        power = power_s[...]
        power_high, power_low = halves(power)
        square = split_dot((power_high, power_low), (power_high, power_low))
        square_halves = halves(square)
        pair = (
            jnp.concatenate([power_high, square_halves[0]], axis=0),
            jnp.concatenate([power_low, square_halves[1]], axis=0),
        )
        pair_ref[sweep, 0], pair_ref[sweep, 1] = pair
        higher = split_dot(pair, square_halves)
        cube, fourth = higher[:M], higher[M:]
        weight = halves(
            0.25 * (13.0 * identity_matrix() - 15.0 * power + 7.0 * square - cube)
        )
        power_s[...] = 0.25 * (13.0 * power - 15.0 * square + 7.0 * cube - fourth)
        weight_ref[sweep, 0], weight_ref[sweep, 1] = weight
        iterate = halves(iterate_s[...])
        growth_ref[sweep, 0], growth_ref[sweep, 1] = iterate[0][M:], iterate[1][M:]
        iterate_s[...] = split_dot(iterate, weight)
        return carry

    lax.fori_loop(0, PINV_ITERS, newton, 0)
    inverse = iterate_s[0:M]
    inverse_ref[0], inverse_ref[1] = halves(inverse)
    last_growth_ref[0], last_growth_ref[1] = halves(iterate_s[M:])
    for name in names:
        if name not in EARLY_NAMES:
            copies[name].start()
    for name in names:
        copies[name].wait()


def start_reads(sources, held, done):
    reads = [
        pltpu.make_async_copy(source, ref, done.at[index])
        for index, (source, ref) in enumerate(zip(sources, held))
    ]
    for read in reads:
        read.start()
    return reads


def mixing_kernel(*refs):
    count = len(MIXING_NAMES) + 1
    sources, homes, held = refs[:count], refs[count : count + 5], refs[count + 5 : 2 * count + 5]
    results = refs[2 * count + 5 : 2 * count + 10]
    in_done, out_done, part_done = refs[2 * count + 10 :]
    vg_ref, key_low_ref, total_inverse_ref, inverse_ref, token_low_ref, key_plow_ref = held
    reads = start_reads(sources, held, in_done)
    out_ref, mixing_low_ref, mixing_grad_ref, mark_values_ref, values_low_ref = results
    writes = [
        pltpu.make_async_copy(result, home, out_done.at[index])
        for index, (result, home) in enumerate(zip(results[1:], homes[1:]))
    ]
    tokens, rows, chunks = dims_of(vg_ref)
    reads[0].wait()
    values_turned = vg_ref[:, 0].reshape(tokens, HD).T
    for read in reads[1:4]:
        read.wait()
    inverse = (inverse_ref[0], inverse_ref[1])
    landmark_values = wide_dot(values_turned, key_low_ref[...]) * total_inverse_ref[0:1]
    mark_values_ref[...] = landmark_values
    mixing_low = split_dot_nt(halves(landmark_values), inverse).astype(jnp.bfloat16)
    mixing_low_ref[...] = mixing_low
    grad_turned = vg_ref[:, 1].reshape(tokens, HD).T
    reads[4].wait()
    mixing_grad = wide_dot(grad_turned, token_low_ref[...])
    mixing_grad_ref[...] = mixing_grad
    values_low = split_dot(halves(mixing_grad), inverse).astype(jnp.bfloat16)
    values_low_ref[...] = values_low
    for write in writes:
        write.start()
    out_ref[:, 0] = (
        wide_dot_nt(token_low_ref[...], mixing_low).astype(jnp.bfloat16).reshape(-1, rows, HD)
    )
    reads[5].wait()
    for part in range(MIXING_PARTS):
        span = tokens // MIXING_PARTS
        group = slice(part * span // rows, (part + 1) * span // rows)
        place = slice(part * span, (part + 1) * span)
        value_gradient = wide_dot_nt(key_plow_ref[place], values_low).astype(jnp.bfloat16)
        out_ref[group, 1] = value_gradient.reshape(-1, rows, HD)
        heads = pl.ds(group.start, group.stop - group.start)
        copy = pltpu.make_async_copy(out_ref.at[heads], homes[0].at[heads], part_done.at[part])
        copy.start()
        writes.append(copy)
    for copy in writes:
        copy.wait()


def gradient_kernel(*refs):
    count = len(GRADIENT_NAMES) + 5
    sources, home, held = refs[:count], refs[count], refs[count + 1 : 2 * count + 1]
    out_ref, power_s, growth_s, query_s, direct_s, kept_s, in_done, out_done = refs[2 * count + 1 :]
    reads = start_reads(sources, held, in_done)
    (
        values_low_ref,
        mixing_low_ref,
        vg_ref,
        mark_q_ref,
        mark_k_ref,
        key_prob_ref,
        columns_turned_ref,
        token_prob_ref,
        mark_prob_ref,
        factor_ref,
        pair_ref,
        weight_ref,
        growth_ref,
        last_growth_ref,
        mixing_grad_ref,
        mark_values_ref,
    ) = held
    tokens, rows, chunks = dims_of(vg_ref)
    segment_len = tokens // M
    marks_per = CHUNK // segment_len
    score_scale = HD ** (-0.5)
    for read in reads[:8]:
        read.wait()
    landmark_q, landmark_k = mark_q_ref[...], mark_k_ref[...]

    values_low = values_low_ref[...]

    def key_rows(index, row_total):
        place = columns(index)
        key_dgrad = wide_dot(chunk_of(vg_ref, 0, index), values_low)
        kept_s[place] = key_dgrad
        return row_total + jnp.sum(key_prob_ref[place] * key_dgrad, axis=0, keepdims=True)

    row_total = lax.fori_loop(0, chunks, key_rows, jnp.zeros((1, M), jnp.float32))

    def key_side(index, total):
        place = columns(index)
        key_sgrad = (key_prob_ref[place] * (kept_s[place] - row_total)).astype(jnp.bfloat16)
        direct_s[place] = wide_dot(key_sgrad, landmark_q) * score_scale
        return total + wide_dot(columns_turned_ref[1, :, place], key_sgrad)

    mark_qgrad_b = lax.fori_loop(0, chunks, key_side, jnp.zeros((HD, M), jnp.float32))
    mixing_low = mixing_low_ref[...]

    def token_side(index, total):
        place = columns(index)
        prob = token_prob_ref[place]
        token_grad = wide_dot(chunk_of(vg_ref, 1, index), mixing_low)
        token_sgrad = (
            prob * (token_grad - jnp.sum(token_grad * prob, axis=1, keepdims=True))
        ).astype(jnp.bfloat16)
        query_s[place] = wide_dot(token_sgrad, landmark_k) * score_scale
        return total + wide_dot(columns_turned_ref[0, :, place], token_sgrad)

    mark_kgrad_f = lax.fori_loop(0, chunks, token_side, jnp.zeros((HD, M), jnp.float32))

    for read in reads[8:]:
        read.wait()
    mark_prob = mark_prob_ref[...]
    mark_halves = halves(mark_prob)
    factor = factor_ref[0:1, 0:1]
    inverse_grad = split_dot(halves(mixing_grad_ref[...].T), halves(mark_values_ref[...]))
    inverse_grad_halves = halves(inverse_grad)
    toward = split_dot(mark_halves, inverse_grad_halves) * factor
    power_s[...] = 0.5 * (toward + toward.T)
    growth_s[...] = jnp.zeros((M, M), jnp.float32)

    def newton(sweep, carry):
        power = power_s[...]
        pair = (pair_ref[sweep, 0], pair_ref[sweep, 1])
        first = split_dot(pair, halves(power))
        square = first[:M] + first[:M].T
        second = split_dot(pair, halves(square))
        cube = first[M:].T + second[:M]
        fourth = second[M:] + second[M:].T
        weight = halves(0.25 * (7.0 * square - 15.0 * power - cube))
        power_s[...] = 0.25 * (13.0 * power - 15.0 * square + 7.0 * cube - fourth)
        grown_high, grown_low = halves(growth_s[...])
        held_high, held_low = growth_ref[sweep, 0], growth_ref[sweep, 1]
        held_weight_high, held_weight_low = weight_ref[sweep, 0], weight_ref[sweep, 1]
        growth_s[...] = wide_dot(
            jnp.concatenate(
                [grown_high, grown_high, grown_low, held_high, held_high, held_low], axis=1
            ),
            jnp.concatenate(
                [
                    held_weight_high,
                    held_weight_low,
                    held_weight_high,
                    weight[0],
                    weight[1],
                    weight[0],
                ],
                axis=0,
            ),
        )
        return carry

    lax.fori_loop(0, PINV_ITERS, newton, 0)
    growth = growth_s[...]
    mark_grad = factor * (
        split_dot_nt((last_growth_ref[0], last_growth_ref[1]), inverse_grad_halves)
        + split_dot(halves(growth + growth.T), mark_halves)
    )
    mark_sgrad = mark_prob * (mark_grad - jnp.sum(mark_grad * mark_prob, axis=1, keepdims=True))

    def marks_dot(left, right):
        high, low = halves(left)
        return wide_dot(
            jnp.concatenate([high, low], axis=1), jnp.concatenate([right, right], axis=0)
        )

    mark_qgrad_a = marks_dot(mark_sgrad, landmark_k)
    mark_kgrad_a = marks_dot(mark_sgrad.T, landmark_q)
    kept_s[0:M, 0:HD] = (mark_qgrad_a + mark_qgrad_b.T) * (score_scale / segment_len)
    kept_s[0:M, HD:] = (mark_kgrad_a + mark_kgrad_f.T) * (score_scale / segment_len)

    def spread(direct, marks):
        wide = jnp.broadcast_to(marks[:, None], (marks_per, segment_len, HD))
        return (direct + wide.reshape(CHUNK, HD)).astype(jnp.bfloat16)

    def finish(index, carry):
        marks = kept_s[pl.ds(pl.multiple_of(index * marks_per, marks_per), marks_per)]
        place = columns(index)
        store_chunk(out_ref, 0, index, spread(query_s[place], marks[:, :HD]))
        store_chunk(out_ref, 1, index, spread(direct_s[place], marks[:, HD:]))
        return carry

    lax.fori_loop(0, chunks, finish, 0)
    write = pltpu.make_async_copy(out_ref, home, out_done)
    write.start()
    write.wait()


def kernel_call(kernel, out_shape, scratch, flops, operands, limit=VMEM_LIMIT, in_place=None):
    moved = sum(x.size * x.dtype.itemsize for x in operands)
    anywhere = pl.BlockSpec(memory_space=pl.ANY)
    held = pl.BlockSpec(memory_space=pltpu.VMEM)
    return pl.pallas_call(
        kernel,
        out_shape=out_shape,
        in_specs=[held if index == in_place else anywhere for index in range(len(operands))],
        out_specs=jax.tree.map(lambda _: anywhere, out_shape),
        scratch_shapes=scratch,
        compiler_params=pltpu.CompilerParams(vmem_limit_bytes=limit),
        cost_estimate=pl.CostEstimate(flops=flops, bytes_accessed=moved, transcendentals=0),
    )(*operands)


def in_vmem(array):
    return pltpu.VMEM(array.shape, array.dtype)


def pack(first, second):
    rows, width = first.shape
    heads = width // HD
    shape = jax.ShapeDtypeStruct((heads, 2, rows, HD), first.dtype)
    scratch = [
        pltpu.VMEM((2, rows, width), first.dtype),
        pltpu.VMEM((heads, 2, rows, HD), first.dtype),
        pltpu.SemaphoreType.DMA((2, PACK_GROUPS)),
        pltpu.SemaphoreType.DMA((PACK_GROUPS,)),
    ]
    return kernel_call(pack_kernel, shape, scratch, 0, (first, second))


def unpack(packed):
    heads, _, rows, _ = packed.shape
    shape = jax.ShapeDtypeStruct((rows, heads * HD), packed.dtype)
    scratch = [
        pltpu.VMEM((2, rows, heads * HD), packed.dtype),
        pltpu.SemaphoreType.DMA((2, PACK_GROUPS)),
    ]
    return kernel_call(
        unpack_kernel, (shape, shape), scratch, 0, (packed,), limit=SMALL_LIMIT, in_place=0
    )


def forward_part(qk):
    tokens = qk.shape[0] * qk.shape[2]

    def low(*shape):
        return jax.ShapeDtypeStruct(shape, jnp.bfloat16)

    def wide(*shape):
        return jax.ShapeDtypeStruct(shape, jnp.float32)

    shapes = dict(
        mark_q=low(M, HD),
        mark_k=low(M, HD),
        mark_prob=wide(M, M),
        factor=wide(8, HD),
        token_prob=wide(tokens, M),
        token_low=low(tokens, M),
        key_prob=wide(tokens, M),
        key_plow=low(tokens, M),
        key_low=low(tokens, M),
        total_inverse=wide(8, M),
        columns_turned=low(2, HD, tokens),
        pair=low(PINV_ITERS, 2, 2 * M, M),
        weight=low(PINV_ITERS, 2, M, M),
        growth=low(PINV_ITERS, 2, M, M),
        inverse=low(2, M, M),
        last_growth=low(2, M, M),
    )
    scratch = [
        *(in_vmem(shape) for shape in shapes.values()),
        in_vmem(qk),
        pltpu.VMEM((M, M), jnp.float32),
        pltpu.VMEM((2 * M, M), jnp.float32),
        pltpu.SemaphoreType.DMA,
        pltpu.SemaphoreType.DMA((len(shapes),)),
    ]
    results = kernel_call(
        functools.partial(forward_kernel, tuple(shapes)),
        tuple(shapes.values()),
        scratch,
        FORWARD_FLOPS,
        (qk,),
    )
    return dict(zip(shapes, results))


def mixing_part(vg, kept):
    shapes = (
        jax.ShapeDtypeStruct(vg.shape, jnp.bfloat16),
        jax.ShapeDtypeStruct((HD, M), jnp.bfloat16),
        jax.ShapeDtypeStruct((HD, M), jnp.float32),
        jax.ShapeDtypeStruct((HD, M), jnp.float32),
        jax.ShapeDtypeStruct((HD, M), jnp.bfloat16),
    )
    operands = (vg, *(kept[name] for name in MIXING_NAMES))
    scratch = [
        *(in_vmem(array) for array in (*operands, *shapes)),
        pltpu.SemaphoreType.DMA((len(operands),)),
        pltpu.SemaphoreType.DMA((len(shapes) - 1,)),
        pltpu.SemaphoreType.DMA((MIXING_PARTS,)),
    ]
    return kernel_call(mixing_kernel, shapes, scratch, MIXING_FLOPS, operands)


def gradient_part(vg, kept, mixed):
    mixing_low, mixing_grad, mark_values, values_low = mixed
    operands = (
        values_low,
        mixing_low,
        vg,
        *(kept[name] for name in GRADIENT_NAMES),
        mixing_grad,
        mark_values,
    )
    tokens = vg.shape[0] * vg.shape[2]
    scratch = [
        *(in_vmem(array) for array in (*operands, vg)),
        pltpu.VMEM((M, M), jnp.float32),
        pltpu.VMEM((M, M), jnp.float32),
        pltpu.VMEM((tokens, HD), jnp.float32),
        pltpu.VMEM((tokens, HD), jnp.float32),
        pltpu.VMEM((tokens, M), jnp.float32),
        pltpu.SemaphoreType.DMA((len(operands),)),
        pltpu.SemaphoreType.DMA,
    ]
    shape = jax.ShapeDtypeStruct(vg.shape, jnp.bfloat16)
    return kernel_call(gradient_kernel, shape, scratch, GRADIENT_FLOPS, operands)


def exchange(packed):
    return lax.all_to_all(packed, ("seq", "head"), split_axis=0, concat_axis=0, tiled=True)


def body(queries, keys, values, out_grad):
    qk = exchange(pack(queries, keys))
    vg = exchange(pack(values, out_grad))
    kept = forward_part(qk)
    first_results, *mixed = mixing_part(vg, kept)
    second_results = gradient_part(vg, kept, mixed)
    attended, value_gradient_array = unpack(exchange(first_results))
    query_grad, key_grad = unpack(exchange(second_results))
    return attended, query_grad, key_grad, value_gradient_array


def solution(mesh):
    placement = P(("seq", "head"), None)

    def layer(queries, keys, values, out_grad):
        one_head_each = queries.shape[1] // HD == mesh.size and queries.shape[0] % CHUNK == 0
        return jax.shard_map(
            body if one_head_each else shared_body,
            mesh=mesh,
            in_specs=(placement,) * 4,
            out_specs=(placement,) * 4,
            check_vma=False,
        )(queries, keys, values, out_grad)

    return layer
```

```python
import functools

import jax
import jax.numpy as jnp
from jax import lax
from jax.experimental import pallas as pl
from jax.experimental.pallas import tpu as pltpu
from jax.sharding import PartitionSpec as P

HD = 128
M = 256
PINV_ITERS = 6
CHUNK = 256
PACK_GROUPS = 4
SWEEP_NAMES = ("pair", "weight", "growth")
VMEM_LIMIT = 60 * 2**20
SMALL_LIMIT = 16 * 2**20
FORWARD_FLOPS = 10 * 10**9
GRADIENT_FLOPS = 14 * 10**9


precise_setting = lax.Precision.HIGHEST


def newton_inverse(matrix):
    identity = jnp.eye(matrix.shape[0], dtype=matrix.dtype)
    factor = lax.stop_gradient(1.0 / jnp.max(jnp.sum(matrix, axis=0)))
    iterate = matrix.T * factor
    for sweep_index in range(PINV_ITERS):
        product = jnp.matmul(matrix, iterate, precision=precise_setting)
        inner_term = jnp.matmul(product, 7.0 * identity - product, precision=precise_setting)
        inner_term = jnp.matmul(product, 15.0 * identity - inner_term, precision=precise_setting)
        iterate = 0.25 * jnp.matmul(
            iterate, 13.0 * identity - inner_term, precision=precise_setting
        )
    return iterate


def share_heads(own_matrix, head_count):
    seq_index = lax.axis_index("seq")
    slot_mask = (jnp.arange(head_count, dtype=jnp.int32) == seq_index).astype(jnp.float32)
    return lax.psum(slot_mask[:, None, None] * own_matrix[None], "seq")


def shared_body(queries, keys, values, out_grad):
    query_rows, key_rows, value_rows, grad_rows = (
        lax.all_to_all(queries, "head", split_axis=1, concat_axis=0, tiled=True),
        lax.all_to_all(keys, "head", split_axis=1, concat_axis=0, tiled=True),
        lax.all_to_all(values, "head", split_axis=1, concat_axis=0, tiled=True),
        lax.all_to_all(out_grad, "head", split_axis=1, concat_axis=0, tiled=True),
    )
    tok_rows = query_rows.shape[0]
    head_count = query_rows.shape[1] // HD
    local_marks = M // lax.axis_size("seq")
    segment_len = tok_rows // local_marks
    score_scale = HD ** (-0.5)
    seq_index = lax.axis_index("seq")

    def landmark(matrix):
        summed = jnp.sum(
            matrix.reshape(local_marks, segment_len, matrix.shape[1]), axis=1, dtype=jnp.float32
        )
        return (summed / segment_len).astype(jnp.bfloat16)

    mark_queries, mark_keys = (
        lax.all_gather(landmark(query_rows), "seq", axis=0, tiled=True),
        lax.all_gather(landmark(key_rows), "seq", axis=0, tiled=True),
    )
    query_per_head = query_rows.reshape(tok_rows, head_count, HD)
    key_per_head = key_rows.reshape(tok_rows, head_count, HD)
    value_per_head = value_rows.reshape(tok_rows, head_count, HD)
    gradient_per_head = grad_rows.reshape(tok_rows, head_count, HD)
    landmark_query_heads = mark_queries.reshape(M, head_count, HD)
    landmark_key_heads = mark_keys.reshape(M, head_count, HD)
    key_score = (
        jnp.einsum(
            "pcv,gcv->cpg", landmark_query_heads, key_per_head, preferred_element_type=jnp.float32
        )
        * score_scale
    )
    key_max = lax.pmax(jnp.max(key_score, axis=-1), "seq")
    key_exp = jnp.exp(key_score - key_max[..., None])
    partial_num = jnp.einsum(
        "akq,qay->aky",
        key_exp.astype(jnp.bfloat16),
        value_per_head,
        preferred_element_type=jnp.float32,
    )
    key_total, numerator = lax.psum((jnp.sum(key_exp, axis=-1), partial_num), "seq")
    landmark_value_rows = numerator / key_total[..., None]
    token_prob = jax.nn.softmax(
        jnp.einsum(
            "jti,cti->tjc", query_per_head, landmark_key_heads, preferred_element_type=jnp.float32
        )
        * score_scale,
        axis=-1,
    )
    token_probability_lowered = token_prob.astype(jnp.bfloat16)
    mark_prob = jax.nn.softmax(
        jnp.einsum(
            "jou,iou->oji",
            landmark_query_heads,
            landmark_key_heads,
            preferred_element_type=jnp.float32,
        )
        * score_scale,
        axis=-1,
    )
    own_head = seq_index % head_count
    own_mark = lax.dynamic_index_in_dim(mark_prob, own_head, 0, keepdims=False)
    own_inverse, pull_back = jax.vjp(newton_inverse, own_mark)
    pseudo_inverse_matrix = share_heads(own_inverse, head_count)
    mixing_matrix = jnp.einsum(
        "jvy,jys->jvs", pseudo_inverse_matrix, landmark_value_rows, precision=precise_setting
    )
    mixing_matrix_lowered = mixing_matrix.astype(jnp.bfloat16)
    attended = jnp.einsum(
        "yvo,yor->vyr",
        token_probability_lowered,
        mixing_matrix_lowered,
        preferred_element_type=jnp.float32,
    ).astype(jnp.bfloat16)
    token_grad = jnp.einsum(
        "fag,aog->afo", gradient_per_head, mixing_matrix_lowered, preferred_element_type=jnp.float32
    )
    partial_mix = jnp.einsum(
        "klz,lkr->kzr",
        token_probability_lowered,
        gradient_per_head,
        preferred_element_type=jnp.float32,
    )
    mixing_matrix_gradient = lax.psum(partial_mix, "seq")
    token_score_gradient = (
        token_prob * (token_grad - jnp.sum(token_grad * token_prob, axis=-1, keepdims=True))
    ).astype(jnp.bfloat16)
    direct_qgrad = (
        jnp.einsum(
            "ufg,guc->fuc",
            token_score_gradient,
            landmark_key_heads,
            preferred_element_type=jnp.float32,
        )
        * score_scale
    )
    mark_kgrad_f = (
        jnp.einsum(
            "xgi,gxy->ixy", token_score_gradient, query_per_head, preferred_element_type=jnp.float32
        )
        * score_scale
    )
    pseudo_inverse_gradient = jnp.einsum(
        "ktu,kyu->kty", mixing_matrix_gradient, landmark_value_rows, precision=precise_setting
    )
    landmark_value_gradient = jnp.einsum(
        "lrb,lrz->lbz", pseudo_inverse_matrix, mixing_matrix_gradient, precision=precise_setting
    )
    own_igrad = lax.dynamic_index_in_dim(pseudo_inverse_gradient, own_head, 0, keepdims=False)
    (own_mgrad,) = pull_back(own_igrad)
    mark_grad = share_heads(own_mgrad, head_count)
    mark_sgrad = mark_prob * (mark_grad - jnp.sum(mark_grad * mark_prob, axis=-1, keepdims=True))
    first_mark = seq_index * local_marks
    score_gradient_rows = lax.dynamic_slice_in_dim(mark_sgrad, first_mark, local_marks, 1)
    score_gradient_columns = lax.dynamic_slice_in_dim(mark_sgrad, first_mark, local_marks, 2)
    own_qgrad_a = (
        jnp.einsum(
            "txs,ste->xte",
            score_gradient_rows,
            landmark_key_heads.astype(jnp.float32),
            precision=precise_setting,
        )
        * score_scale
    )
    own_kgrad_a = (
        jnp.einsum(
            "eaj,aev->jev",
            score_gradient_columns,
            landmark_query_heads.astype(jnp.float32),
            precision=precise_setting,
        )
        * score_scale
    )
    landmark_value_lowered = landmark_value_gradient.astype(jnp.bfloat16)
    key_prob = key_exp / key_total[..., None]
    key_probability_lowered = key_prob.astype(jnp.bfloat16)
    value_gradient_array = jnp.einsum(
        "zct,zcj->tzj",
        key_probability_lowered,
        landmark_value_lowered,
        preferred_element_type=jnp.float32,
    )
    key_direct_gradient = jnp.einsum(
        "exb,geb->exg", landmark_value_lowered, value_per_head, preferred_element_type=jnp.float32
    )
    row_total = lax.psum(jnp.sum(key_prob * key_direct_gradient, axis=-1), "seq")
    key_score_gradient = (key_prob * (key_direct_gradient - row_total[..., None])).astype(
        jnp.bfloat16
    )
    direct_kgrad = (
        jnp.einsum(
            "pbo,bpx->opx",
            key_score_gradient,
            landmark_query_heads,
            preferred_element_type=jnp.float32,
        )
        * score_scale
    )
    mark_qgrad_b = (
        jnp.einsum(
            "cbj,jcp->bcp", key_score_gradient, key_per_head, preferred_element_type=jnp.float32
        )
        * score_scale
    )
    own_kgrad_f, own_qgrad_b = (
        lax.psum_scatter(mark_kgrad_f, "seq", scatter_dimension=0, tiled=True),
        lax.psum_scatter(mark_qgrad_b, "seq", scatter_dimension=0, tiled=True),
    )
    mark_qtotal = (own_qgrad_a + own_qgrad_b) / segment_len
    mark_ktotal = (own_kgrad_a + own_kgrad_f) / segment_len
    query_grad = (
        direct_qgrad.reshape(local_marks, segment_len, head_count, HD) + mark_qtotal[:, None]
    )
    key_grad = direct_kgrad.reshape(local_marks, segment_len, head_count, HD) + mark_ktotal[:, None]
    width = head_count * HD
    results = (
        attended.reshape(tok_rows, width),
        query_grad.astype(jnp.bfloat16).reshape(tok_rows, width),
        key_grad.astype(jnp.bfloat16).reshape(tok_rows, width),
        value_gradient_array.astype(jnp.bfloat16).reshape(tok_rows, width),
    )
    attended_out, query_out, key_out, value_out = (
        lax.all_to_all(results[0], "head", split_axis=0, concat_axis=1, tiled=True),
        lax.all_to_all(results[1], "head", split_axis=0, concat_axis=1, tiled=True),
        lax.all_to_all(results[2], "head", split_axis=0, concat_axis=1, tiled=True),
        lax.all_to_all(results[3], "head", split_axis=0, concat_axis=1, tiled=True),
    )
    return (attended_out, query_out, key_out, value_out)


def dims_of(rows):
    tokens = rows.shape[0] * rows.shape[2]
    return tokens, rows.shape[2], tokens // CHUNK


def halves(matrix):
    high = matrix.astype(jnp.bfloat16)
    return high, (matrix - high.astype(jnp.float32)).astype(jnp.bfloat16)


def wide_dot(left, right):
    return jnp.dot(left, right, preferred_element_type=jnp.float32)


def wide_dot_nt(left, right):
    return lax.dot_general(
        left, right, (((1,), (1,)), ((), ())), preferred_element_type=jnp.float32
    )


def split_dot(left, right):
    left_high, left_low = left
    right_high, right_low = right
    return wide_dot(
        jnp.concatenate([left_high, left_high, left_low], axis=1),
        jnp.concatenate([right_high, right_low, right_high], axis=0),
    )


def split_dot_nt(left, right):
    left_high, left_low = left
    right_high, right_low = right
    return wide_dot_nt(
        jnp.concatenate([left_high, left_high, left_low], axis=1),
        jnp.concatenate([right_high, right_low, right_high], axis=1),
    )


def identity_matrix():
    return (
        lax.broadcasted_iota(jnp.int32, (M, M), 0) == lax.broadcasted_iota(jnp.int32, (M, M), 1)
    ).astype(jnp.float32)


def chunk_of(ref, slot, index):
    rows = ref.shape[2]
    per = CHUNK // rows
    return ref[pl.ds(index * per, per), slot].reshape(CHUNK, HD)


def store_chunk(ref, slot, index, value):
    rows = ref.shape[2]
    per = CHUNK // rows
    ref[pl.ds(index * per, per), slot] = value.reshape(per, rows, HD)


def columns(index):
    return pl.ds(pl.multiple_of(index * CHUNK, CHUNK), CHUNK)


def pack_kernel(*refs):
    arrays = len(refs) - 5
    sources, (out_ref, rows_s, packed_s, in_done, out_done) = refs[:arrays], refs[arrays:]
    group = out_ref.shape[0] // PACK_GROUPS
    reads, writes = [], []
    for index in range(PACK_GROUPS):
        for slot, ref in enumerate(sources):
            place = pl.ds(index * group * HD, group * HD)
            reads.append(
                pltpu.make_async_copy(
                    ref.at[:, place], rows_s.at[slot, :, place], in_done.at[slot, index]
                )
            )
        place = pl.ds(index * group, group)
        writes.append(
            pltpu.make_async_copy(packed_s.at[place], out_ref.at[place], out_done.at[index])
        )
    for copy in reads:
        copy.start()
    for index in range(PACK_GROUPS):
        for slot in range(arrays):
            reads[arrays * index + slot].wait()
            for head in range(index * group, (index + 1) * group):
                packed_s[head, slot] = rows_s[slot, :, head * HD : (head + 1) * HD]
        writes[index].start()
    for copy in writes:
        copy.wait()


def unpack_kernel(packed_ref, *refs):
    homes, (rows_s, out_done) = refs[:-2], refs[-2:]
    group = packed_ref.shape[0] // PACK_GROUPS
    writes = []
    for index in range(PACK_GROUPS):
        for slot, ref in enumerate(homes):
            for head in range(index * group, (index + 1) * group):
                rows_s[slot, :, head * HD : (head + 1) * HD] = packed_ref[head, slot]
            place = pl.ds(index * group * HD, group * HD)
            write = pltpu.make_async_copy(
                rows_s.at[slot, :, place], ref.at[:, place], out_done.at[slot, index]
            )
            write.start()
            writes.append(write)
    for copy in writes:
        copy.wait()


def sweep_forward(power_s, iterate_s, saved, sweep, work):
    pair_ref, weight_ref, growth_ref = saved
    power = power_s[...]
    power_high, power_low = halves(power)
    square = split_dot((power_high, power_low), (power_high, power_low))
    next(work)()
    square_halves = halves(square)
    pair = (
        jnp.concatenate([power_high, square_halves[0]], axis=0),
        jnp.concatenate([power_low, square_halves[1]], axis=0),
    )
    pair_ref[sweep, 0], pair_ref[sweep, 1] = pair
    higher = split_dot(pair, square_halves)
    next(work)()
    cube, fourth = higher[:M], higher[M:]
    weight = halves(0.25 * (13.0 * identity_matrix() - 15.0 * power + 7.0 * square - cube))
    power_s[...] = 0.25 * (13.0 * power - 15.0 * square + 7.0 * cube - fourth)
    weight_ref[sweep, 0], weight_ref[sweep, 1] = weight
    iterate = halves(iterate_s[...])
    growth_ref[sweep, 0], growth_ref[sweep, 1] = iterate[0][M:], iterate[1][M:]
    iterate_s[...] = split_dot(iterate, weight)


def forward_kernel(names, qkv_hbm, *refs):
    count = len(names)
    homes, refs = dict(zip(names, refs[:count])), refs[count:]
    held, refs = dict(zip(names, refs[:count])), refs[count:]
    qkv_ref, power_s, iterate_s, token_low_s, key_low_s, in_done, out_done, sweep_done = refs
    copies = {
        name: pltpu.make_async_copy(held[name], homes[name], out_done.at[index])
        for index, name in enumerate(names)
        if name not in SWEEP_NAMES
    }
    sent = []

    def send(*chosen):
        for name in chosen:
            copies[name].start()
            sent.append(copies[name])

    arrive = [
        pltpu.make_async_copy(qkv_hbm.at[:, slot], qkv_ref.at[:, slot], in_done.at[slot])
        for slot in range(3)
    ]
    for copy in arrive:
        copy.start()
    for copy in arrive[:2]:
        copy.wait()
    tokens, rows, chunks = dims_of(qkv_ref)
    segment_len = tokens // M
    marks_per = CHUNK // segment_len
    score_scale = HD ** (-0.5)
    member = (
        lax.broadcasted_iota(jnp.int32, (marks_per, CHUNK), 1) // segment_len
        == lax.broadcasted_iota(jnp.int32, (marks_per, CHUNK), 0)
    ).astype(jnp.bfloat16)
    for index in range(chunks):
        both = jnp.concatenate([chunk_of(qkv_ref, 0, index), chunk_of(qkv_ref, 1, index)], axis=1)
        mean = (wide_dot(member, both) / segment_len).astype(jnp.bfloat16)
        held["mark_q"][index * marks_per : (index + 1) * marks_per] = mean[:, :HD]
        held["mark_k"][index * marks_per : (index + 1) * marks_per] = mean[:, HD:]
    landmark_q, landmark_k = held["mark_q"][...], held["mark_k"][...]

    mark_score = wide_dot_nt(landmark_q, landmark_k) * score_scale
    mark_exp = jnp.exp(mark_score - jnp.max(mark_score, axis=1, keepdims=True))
    mark_prob = mark_exp / jnp.sum(mark_exp, axis=1, keepdims=True)
    held["mark_prob"][...] = mark_prob
    factor = 1.0 / jnp.max(jnp.sum(mark_prob, axis=0, keepdims=True), axis=1, keepdims=True)
    held["factor"][...] = jnp.broadcast_to(factor, held["factor"].shape)
    mark_halves = halves(mark_prob)
    power_s[...] = split_dot_nt(mark_halves, mark_halves) * factor
    iterate_s[0:M] = mark_prob.T * factor
    iterate_s[M:] = identity_matrix()
    send("mark_q", "mark_k", "mark_prob", "factor")

    tops, totals = [], []
    places = [slice(index * CHUNK, (index + 1) * CHUNK) for index in range(chunks)]

    def scores(index):
        query_chunk, key_chunk = chunk_of(qkv_ref, 0, index), chunk_of(qkv_ref, 1, index)
        place = places[index]
        held["turned"][0, :, place] = query_chunk.T
        held["turned"][1, :, place] = key_chunk.T
        score = wide_dot_nt(query_chunk, landmark_k) * score_scale
        grown = jnp.exp(score - jnp.max(score, axis=1, keepdims=True))
        prob = grown * (1.0 / jnp.sum(grown, axis=1, keepdims=True))
        held["token_prob"][place] = prob
        token_low_s[place] = prob.astype(jnp.bfloat16)
        key_score = wide_dot_nt(key_chunk, landmark_q) * score_scale
        held["key_prob"][place] = key_score
        tops.append(jnp.max(key_score, axis=0, keepdims=True))

    def grow(index):
        if index == 0:
            tops[0] = functools.reduce(jnp.maximum, tops)
        place = places[index]
        grown = jnp.exp(held["key_prob"][place] - tops[0])
        held["key_prob"][place] = grown
        key_low_s[place] = grown.astype(jnp.bfloat16)
        totals.append(jnp.sum(grown, axis=0, keepdims=True))

    def units():
        half = (chunks + 3) // 4
        for first in range(0, chunks, max(1, chunks // 8)):
            yield functools.partial(
                lambda start: [scores(x) for x in range(start, min(chunks, start + chunks // 8))],
                first,
            )
        for first in range(0, chunks, half):
            yield functools.partial(
                lambda start: [grow(x) for x in range(start, min(chunks, start + half))], first
            )

    work = units()
    saved = tuple(held[name] for name in SWEEP_NAMES)
    for sweep in range(PINV_ITERS):
        sweep_forward(power_s, iterate_s, saved, sweep, work)
        for place, name in enumerate(SWEEP_NAMES):
            copy = pltpu.make_async_copy(
                held[name].at[sweep], homes[name].at[sweep], sweep_done.at[place, sweep]
            )
            copy.start()
            sent.append(copy)
        if sweep == 3:
            send("token_prob", "turned")
    inverse = halves(iterate_s[0:M])
    held["inverse"][0], held["inverse"][1] = inverse
    held["last_growth"][0], held["last_growth"][1] = halves(iterate_s[M:])
    send("inverse", "last_growth")
    total_inverse = 1.0 / sum(totals[1:], totals[0])
    arrive[2].wait()
    values_turned = qkv_ref[:, 2].reshape(tokens, HD).T
    landmark_values = wide_dot(values_turned, key_low_s[...]) * total_inverse
    held["mark_values"][...] = landmark_values
    mixing_low = split_dot_nt(halves(landmark_values), inverse).astype(jnp.bfloat16)
    held["mixing_low"][...] = mixing_low
    attended = wide_dot_nt(token_low_s[...], mixing_low).astype(jnp.bfloat16)
    held["attended"][:, 0] = attended.reshape(-1, rows, HD)
    send("attended", "mark_values", "mixing_low")
    for place in places:
        held["key_prob"][place] = held["key_prob"][place] * total_inverse
    send("key_prob")
    for copy in sent:
        copy.wait()


def gradient_kernel(names, qkv_hbm, grad_hbm, *refs):
    count = len(names)
    sources, home, refs = dict(zip(names, refs[:count])), refs[count], refs[count + 1 :]
    held, refs = dict(zip(names, refs[:count])), refs[count:]
    values_s, grads_s, out_ref, query_s, direct_s, kept_s, in_done, sweep_done, out_done = refs
    reads = {
        name: pltpu.make_async_copy(sources[name], held[name], in_done.at[index])
        for index, name in enumerate(names)
        if name not in SWEEP_NAMES
    }
    fetch_grads = pltpu.make_async_copy(grad_hbm.at[:, 0], grads_s, in_done.at[count])
    fetch_values = pltpu.make_async_copy(qkv_hbm.at[:, 2], values_s, in_done.at[count + 1])
    sweeps = [
        [
            pltpu.make_async_copy(
                sources[name].at[sweep], held[name].at[sweep], sweep_done.at[place, sweep]
            )
            for place, name in enumerate(SWEEP_NAMES)
        ]
        for sweep in range(PINV_ITERS)
    ]

    def start(*chosen):
        for name in chosen:
            reads[name].start()

    def wait(*chosen):
        for name in chosen:
            reads[name].wait()

    fetch_grads.start()
    start("token_prob", "inverse", "mark_values", "mark_prob", "factor")
    for copy in sweeps[0]:
        copy.start()
    fetch_values.start()
    start("key_prob")
    for copies in sweeps[1:3]:
        for copy in copies:
            copy.start()
    start("mark_q", "turned", "mark_k", "mixing_low")
    for copies in sweeps[3:]:
        for copy in copies:
            copy.start()
    start("last_growth")

    heads, rows, _ = values_s.shape
    tokens = heads * rows
    chunks, per = tokens // CHUNK, CHUNK // rows
    segment_len = tokens // M
    marks_per = CHUNK // segment_len
    score_scale = HD ** (-0.5)
    places = [slice(index * CHUNK, (index + 1) * CHUNK) for index in range(chunks)]

    def block(ref, index):
        return ref[index * per : (index + 1) * per].reshape(CHUNK, HD)

    fetch_grads.wait()
    grads_turned = grads_s[...].reshape(tokens, HD).T
    wait("token_prob")
    mixing_grad = wide_dot(grads_turned, held["token_prob"][...].astype(jnp.bfloat16))
    wait("inverse", "mark_values", "mark_prob", "factor")
    values_low = split_dot(
        halves(mixing_grad), (held["inverse"][0], held["inverse"][1])
    ).astype(jnp.bfloat16)
    mark_prob = held["mark_prob"][...]
    mark_halves = halves(mark_prob)
    factor = held["factor"][0:1, 0:1]
    inverse_grad = split_dot(halves(mixing_grad.T), halves(held["mark_values"][...]))
    inverse_grad_halves = halves(inverse_grad)
    toward = split_dot(mark_halves, inverse_grad_halves) * factor
    power = 0.5 * (toward + toward.T)
    growth = None

    row_totals, query_sums, key_sums = [], [], []

    def key_rows(index):
        place = places[index]
        key_prob = held["key_prob"][place]
        value_gradient = wide_dot_nt(key_prob.astype(jnp.bfloat16), values_low)
        out_ref[index * per : (index + 1) * per, 0] = value_gradient.astype(
            jnp.bfloat16
        ).reshape(per, rows, HD)
        key_dgrad = wide_dot(block(values_s, index), values_low)
        kept_s[place] = key_dgrad
        row_totals.append(jnp.sum(key_prob * key_dgrad, axis=0, keepdims=True))

    def key_side(index):
        if index == 0:
            row_totals[0] = sum(row_totals[1:], row_totals[0])
        place = places[index]
        key_sgrad = (held["key_prob"][place] * (kept_s[place] - row_totals[0])).astype(
            jnp.bfloat16
        )
        direct_s[place] = wide_dot(key_sgrad, held["mark_q"][...]) * score_scale
        query_sums.append(wide_dot(held["turned"][1, :, place], key_sgrad))

    def token_side(index):
        place = places[index]
        prob = held["token_prob"][place]
        token_grad = wide_dot(block(grads_s, index), held["mixing_low"][...])
        token_sgrad = (
            prob * (token_grad - jnp.sum(token_grad * prob, axis=1, keepdims=True))
        ).astype(jnp.bfloat16)
        query_s[place] = wide_dot(token_sgrad, held["mark_k"][...]) * score_scale
        key_sums.append(wide_dot(held["turned"][0, :, place], token_sgrad))

    span = (chunks + 3) // 4
    work = iter(
        [
            (unit, range(first, min(chunks, first + span)))
            for unit in (key_rows, key_side, token_side)
            for first in range(0, chunks, span)
        ]
    )

    def beside():
        unit, indices = next(work)
        for index in indices:
            unit(index)

    for sweep in range(PINV_ITERS):
        if sweep == 0:
            fetch_values.wait()
            wait("key_prob")
        if sweep == 2:
            wait("mark_q", "turned", "mark_k", "mixing_low")
        for copy in sweeps[sweep]:
            copy.wait()
        pair_ref, weight_ref, growth_ref = (held[name] for name in SWEEP_NAMES)
        pair = (pair_ref[sweep, 0], pair_ref[sweep, 1])
        first = split_dot(pair, halves(power))
        beside()
        square = first[:M] + first[:M].T
        second = split_dot(pair, halves(square))
        beside()
        cube = first[M:].T + second[:M]
        fourth = second[M:] + second[M:].T
        weight = halves(0.25 * (7.0 * square - 15.0 * power - cube))
        power = 0.25 * (13.0 * power - 15.0 * square + 7.0 * cube - fourth)
        held_growth = (growth_ref[sweep, 0], growth_ref[sweep, 1])
        left = [held_growth[0], held_growth[0], held_growth[1]]
        right = [weight[0], weight[1], weight[0]]
        if growth is not None:
            grown = halves(growth)
            left += [grown[0], grown[0], grown[1]]
            right += [weight_ref[sweep, 0], weight_ref[sweep, 1], weight_ref[sweep, 0]]
        growth = wide_dot(jnp.concatenate(left, axis=1), jnp.concatenate(right, axis=0))
    wait("last_growth")
    mark_grad = factor * (
        split_dot_nt((held["last_growth"][0], held["last_growth"][1]), inverse_grad_halves)
        + split_dot(halves(growth + growth.T), mark_halves)
    )
    mark_sgrad = mark_prob * (mark_grad - jnp.sum(mark_grad * mark_prob, axis=1, keepdims=True))

    def marks_dot(left, right):
        high, low = halves(left)
        return wide_dot(
            jnp.concatenate([high, low], axis=1), jnp.concatenate([right, right], axis=0)
        )

    marks_scale = score_scale / segment_len
    query_marks = (
        marks_dot(mark_sgrad, held["mark_k"][...]) + sum(query_sums[1:], query_sums[0]).T
    ) * marks_scale
    key_marks = (
        marks_dot(mark_sgrad.T, held["mark_q"][...]) + sum(key_sums[1:], key_sums[0]).T
    ) * marks_scale

    writes = []
    for index, place in enumerate(places):
        group = slice(index * per, (index + 1) * per)
        marked = slice(index * marks_per, (index + 1) * marks_per)
        for slot, direct, marks in ((1, query_s, query_marks), (2, direct_s, key_marks)):
            wide = jnp.broadcast_to(marks[marked][:, None], (marks_per, segment_len, HD))
            total = direct[place] + wide.reshape(CHUNK, HD)
            out_ref[group, slot] = total.astype(jnp.bfloat16).reshape(per, rows, HD)
        write = pltpu.make_async_copy(
            out_ref.at[pl.ds(index * per, per)],
            home.at[pl.ds(index * per, per)],
            out_done.at[index],
        )
        write.start()
        writes.append(write)
    for write in writes:
        write.wait()


def kernel_call(kernel, out_shape, scratch, flops, operands, limit=VMEM_LIMIT, in_place=None):
    moved = sum(x.size * x.dtype.itemsize for x in operands)
    anywhere = pl.BlockSpec(memory_space=pl.ANY)
    held = pl.BlockSpec(memory_space=pltpu.VMEM)
    return pl.pallas_call(
        kernel,
        out_shape=out_shape,
        in_specs=[held if index == in_place else anywhere for index in range(len(operands))],
        out_specs=jax.tree.map(lambda _: anywhere, out_shape),
        scratch_shapes=scratch,
        compiler_params=pltpu.CompilerParams(vmem_limit_bytes=limit),
        cost_estimate=pl.CostEstimate(flops=flops, bytes_accessed=moved, transcendentals=0),
    )(*operands)


def in_vmem(array):
    return pltpu.VMEM(array.shape, array.dtype)


def pack(*sources):
    rows, width = sources[0].shape
    heads, arrays = width // HD, len(sources)
    shape = jax.ShapeDtypeStruct((heads, arrays, rows, HD), sources[0].dtype)
    scratch = [
        pltpu.VMEM((arrays, rows, width), sources[0].dtype),
        pltpu.VMEM(shape.shape, sources[0].dtype),
        pltpu.SemaphoreType.DMA((arrays, PACK_GROUPS)),
        pltpu.SemaphoreType.DMA((PACK_GROUPS,)),
    ]
    return kernel_call(pack_kernel, shape, scratch, 0, sources)


def unpack(packed):
    heads, arrays, rows, _ = packed.shape
    shape = jax.ShapeDtypeStruct((rows, heads * HD), packed.dtype)
    scratch = [
        pltpu.VMEM((arrays, rows, heads * HD), packed.dtype),
        pltpu.SemaphoreType.DMA((arrays, PACK_GROUPS)),
    ]
    return kernel_call(
        unpack_kernel, (shape,) * arrays, scratch, 0, (packed,), limit=SMALL_LIMIT, in_place=0
    )


def low(*shape):
    return jax.ShapeDtypeStruct(shape, jnp.bfloat16)


def wide(*shape):
    return jax.ShapeDtypeStruct(shape, jnp.float32)


def forward_part(qkv):
    heads, _, rows, _ = qkv.shape
    tokens = heads * rows
    shapes = dict(
        attended=low(heads, 1, rows, HD),
        mark_q=low(M, HD),
        mark_k=low(M, HD),
        mark_prob=wide(M, M),
        factor=wide(8, HD),
        token_prob=wide(tokens, M),
        key_prob=wide(tokens, M),
        turned=low(2, HD, tokens),
        pair=low(PINV_ITERS, 2, 2 * M, M),
        weight=low(PINV_ITERS, 2, M, M),
        growth=low(PINV_ITERS, 2, M, M),
        inverse=low(2, M, M),
        last_growth=low(2, M, M),
        mark_values=wide(HD, M),
        mixing_low=low(HD, M),
    )
    scratch = [
        *(in_vmem(shape) for shape in shapes.values()),
        in_vmem(qkv),
        pltpu.VMEM((M, M), jnp.float32),
        pltpu.VMEM((2 * M, M), jnp.float32),
        pltpu.VMEM((tokens, M), jnp.bfloat16),
        pltpu.VMEM((tokens, M), jnp.bfloat16),
        pltpu.SemaphoreType.DMA((3,)),
        pltpu.SemaphoreType.DMA((len(shapes),)),
        pltpu.SemaphoreType.DMA((len(SWEEP_NAMES), PINV_ITERS)),
    ]
    results = kernel_call(
        functools.partial(forward_kernel, tuple(shapes)),
        tuple(shapes.values()),
        scratch,
        FORWARD_FLOPS,
        (qkv,),
    )
    return dict(zip(shapes, results))


def gradient_part(qkv, grads, kept):
    heads, _, rows, _ = qkv.shape
    tokens = heads * rows
    names = tuple(name for name in kept if name != "attended")
    operands = tuple(kept[name] for name in names)
    shape = low(heads, 3, rows, HD)
    scratch = [
        *(in_vmem(array) for array in operands),
        pltpu.VMEM((heads, rows, HD), jnp.bfloat16),
        pltpu.VMEM((heads, rows, HD), jnp.bfloat16),
        in_vmem(shape),
        pltpu.VMEM((tokens, HD), jnp.float32),
        pltpu.VMEM((tokens, HD), jnp.float32),
        pltpu.VMEM((tokens, M), jnp.float32),
        pltpu.SemaphoreType.DMA((len(names) + 2,)),
        pltpu.SemaphoreType.DMA((len(SWEEP_NAMES), PINV_ITERS)),
        pltpu.SemaphoreType.DMA((tokens // CHUNK,)),
    ]
    return kernel_call(
        functools.partial(gradient_kernel, names),
        shape,
        scratch,
        GRADIENT_FLOPS,
        (qkv, grads, *operands),
    )


def exchange(packed):
    return lax.all_to_all(packed, ("seq", "head"), split_axis=0, concat_axis=0, tiled=True)


def body(queries, keys, values, out_grad):
    qkv = exchange(pack(queries, keys, values))
    grads = exchange(pack(out_grad))
    kept = forward_part(qkv)
    (attended,) = unpack(exchange(kept["attended"]))
    value_gradient_array, query_grad, key_grad = unpack(
        exchange(gradient_part(qkv, grads, kept))
    )
    return attended, query_grad, key_grad, value_gradient_array


def solution(mesh):
    placement = P(("seq", "head"), None)

    def layer(queries, keys, values, out_grad):
        one_head_each = queries.shape[1] // HD == mesh.size and queries.shape[0] == 8 * CHUNK
        return jax.shard_map(
            body if one_head_each else shared_body,
            mesh=mesh,
            in_specs=(placement,) * 4,
            out_specs=(placement,) * 4,
            check_vma=False,
        )(queries, keys, values, out_grad)

    return layer
```

```python
import functools

import jax
import jax.numpy as jnp
from jax import lax
from jax.experimental import pallas as pl
from jax.experimental.pallas import tpu as pltpu
from jax.sharding import PartitionSpec as P

HD = 128
M = 256
PINV_ITERS = 6
CHUNK = 256
PACK_GROUPS = 8
SWEEP_NAMES = ("pair", "weight", "growth")
VMEM_LIMIT = 60 * 2**20
SMALL_LIMIT = 16 * 2**20
FORWARD_FLOPS = 10 * 10**9
GRADIENT_FLOPS = 14 * 10**9


precise_setting = lax.Precision.HIGHEST


def newton_inverse(matrix):
    identity = jnp.eye(matrix.shape[0], dtype=matrix.dtype)
    factor = lax.stop_gradient(1.0 / jnp.max(jnp.sum(matrix, axis=0)))
    iterate = matrix.T * factor
    for sweep_index in range(PINV_ITERS):
        product = jnp.matmul(matrix, iterate, precision=precise_setting)
        inner_term = jnp.matmul(product, 7.0 * identity - product, precision=precise_setting)
        inner_term = jnp.matmul(product, 15.0 * identity - inner_term, precision=precise_setting)
        iterate = 0.25 * jnp.matmul(
            iterate, 13.0 * identity - inner_term, precision=precise_setting
        )
    return iterate


def share_heads(own_matrix, head_count):
    seq_index = lax.axis_index("seq")
    slot_mask = (jnp.arange(head_count, dtype=jnp.int32) == seq_index).astype(jnp.float32)
    return lax.psum(slot_mask[:, None, None] * own_matrix[None], "seq")


def shared_body(queries, keys, values, out_grad):
    query_rows, key_rows, value_rows, grad_rows = (
        lax.all_to_all(queries, "head", split_axis=1, concat_axis=0, tiled=True),
        lax.all_to_all(keys, "head", split_axis=1, concat_axis=0, tiled=True),
        lax.all_to_all(values, "head", split_axis=1, concat_axis=0, tiled=True),
        lax.all_to_all(out_grad, "head", split_axis=1, concat_axis=0, tiled=True),
    )
    tok_rows = query_rows.shape[0]
    head_count = query_rows.shape[1] // HD
    local_marks = M // lax.axis_size("seq")
    segment_len = tok_rows // local_marks
    score_scale = HD ** (-0.5)
    seq_index = lax.axis_index("seq")

    def landmark(matrix):
        summed = jnp.sum(
            matrix.reshape(local_marks, segment_len, matrix.shape[1]), axis=1, dtype=jnp.float32
        )
        return (summed / segment_len).astype(jnp.bfloat16)

    mark_queries, mark_keys = (
        lax.all_gather(landmark(query_rows), "seq", axis=0, tiled=True),
        lax.all_gather(landmark(key_rows), "seq", axis=0, tiled=True),
    )
    query_per_head = query_rows.reshape(tok_rows, head_count, HD)
    key_per_head = key_rows.reshape(tok_rows, head_count, HD)
    value_per_head = value_rows.reshape(tok_rows, head_count, HD)
    gradient_per_head = grad_rows.reshape(tok_rows, head_count, HD)
    landmark_query_heads = mark_queries.reshape(M, head_count, HD)
    landmark_key_heads = mark_keys.reshape(M, head_count, HD)
    key_score = (
        jnp.einsum(
            "pcv,gcv->cpg", landmark_query_heads, key_per_head, preferred_element_type=jnp.float32
        )
        * score_scale
    )
    key_max = lax.pmax(jnp.max(key_score, axis=-1), "seq")
    key_exp = jnp.exp(key_score - key_max[..., None])
    partial_num = jnp.einsum(
        "akq,qay->aky",
        key_exp.astype(jnp.bfloat16),
        value_per_head,
        preferred_element_type=jnp.float32,
    )
    key_total, numerator = lax.psum((jnp.sum(key_exp, axis=-1), partial_num), "seq")
    landmark_value_rows = numerator / key_total[..., None]
    token_prob = jax.nn.softmax(
        jnp.einsum(
            "jti,cti->tjc", query_per_head, landmark_key_heads, preferred_element_type=jnp.float32
        )
        * score_scale,
        axis=-1,
    )
    token_probability_lowered = token_prob.astype(jnp.bfloat16)
    mark_prob = jax.nn.softmax(
        jnp.einsum(
            "jou,iou->oji",
            landmark_query_heads,
            landmark_key_heads,
            preferred_element_type=jnp.float32,
        )
        * score_scale,
        axis=-1,
    )
    own_head = seq_index % head_count
    own_mark = lax.dynamic_index_in_dim(mark_prob, own_head, 0, keepdims=False)
    own_inverse, pull_back = jax.vjp(newton_inverse, own_mark)
    pseudo_inverse_matrix = share_heads(own_inverse, head_count)
    mixing_matrix = jnp.einsum(
        "jvy,jys->jvs", pseudo_inverse_matrix, landmark_value_rows, precision=precise_setting
    )
    mixing_matrix_lowered = mixing_matrix.astype(jnp.bfloat16)
    attended = jnp.einsum(
        "yvo,yor->vyr",
        token_probability_lowered,
        mixing_matrix_lowered,
        preferred_element_type=jnp.float32,
    ).astype(jnp.bfloat16)
    token_grad = jnp.einsum(
        "fag,aog->afo", gradient_per_head, mixing_matrix_lowered, preferred_element_type=jnp.float32
    )
    partial_mix = jnp.einsum(
        "klz,lkr->kzr",
        token_probability_lowered,
        gradient_per_head,
        preferred_element_type=jnp.float32,
    )
    mixing_matrix_gradient = lax.psum(partial_mix, "seq")
    token_score_gradient = (
        token_prob * (token_grad - jnp.sum(token_grad * token_prob, axis=-1, keepdims=True))
    ).astype(jnp.bfloat16)
    direct_qgrad = (
        jnp.einsum(
            "ufg,guc->fuc",
            token_score_gradient,
            landmark_key_heads,
            preferred_element_type=jnp.float32,
        )
        * score_scale
    )
    mark_kgrad_f = (
        jnp.einsum(
            "xgi,gxy->ixy", token_score_gradient, query_per_head, preferred_element_type=jnp.float32
        )
        * score_scale
    )
    pseudo_inverse_gradient = jnp.einsum(
        "ktu,kyu->kty", mixing_matrix_gradient, landmark_value_rows, precision=precise_setting
    )
    landmark_value_gradient = jnp.einsum(
        "lrb,lrz->lbz", pseudo_inverse_matrix, mixing_matrix_gradient, precision=precise_setting
    )
    own_igrad = lax.dynamic_index_in_dim(pseudo_inverse_gradient, own_head, 0, keepdims=False)
    (own_mgrad,) = pull_back(own_igrad)
    mark_grad = share_heads(own_mgrad, head_count)
    mark_sgrad = mark_prob * (mark_grad - jnp.sum(mark_grad * mark_prob, axis=-1, keepdims=True))
    first_mark = seq_index * local_marks
    score_gradient_rows = lax.dynamic_slice_in_dim(mark_sgrad, first_mark, local_marks, 1)
    score_gradient_columns = lax.dynamic_slice_in_dim(mark_sgrad, first_mark, local_marks, 2)
    own_qgrad_a = (
        jnp.einsum(
            "txs,ste->xte",
            score_gradient_rows,
            landmark_key_heads.astype(jnp.float32),
            precision=precise_setting,
        )
        * score_scale
    )
    own_kgrad_a = (
        jnp.einsum(
            "eaj,aev->jev",
            score_gradient_columns,
            landmark_query_heads.astype(jnp.float32),
            precision=precise_setting,
        )
        * score_scale
    )
    landmark_value_lowered = landmark_value_gradient.astype(jnp.bfloat16)
    key_prob = key_exp / key_total[..., None]
    key_probability_lowered = key_prob.astype(jnp.bfloat16)
    value_gradient_array = jnp.einsum(
        "zct,zcj->tzj",
        key_probability_lowered,
        landmark_value_lowered,
        preferred_element_type=jnp.float32,
    )
    key_direct_gradient = jnp.einsum(
        "exb,geb->exg", landmark_value_lowered, value_per_head, preferred_element_type=jnp.float32
    )
    row_total = lax.psum(jnp.sum(key_prob * key_direct_gradient, axis=-1), "seq")
    key_score_gradient = (key_prob * (key_direct_gradient - row_total[..., None])).astype(
        jnp.bfloat16
    )
    direct_kgrad = (
        jnp.einsum(
            "pbo,bpx->opx",
            key_score_gradient,
            landmark_query_heads,
            preferred_element_type=jnp.float32,
        )
        * score_scale
    )
    mark_qgrad_b = (
        jnp.einsum(
            "cbj,jcp->bcp", key_score_gradient, key_per_head, preferred_element_type=jnp.float32
        )
        * score_scale
    )
    own_kgrad_f, own_qgrad_b = (
        lax.psum_scatter(mark_kgrad_f, "seq", scatter_dimension=0, tiled=True),
        lax.psum_scatter(mark_qgrad_b, "seq", scatter_dimension=0, tiled=True),
    )
    mark_qtotal = (own_qgrad_a + own_qgrad_b) / segment_len
    mark_ktotal = (own_kgrad_a + own_kgrad_f) / segment_len
    query_grad = (
        direct_qgrad.reshape(local_marks, segment_len, head_count, HD) + mark_qtotal[:, None]
    )
    key_grad = direct_kgrad.reshape(local_marks, segment_len, head_count, HD) + mark_ktotal[:, None]
    width = head_count * HD
    results = (
        attended.reshape(tok_rows, width),
        query_grad.astype(jnp.bfloat16).reshape(tok_rows, width),
        key_grad.astype(jnp.bfloat16).reshape(tok_rows, width),
        value_gradient_array.astype(jnp.bfloat16).reshape(tok_rows, width),
    )
    attended_out, query_out, key_out, value_out = (
        lax.all_to_all(results[0], "head", split_axis=0, concat_axis=1, tiled=True),
        lax.all_to_all(results[1], "head", split_axis=0, concat_axis=1, tiled=True),
        lax.all_to_all(results[2], "head", split_axis=0, concat_axis=1, tiled=True),
        lax.all_to_all(results[3], "head", split_axis=0, concat_axis=1, tiled=True),
    )
    return (attended_out, query_out, key_out, value_out)


def dims_of(rows):
    tokens = rows.shape[0] * rows.shape[2]
    return tokens, rows.shape[2], tokens // CHUNK


def halves(matrix):
    high = matrix.astype(jnp.bfloat16)
    return high, (matrix - high.astype(jnp.float32)).astype(jnp.bfloat16)


def wide_dot(left, right):
    return jnp.dot(left, right, preferred_element_type=jnp.float32)


def wide_dot_nt(left, right):
    return lax.dot_general(
        left, right, (((1,), (1,)), ((), ())), preferred_element_type=jnp.float32
    )


def split_dot(left, right):
    left_high, left_low = left
    right_high, right_low = right
    return wide_dot(
        jnp.concatenate([left_high, left_high, left_low], axis=1),
        jnp.concatenate([right_high, right_low, right_high], axis=0),
    )


def split_dot_nt(left, right):
    left_high, left_low = left
    right_high, right_low = right
    return wide_dot_nt(
        jnp.concatenate([left_high, left_high, left_low], axis=1),
        jnp.concatenate([right_high, right_low, right_high], axis=1),
    )


def identity_matrix():
    return (
        lax.broadcasted_iota(jnp.int32, (M, M), 0) == lax.broadcasted_iota(jnp.int32, (M, M), 1)
    ).astype(jnp.float32)


def chunk_of(ref, slot, index):
    rows = ref.shape[2]
    per = CHUNK // rows
    return ref[pl.ds(index * per, per), slot].reshape(CHUNK, HD)


def store_chunk(ref, slot, index, value):
    rows = ref.shape[2]
    per = CHUNK // rows
    ref[pl.ds(index * per, per), slot] = value.reshape(per, rows, HD)


def columns(index):
    return pl.ds(pl.multiple_of(index * CHUNK, CHUNK), CHUNK)


def pack_kernel(*refs):
    arrays = len(refs) - 5
    sources, (out_ref, rows_s, packed_s, in_done, out_done) = refs[:arrays], refs[arrays:]
    group = out_ref.shape[0] // PACK_GROUPS
    reads, writes = [], []
    for index in range(PACK_GROUPS):
        for slot, ref in enumerate(sources):
            place = pl.ds(index * group * HD, group * HD)
            reads.append(
                pltpu.make_async_copy(
                    ref.at[:, place], rows_s.at[slot, :, place], in_done.at[slot, index]
                )
            )
        place = pl.ds(index * group, group)
        writes.append(
            pltpu.make_async_copy(packed_s.at[place], out_ref.at[place], out_done.at[index])
        )
    for copy in reads:
        copy.start()
    for index in range(PACK_GROUPS):
        for slot in range(arrays):
            reads[arrays * index + slot].wait()
            for head in range(index * group, (index + 1) * group):
                packed_s[head, slot] = rows_s[slot, :, head * HD : (head + 1) * HD]
        writes[index].start()
    for copy in writes:
        copy.wait()


def unpack_kernel(packed_ref, *refs):
    homes, (rows_s, out_done) = refs[:-2], refs[-2:]
    group = packed_ref.shape[0] // PACK_GROUPS
    writes = []
    for index in range(PACK_GROUPS):
        for slot, ref in enumerate(homes):
            for head in range(index * group, (index + 1) * group):
                rows_s[slot, :, head * HD : (head + 1) * HD] = packed_ref[head, slot]
            place = pl.ds(index * group * HD, group * HD)
            write = pltpu.make_async_copy(
                rows_s.at[slot, :, place], ref.at[:, place], out_done.at[slot, index]
            )
            write.start()
            writes.append(write)
    for copy in writes:
        copy.wait()


def sweep_forward(power_s, iterate_s, saved, sweep, work):
    pair_ref, weight_ref, growth_ref = saved
    power = power_s[...]
    power_high, power_low = halves(power)
    square = split_dot((power_high, power_low), (power_high, power_low))
    next(work)()
    square_halves = halves(square)
    pair = (
        jnp.concatenate([power_high, square_halves[0]], axis=0),
        jnp.concatenate([power_low, square_halves[1]], axis=0),
    )
    pair_ref[sweep, 0], pair_ref[sweep, 1] = pair
    higher = split_dot(pair, square_halves)
    next(work)()
    cube, fourth = higher[:M], higher[M:]
    weight = halves(0.25 * (13.0 * identity_matrix() - 15.0 * power + 7.0 * square - cube))
    power_s[...] = 0.25 * (13.0 * power - 15.0 * square + 7.0 * cube - fourth)
    weight_ref[sweep, 0], weight_ref[sweep, 1] = weight
    iterate = halves(iterate_s[...])
    growth_ref[sweep, 0], growth_ref[sweep, 1] = iterate[0][M:], iterate[1][M:]
    iterate_s[...] = split_dot(iterate, weight)


def forward_kernel(names, qkv_hbm, *refs):
    count = len(names)
    homes, refs = dict(zip(names, refs[:count])), refs[count:]
    held, refs = dict(zip(names, refs[:count])), refs[count:]
    qkv_ref, power_s, iterate_s, token_low_s, key_low_s, in_done, out_done, sweep_done = refs
    copies = {
        name: pltpu.make_async_copy(held[name], homes[name], out_done.at[index])
        for index, name in enumerate(names)
        if name not in SWEEP_NAMES
    }
    sent = []

    def send(*chosen):
        for name in chosen:
            copies[name].start()
            sent.append(copies[name])

    arrive = [
        pltpu.make_async_copy(qkv_hbm.at[:, slot], qkv_ref.at[:, slot], in_done.at[slot])
        for slot in range(3)
    ]
    for copy in arrive:
        copy.start()
    for copy in arrive[:2]:
        copy.wait()
    tokens, rows, chunks = dims_of(qkv_ref)
    segment_len = tokens // M
    marks_per = CHUNK // segment_len
    score_scale = HD ** (-0.5)
    member = (
        lax.broadcasted_iota(jnp.int32, (marks_per, CHUNK), 1) // segment_len
        == lax.broadcasted_iota(jnp.int32, (marks_per, CHUNK), 0)
    ).astype(jnp.bfloat16)
    for index in range(chunks):
        both = jnp.concatenate([chunk_of(qkv_ref, 0, index), chunk_of(qkv_ref, 1, index)], axis=1)
        mean = (wide_dot(member, both) / segment_len).astype(jnp.bfloat16)
        held["mark_q"][index * marks_per : (index + 1) * marks_per] = mean[:, :HD]
        held["mark_k"][index * marks_per : (index + 1) * marks_per] = mean[:, HD:]
    landmark_q, landmark_k = held["mark_q"][...], held["mark_k"][...]

    mark_score = wide_dot_nt(landmark_q, landmark_k) * score_scale
    mark_exp = jnp.exp(mark_score - jnp.max(mark_score, axis=1, keepdims=True))
    mark_prob = mark_exp / jnp.sum(mark_exp, axis=1, keepdims=True)
    held["mark_prob"][...] = mark_prob
    factor = 1.0 / jnp.max(jnp.sum(mark_prob, axis=0, keepdims=True), axis=1, keepdims=True)
    held["factor"][...] = jnp.broadcast_to(factor, held["factor"].shape)
    mark_halves = halves(mark_prob)
    power_s[...] = split_dot_nt(mark_halves, mark_halves) * factor
    iterate_s[0:M] = mark_prob.T * factor
    iterate_s[M:] = identity_matrix()
    send("mark_q", "mark_k", "mark_prob", "factor")

    tops, totals = [], []
    places = [slice(index * CHUNK, (index + 1) * CHUNK) for index in range(chunks)]

    def scores(index):
        query_chunk, key_chunk = chunk_of(qkv_ref, 0, index), chunk_of(qkv_ref, 1, index)
        place = places[index]
        held["turned"][0, :, place] = query_chunk.T
        held["turned"][1, :, place] = key_chunk.T
        score = wide_dot_nt(query_chunk, landmark_k) * score_scale
        grown = jnp.exp(score - jnp.max(score, axis=1, keepdims=True))
        prob = grown * (1.0 / jnp.sum(grown, axis=1, keepdims=True))
        held["token_prob"][place] = prob
        token_low_s[place] = prob.astype(jnp.bfloat16)
        key_score = wide_dot_nt(key_chunk, landmark_q) * score_scale
        held["key_prob"][place] = key_score
        tops.append(jnp.max(key_score, axis=0, keepdims=True))

    def grow(index):
        if index == 0:
            tops[0] = functools.reduce(jnp.maximum, tops)
        place = places[index]
        grown = jnp.exp(held["key_prob"][place] - tops[0])
        held["key_prob"][place] = grown
        key_low_s[place] = grown.astype(jnp.bfloat16)
        totals.append(jnp.sum(grown, axis=0, keepdims=True))

    def units():
        half = (chunks + 3) // 4
        for first in range(0, chunks, max(1, chunks // 8)):
            yield functools.partial(
                lambda start: [scores(x) for x in range(start, min(chunks, start + chunks // 8))],
                first,
            )
        for first in range(0, chunks, half):
            yield functools.partial(
                lambda start: [grow(x) for x in range(start, min(chunks, start + half))], first
            )

    work = units()
    saved = tuple(held[name] for name in SWEEP_NAMES)
    for sweep in range(PINV_ITERS):
        sweep_forward(power_s, iterate_s, saved, sweep, work)
        for place, name in enumerate(SWEEP_NAMES):
            copy = pltpu.make_async_copy(
                held[name].at[sweep], homes[name].at[sweep], sweep_done.at[place, sweep]
            )
            copy.start()
            sent.append(copy)
        if sweep == 3:
            send("token_prob", "turned")
    inverse = halves(iterate_s[0:M])
    held["inverse"][0], held["inverse"][1] = inverse
    held["last_growth"][0], held["last_growth"][1] = halves(iterate_s[M:])
    send("inverse", "last_growth")
    total_inverse = 1.0 / sum(totals[1:], totals[0])
    arrive[2].wait()
    values_turned = qkv_ref[:, 2].reshape(tokens, HD).T
    landmark_values = wide_dot(values_turned, key_low_s[...]) * total_inverse
    held["mark_values"][...] = landmark_values
    mixing_low = split_dot_nt(halves(landmark_values), inverse).astype(jnp.bfloat16)
    held["mixing_low"][...] = mixing_low
    attended = wide_dot_nt(token_low_s[...], mixing_low).astype(jnp.bfloat16)
    held["attended"][:, 0] = attended.reshape(-1, rows, HD)
    send("attended", "mark_values", "mixing_low")
    for place in places:
        held["key_prob"][place] = held["key_prob"][place] * total_inverse
    send("key_prob")
    for copy in sent:
        copy.wait()


def gradient_kernel(names, qkv_hbm, grad_hbm, *refs):
    count = len(names)
    sources, home, refs = dict(zip(names, refs[:count])), refs[count], refs[count + 1 :]
    held, refs = dict(zip(names, refs[:count])), refs[count:]
    values_s, grads_s, out_ref, query_s, direct_s, kept_s, in_done, sweep_done, out_done = refs
    reads = {
        name: pltpu.make_async_copy(sources[name], held[name], in_done.at[index])
        for index, name in enumerate(names)
        if name not in SWEEP_NAMES
    }
    fetch_grads = pltpu.make_async_copy(grad_hbm.at[:, 0], grads_s, in_done.at[count])
    fetch_values = pltpu.make_async_copy(qkv_hbm.at[:, 2], values_s, in_done.at[count + 1])
    sweeps = [
        [
            pltpu.make_async_copy(
                sources[name].at[sweep], held[name].at[sweep], sweep_done.at[place, sweep]
            )
            for place, name in enumerate(SWEEP_NAMES)
        ]
        for sweep in range(PINV_ITERS)
    ]

    def start(*chosen):
        for name in chosen:
            reads[name].start()

    def wait(*chosen):
        for name in chosen:
            reads[name].wait()

    fetch_grads.start()
    start("token_prob", "mixing_low", "mark_k", "turned", "inverse")
    start("mark_values", "mark_prob", "factor")
    for copy in sweeps[0]:
        copy.start()
    fetch_values.start()
    start("key_prob", "mark_q")
    for copies in sweeps[1:]:
        for copy in copies:
            copy.start()
    start("last_growth")

    heads, rows, _ = values_s.shape
    tokens = heads * rows
    chunks, per = tokens // CHUNK, CHUNK // rows
    segment_len = tokens // M
    marks_per = CHUNK // segment_len
    score_scale = HD ** (-0.5)
    places = [slice(index * CHUNK, (index + 1) * CHUNK) for index in range(chunks)]

    def block(ref, index):
        return ref[index * per : (index + 1) * per].reshape(CHUNK, HD)

    row_totals, query_sums, key_sums = [], [], []

    def key_rows(index):
        place = places[index]
        key_prob = held["key_prob"][place]
        value_gradient = wide_dot_nt(key_prob.astype(jnp.bfloat16), values_low)
        out_ref[index * per : (index + 1) * per, 0] = value_gradient.astype(
            jnp.bfloat16
        ).reshape(per, rows, HD)
        key_dgrad = wide_dot(block(values_s, index), values_low)
        kept_s[place] = key_dgrad
        row_totals.append(jnp.sum(key_prob * key_dgrad, axis=0, keepdims=True))

    def key_side(index):
        if index == 0:
            row_totals[0] = sum(row_totals[1:], row_totals[0])
        place = places[index]
        key_sgrad = (held["key_prob"][place] * (kept_s[place] - row_totals[0])).astype(
            jnp.bfloat16
        )
        direct_s[place] = wide_dot(key_sgrad, held["mark_q"][...]) * score_scale
        query_sums.append(wide_dot(held["turned"][1, :, place], key_sgrad))

    def token_side(index):
        place = places[index]
        prob = held["token_prob"][place]
        token_grad = wide_dot(block(grads_s, index), held["mixing_low"][...])
        token_sgrad = (
            prob * (token_grad - jnp.sum(token_grad * prob, axis=1, keepdims=True))
        ).astype(jnp.bfloat16)
        query_s[place] = wide_dot(token_sgrad, held["mark_k"][...]) * score_scale
        key_sums.append(wide_dot(held["turned"][0, :, place], token_sgrad))

    span = (chunks + 3) // 4
    work = iter(
        [
            (unit, range(first, min(chunks, first + span)))
            for unit in (token_side, key_rows, key_side)
            for first in range(0, chunks, span)
        ]
    )

    def beside():
        unit, indices = next(work, (None, ()))
        for index in indices:
            unit(index)

    fetch_grads.wait()
    grads_turned = grads_s[...].reshape(tokens, HD).T
    wait("token_prob")
    mixing_grad = wide_dot(grads_turned, held["token_prob"][...].astype(jnp.bfloat16))
    wait("mixing_low", "mark_k", "turned", "inverse", "mark_values", "mark_prob", "factor")
    beside()
    values_low = split_dot(
        halves(mixing_grad), (held["inverse"][0], held["inverse"][1])
    ).astype(jnp.bfloat16)
    mark_prob = held["mark_prob"][...]
    mark_halves = halves(mark_prob)
    factor = held["factor"][0:1, 0:1]
    inverse_grad = split_dot(halves(mixing_grad.T), halves(held["mark_values"][...]))
    inverse_grad_halves = halves(inverse_grad)
    beside()
    toward = split_dot(mark_halves, inverse_grad_halves) * factor
    power = 0.5 * (toward + toward.T)
    growth = None

    sent = []
    for sweep in range(PINV_ITERS):
        if sweep == 1:
            fetch_values.wait()
            wait("key_prob", "mark_q")
        if sweep == 3:
            sent.append(
                pltpu.make_async_copy(out_ref.at[:, 0], home.at[:, 0], out_done.at[chunks])
            )
            sent[0].start()
        for copy in sweeps[sweep]:
            copy.wait()
        pair_ref, weight_ref, growth_ref = (held[name] for name in SWEEP_NAMES)
        pair = (pair_ref[sweep, 0], pair_ref[sweep, 1])
        first = split_dot(pair, halves(power))
        beside()
        square = first[:M] + first[:M].T
        second = split_dot(pair, halves(square))
        beside()
        cube = first[M:].T + second[:M]
        fourth = second[M:] + second[M:].T
        weight = halves(0.25 * (7.0 * square - 15.0 * power - cube))
        power = 0.25 * (13.0 * power - 15.0 * square + 7.0 * cube - fourth)
        held_growth = (growth_ref[sweep, 0], growth_ref[sweep, 1])
        left = [held_growth[0], held_growth[0], held_growth[1]]
        right = [weight[0], weight[1], weight[0]]
        if growth is not None:
            grown = halves(growth)
            left += [grown[0], grown[0], grown[1]]
            right += [weight_ref[sweep, 0], weight_ref[sweep, 1], weight_ref[sweep, 0]]
        growth = wide_dot(jnp.concatenate(left, axis=1), jnp.concatenate(right, axis=0))
    wait("last_growth")
    mark_grad = factor * (
        split_dot_nt((held["last_growth"][0], held["last_growth"][1]), inverse_grad_halves)
        + split_dot(halves(growth + growth.T), mark_halves)
    )
    mark_sgrad = mark_prob * (mark_grad - jnp.sum(mark_grad * mark_prob, axis=1, keepdims=True))

    def marks_dot(left, right):
        high, low = halves(left)
        return wide_dot(
            jnp.concatenate([high, low], axis=1), jnp.concatenate([right, right], axis=0)
        )

    marks_scale = score_scale / segment_len
    query_marks = (
        marks_dot(mark_sgrad, held["mark_k"][...]) + sum(query_sums[1:], query_sums[0]).T
    ) * marks_scale
    key_marks = (
        marks_dot(mark_sgrad.T, held["mark_q"][...]) + sum(key_sums[1:], key_sums[0]).T
    ) * marks_scale

    for index, place in enumerate(places):
        group = slice(index * per, (index + 1) * per)
        marked = slice(index * marks_per, (index + 1) * marks_per)
        for slot, direct, marks in ((1, query_s, query_marks), (2, direct_s, key_marks)):
            wide = jnp.broadcast_to(marks[marked][:, None], (marks_per, segment_len, HD))
            total = direct[place] + wide.reshape(CHUNK, HD)
            out_ref[group, slot] = total.astype(jnp.bfloat16).reshape(per, rows, HD)
        ends = pl.ds(index * per, per), pl.ds(1, 2)
        copy = pltpu.make_async_copy(out_ref.at[ends], home.at[ends], out_done.at[index])
        copy.start()
        sent.append(copy)
    for copy in sent:
        copy.wait()


def kernel_call(kernel, out_shape, scratch, flops, operands, limit=VMEM_LIMIT, in_place=None):
    moved = sum(x.size * x.dtype.itemsize for x in operands)
    anywhere = pl.BlockSpec(memory_space=pl.ANY)
    held = pl.BlockSpec(memory_space=pltpu.VMEM)
    return pl.pallas_call(
        kernel,
        out_shape=out_shape,
        in_specs=[held if index == in_place else anywhere for index in range(len(operands))],
        out_specs=jax.tree.map(lambda _: anywhere, out_shape),
        scratch_shapes=scratch,
        compiler_params=pltpu.CompilerParams(vmem_limit_bytes=limit),
        cost_estimate=pl.CostEstimate(flops=flops, bytes_accessed=moved, transcendentals=0),
    )(*operands)


def in_vmem(array):
    return pltpu.VMEM(array.shape, array.dtype)


def pack(*sources):
    rows, width = sources[0].shape
    heads, arrays = width // HD, len(sources)
    shape = jax.ShapeDtypeStruct((heads, arrays, rows, HD), sources[0].dtype)
    scratch = [
        pltpu.VMEM((arrays, rows, width), sources[0].dtype),
        pltpu.VMEM(shape.shape, sources[0].dtype),
        pltpu.SemaphoreType.DMA((arrays, PACK_GROUPS)),
        pltpu.SemaphoreType.DMA((PACK_GROUPS,)),
    ]
    return kernel_call(pack_kernel, shape, scratch, 0, sources)


def unpack(packed):
    heads, arrays, rows, _ = packed.shape
    shape = jax.ShapeDtypeStruct((rows, heads * HD), packed.dtype)
    scratch = [
        pltpu.VMEM((arrays, rows, heads * HD), packed.dtype),
        pltpu.SemaphoreType.DMA((arrays, PACK_GROUPS)),
    ]
    return kernel_call(
        unpack_kernel, (shape,) * arrays, scratch, 0, (packed,), limit=SMALL_LIMIT, in_place=0
    )


def low(*shape):
    return jax.ShapeDtypeStruct(shape, jnp.bfloat16)


def wide(*shape):
    return jax.ShapeDtypeStruct(shape, jnp.float32)


def forward_part(qkv):
    heads, _, rows, _ = qkv.shape
    tokens = heads * rows
    shapes = dict(
        attended=low(heads, 1, rows, HD),
        mark_q=low(M, HD),
        mark_k=low(M, HD),
        mark_prob=wide(M, M),
        factor=wide(8, HD),
        token_prob=wide(tokens, M),
        key_prob=wide(tokens, M),
        turned=low(2, HD, tokens),
        pair=low(PINV_ITERS, 2, 2 * M, M),
        weight=low(PINV_ITERS, 2, M, M),
        growth=low(PINV_ITERS, 2, M, M),
        inverse=low(2, M, M),
        last_growth=low(2, M, M),
        mark_values=wide(HD, M),
        mixing_low=low(HD, M),
    )
    scratch = [
        *(in_vmem(shape) for shape in shapes.values()),
        in_vmem(qkv),
        pltpu.VMEM((M, M), jnp.float32),
        pltpu.VMEM((2 * M, M), jnp.float32),
        pltpu.VMEM((tokens, M), jnp.bfloat16),
        pltpu.VMEM((tokens, M), jnp.bfloat16),
        pltpu.SemaphoreType.DMA((3,)),
        pltpu.SemaphoreType.DMA((len(shapes),)),
        pltpu.SemaphoreType.DMA((len(SWEEP_NAMES), PINV_ITERS)),
    ]
    results = kernel_call(
        functools.partial(forward_kernel, tuple(shapes)),
        tuple(shapes.values()),
        scratch,
        FORWARD_FLOPS,
        (qkv,),
    )
    return dict(zip(shapes, results))


def gradient_part(qkv, grads, kept):
    heads, _, rows, _ = qkv.shape
    tokens = heads * rows
    names = tuple(name for name in kept if name != "attended")
    operands = tuple(kept[name] for name in names)
    shape = low(heads, 3, rows, HD)
    scratch = [
        *(in_vmem(array) for array in operands),
        pltpu.VMEM((heads, rows, HD), jnp.bfloat16),
        pltpu.VMEM((heads, rows, HD), jnp.bfloat16),
        in_vmem(shape),
        pltpu.VMEM((tokens, HD), jnp.float32),
        pltpu.VMEM((tokens, HD), jnp.float32),
        pltpu.VMEM((tokens, M), jnp.float32),
        pltpu.SemaphoreType.DMA((len(names) + 2,)),
        pltpu.SemaphoreType.DMA((len(SWEEP_NAMES), PINV_ITERS)),
        pltpu.SemaphoreType.DMA((tokens // CHUNK + 1,)),
    ]
    return kernel_call(
        functools.partial(gradient_kernel, names),
        shape,
        scratch,
        GRADIENT_FLOPS,
        (qkv, grads, *operands),
    )


def exchange(packed):
    return lax.all_to_all(packed, ("seq", "head"), split_axis=0, concat_axis=0, tiled=True)


def body(queries, keys, values, out_grad):
    qkv = exchange(pack(queries, keys, values))
    grads = exchange(pack(out_grad))
    kept = forward_part(qkv)
    (attended,) = unpack(exchange(kept["attended"]))
    value_gradient_array, query_grad, key_grad = unpack(
        exchange(gradient_part(qkv, grads, kept))
    )
    return attended, query_grad, key_grad, value_gradient_array


def solution(mesh):
    placement = P(("seq", "head"), None)

    def layer(queries, keys, values, out_grad):
        one_head_each = queries.shape[1] // HD == mesh.size and queries.shape[0] == 8 * CHUNK
        return jax.shard_map(
            body if one_head_each else shared_body,
            mesh=mesh,
            in_specs=(placement,) * 4,
            out_specs=(placement,) * 4,
            check_vma=False,
        )(queries, keys, values, out_grad)

    return layer
```

```python
import functools
from types import SimpleNamespace

import jax
import jax.numpy as jnp
from jax import lax
from jax.experimental import pallas as pl
from jax.experimental.pallas import tpu as pltpu
from jax.sharding import PartitionSpec as P

HD = 128
M = 256
PINV_ITERS = 6
CHUNK = 256
PACK_GROUPS = 4
HALF = M // 2
SWAP = ((0, 1), (1, 0))
VMEM_LIMIT = 60 * 2**20
SMALL_LIMIT = 16 * 2**20
WHOLE, LEAD, GROUPS = range(3)
SLOTS = (10, 11)


precise_setting = lax.Precision.HIGHEST


def newton_inverse(matrix):
    identity = jnp.eye(matrix.shape[0], dtype=matrix.dtype)
    factor = lax.stop_gradient(1.0 / jnp.max(jnp.sum(matrix, axis=0)))
    iterate = matrix.T * factor
    for sweep_index in range(PINV_ITERS):
        product = jnp.matmul(matrix, iterate, precision=precise_setting)
        inner_term = jnp.matmul(product, 7.0 * identity - product, precision=precise_setting)
        inner_term = jnp.matmul(product, 15.0 * identity - inner_term, precision=precise_setting)
        iterate = 0.25 * jnp.matmul(
            iterate, 13.0 * identity - inner_term, precision=precise_setting
        )
    return iterate


def share_heads(own_matrix, head_count):
    seq_index = lax.axis_index("seq")
    slot_mask = (jnp.arange(head_count, dtype=jnp.int32) == seq_index).astype(jnp.float32)
    return lax.psum(slot_mask[:, None, None] * own_matrix[None], "seq")


def shared_body(queries, keys, values, out_grad):
    query_rows, key_rows, value_rows, grad_rows = (
        lax.all_to_all(queries, "head", split_axis=1, concat_axis=0, tiled=True),
        lax.all_to_all(keys, "head", split_axis=1, concat_axis=0, tiled=True),
        lax.all_to_all(values, "head", split_axis=1, concat_axis=0, tiled=True),
        lax.all_to_all(out_grad, "head", split_axis=1, concat_axis=0, tiled=True),
    )
    tok_rows = query_rows.shape[0]
    head_count = query_rows.shape[1] // HD
    local_marks = M // lax.axis_size("seq")
    segment_len = tok_rows // local_marks
    score_scale = HD ** (-0.5)
    seq_index = lax.axis_index("seq")

    def landmark(matrix):
        summed = jnp.sum(
            matrix.reshape(local_marks, segment_len, matrix.shape[1]), axis=1, dtype=jnp.float32
        )
        return (summed / segment_len).astype(jnp.bfloat16)

    mark_queries, mark_keys = (
        lax.all_gather(landmark(query_rows), "seq", axis=0, tiled=True),
        lax.all_gather(landmark(key_rows), "seq", axis=0, tiled=True),
    )
    query_per_head = query_rows.reshape(tok_rows, head_count, HD)
    key_per_head = key_rows.reshape(tok_rows, head_count, HD)
    value_per_head = value_rows.reshape(tok_rows, head_count, HD)
    gradient_per_head = grad_rows.reshape(tok_rows, head_count, HD)
    landmark_query_heads = mark_queries.reshape(M, head_count, HD)
    landmark_key_heads = mark_keys.reshape(M, head_count, HD)
    key_score = (
        jnp.einsum(
            "pcv,gcv->cpg", landmark_query_heads, key_per_head, preferred_element_type=jnp.float32
        )
        * score_scale
    )
    key_max = lax.pmax(jnp.max(key_score, axis=-1), "seq")
    key_exp = jnp.exp(key_score - key_max[..., None])
    partial_num = jnp.einsum(
        "akq,qay->aky",
        key_exp.astype(jnp.bfloat16),
        value_per_head,
        preferred_element_type=jnp.float32,
    )
    key_total, numerator = lax.psum((jnp.sum(key_exp, axis=-1), partial_num), "seq")
    landmark_value_rows = numerator / key_total[..., None]
    token_prob = jax.nn.softmax(
        jnp.einsum(
            "jti,cti->tjc", query_per_head, landmark_key_heads, preferred_element_type=jnp.float32
        )
        * score_scale,
        axis=-1,
    )
    token_probability_lowered = token_prob.astype(jnp.bfloat16)
    mark_prob = jax.nn.softmax(
        jnp.einsum(
            "jou,iou->oji",
            landmark_query_heads,
            landmark_key_heads,
            preferred_element_type=jnp.float32,
        )
        * score_scale,
        axis=-1,
    )
    own_head = seq_index % head_count
    own_mark = lax.dynamic_index_in_dim(mark_prob, own_head, 0, keepdims=False)
    own_inverse, pull_back = jax.vjp(newton_inverse, own_mark)
    pseudo_inverse_matrix = share_heads(own_inverse, head_count)
    mixing_matrix = jnp.einsum(
        "jvy,jys->jvs", pseudo_inverse_matrix, landmark_value_rows, precision=precise_setting
    )
    mixing_matrix_lowered = mixing_matrix.astype(jnp.bfloat16)
    attended = jnp.einsum(
        "yvo,yor->vyr",
        token_probability_lowered,
        mixing_matrix_lowered,
        preferred_element_type=jnp.float32,
    ).astype(jnp.bfloat16)
    token_grad = jnp.einsum(
        "fag,aog->afo", gradient_per_head, mixing_matrix_lowered, preferred_element_type=jnp.float32
    )
    partial_mix = jnp.einsum(
        "klz,lkr->kzr",
        token_probability_lowered,
        gradient_per_head,
        preferred_element_type=jnp.float32,
    )
    mixing_matrix_gradient = lax.psum(partial_mix, "seq")
    token_score_gradient = (
        token_prob * (token_grad - jnp.sum(token_grad * token_prob, axis=-1, keepdims=True))
    ).astype(jnp.bfloat16)
    direct_qgrad = (
        jnp.einsum(
            "ufg,guc->fuc",
            token_score_gradient,
            landmark_key_heads,
            preferred_element_type=jnp.float32,
        )
        * score_scale
    )
    mark_kgrad_f = (
        jnp.einsum(
            "xgi,gxy->ixy", token_score_gradient, query_per_head, preferred_element_type=jnp.float32
        )
        * score_scale
    )
    pseudo_inverse_gradient = jnp.einsum(
        "ktu,kyu->kty", mixing_matrix_gradient, landmark_value_rows, precision=precise_setting
    )
    landmark_value_gradient = jnp.einsum(
        "lrb,lrz->lbz", pseudo_inverse_matrix, mixing_matrix_gradient, precision=precise_setting
    )
    own_igrad = lax.dynamic_index_in_dim(pseudo_inverse_gradient, own_head, 0, keepdims=False)
    (own_mgrad,) = pull_back(own_igrad)
    mark_grad = share_heads(own_mgrad, head_count)
    mark_sgrad = mark_prob * (mark_grad - jnp.sum(mark_grad * mark_prob, axis=-1, keepdims=True))
    first_mark = seq_index * local_marks
    score_gradient_rows = lax.dynamic_slice_in_dim(mark_sgrad, first_mark, local_marks, 1)
    score_gradient_columns = lax.dynamic_slice_in_dim(mark_sgrad, first_mark, local_marks, 2)
    own_qgrad_a = (
        jnp.einsum(
            "txs,ste->xte",
            score_gradient_rows,
            landmark_key_heads.astype(jnp.float32),
            precision=precise_setting,
        )
        * score_scale
    )
    own_kgrad_a = (
        jnp.einsum(
            "eaj,aev->jev",
            score_gradient_columns,
            landmark_query_heads.astype(jnp.float32),
            precision=precise_setting,
        )
        * score_scale
    )
    landmark_value_lowered = landmark_value_gradient.astype(jnp.bfloat16)
    key_prob = key_exp / key_total[..., None]
    key_probability_lowered = key_prob.astype(jnp.bfloat16)
    value_gradient_array = jnp.einsum(
        "zct,zcj->tzj",
        key_probability_lowered,
        landmark_value_lowered,
        preferred_element_type=jnp.float32,
    )
    key_direct_gradient = jnp.einsum(
        "exb,geb->exg", landmark_value_lowered, value_per_head, preferred_element_type=jnp.float32
    )
    row_total = lax.psum(jnp.sum(key_prob * key_direct_gradient, axis=-1), "seq")
    key_score_gradient = (key_prob * (key_direct_gradient - row_total[..., None])).astype(
        jnp.bfloat16
    )
    direct_kgrad = (
        jnp.einsum(
            "pbo,bpx->opx",
            key_score_gradient,
            landmark_query_heads,
            preferred_element_type=jnp.float32,
        )
        * score_scale
    )
    mark_qgrad_b = (
        jnp.einsum(
            "cbj,jcp->bcp", key_score_gradient, key_per_head, preferred_element_type=jnp.float32
        )
        * score_scale
    )
    own_kgrad_f, own_qgrad_b = (
        lax.psum_scatter(mark_kgrad_f, "seq", scatter_dimension=0, tiled=True),
        lax.psum_scatter(mark_qgrad_b, "seq", scatter_dimension=0, tiled=True),
    )
    mark_qtotal = (own_qgrad_a + own_qgrad_b) / segment_len
    mark_ktotal = (own_kgrad_a + own_kgrad_f) / segment_len
    query_grad = (
        direct_qgrad.reshape(local_marks, segment_len, head_count, HD) + mark_qtotal[:, None]
    )
    key_grad = direct_kgrad.reshape(local_marks, segment_len, head_count, HD) + mark_ktotal[:, None]
    width = head_count * HD
    results = (
        attended.reshape(tok_rows, width),
        query_grad.astype(jnp.bfloat16).reshape(tok_rows, width),
        key_grad.astype(jnp.bfloat16).reshape(tok_rows, width),
        value_gradient_array.astype(jnp.bfloat16).reshape(tok_rows, width),
    )
    attended_out, query_out, key_out, value_out = (
        lax.all_to_all(results[0], "head", split_axis=0, concat_axis=1, tiled=True),
        lax.all_to_all(results[1], "head", split_axis=0, concat_axis=1, tiled=True),
        lax.all_to_all(results[2], "head", split_axis=0, concat_axis=1, tiled=True),
        lax.all_to_all(results[3], "head", split_axis=0, concat_axis=1, tiled=True),
    )
    return (attended_out, query_out, key_out, value_out)


def halves(matrix):
    high = matrix.astype(jnp.bfloat16)
    return high, (matrix - high.astype(jnp.float32)).astype(jnp.bfloat16)


def wide_dot(left, right):
    return jnp.dot(left, right, preferred_element_type=jnp.float32)


def wide_dot_nt(left, right):
    return lax.dot_general(
        left, right, (((1,), (1,)), ((), ())), preferred_element_type=jnp.float32
    )


def split_dot(left, right):
    left_high, left_low = left
    right_high, right_low = right
    return wide_dot(
        jnp.concatenate([left_high, left_high, left_low], axis=1),
        jnp.concatenate([right_high, right_low, right_high], axis=0),
    )


def split_dot_nt(left, right):
    left_high, left_low = left
    right_high, right_low = right
    return wide_dot_nt(
        jnp.concatenate([left_high, left_high, left_low], axis=1),
        jnp.concatenate([right_high, right_low, right_high], axis=1),
    )


def identity_matrix():
    return (
        lax.broadcasted_iota(jnp.int32, (M, M), 0) == lax.broadcasted_iota(jnp.int32, (M, M), 1)
    ).astype(jnp.float32)


def chunk_of(ref, array, slot, index):
    per = CHUNK // ref.shape[3]
    return ref[index * per : (index + 1) * per, array, slot].reshape(CHUNK, HD)


def store_chunk(ref, lead, index, value):
    rows = ref.shape[-2]
    per = CHUNK // rows
    ref[(slice(index * per, (index + 1) * per), *lead)] = value.reshape(per, rows, HD)


def all_tokens(ref, array, slot):
    return ref[:, array, slot].reshape(ref.shape[0] * ref.shape[3], HD)


def tokens_of(ref):
    return ref.shape[0] * ref.shape[3]


def columns(index):
    return pl.ds(pl.multiple_of(index * CHUNK, CHUNK), CHUNK)


def swap_lanes(matrix):
    return jnp.concatenate([matrix[:, HALF:], matrix[:, :HALF]], axis=1)


def thirds(rows):
    first = rows.astype(jnp.bfloat16).astype(jnp.float32)
    second = (rows - first).astype(jnp.bfloat16).astype(jnp.float32)
    return jnp.concatenate([first, second, rows - first - second], axis=0)


def joined_thirds(rows):
    count = rows.shape[0] // 3
    return rows[:count] + (rows[count : 2 * count] + rows[2 * count :])


def held_shape(kind, shape):
    return shape[1:] if kind in SLOTS else shape


def pieces_of(kind, shape):
    if kind == LEAD:
        return [(index,) for index in range(shape[0])]
    if kind == GROUPS:
        per = CHUNK // shape[-2]
        return [(slice(place, place + per),) for place in range(0, shape[0], per)]
    return [()]


def window(ref, piece):
    place = tuple(
        pl.ds(part.start, part.stop - part.start) if isinstance(part, slice) else part
        for part in piece
    )
    return ref.at[place] if place else ref


class Staged:
    def __init__(self, names, kinds, outer, inner, done, outward):
        self.refs = SimpleNamespace(**dict(zip(names, inner)))
        self.copies, self.order = [], []
        count = 0
        steps = []
        for place, (kind, home, held) in enumerate(zip(kinds, outer, inner)):
            home = home.at[kind - SLOTS[0]] if kind in SLOTS else home
            copies = {}
            for step, piece in enumerate(pieces_of(kind, held.shape)):
                ends = (window(held, piece), window(home, piece))
                source, target = ends if outward else ends[::-1]
                key = tuple(
                    part.start if isinstance(part, slice) else part for part in piece
                )
                copies[key] = pltpu.make_async_copy(source, target, done.at[count])
                steps.append((step if kind != WHOLE else -1, place, key))
                count += 1
            self.copies.append(copies)
        self.inner = inner
        self.order = sorted(steps, key=lambda item: item[:2])
        self.started, self.waited = set(), set()

    def place_of(self, ref):
        return next(index for index, held in enumerate(self.inner) if held is ref)

    def start(self, ref=None, *key):
        chosen = [
            (place, name)
            for _, place, name in self.order
            if (ref is None or place == self.place_of(ref)) and (not key or name == key)
        ]
        for item in chosen:
            if item not in self.started:
                self.started.add(item)
                self.copies[item[0]][item[1]].start()

    def wait(self, ref=None, *key):
        chosen = [
            (place, name)
            for _, place, name in self.order
            if (ref is None or place == self.place_of(ref)) and (not key or name == key)
        ]
        for item in chosen:
            if item not in self.waited:
                self.waited.add(item)
                self.copies[item[0]][item[1]].wait()


def staged_call(compute, inputs, outputs, flops, extra=(), after=(), in_place=False):
    names_in, names_out = tuple(inputs), tuple(outputs)
    kinds_in = [x[1] if isinstance(x, tuple) else WHOLE for x in inputs.values()]
    kinds_out = [x[1] if isinstance(x, tuple) else WHOLE for x in outputs.values()]
    operands = tuple(x[0] if isinstance(x, tuple) else x for x in inputs.values())
    shapes = tuple(x[0] if isinstance(x, tuple) else x for x in outputs.values())
    n_in, n_out, n_after = len(operands), len(shapes), len(after)
    moved = sum(x.size * x.dtype.itemsize for x in (*operands, *shapes))
    anywhere = pl.BlockSpec(memory_space=pl.ANY)

    def count(kinds, arrays):
        return sum(len(pieces_of(kind, x.shape)) for kind, x in zip(kinds, arrays))

    def kernel(*refs):
        sources, refs = refs[:n_in], refs[n_in + n_after :]
        homes, refs = refs[:n_out], refs[n_out:]
        held_in, held_out = refs[:n_in], refs[n_in : n_in + n_out]
        *scratch, in_done, out_done = refs[n_in + n_out :]
        reads = Staged(names_in, kinds_in, sources, held_in, in_done, False)
        writes = Staged(names_out, kinds_out, homes, held_out, out_done, True)
        reads.start()
        compute(reads.refs, writes.refs, reads.wait, writes.start, *scratch)
        reads.wait()
        writes.start()
        writes.wait()

    results = pl.pallas_call(
        kernel,
        out_shape=shapes,
        in_specs=[anywhere] * (n_in + n_after),
        out_specs=(anywhere,) * n_out,
        scratch_shapes=[
            *(
                pltpu.VMEM(held_shape(kind, x.shape), x.dtype)
                for kind, x in zip((*kinds_in, *kinds_out), (*operands, *shapes))
            ),
            *extra,
            pltpu.SemaphoreType.DMA((count(kinds_in, operands),)),
            pltpu.SemaphoreType.DMA((count(kinds_out, shapes),)),
        ],
        compiler_params=pltpu.CompilerParams(vmem_limit_bytes=VMEM_LIMIT),
        cost_estimate=pl.CostEstimate(
            flops=int(flops * 10**9), bytes_accessed=moved, transcendentals=0
        ),
    )(*operands, *after)
    return SimpleNamespace(**dict(zip(outputs, results)))


def low(*shape):
    return jax.ShapeDtypeStruct(shape, jnp.bfloat16)


def wide(*shape):
    return jax.ShapeDtypeStruct(shape, jnp.float32)


def pack_kernel(half_ref, first_ref, second_ref, out_ref, rows_s, packed_s, in_done, out_done):
    half = half_ref[0]
    pairs = out_ref.shape[0]
    group = pairs // PACK_GROUPS
    span = 2 * HD
    reads, writes = [], []
    for index in range(PACK_GROUPS):
        for array, ref in enumerate((first_ref, second_ref)):
            place = pl.ds(index * group * span, group * span)
            reads.append(
                pltpu.make_async_copy(
                    ref.at[:, place], rows_s.at[array, :, place], in_done.at[array, index]
                )
            )
        place = pl.ds(index * group, group)
        writes.append(
            pltpu.make_async_copy(packed_s.at[place], out_ref.at[place], out_done.at[index])
        )
    for copy in reads:
        copy.start()
    for index in range(PACK_GROUPS):
        for array in range(2):
            reads[2 * index + array].wait()
            for pair in range(index * group, (index + 1) * group):
                start = pair * span
                packed_s[pair, array, half] = rows_s[array, :, start : start + HD]
                packed_s[pair, array, 1 - half] = rows_s[array, :, start + HD : start + span]
        writes[index].start()
    for copy in writes:
        copy.wait()


def unpack_kernel(half_ref, packed_ref, first_ref, second_ref, rows_s, out_done):
    half = half_ref[0]
    pairs = packed_ref.shape[0]
    group = pairs // PACK_GROUPS
    span = 2 * HD
    writes = []
    for index in range(PACK_GROUPS):
        for array, ref in enumerate((first_ref, second_ref)):
            for pair in range(index * group, (index + 1) * group):
                start = pair * span
                rows_s[array, :, start : start + HD] = packed_ref[pair, array, half]
                rows_s[array, :, start + HD : start + span] = packed_ref[pair, array, 1 - half]
            place = pl.ds(index * group * span, group * span)
            write = pltpu.make_async_copy(
                rows_s.at[array, :, place], ref.at[:, place], out_done.at[array, index]
            )
            write.start()
            writes.append(write)
    for copy in writes:
        copy.wait()


def layout_call(kernel, half, operands, out_shape, scratch, in_space, limit):
    anywhere = pl.BlockSpec(memory_space=pl.ANY)
    moved = 2 * sum(x.size * x.dtype.itemsize for x in operands)
    return pl.pallas_call(
        kernel,
        out_shape=out_shape,
        in_specs=[pl.BlockSpec(memory_space=pltpu.SMEM)]
        + [pl.BlockSpec(memory_space=in_space)] * len(operands),
        out_specs=jax.tree.map(lambda _: anywhere, out_shape),
        scratch_shapes=scratch,
        compiler_params=pltpu.CompilerParams(vmem_limit_bytes=limit),
        cost_estimate=pl.CostEstimate(flops=0, bytes_accessed=moved, transcendentals=0),
    )(half, *operands)


def pack(half, first, second):
    rows, width = first.shape
    shape = low(width // (2 * HD), 2, 2, rows, HD)
    scratch = [
        pltpu.VMEM((2, rows, width), jnp.bfloat16),
        pltpu.VMEM(shape.shape, jnp.bfloat16),
        pltpu.SemaphoreType.DMA((2, PACK_GROUPS)),
        pltpu.SemaphoreType.DMA((PACK_GROUPS,)),
    ]
    return layout_call(
        pack_kernel, half, (first, second), shape, scratch, pl.ANY, VMEM_LIMIT
    )


def unpack(half, packed):
    pairs, _, _, rows, _ = packed.shape
    shape = low(rows, pairs * 2 * HD)
    scratch = [
        pltpu.VMEM((2, *shape.shape), jnp.bfloat16),
        pltpu.SemaphoreType.DMA((2, PACK_GROUPS)),
    ]
    return layout_call(
        unpack_kernel, half, (packed,), (shape, shape), scratch, pltpu.VMEM, SMALL_LIMIT
    )


def landmark_kernel(qk_ref, marks_ref):
    tokens = tokens_of(qk_ref)
    segment_len = tokens // HALF
    per = CHUNK // segment_len
    member = (
        lax.broadcasted_iota(jnp.int32, (per, CHUNK), 1) // segment_len
        == lax.broadcasted_iota(jnp.int32, (per, CHUNK), 0)
    ).astype(jnp.bfloat16)
    kinds = [(slot, array) for slot in range(2) for array in range(2)]
    for index in range(tokens // CHUNK):
        parts = [chunk_of(qk_ref, array, slot, index) for slot, array in kinds]
        summed = wide_dot(member, jnp.concatenate(parts, axis=1))
        mean = (summed / segment_len).astype(jnp.bfloat16)
        for place, (slot, array) in enumerate(kinds):
            marks_ref[slot, array, index * per : (index + 1) * per] = mean[
                :, place * HD : (place + 1) * HD
            ]


def landmarks_of(qk):
    held = pl.BlockSpec(memory_space=pltpu.VMEM)
    return pl.pallas_call(
        landmark_kernel,
        out_shape=low(2, 2, HALF, HD),
        in_specs=[held],
        out_specs=held,
        compiler_params=pltpu.CompilerParams(vmem_limit_bytes=SMALL_LIMIT),
        cost_estimate=pl.CostEstimate(
            flops=2 * 10**8, bytes_accessed=qk.size * 2, transcendentals=0
        ),
    )(qk)


def sweep_forward(power_s, iterate_s, saved, sweep, work):
    pair_ref, weight_ref, growth_ref = saved
    power = power_s[...]
    power_high, power_low = halves(power)
    square = split_dot((power_high, power_low), (power_high, power_low))
    next(work)()
    square_halves = halves(square)
    pair = (
        jnp.concatenate([power_high, square_halves[0]], axis=0),
        jnp.concatenate([power_low, square_halves[1]], axis=0),
    )
    pair_ref[sweep, 0], pair_ref[sweep, 1] = pair
    higher = split_dot(pair, square_halves)
    next(work)()
    cube, fourth = higher[:M], higher[M:]
    weight = halves(0.25 * (13.0 * identity_matrix() - 15.0 * power + 7.0 * square - cube))
    power_s[...] = 0.25 * (13.0 * power - 15.0 * square + 7.0 * cube - fourth)
    weight_ref[sweep, 0], weight_ref[sweep, 1] = weight
    iterate = halves(iterate_s[...])
    growth_ref[sweep, 0], growth_ref[sweep, 1] = iterate[0][M:], iterate[1][M:]
    iterate_s[...] = split_dot(iterate, weight)


def probability_compute(ins, outs, need, put, power_s, iterate_s):
    need()
    qk_ref = ins.qk
    chunks = tokens_of(qk_ref) // CHUNK
    score_scale = HD ** (-0.5)
    for slot in range(2):
        for array in range(2):
            outs.marks[slot, array] = jnp.concatenate(
                [ins.mine[slot, array], ins.theirs[1 - slot, array]], axis=0
            )
    put(outs.marks)
    landmark_q, landmark_k = outs.marks[0, 0], outs.marks[0, 1]
    mark_score = wide_dot_nt(landmark_q, landmark_k) * score_scale
    mark_exp = jnp.exp(mark_score - jnp.max(mark_score, axis=1, keepdims=True))
    mark_prob = mark_exp / jnp.sum(mark_exp, axis=1, keepdims=True)
    outs.mark_prob[...] = mark_prob
    factor = 1.0 / jnp.max(jnp.sum(mark_prob, axis=0, keepdims=True), axis=1, keepdims=True)
    outs.factor[...] = jnp.broadcast_to(factor, outs.factor.shape)
    mark_halves = halves(mark_prob)
    power_s[...] = split_dot_nt(mark_halves, mark_halves) * factor
    iterate_s[0:M] = mark_prob.T * factor
    iterate_s[M:] = identity_matrix()
    tops, totals = [[], []], [[], []]

    def scores(slot, index):
        query_chunk, key_chunk = (chunk_of(qk_ref, array, slot, index) for array in range(2))
        place = slice(index * CHUNK, (index + 1) * CHUNK)
        outs.turned[slot, 0, :, place] = query_chunk.T
        outs.turned[slot, 1, :, place] = key_chunk.T
        score = wide_dot_nt(query_chunk, outs.marks[slot, 1]) * score_scale
        grown = jnp.exp(score - jnp.max(score, axis=1, keepdims=True))
        prob = grown * (1.0 / jnp.sum(grown, axis=1, keepdims=True))
        outs.token_prob[slot, place] = prob
        outs.token_low[slot, place] = prob.astype(jnp.bfloat16)
        key_score = wide_dot_nt(key_chunk, outs.marks[slot, 0]) * score_scale
        outs.key_exp[slot, place] = key_score
        tops[slot].append(jnp.max(key_score, axis=0, keepdims=True))

    def grow(slot, index):
        if index == 0:
            tops[slot] = functools.reduce(jnp.maximum, tops[slot])
        place = slice(index * CHUNK, (index + 1) * CHUNK)
        grown = jnp.exp(outs.key_exp[slot, place] - tops[slot])
        outs.key_exp[slot, place] = grown
        outs.key_low[slot, place] = grown.astype(jnp.bfloat16)
        totals[slot].append(jnp.sum(grown, axis=0, keepdims=True))

    def several(unit, pairs):
        for slot, index in pairs:
            unit(slot, index)

    pairs = [(slot, index) for slot in range(2) for index in range(chunks)]
    work = iter(
        [functools.partial(several, scores, [pair]) for pair in pairs]
        + [
            functools.partial(several, grow, pairs[first : first + 2])
            for first in range(0, len(pairs), 2)
        ]
    )
    saved = (outs.pair, outs.weight, outs.growth)
    for sweep in range(PINV_ITERS):
        sweep_forward(power_s, iterate_s, saved, sweep, work)
        for ref in saved:
            put(ref, sweep)
        if sweep == 3:
            for ref in (outs.token_low, outs.token_prob, outs.turned):
                put(ref)
    put(outs.key_low)
    put(outs.key_exp)
    outs.inverse[0], outs.inverse[1] = halves(iterate_s[0:M])
    outs.last_growth[0], outs.last_growth[1] = halves(iterate_s[M:])
    stats = [x for slot in range(2) for x in (tops[slot], sum(totals[slot][1:], totals[slot][0]))]
    outs.stats[0:4] = jnp.concatenate(stats, axis=0)
    outs.stats[4:8] = jnp.zeros((4, M), jnp.float32)


def partial_compute(ins, outs, need, put):
    need(ins.vg)
    turned = [[all_tokens(ins.vg, array, slot).T for array in range(2)] for slot in range(2)]
    need()
    rows = thirds(ins.stats[0:4])
    outs.send[2 * HD :] = jnp.concatenate([rows, jnp.zeros((4, M), jnp.float32)], axis=0).astype(
        jnp.bfloat16
    )
    for slot, home in ((1, outs.send), (0, outs.keep)):
        home[0:HD] = wide_dot(turned[slot][0], ins.key_low[slot]).astype(home.dtype)
        home[HD : 2 * HD] = wide_dot(turned[slot][1], ins.token_low[slot]).astype(home.dtype)
        put(home)


def mixing_compute(ins, outs, need, put):
    need()
    got = ins.got[...].astype(jnp.float32)
    others = swap_lanes(joined_thirds(got[2 * HD : 2 * HD + 12]))
    scales = []
    for slot in range(2):
        own_max, own_total = ins.stats[2 * slot : 2 * slot + 1], ins.stats[2 * slot + 1 : 2 * slot + 2]
        other = 1 - slot
        other_max, other_total = others[2 * other : 2 * other + 1], others[2 * other + 1 : 2 * other + 2]
        key_max = jnp.maximum(own_max, other_max)
        own_factor, other_factor = jnp.exp(own_max - key_max), jnp.exp(other_max - key_max)
        inverse_total = 1.0 / (own_total * own_factor + other_total * other_factor)
        scales.append((own_factor * inverse_total, other_factor * inverse_total))
    outs.scales[...] = jnp.concatenate(
        [scales[0][0], scales[1][0], jnp.zeros((6, M), jnp.float32)], axis=0
    )
    landmark_values = ins.keep[0:HD] * scales[0][0] + swap_lanes(got[0:HD]) * scales[0][1]
    mixing_grad = ins.keep[HD : 2 * HD] + swap_lanes(got[HD : 2 * HD])
    inverse = (ins.inverse[0], ins.inverse[1])
    outs.share[0:HD] = split_dot_nt(halves(landmark_values), inverse).astype(jnp.bfloat16)
    values_low = split_dot(halves(mixing_grad), inverse).astype(jnp.bfloat16)
    outs.share[HD : 2 * HD] = values_low
    row_total = jnp.sum(values_low.astype(jnp.float32) * landmark_values, axis=0, keepdims=True)
    outs.share[2 * HD :] = jnp.concatenate(
        [thirds(row_total), jnp.zeros((13, M), jnp.float32)], axis=0
    ).astype(jnp.bfloat16)
    put(outs.share)
    outs.mixing_grad[...] = mixing_grad
    outs.mark_values[...] = landmark_values


def head_units(ins, slot, out_ref, lead, direct_ref, share):
    score_scale = HD ** (-0.5)
    mixing_low, values_low, row_total = share
    query_sums, key_sums = [], []
    scale = ins.scales[slot : slot + 1]

    def token_side(index):
        place = slice(index * CHUNK, (index + 1) * CHUNK)
        prob = ins.token_prob[place]
        attended = wide_dot_nt(prob.astype(jnp.bfloat16), mixing_low)
        store_chunk(out_ref, (0, *lead), index, attended.astype(jnp.bfloat16))
        token_grad = wide_dot(chunk_of(ins.vg, 1, slot, index), mixing_low)
        token_sgrad = (
            prob * (token_grad - jnp.sum(token_grad * prob, axis=1, keepdims=True))
        ).astype(jnp.bfloat16)
        direct_ref[0, place] = wide_dot(token_sgrad, ins.marks[slot, 1]) * score_scale
        key_sums.append(wide_dot(ins.turned[0, :, place], token_sgrad))

    def key_side(index):
        place = slice(index * CHUNK, (index + 1) * CHUNK)
        key_prob = ins.key_exp[place] * scale
        value_gradient = wide_dot_nt(key_prob.astype(jnp.bfloat16), values_low)
        store_chunk(out_ref, (1, *lead), index, value_gradient.astype(jnp.bfloat16))
        key_dgrad = wide_dot(chunk_of(ins.vg, 0, slot, index), values_low)
        key_sgrad = (key_prob * (key_dgrad - row_total)).astype(jnp.bfloat16)
        direct_ref[1, place] = wide_dot(key_sgrad, ins.marks[slot, 0]) * score_scale
        query_sums.append(wide_dot(ins.turned[1, :, place], key_sgrad))

    chunks = tokens_of(ins.vg) // CHUNK
    units = [
        functools.partial(unit, index) for unit in (key_side, token_side) for index in range(chunks)
    ]
    return units, query_sums, key_sums


def share_parts(ref, swap):
    parts = [ref[0:HD], ref[HD : 2 * HD], joined_thirds(ref[2 * HD :].astype(jnp.float32)[0:3])]
    return [swap_lanes(part) for part in parts] if swap else parts


def own_gradient_compute(ins, outs, need, put):
    for ref in (ins.mark_prob, ins.factor, ins.mixing_grad, ins.mark_values, ins.share, ins.scales):
        need(ref)
    mark_prob = ins.mark_prob[...]
    mark_halves = halves(mark_prob)
    factor = ins.factor[0:1, 0:1]
    inverse_grad = split_dot(halves(ins.mixing_grad[...].T), halves(ins.mark_values[...]))
    inverse_grad_halves = halves(inverse_grad)
    toward = split_dot(mark_halves, inverse_grad_halves) * factor
    power = 0.5 * (toward + toward.T)
    growth = None
    units, query_sums, key_sums = head_units(
        ins, 0, outs.out, (), outs.direct, share_parts(ins.share, False)
    )
    work = iter(units)

    def beside():
        next(work, lambda: None)()

    for sweep in range(PINV_ITERS):
        if sweep == 0:
            for ref in (ins.marks, ins.vg, ins.key_exp, ins.turned):
                need(ref)
        if sweep == 2:
            need(ins.token_prob)
        for ref in (ins.pair, ins.weight, ins.growth):
            need(ref, sweep)
        pair = (ins.pair[sweep, 0], ins.pair[sweep, 1])
        first = split_dot(pair, halves(power))
        beside()
        square = first[:M] + first[:M].T
        last = sweep == PINV_ITERS - 1
        second = split_dot(tuple(x[:M] for x in pair) if last else pair, halves(square))
        beside()
        cube = first[M:].T + second[:M]
        weight = halves(0.25 * (7.0 * square - 15.0 * power - cube))
        if not last:
            fourth = second[M:] + second[M:].T
            power = 0.25 * (13.0 * power - 15.0 * square + 7.0 * cube - fourth)
        left = [ins.growth[sweep, 0], ins.growth[sweep, 0], ins.growth[sweep, 1]]
        right = [weight[0], weight[1], weight[0]]
        if growth is not None:
            grown = halves(growth)
            left += [grown[0], grown[0], grown[1]]
            right += [ins.weight[sweep, 0], ins.weight[sweep, 1], ins.weight[sweep, 0]]
        growth = wide_dot(jnp.concatenate(left, axis=1), jnp.concatenate(right, axis=0))
    for unit in work:
        unit()
    put(outs.out)
    put(outs.direct)
    need()
    mark_grad = factor * (
        split_dot_nt((ins.last_growth[0], ins.last_growth[1]), inverse_grad_halves)
        + split_dot(halves(growth + growth.T), mark_halves)
    )
    mark_sgrad = mark_prob * (mark_grad - jnp.sum(mark_grad * mark_prob, axis=1, keepdims=True))

    def marks_dot(left, right):
        left_high, left_low = halves(left)
        return wide_dot(
            jnp.concatenate([left_high, left_low], axis=1), jnp.concatenate([right, right], axis=0)
        )

    outs.totals[0] = marks_dot(mark_sgrad, ins.marks[0, 1]) + sum(query_sums[1:], query_sums[0]).T
    outs.totals[1] = marks_dot(mark_sgrad.T, ins.marks[0, 0]) + sum(key_sums[1:], key_sums[0]).T


def other_gradient_compute(ins, outs, need, put):
    need()
    outs.out[:, :, 0] = ins.own_out[...]
    units, query_sums, key_sums = head_units(
        ins, 1, outs.out, (1,), outs.direct, share_parts(ins.got_share, True)
    )
    for unit in units:
        unit()
    put(outs.out)
    marks_scale = HD ** (-0.5) / (tokens_of(ins.vg) // HALF)
    for kind, sums in enumerate((query_sums, key_sums)):
        for slot, total in ((0, ins.totals[kind]), (1, sum(sums[1:], sums[0]).T)):
            total = total * marks_scale
            outs.near[kind, slot] = total[:HALF]
            outs.far[kind, slot] = total[HALF:].astype(jnp.bfloat16)


def finish_compute(ins, outs, need, put):
    need()
    out_ref = outs.out
    group = CHUNK // out_ref.shape[3]
    segment_len = tokens_of(out_ref) // HALF
    per = CHUNK // segment_len
    for index in range(tokens_of(out_ref) // CHUNK):
        place, start = slice(index * per, (index + 1) * per), index * CHUNK
        for slot, direct_ref in enumerate((ins.own_direct, ins.other_direct)):
            for kind in range(2):
                marks = ins.near[kind, slot, place] + ins.got_far[
                    kind, 1 - slot, place
                ].astype(jnp.float32)
                spread = jnp.broadcast_to(marks[:, None], (per, segment_len, HD))
                total = direct_ref[kind, start : start + CHUNK] + spread.reshape(CHUNK, HD)
                store_chunk(out_ref, (kind, slot), index, total.astype(jnp.bfloat16))
        put(out_ref, index * group)


def exchange(packed):
    return lax.all_to_all(packed, "cube", split_axis=0, concat_axis=0, tiled=True)


def partner(array):
    return lax.ppermute(array, "half", SWAP)


def body(queries, keys, values, out_grad):
    half = lax.axis_index("half").reshape(1)
    qk = exchange(pack(half, queries, keys))
    tokens = qk.shape[0] * qk.shape[3]
    mine = landmarks_of(qk)
    theirs = partner(mine)
    values, mine = lax.optimization_barrier((values, mine))
    vg = exchange(pack(half, values, out_grad))
    kept = staged_call(
        probability_compute,
        dict(qk=qk, mine=mine, theirs=theirs),
        dict(
            marks=low(2, 2, M, HD),
            token_prob=wide(2, tokens, M),
            token_low=low(2, tokens, M),
            key_exp=wide(2, tokens, M),
            key_low=low(2, tokens, M),
            turned=low(2, 2, HD, tokens),
            stats=wide(8, M),
            mark_prob=wide(M, M),
            factor=wide(8, HD),
            pair=(low(PINV_ITERS, 2, 2 * M, M), LEAD),
            weight=(low(PINV_ITERS, 2, M, M), LEAD),
            growth=(low(PINV_ITERS, 2, M, M), LEAD),
            inverse=low(2, M, M),
            last_growth=low(2, M, M),
        ),
        12,
        extra=(pltpu.VMEM((M, M), jnp.float32), pltpu.VMEM((2 * M, M), jnp.float32)),
    )
    sums = staged_call(
        partial_compute,
        dict(vg=vg, stats=kept.stats, key_low=kept.key_low, token_low=kept.token_low),
        dict(send=low(2 * HD + 16, M), keep=wide(2 * HD, M)),
        2,
    )
    mixed = staged_call(
        mixing_compute,
        dict(got=partner(sums.send), keep=sums.keep, stats=kept.stats, inverse=kept.inverse),
        dict(
            share=low(2 * HD + 16, M),
            scales=wide(8, M),
            mixing_grad=wide(HD, M),
            mark_values=wide(HD, M),
        ),
        1,
    )
    got_share = partner(mixed.share)
    own = staged_call(
        own_gradient_compute,
        dict(
            mark_prob=kept.mark_prob,
            factor=kept.factor,
            mixing_grad=mixed.mixing_grad,
            mark_values=mixed.mark_values,
            share=mixed.share,
            scales=mixed.scales,
            marks=kept.marks,
            vg=vg,
            key_exp=(kept.key_exp, SLOTS[0]),
            turned=(kept.turned, SLOTS[0]),
            pair=(kept.pair, LEAD),
            weight=(kept.weight, LEAD),
            growth=(kept.growth, LEAD),
            token_prob=(kept.token_prob, SLOTS[0]),
            last_growth=kept.last_growth,
        ),
        dict(
            out=low(qk.shape[0], 2, *qk.shape[3:]),
            direct=wide(2, tokens, HD),
            totals=wide(2, M, HD),
        ),
        14,
    )
    other = staged_call(
        other_gradient_compute,
        dict(
            got_share=got_share,
            scales=mixed.scales,
            marks=kept.marks,
            vg=vg,
            key_exp=(kept.key_exp, SLOTS[1]),
            turned=(kept.turned, SLOTS[1]),
            token_prob=(kept.token_prob, SLOTS[1]),
            own_out=own.out,
            totals=own.totals,
        ),
        dict(
            out=low(*qk.shape),
            far=low(2, 2, HALF, HD),
            near=wide(2, 2, HALF, HD),
            direct=wide(2, tokens, HD),
        ),
        3,
    )
    attended, value_gradient_array = unpack(half, exchange(other.out))
    results = staged_call(
        finish_compute,
        dict(
            got_far=partner(other.far),
            near=other.near,
            own_direct=own.direct,
            other_direct=other.direct,
        ),
        dict(out=(low(*qk.shape), GROUPS)),
        0.5,
    ).out
    query_grad, key_grad = unpack(half, exchange(results))
    return attended, query_grad, key_grad, value_gradient_array


def solution(mesh):
    whole_placement = P(("seq", "head"), None)
    halves_placement = P(("half", "cube"), None)

    def layer(queries, keys, values, out_grad):
        tokens, width = queries.shape
        own_head_each = width // HD == mesh.size and tokens == 8 * CHUNK
        if own_head_each:
            split = jax.sharding.Mesh(
                mesh.devices.reshape(2, mesh.size // 2), ("half", "cube")
            )
        return jax.shard_map(
            body if own_head_each else shared_body,
            mesh=split if own_head_each else mesh,
            in_specs=(halves_placement if own_head_each else whole_placement,) * 4,
            out_specs=(halves_placement if own_head_each else whole_placement,) * 4,
            check_vma=False,
        )(queries, keys, values, out_grad)

    return layer
```

```python
import functools
from types import SimpleNamespace

import jax
import jax.numpy as jnp
from jax import lax
from jax.experimental import pallas as pl
from jax.experimental.pallas import tpu as pltpu
from jax.sharding import PartitionSpec as P

HD = 128
M = 256
PINV_ITERS = 6
CHUNK = 256
PACK_GROUPS = 4
HALF = M // 2
SWAP = ((0, 1), (1, 0))
VMEM_LIMIT = 60 * 2**20
SMALL_LIMIT = 16 * 2**20
WHOLE, LEAD, GROUPS = range(3)
SLOTS = (10, 11)
LONG = 200


precise_setting = lax.Precision.HIGHEST


def newton_inverse(matrix):
    identity = jnp.eye(matrix.shape[0], dtype=matrix.dtype)
    factor = lax.stop_gradient(1.0 / jnp.max(jnp.sum(matrix, axis=0)))
    iterate = matrix.T * factor
    for sweep_index in range(PINV_ITERS):
        product = jnp.matmul(matrix, iterate, precision=precise_setting)
        inner_term = jnp.matmul(product, 7.0 * identity - product, precision=precise_setting)
        inner_term = jnp.matmul(product, 15.0 * identity - inner_term, precision=precise_setting)
        iterate = 0.25 * jnp.matmul(
            iterate, 13.0 * identity - inner_term, precision=precise_setting
        )
    return iterate


def share_heads(own_matrix, head_count):
    seq_index = lax.axis_index("seq")
    slot_mask = (jnp.arange(head_count, dtype=jnp.int32) == seq_index).astype(jnp.float32)
    return lax.psum(slot_mask[:, None, None] * own_matrix[None], "seq")


def shared_body(queries, keys, values, out_grad):
    query_rows, key_rows, value_rows, grad_rows = (
        lax.all_to_all(queries, "head", split_axis=1, concat_axis=0, tiled=True),
        lax.all_to_all(keys, "head", split_axis=1, concat_axis=0, tiled=True),
        lax.all_to_all(values, "head", split_axis=1, concat_axis=0, tiled=True),
        lax.all_to_all(out_grad, "head", split_axis=1, concat_axis=0, tiled=True),
    )
    tok_rows = query_rows.shape[0]
    head_count = query_rows.shape[1] // HD
    local_marks = M // lax.axis_size("seq")
    segment_len = tok_rows // local_marks
    score_scale = HD ** (-0.5)
    seq_index = lax.axis_index("seq")

    def landmark(matrix):
        summed = jnp.sum(
            matrix.reshape(local_marks, segment_len, matrix.shape[1]), axis=1, dtype=jnp.float32
        )
        return (summed / segment_len).astype(jnp.bfloat16)

    mark_queries, mark_keys = (
        lax.all_gather(landmark(query_rows), "seq", axis=0, tiled=True),
        lax.all_gather(landmark(key_rows), "seq", axis=0, tiled=True),
    )
    query_per_head = query_rows.reshape(tok_rows, head_count, HD)
    key_per_head = key_rows.reshape(tok_rows, head_count, HD)
    value_per_head = value_rows.reshape(tok_rows, head_count, HD)
    gradient_per_head = grad_rows.reshape(tok_rows, head_count, HD)
    landmark_query_heads = mark_queries.reshape(M, head_count, HD)
    landmark_key_heads = mark_keys.reshape(M, head_count, HD)
    key_score = (
        jnp.einsum(
            "pcv,gcv->cpg", landmark_query_heads, key_per_head, preferred_element_type=jnp.float32
        )
        * score_scale
    )
    key_max = lax.pmax(jnp.max(key_score, axis=-1), "seq")
    key_exp = jnp.exp(key_score - key_max[..., None])
    partial_num = jnp.einsum(
        "akq,qay->aky",
        key_exp.astype(jnp.bfloat16),
        value_per_head,
        preferred_element_type=jnp.float32,
    )
    key_total, numerator = lax.psum((jnp.sum(key_exp, axis=-1), partial_num), "seq")
    landmark_value_rows = numerator / key_total[..., None]
    token_prob = jax.nn.softmax(
        jnp.einsum(
            "jti,cti->tjc", query_per_head, landmark_key_heads, preferred_element_type=jnp.float32
        )
        * score_scale,
        axis=-1,
    )
    token_probability_lowered = token_prob.astype(jnp.bfloat16)
    mark_prob = jax.nn.softmax(
        jnp.einsum(
            "jou,iou->oji",
            landmark_query_heads,
            landmark_key_heads,
            preferred_element_type=jnp.float32,
        )
        * score_scale,
        axis=-1,
    )
    own_head = seq_index % head_count
    own_mark = lax.dynamic_index_in_dim(mark_prob, own_head, 0, keepdims=False)
    own_inverse, pull_back = jax.vjp(newton_inverse, own_mark)
    pseudo_inverse_matrix = share_heads(own_inverse, head_count)
    mixing_matrix = jnp.einsum(
        "jvy,jys->jvs", pseudo_inverse_matrix, landmark_value_rows, precision=precise_setting
    )
    mixing_matrix_lowered = mixing_matrix.astype(jnp.bfloat16)
    attended = jnp.einsum(
        "yvo,yor->vyr",
        token_probability_lowered,
        mixing_matrix_lowered,
        preferred_element_type=jnp.float32,
    ).astype(jnp.bfloat16)
    token_grad = jnp.einsum(
        "fag,aog->afo", gradient_per_head, mixing_matrix_lowered, preferred_element_type=jnp.float32
    )
    partial_mix = jnp.einsum(
        "klz,lkr->kzr",
        token_probability_lowered,
        gradient_per_head,
        preferred_element_type=jnp.float32,
    )
    mixing_matrix_gradient = lax.psum(partial_mix, "seq")
    token_score_gradient = (
        token_prob * (token_grad - jnp.sum(token_grad * token_prob, axis=-1, keepdims=True))
    ).astype(jnp.bfloat16)
    direct_qgrad = (
        jnp.einsum(
            "ufg,guc->fuc",
            token_score_gradient,
            landmark_key_heads,
            preferred_element_type=jnp.float32,
        )
        * score_scale
    )
    mark_kgrad_f = (
        jnp.einsum(
            "xgi,gxy->ixy", token_score_gradient, query_per_head, preferred_element_type=jnp.float32
        )
        * score_scale
    )
    pseudo_inverse_gradient = jnp.einsum(
        "ktu,kyu->kty", mixing_matrix_gradient, landmark_value_rows, precision=precise_setting
    )
    landmark_value_gradient = jnp.einsum(
        "lrb,lrz->lbz", pseudo_inverse_matrix, mixing_matrix_gradient, precision=precise_setting
    )
    own_igrad = lax.dynamic_index_in_dim(pseudo_inverse_gradient, own_head, 0, keepdims=False)
    (own_mgrad,) = pull_back(own_igrad)
    mark_grad = share_heads(own_mgrad, head_count)
    mark_sgrad = mark_prob * (mark_grad - jnp.sum(mark_grad * mark_prob, axis=-1, keepdims=True))
    first_mark = seq_index * local_marks
    score_gradient_rows = lax.dynamic_slice_in_dim(mark_sgrad, first_mark, local_marks, 1)
    score_gradient_columns = lax.dynamic_slice_in_dim(mark_sgrad, first_mark, local_marks, 2)
    own_qgrad_a = (
        jnp.einsum(
            "txs,ste->xte",
            score_gradient_rows,
            landmark_key_heads.astype(jnp.float32),
            precision=precise_setting,
        )
        * score_scale
    )
    own_kgrad_a = (
        jnp.einsum(
            "eaj,aev->jev",
            score_gradient_columns,
            landmark_query_heads.astype(jnp.float32),
            precision=precise_setting,
        )
        * score_scale
    )
    landmark_value_lowered = landmark_value_gradient.astype(jnp.bfloat16)
    key_prob = key_exp / key_total[..., None]
    key_probability_lowered = key_prob.astype(jnp.bfloat16)
    value_gradient_array = jnp.einsum(
        "zct,zcj->tzj",
        key_probability_lowered,
        landmark_value_lowered,
        preferred_element_type=jnp.float32,
    )
    key_direct_gradient = jnp.einsum(
        "exb,geb->exg", landmark_value_lowered, value_per_head, preferred_element_type=jnp.float32
    )
    row_total = lax.psum(jnp.sum(key_prob * key_direct_gradient, axis=-1), "seq")
    key_score_gradient = (key_prob * (key_direct_gradient - row_total[..., None])).astype(
        jnp.bfloat16
    )
    direct_kgrad = (
        jnp.einsum(
            "pbo,bpx->opx",
            key_score_gradient,
            landmark_query_heads,
            preferred_element_type=jnp.float32,
        )
        * score_scale
    )
    mark_qgrad_b = (
        jnp.einsum(
            "cbj,jcp->bcp", key_score_gradient, key_per_head, preferred_element_type=jnp.float32
        )
        * score_scale
    )
    own_kgrad_f, own_qgrad_b = (
        lax.psum_scatter(mark_kgrad_f, "seq", scatter_dimension=0, tiled=True),
        lax.psum_scatter(mark_qgrad_b, "seq", scatter_dimension=0, tiled=True),
    )
    mark_qtotal = (own_qgrad_a + own_qgrad_b) / segment_len
    mark_ktotal = (own_kgrad_a + own_kgrad_f) / segment_len
    query_grad = (
        direct_qgrad.reshape(local_marks, segment_len, head_count, HD) + mark_qtotal[:, None]
    )
    key_grad = direct_kgrad.reshape(local_marks, segment_len, head_count, HD) + mark_ktotal[:, None]
    width = head_count * HD
    results = (
        attended.reshape(tok_rows, width),
        query_grad.astype(jnp.bfloat16).reshape(tok_rows, width),
        key_grad.astype(jnp.bfloat16).reshape(tok_rows, width),
        value_gradient_array.astype(jnp.bfloat16).reshape(tok_rows, width),
    )
    attended_out, query_out, key_out, value_out = (
        lax.all_to_all(results[0], "head", split_axis=0, concat_axis=1, tiled=True),
        lax.all_to_all(results[1], "head", split_axis=0, concat_axis=1, tiled=True),
        lax.all_to_all(results[2], "head", split_axis=0, concat_axis=1, tiled=True),
        lax.all_to_all(results[3], "head", split_axis=0, concat_axis=1, tiled=True),
    )
    return (attended_out, query_out, key_out, value_out)


def halves(matrix):
    high = matrix.astype(jnp.bfloat16)
    return high, (matrix - high.astype(jnp.float32)).astype(jnp.bfloat16)


def wide_dot(left, right):
    return jnp.dot(left, right, preferred_element_type=jnp.float32)


def wide_dot_nt(left, right):
    return lax.dot_general(
        left, right, (((1,), (1,)), ((), ())), preferred_element_type=jnp.float32
    )


def split_dot(left, right):
    left_high, left_low = left
    right_high, right_low = right
    return wide_dot(
        jnp.concatenate([left_high, left_high, left_low], axis=1),
        jnp.concatenate([right_high, right_low, right_high], axis=0),
    )


def split_dot_nt(left, right):
    left_high, left_low = left
    right_high, right_low = right
    return wide_dot_nt(
        jnp.concatenate([left_high, left_high, left_low], axis=1),
        jnp.concatenate([right_high, right_low, right_high], axis=1),
    )


def identity_matrix():
    return (
        lax.broadcasted_iota(jnp.int32, (M, M), 0) == lax.broadcasted_iota(jnp.int32, (M, M), 1)
    ).astype(jnp.float32)


def chunk_of(ref, array, slot, index):
    per = CHUNK // ref.shape[3]
    return ref[index * per : (index + 1) * per, array, slot].reshape(CHUNK, HD)


def store_chunk(ref, lead, index, value):
    rows = ref.shape[-2]
    per = CHUNK // rows
    ref[(slice(index * per, (index + 1) * per), *lead)] = value.reshape(per, rows, HD)


def all_tokens(ref, array, slot):
    return ref[:, array, slot].reshape(ref.shape[0] * ref.shape[3], HD)


def tokens_of(ref):
    return ref.shape[0] * ref.shape[3]


def columns(index):
    return pl.ds(pl.multiple_of(index * CHUNK, CHUNK), CHUNK)


def swap_lanes(matrix):
    return jnp.concatenate([matrix[:, HALF:], matrix[:, :HALF]], axis=1)


def thirds(rows):
    first = rows.astype(jnp.bfloat16).astype(jnp.float32)
    second = (rows - first).astype(jnp.bfloat16).astype(jnp.float32)
    return jnp.concatenate([first, second, rows - first - second], axis=0)


def joined_thirds(rows):
    count = rows.shape[0] // 3
    return rows[:count] + (rows[count : 2 * count] + rows[2 * count :])


def held_shape(kind, shape):
    return shape[1:] if kind in SLOTS else shape


def pieces_of(kind, shape):
    if kind == LEAD:
        return [(index,) for index in range(shape[0])]
    if kind == GROUPS:
        per = CHUNK // shape[-2]
        return [(slice(place, place + per),) for place in range(0, shape[0], per)]
    return [()]


def window(ref, piece):
    place = tuple(
        pl.ds(part.start, part.stop - part.start) if isinstance(part, slice) else part
        for part in piece
    )
    return ref.at[place] if place else ref


class Staged:
    def __init__(self, names, kinds, outer, inner, done, outward):
        self.refs = SimpleNamespace(**dict(zip(names, inner)))
        self.copies, self.order = [], []
        count = 0
        steps = []
        for place, (kind, home, held) in enumerate(zip(kinds, outer, inner)):
            home = home.at[kind - SLOTS[0]] if kind in SLOTS else home
            copies = {}
            for step, piece in enumerate(pieces_of(kind, held.shape)):
                ends = (window(held, piece), window(home, piece))
                source, target = ends if outward else ends[::-1]
                key = tuple(
                    part.start if isinstance(part, slice) else part for part in piece
                )
                copies[key] = pltpu.make_async_copy(source, target, done.at[count])
                steps.append((step if kind != WHOLE else -1, place, key))
                count += 1
            self.copies.append(copies)
        self.inner = inner
        self.order = sorted(steps, key=lambda item: item[:2])
        self.started, self.waited = set(), set()

    def place_of(self, ref):
        return next(index for index, held in enumerate(self.inner) if held is ref)

    def start(self, ref=None, *key):
        chosen = [
            (place, name)
            for _, place, name in self.order
            if (ref is None or place == self.place_of(ref)) and (not key or name == key)
        ]
        for item in chosen:
            if item not in self.started:
                self.started.add(item)
                self.copies[item[0]][item[1]].start()

    def wait(self, ref=None, *key):
        chosen = [
            (place, name)
            for _, place, name in self.order
            if (ref is None or place == self.place_of(ref)) and (not key or name == key)
        ]
        for item in chosen:
            if item not in self.waited:
                self.waited.add(item)
                self.copies[item[0]][item[1]].wait()


def staged_call(compute, inputs, outputs, flops, extra=(), after=(), in_place=False):
    names_in, names_out = tuple(inputs), tuple(outputs)
    kinds_in = [x[1] if isinstance(x, tuple) else WHOLE for x in inputs.values()]
    kinds_out = [x[1] if isinstance(x, tuple) else WHOLE for x in outputs.values()]
    operands = tuple(x[0] if isinstance(x, tuple) else x for x in inputs.values())
    shapes = tuple(x[0] if isinstance(x, tuple) else x for x in outputs.values())
    n_in, n_out, n_after = len(operands), len(shapes), len(after)
    moved = sum(x.size * x.dtype.itemsize for x in (*operands, *shapes))
    anywhere = pl.BlockSpec(memory_space=pl.ANY)

    def count(kinds, arrays):
        return sum(len(pieces_of(kind, x.shape)) for kind, x in zip(kinds, arrays))

    def kernel(*refs):
        sources, refs = refs[:n_in], refs[n_in + n_after :]
        homes, refs = refs[:n_out], refs[n_out:]
        held_in, held_out = refs[:n_in], refs[n_in : n_in + n_out]
        *scratch, in_done, out_done = refs[n_in + n_out :]
        reads = Staged(names_in, kinds_in, sources, held_in, in_done, False)
        writes = Staged(names_out, kinds_out, homes, held_out, out_done, True)
        reads.start()
        compute(reads.refs, writes.refs, reads.wait, writes.start, *scratch)
        reads.wait()
        writes.start()
        writes.wait()

    results = pl.pallas_call(
        kernel,
        out_shape=shapes,
        in_specs=[anywhere] * (n_in + n_after),
        out_specs=(anywhere,) * n_out,
        scratch_shapes=[
            *(
                pltpu.VMEM(held_shape(kind, x.shape), x.dtype)
                for kind, x in zip((*kinds_in, *kinds_out), (*operands, *shapes))
            ),
            *extra,
            pltpu.SemaphoreType.DMA((count(kinds_in, operands),)),
            pltpu.SemaphoreType.DMA((count(kinds_out, shapes),)),
        ],
        compiler_params=pltpu.CompilerParams(vmem_limit_bytes=VMEM_LIMIT),
        cost_estimate=pl.CostEstimate(
            flops=int(flops * 10**9), bytes_accessed=moved, transcendentals=0
        ),
    )(*operands, *after)
    return SimpleNamespace(**dict(zip(outputs, results)))


def low(*shape):
    return jax.ShapeDtypeStruct(shape, jnp.bfloat16)


def wide(*shape):
    return jax.ShapeDtypeStruct(shape, jnp.float32)


def pack_kernel(half_ref, first_ref, second_ref, out_ref, rows_s, packed_s, in_done, out_done):
    half = half_ref[0]
    pairs = out_ref.shape[0]
    group = pairs // PACK_GROUPS
    span = 2 * HD
    reads, writes = [], []
    for index in range(PACK_GROUPS):
        for array, ref in enumerate((first_ref, second_ref)):
            place = pl.ds(index * group * span, group * span)
            reads.append(
                pltpu.make_async_copy(
                    ref.at[:, place], rows_s.at[array, :, place], in_done.at[array, index]
                )
            )
        place = pl.ds(index * group, group)
        writes.append(
            pltpu.make_async_copy(packed_s.at[place], out_ref.at[place], out_done.at[index])
        )
    for copy in reads:
        copy.start()
    for index in range(PACK_GROUPS):
        for array in range(2):
            reads[2 * index + array].wait()
            for pair in range(index * group, (index + 1) * group):
                start = pair * span
                packed_s[pair, array, half] = rows_s[array, :, start : start + HD]
                packed_s[pair, array, 1 - half] = rows_s[array, :, start + HD : start + span]
        writes[index].start()
    for copy in writes:
        copy.wait()


def unpack_kernel(half_ref, packed_ref, first_ref, second_ref, rows_s, out_done):
    half = half_ref[0]
    pairs = packed_ref.shape[0]
    group = pairs // PACK_GROUPS
    span = 2 * HD
    writes = []
    for index in range(PACK_GROUPS):
        for array, ref in enumerate((first_ref, second_ref)):
            for pair in range(index * group, (index + 1) * group):
                start = pair * span
                rows_s[array, :, start : start + HD] = packed_ref[pair, array, half]
                rows_s[array, :, start + HD : start + span] = packed_ref[pair, array, 1 - half]
            place = pl.ds(index * group * span, group * span)
            write = pltpu.make_async_copy(
                rows_s.at[array, :, place], ref.at[:, place], out_done.at[array, index]
            )
            write.start()
            writes.append(write)
    for copy in writes:
        copy.wait()


def layout_call(kernel, half, operands, out_shape, scratch, in_space, limit):
    anywhere = pl.BlockSpec(memory_space=pl.ANY)
    moved = 2 * sum(x.size * x.dtype.itemsize for x in operands)
    return pl.pallas_call(
        kernel,
        out_shape=out_shape,
        in_specs=[pl.BlockSpec(memory_space=pltpu.SMEM)]
        + [pl.BlockSpec(memory_space=in_space)] * len(operands),
        out_specs=jax.tree.map(lambda _: anywhere, out_shape),
        scratch_shapes=scratch,
        compiler_params=pltpu.CompilerParams(vmem_limit_bytes=limit),
        cost_estimate=pl.CostEstimate(flops=0, bytes_accessed=moved, transcendentals=0),
    )(half, *operands)


def pack(half, first, second):
    rows, width = first.shape
    shape = low(width // (2 * HD), 2, 2, rows, HD)
    scratch = [
        pltpu.VMEM((2, rows, width), jnp.bfloat16),
        pltpu.VMEM(shape.shape, jnp.bfloat16),
        pltpu.SemaphoreType.DMA((2, PACK_GROUPS)),
        pltpu.SemaphoreType.DMA((PACK_GROUPS,)),
    ]
    return layout_call(
        pack_kernel, half, (first, second), shape, scratch, pl.ANY, VMEM_LIMIT
    )


def unpack(half, packed):
    pairs, _, _, rows, _ = packed.shape
    shape = low(rows, pairs * 2 * HD)
    scratch = [
        pltpu.VMEM((2, *shape.shape), jnp.bfloat16),
        pltpu.SemaphoreType.DMA((2, PACK_GROUPS)),
    ]
    return layout_call(
        unpack_kernel, half, (packed,), (shape, shape), scratch, pltpu.VMEM, SMALL_LIMIT
    )


def landmark_kernel(qk_ref, marks_ref):
    tokens = tokens_of(qk_ref)
    segment_len = tokens // HALF
    per = CHUNK // segment_len
    member = (
        lax.broadcasted_iota(jnp.int32, (per, CHUNK), 1) // segment_len
        == lax.broadcasted_iota(jnp.int32, (per, CHUNK), 0)
    ).astype(jnp.bfloat16)
    kinds = [(slot, array) for slot in range(2) for array in range(2)]
    for index in range(tokens // CHUNK):
        parts = [chunk_of(qk_ref, array, slot, index) for slot, array in kinds]
        summed = wide_dot(member, jnp.concatenate(parts, axis=1))
        mean = (summed / segment_len).astype(jnp.bfloat16)
        for place, (slot, array) in enumerate(kinds):
            marks_ref[slot, array, index * per : (index + 1) * per] = mean[
                :, place * HD : (place + 1) * HD
            ]


def landmarks_of(qk):
    held = pl.BlockSpec(memory_space=pltpu.VMEM)
    return pl.pallas_call(
        landmark_kernel,
        out_shape=low(2, 2, HALF, HD),
        in_specs=[held],
        out_specs=held,
        compiler_params=pltpu.CompilerParams(vmem_limit_bytes=SMALL_LIMIT),
        cost_estimate=pl.CostEstimate(
            flops=2 * 10**8, bytes_accessed=qk.size * 2, transcendentals=0
        ),
    )(qk)


def sweep_forward(power_s, iterate_s, saved, sweep, work):
    pair_ref, weight_ref, growth_ref = saved
    power = power_s[...]
    power_high, power_low = halves(power)
    square = split_dot((power_high, power_low), (power_high, power_low))
    next(work)()
    square_halves = halves(square)
    pair = (
        jnp.concatenate([power_high, square_halves[0]], axis=0),
        jnp.concatenate([power_low, square_halves[1]], axis=0),
    )
    pair_ref[sweep, 0], pair_ref[sweep, 1] = pair
    higher = split_dot(pair, square_halves)
    next(work)()
    cube, fourth = higher[:M], higher[M:]
    weight = halves(0.25 * (13.0 * identity_matrix() - 15.0 * power + 7.0 * square - cube))
    power_s[...] = 0.25 * (13.0 * power - 15.0 * square + 7.0 * cube - fourth)
    weight_ref[sweep, 0], weight_ref[sweep, 1] = weight
    iterate = halves(iterate_s[...])
    growth_ref[sweep, 0], growth_ref[sweep, 1] = iterate[0][M:], iterate[1][M:]
    iterate_s[...] = split_dot(iterate, weight)


def probability_compute(ins, outs, need, put, power_s, iterate_s):
    need()
    qk_ref = ins.qk
    chunks = tokens_of(qk_ref) // CHUNK
    score_scale = HD ** (-0.5)
    for slot in range(2):
        for array in range(2):
            outs.marks[slot, array] = jnp.concatenate(
                [ins.mine[slot, array], ins.theirs[1 - slot, array]], axis=0
            )
    put(outs.marks)
    landmark_q, landmark_k = outs.marks[0, 0], outs.marks[0, 1]
    mark_score = wide_dot_nt(landmark_q, landmark_k) * score_scale
    mark_exp = jnp.exp(mark_score - jnp.max(mark_score, axis=1, keepdims=True))
    mark_prob = mark_exp / jnp.sum(mark_exp, axis=1, keepdims=True)
    outs.mark_prob[...] = mark_prob
    factor = 1.0 / jnp.max(jnp.sum(mark_prob, axis=0, keepdims=True), axis=1, keepdims=True)
    outs.factor[...] = jnp.broadcast_to(factor, outs.factor.shape)
    mark_halves = halves(mark_prob)
    power_s[...] = split_dot_nt(mark_halves, mark_halves) * factor
    iterate_s[0:M] = mark_prob.T * factor
    iterate_s[M:] = identity_matrix()
    tops, totals = [[], []], [[], []]

    def scores(slot, index):
        query_chunk, key_chunk = (chunk_of(qk_ref, array, slot, index) for array in range(2))
        place = slice(index * CHUNK, (index + 1) * CHUNK)
        outs.turned[slot, 0, :, place] = query_chunk.T
        outs.turned[slot, 1, :, place] = key_chunk.T
        score = wide_dot_nt(query_chunk, outs.marks[slot, 1]) * score_scale
        grown = jnp.exp(score - jnp.max(score, axis=1, keepdims=True))
        prob = grown * (1.0 / jnp.sum(grown, axis=1, keepdims=True))
        outs.token_prob[slot, place] = prob
        outs.token_low[slot, place] = prob.astype(jnp.bfloat16)
        key_score = wide_dot_nt(key_chunk, outs.marks[slot, 0]) * score_scale
        outs.key_exp[slot, place] = key_score
        tops[slot].append(jnp.max(key_score, axis=0, keepdims=True))

    def grow(slot, index):
        if index == 0:
            tops[slot] = functools.reduce(jnp.maximum, tops[slot])
        place = slice(index * CHUNK, (index + 1) * CHUNK)
        grown = jnp.exp(outs.key_exp[slot, place] - tops[slot])
        outs.key_exp[slot, place] = grown
        outs.key_low[slot, place] = grown.astype(jnp.bfloat16)
        totals[slot].append(jnp.sum(grown, axis=0, keepdims=True))

    def several(unit, pairs):
        for slot, index in pairs:
            unit(slot, index)

    pairs = [(slot, index) for slot in range(2) for index in range(chunks)]
    work = iter(
        [functools.partial(several, scores, [pair]) for pair in pairs]
        + [
            functools.partial(several, grow, pairs[first : first + 2])
            for first in range(0, len(pairs), 2)
        ]
    )
    saved = (outs.pair, outs.weight, outs.growth)
    for sweep in range(PINV_ITERS):
        sweep_forward(power_s, iterate_s, saved, sweep, work)
        for ref in saved:
            put(ref, sweep)
        if sweep == 3:
            for ref in (outs.token_low, outs.token_prob, outs.turned):
                put(ref)
    put(outs.key_low)
    put(outs.key_exp)
    outs.inverse[0], outs.inverse[1] = halves(iterate_s[0:M])
    outs.last_growth[0], outs.last_growth[1] = halves(iterate_s[M:])
    stats = [x for slot in range(2) for x in (tops[slot], sum(totals[slot][1:], totals[slot][0]))]
    outs.stats[0:4] = jnp.concatenate(stats, axis=0)
    outs.stats[4:8] = jnp.zeros((4, M), jnp.float32)


def partial_compute(ins, outs, need, put):
    need(ins.vg)
    turned = [[all_tokens(ins.vg, array, slot).T for array in range(2)] for slot in range(2)]
    need()
    rows = thirds(ins.stats[0:4])
    outs.send[2 * HD :] = jnp.concatenate([rows, jnp.zeros((4, M), jnp.float32)], axis=0).astype(
        jnp.bfloat16
    )
    for slot, home in ((1, outs.send), (0, outs.keep)):
        home[0:HD] = wide_dot(turned[slot][0], ins.key_low[slot]).astype(home.dtype)
        home[HD : 2 * HD] = wide_dot(turned[slot][1], ins.token_low[slot]).astype(home.dtype)
        put(home)


def mixing_compute(ins, outs, need, put):
    need()
    got = ins.got[...].astype(jnp.float32)
    others = swap_lanes(joined_thirds(got[2 * HD : 2 * HD + 12]))
    scales = []
    for slot in range(2):
        own_max, own_total = ins.stats[2 * slot : 2 * slot + 1], ins.stats[2 * slot + 1 : 2 * slot + 2]
        other = 1 - slot
        other_max, other_total = others[2 * other : 2 * other + 1], others[2 * other + 1 : 2 * other + 2]
        key_max = jnp.maximum(own_max, other_max)
        own_factor, other_factor = jnp.exp(own_max - key_max), jnp.exp(other_max - key_max)
        inverse_total = 1.0 / (own_total * own_factor + other_total * other_factor)
        scales.append((own_factor * inverse_total, other_factor * inverse_total))
    outs.scales[...] = jnp.concatenate(
        [scales[0][0], scales[1][0], jnp.zeros((6, M), jnp.float32)], axis=0
    )
    landmark_values = ins.keep[0:HD] * scales[0][0] + swap_lanes(got[0:HD]) * scales[0][1]
    mixing_grad = ins.keep[HD : 2 * HD] + swap_lanes(got[HD : 2 * HD])
    inverse = (ins.inverse[0], ins.inverse[1])
    outs.share[0:HD] = split_dot_nt(halves(landmark_values), inverse).astype(jnp.bfloat16)
    values_low = split_dot(halves(mixing_grad), inverse).astype(jnp.bfloat16)
    outs.share[HD : 2 * HD] = values_low
    row_total = jnp.sum(values_low.astype(jnp.float32) * landmark_values, axis=0, keepdims=True)
    outs.share[2 * HD :] = jnp.concatenate(
        [thirds(row_total), jnp.zeros((13, M), jnp.float32)], axis=0
    ).astype(jnp.bfloat16)
    put(outs.share)
    outs.mixing_grad[...] = mixing_grad
    outs.mark_values[...] = landmark_values


def head_units(ins, slot, out_ref, lead, direct_ref, share):
    score_scale = HD ** (-0.5)
    mixing_low, values_low, row_total = share
    query_sums, key_sums = [], []
    scale = ins.scales[slot : slot + 1]

    def token_side(index):
        place = slice(index * CHUNK, (index + 1) * CHUNK)
        prob = ins.token_prob[place]
        attended = wide_dot_nt(prob.astype(jnp.bfloat16), mixing_low)
        store_chunk(out_ref, (0, *lead), index, attended.astype(jnp.bfloat16))
        token_grad = wide_dot(chunk_of(ins.vg, 1, slot, index), mixing_low)
        token_sgrad = (
            prob * (token_grad - jnp.sum(token_grad * prob, axis=1, keepdims=True))
        ).astype(jnp.bfloat16)
        direct_ref[0, place] = wide_dot(token_sgrad, ins.marks[slot, 1]) * score_scale
        key_sums.append(wide_dot(ins.turned[0, :, place], token_sgrad))

    def key_side(index):
        place = slice(index * CHUNK, (index + 1) * CHUNK)
        key_prob = ins.key_exp[place] * scale
        value_gradient = wide_dot_nt(key_prob.astype(jnp.bfloat16), values_low)
        store_chunk(out_ref, (1, *lead), index, value_gradient.astype(jnp.bfloat16))
        key_dgrad = wide_dot(chunk_of(ins.vg, 0, slot, index), values_low)
        key_sgrad = (key_prob * (key_dgrad - row_total)).astype(jnp.bfloat16)
        direct_ref[1, place] = wide_dot(key_sgrad, ins.marks[slot, 0]) * score_scale
        query_sums.append(wide_dot(ins.turned[1, :, place], key_sgrad))

    chunks = tokens_of(ins.vg) // CHUNK
    units = [
        functools.partial(unit, index) for unit in (key_side, token_side) for index in range(chunks)
    ]
    return units, query_sums, key_sums


def share_parts(ref, swap):
    parts = [ref[0:HD], ref[HD : 2 * HD], joined_thirds(ref[2 * HD :].astype(jnp.float32)[0:3])]
    return [swap_lanes(part) for part in parts] if swap else parts


def own_gradient_compute(ins, outs, need, put):
    for ref in (ins.mark_prob, ins.factor, ins.mixing_grad, ins.mark_values, ins.share, ins.scales):
        need(ref)
    mark_prob = ins.mark_prob[...]
    mark_halves = halves(mark_prob)
    factor = ins.factor[0:1, 0:1]
    inverse_grad = split_dot(halves(ins.mixing_grad[...].T), halves(ins.mark_values[...]))
    inverse_grad_halves = halves(inverse_grad)
    toward = split_dot(mark_halves, inverse_grad_halves) * factor
    power = 0.5 * (toward + toward.T)
    growth = None
    units, query_sums, key_sums = head_units(
        ins, 0, outs.out, (), outs.direct, share_parts(ins.share, False)
    )
    work = iter(units)

    def beside():
        next(work, lambda: None)()

    for sweep in range(PINV_ITERS):
        if sweep == 0:
            for ref in (ins.marks, ins.vg, ins.key_exp, ins.turned):
                need(ref)
        if sweep == 2:
            need(ins.token_prob)
        for ref in (ins.pair, ins.weight, ins.growth):
            need(ref, sweep)
        pair = (ins.pair[sweep, 0], ins.pair[sweep, 1])
        first = split_dot(pair, halves(power))
        beside()
        square = first[:M] + first[:M].T
        last = sweep == PINV_ITERS - 1
        second = split_dot(tuple(x[:M] for x in pair) if last else pair, halves(square))
        beside()
        cube = first[M:].T + second[:M]
        weight = halves(0.25 * (7.0 * square - 15.0 * power - cube))
        if not last:
            fourth = second[M:] + second[M:].T
            power = 0.25 * (13.0 * power - 15.0 * square + 7.0 * cube - fourth)
        left = [ins.growth[sweep, 0], ins.growth[sweep, 0], ins.growth[sweep, 1]]
        right = [weight[0], weight[1], weight[0]]
        if growth is not None:
            grown = halves(growth)
            left += [grown[0], grown[0], grown[1]]
            right += [ins.weight[sweep, 0], ins.weight[sweep, 1], ins.weight[sweep, 0]]
        growth = wide_dot(jnp.concatenate(left, axis=1), jnp.concatenate(right, axis=0))
    for unit in work:
        unit()
    put(outs.out)
    put(outs.direct)
    need()
    mark_grad = factor * (
        split_dot_nt((ins.last_growth[0], ins.last_growth[1]), inverse_grad_halves)
        + split_dot(halves(growth + growth.T), mark_halves)
    )
    mark_sgrad = mark_prob * (mark_grad - jnp.sum(mark_grad * mark_prob, axis=1, keepdims=True))

    def marks_dot(left, right):
        left_high, left_low = halves(left)
        return wide_dot(
            jnp.concatenate([left_high, left_low], axis=1), jnp.concatenate([right, right], axis=0)
        )

    outs.totals[0] = marks_dot(mark_sgrad, ins.marks[0, 1]) + sum(query_sums[1:], query_sums[0]).T
    outs.totals[1] = marks_dot(mark_sgrad.T, ins.marks[0, 0]) + sum(key_sums[1:], key_sums[0]).T


def other_gradient_compute(ins, outs, need, put):
    need()
    outs.out[:, :, 0] = ins.own_out[...]
    units, query_sums, key_sums = head_units(
        ins, 1, outs.out, (1,), outs.direct, share_parts(ins.got_share, True)
    )
    for unit in units:
        unit()
    put(outs.out)
    marks_scale = HD ** (-0.5) / (tokens_of(ins.vg) // HALF)
    for kind, sums in enumerate((query_sums, key_sums)):
        for slot, total in ((0, ins.totals[kind]), (1, sum(sums[1:], sums[0]).T)):
            total = total * marks_scale
            outs.near[kind, slot] = total[:HALF]
            outs.far[kind, slot] = total[HALF:].astype(jnp.bfloat16)


def finish_compute(ins, outs, need, put):
    need()
    out_ref = outs.out
    group = CHUNK // out_ref.shape[3]
    segment_len = tokens_of(out_ref) // HALF
    per = CHUNK // segment_len
    for index in range(tokens_of(out_ref) // CHUNK):
        place, start = slice(index * per, (index + 1) * per), index * CHUNK
        for slot, direct_ref in enumerate((ins.own_direct, ins.other_direct)):
            for kind in range(2):
                marks = ins.near[kind, slot, place] + ins.got_far[
                    kind, 1 - slot, place
                ].astype(jnp.float32)
                spread = jnp.broadcast_to(marks[:, None], (per, segment_len, HD))
                total = direct_ref[kind, start : start + CHUNK] + spread.reshape(CHUNK, HD)
                store_chunk(out_ref, (kind, slot), index, total.astype(jnp.bfloat16))
        put(out_ref, index * group)


def exchange(packed):
    return lax.all_to_all(packed, "cube", split_axis=0, concat_axis=0, tiled=True)


def partner(array):
    return lax.ppermute(array, "half", SWAP)


def body(queries, keys, values, out_grad):
    half = lax.axis_index("half").reshape(1)
    qk = exchange(pack(half, queries, keys))
    tokens = qk.shape[0] * qk.shape[3]
    mine = landmarks_of(qk)
    theirs = partner(mine)
    vg_packed, mine = lax.optimization_barrier((pack(half, values, out_grad), mine))
    vg = exchange(vg_packed)
    kept = staged_call(
        probability_compute,
        dict(qk=qk, mine=mine, theirs=theirs),
        dict(
            marks=low(2, 2, M, HD),
            token_prob=wide(2, tokens, M),
            token_low=low(2, tokens, M),
            key_exp=wide(2, tokens, M),
            key_low=low(2, tokens, M),
            turned=low(2, 2, HD, tokens),
            stats=wide(8, M),
            mark_prob=wide(M, M),
            factor=wide(8, HD),
            pair=(low(PINV_ITERS, 2, 2 * M, M), LEAD),
            weight=(low(PINV_ITERS, 2, M, M), LEAD),
            growth=(low(PINV_ITERS, 2, M, M), LEAD),
            inverse=low(2, M, M),
            last_growth=low(2, M, M),
        ),
        LONG,
        extra=(pltpu.VMEM((M, M), jnp.float32), pltpu.VMEM((2 * M, M), jnp.float32)),
    )
    sums = staged_call(
        partial_compute,
        dict(vg=vg, stats=kept.stats, key_low=kept.key_low, token_low=kept.token_low),
        dict(send=low(2 * HD + 16, M), keep=wide(2 * HD, M)),
        2,
    )
    mixed = staged_call(
        mixing_compute,
        dict(got=partner(sums.send), keep=sums.keep, stats=kept.stats, inverse=kept.inverse),
        dict(
            share=low(2 * HD + 16, M),
            scales=wide(8, M),
            mixing_grad=wide(HD, M),
            mark_values=wide(HD, M),
        ),
        1,
    )
    got_share = partner(mixed.share)
    own = staged_call(
        own_gradient_compute,
        dict(
            mark_prob=kept.mark_prob,
            factor=kept.factor,
            mixing_grad=mixed.mixing_grad,
            mark_values=mixed.mark_values,
            share=mixed.share,
            scales=mixed.scales,
            marks=kept.marks,
            vg=vg,
            key_exp=(kept.key_exp, SLOTS[0]),
            turned=(kept.turned, SLOTS[0]),
            pair=(kept.pair, LEAD),
            weight=(kept.weight, LEAD),
            growth=(kept.growth, LEAD),
            token_prob=(kept.token_prob, SLOTS[0]),
            last_growth=kept.last_growth,
        ),
        dict(
            out=low(qk.shape[0], 2, *qk.shape[3:]),
            direct=wide(2, tokens, HD),
            totals=wide(2, M, HD),
        ),
        14,
    )
    other = staged_call(
        other_gradient_compute,
        dict(
            got_share=got_share,
            scales=mixed.scales,
            marks=kept.marks,
            vg=vg,
            key_exp=(kept.key_exp, SLOTS[1]),
            turned=(kept.turned, SLOTS[1]),
            token_prob=(kept.token_prob, SLOTS[1]),
            own_out=own.out,
            totals=own.totals,
        ),
        dict(
            out=low(*qk.shape),
            far=low(2, 2, HALF, HD),
            near=wide(2, 2, HALF, HD),
            direct=wide(2, tokens, HD),
        ),
        3,
    )
    attended, value_gradient_array = unpack(half, exchange(other.out))
    results = staged_call(
        finish_compute,
        dict(
            got_far=partner(other.far),
            near=other.near,
            own_direct=own.direct,
            other_direct=other.direct,
        ),
        dict(out=(low(*qk.shape), GROUPS)),
        LONG,
    ).out
    query_grad, key_grad = unpack(half, exchange(results))
    return attended, query_grad, key_grad, value_gradient_array


def solution(mesh):
    whole_placement = P(("seq", "head"), None)
    halves_placement = P(("half", "cube"), None)

    def layer(queries, keys, values, out_grad):
        tokens, width = queries.shape
        own_head_each = width // HD == mesh.size and tokens == 8 * CHUNK
        if own_head_each:
            split = jax.sharding.Mesh(
                mesh.devices.reshape(2, mesh.size // 2), ("half", "cube")
            )
        return jax.shard_map(
            body if own_head_each else shared_body,
            mesh=split if own_head_each else mesh,
            in_specs=(halves_placement if own_head_each else whole_placement,) * 4,
            out_specs=(halves_placement if own_head_each else whole_placement,) * 4,
            check_vma=False,
        )(queries, keys, values, out_grad)

    return layer
```

```python
import functools
from types import SimpleNamespace

import jax
import jax.numpy as jnp
from jax import lax
from jax.experimental import pallas as pl
from jax.experimental.pallas import tpu as pltpu
from jax.sharding import PartitionSpec as P

HD = 128
M = 256
PINV_ITERS = 6
CHUNK = 256
PACK_GROUPS = 4
HALF = M // 2
SWAP = ((0, 1), (1, 0))
VMEM_LIMIT = 60 * 2**20
SMALL_LIMIT = 16 * 2**20
WHOLE, LEAD, GROUPS = range(3)
SLOTS = (10, 11)
LONG = 200


precise_setting = lax.Precision.HIGHEST


def newton_inverse(matrix):
    identity = jnp.eye(matrix.shape[0], dtype=matrix.dtype)
    factor = lax.stop_gradient(1.0 / jnp.max(jnp.sum(matrix, axis=0)))
    iterate = matrix.T * factor
    for sweep_index in range(PINV_ITERS):
        product = jnp.matmul(matrix, iterate, precision=precise_setting)
        inner_term = jnp.matmul(product, 7.0 * identity - product, precision=precise_setting)
        inner_term = jnp.matmul(product, 15.0 * identity - inner_term, precision=precise_setting)
        iterate = 0.25 * jnp.matmul(
            iterate, 13.0 * identity - inner_term, precision=precise_setting
        )
    return iterate


def share_heads(own_matrix, head_count):
    seq_index = lax.axis_index("seq")
    slot_mask = (jnp.arange(head_count, dtype=jnp.int32) == seq_index).astype(jnp.float32)
    return lax.psum(slot_mask[:, None, None] * own_matrix[None], "seq")


def shared_body(queries, keys, values, out_grad):
    query_rows, key_rows, value_rows, grad_rows = (
        lax.all_to_all(queries, "head", split_axis=1, concat_axis=0, tiled=True),
        lax.all_to_all(keys, "head", split_axis=1, concat_axis=0, tiled=True),
        lax.all_to_all(values, "head", split_axis=1, concat_axis=0, tiled=True),
        lax.all_to_all(out_grad, "head", split_axis=1, concat_axis=0, tiled=True),
    )
    tok_rows = query_rows.shape[0]
    head_count = query_rows.shape[1] // HD
    local_marks = M // lax.axis_size("seq")
    segment_len = tok_rows // local_marks
    score_scale = HD ** (-0.5)
    seq_index = lax.axis_index("seq")

    def landmark(matrix):
        summed = jnp.sum(
            matrix.reshape(local_marks, segment_len, matrix.shape[1]), axis=1, dtype=jnp.float32
        )
        return (summed / segment_len).astype(jnp.bfloat16)

    mark_queries, mark_keys = (
        lax.all_gather(landmark(query_rows), "seq", axis=0, tiled=True),
        lax.all_gather(landmark(key_rows), "seq", axis=0, tiled=True),
    )
    query_per_head = query_rows.reshape(tok_rows, head_count, HD)
    key_per_head = key_rows.reshape(tok_rows, head_count, HD)
    value_per_head = value_rows.reshape(tok_rows, head_count, HD)
    gradient_per_head = grad_rows.reshape(tok_rows, head_count, HD)
    landmark_query_heads = mark_queries.reshape(M, head_count, HD)
    landmark_key_heads = mark_keys.reshape(M, head_count, HD)
    key_score = (
        jnp.einsum(
            "pcv,gcv->cpg", landmark_query_heads, key_per_head, preferred_element_type=jnp.float32
        )
        * score_scale
    )
    key_max = lax.pmax(jnp.max(key_score, axis=-1), "seq")
    key_exp = jnp.exp(key_score - key_max[..., None])
    partial_num = jnp.einsum(
        "akq,qay->aky",
        key_exp.astype(jnp.bfloat16),
        value_per_head,
        preferred_element_type=jnp.float32,
    )
    key_total, numerator = lax.psum((jnp.sum(key_exp, axis=-1), partial_num), "seq")
    landmark_value_rows = numerator / key_total[..., None]
    token_prob = jax.nn.softmax(
        jnp.einsum(
            "jti,cti->tjc", query_per_head, landmark_key_heads, preferred_element_type=jnp.float32
        )
        * score_scale,
        axis=-1,
    )
    token_probability_lowered = token_prob.astype(jnp.bfloat16)
    mark_prob = jax.nn.softmax(
        jnp.einsum(
            "jou,iou->oji",
            landmark_query_heads,
            landmark_key_heads,
            preferred_element_type=jnp.float32,
        )
        * score_scale,
        axis=-1,
    )
    own_head = seq_index % head_count
    own_mark = lax.dynamic_index_in_dim(mark_prob, own_head, 0, keepdims=False)
    own_inverse, pull_back = jax.vjp(newton_inverse, own_mark)
    pseudo_inverse_matrix = share_heads(own_inverse, head_count)
    mixing_matrix = jnp.einsum(
        "jvy,jys->jvs", pseudo_inverse_matrix, landmark_value_rows, precision=precise_setting
    )
    mixing_matrix_lowered = mixing_matrix.astype(jnp.bfloat16)
    attended = jnp.einsum(
        "yvo,yor->vyr",
        token_probability_lowered,
        mixing_matrix_lowered,
        preferred_element_type=jnp.float32,
    ).astype(jnp.bfloat16)
    token_grad = jnp.einsum(
        "fag,aog->afo", gradient_per_head, mixing_matrix_lowered, preferred_element_type=jnp.float32
    )
    partial_mix = jnp.einsum(
        "klz,lkr->kzr",
        token_probability_lowered,
        gradient_per_head,
        preferred_element_type=jnp.float32,
    )
    mixing_matrix_gradient = lax.psum(partial_mix, "seq")
    token_score_gradient = (
        token_prob * (token_grad - jnp.sum(token_grad * token_prob, axis=-1, keepdims=True))
    ).astype(jnp.bfloat16)
    direct_qgrad = (
        jnp.einsum(
            "ufg,guc->fuc",
            token_score_gradient,
            landmark_key_heads,
            preferred_element_type=jnp.float32,
        )
        * score_scale
    )
    mark_kgrad_f = (
        jnp.einsum(
            "xgi,gxy->ixy", token_score_gradient, query_per_head, preferred_element_type=jnp.float32
        )
        * score_scale
    )
    pseudo_inverse_gradient = jnp.einsum(
        "ktu,kyu->kty", mixing_matrix_gradient, landmark_value_rows, precision=precise_setting
    )
    landmark_value_gradient = jnp.einsum(
        "lrb,lrz->lbz", pseudo_inverse_matrix, mixing_matrix_gradient, precision=precise_setting
    )
    own_igrad = lax.dynamic_index_in_dim(pseudo_inverse_gradient, own_head, 0, keepdims=False)
    (own_mgrad,) = pull_back(own_igrad)
    mark_grad = share_heads(own_mgrad, head_count)
    mark_sgrad = mark_prob * (mark_grad - jnp.sum(mark_grad * mark_prob, axis=-1, keepdims=True))
    first_mark = seq_index * local_marks
    score_gradient_rows = lax.dynamic_slice_in_dim(mark_sgrad, first_mark, local_marks, 1)
    score_gradient_columns = lax.dynamic_slice_in_dim(mark_sgrad, first_mark, local_marks, 2)
    own_qgrad_a = (
        jnp.einsum(
            "txs,ste->xte",
            score_gradient_rows,
            landmark_key_heads.astype(jnp.float32),
            precision=precise_setting,
        )
        * score_scale
    )
    own_kgrad_a = (
        jnp.einsum(
            "eaj,aev->jev",
            score_gradient_columns,
            landmark_query_heads.astype(jnp.float32),
            precision=precise_setting,
        )
        * score_scale
    )
    landmark_value_lowered = landmark_value_gradient.astype(jnp.bfloat16)
    key_prob = key_exp / key_total[..., None]
    key_probability_lowered = key_prob.astype(jnp.bfloat16)
    value_gradient_array = jnp.einsum(
        "zct,zcj->tzj",
        key_probability_lowered,
        landmark_value_lowered,
        preferred_element_type=jnp.float32,
    )
    key_direct_gradient = jnp.einsum(
        "exb,geb->exg", landmark_value_lowered, value_per_head, preferred_element_type=jnp.float32
    )
    row_total = lax.psum(jnp.sum(key_prob * key_direct_gradient, axis=-1), "seq")
    key_score_gradient = (key_prob * (key_direct_gradient - row_total[..., None])).astype(
        jnp.bfloat16
    )
    direct_kgrad = (
        jnp.einsum(
            "pbo,bpx->opx",
            key_score_gradient,
            landmark_query_heads,
            preferred_element_type=jnp.float32,
        )
        * score_scale
    )
    mark_qgrad_b = (
        jnp.einsum(
            "cbj,jcp->bcp", key_score_gradient, key_per_head, preferred_element_type=jnp.float32
        )
        * score_scale
    )
    own_kgrad_f, own_qgrad_b = (
        lax.psum_scatter(mark_kgrad_f, "seq", scatter_dimension=0, tiled=True),
        lax.psum_scatter(mark_qgrad_b, "seq", scatter_dimension=0, tiled=True),
    )
    mark_qtotal = (own_qgrad_a + own_qgrad_b) / segment_len
    mark_ktotal = (own_kgrad_a + own_kgrad_f) / segment_len
    query_grad = (
        direct_qgrad.reshape(local_marks, segment_len, head_count, HD) + mark_qtotal[:, None]
    )
    key_grad = direct_kgrad.reshape(local_marks, segment_len, head_count, HD) + mark_ktotal[:, None]
    width = head_count * HD
    results = (
        attended.reshape(tok_rows, width),
        query_grad.astype(jnp.bfloat16).reshape(tok_rows, width),
        key_grad.astype(jnp.bfloat16).reshape(tok_rows, width),
        value_gradient_array.astype(jnp.bfloat16).reshape(tok_rows, width),
    )
    attended_out, query_out, key_out, value_out = (
        lax.all_to_all(results[0], "head", split_axis=0, concat_axis=1, tiled=True),
        lax.all_to_all(results[1], "head", split_axis=0, concat_axis=1, tiled=True),
        lax.all_to_all(results[2], "head", split_axis=0, concat_axis=1, tiled=True),
        lax.all_to_all(results[3], "head", split_axis=0, concat_axis=1, tiled=True),
    )
    return (attended_out, query_out, key_out, value_out)


def halves(matrix):
    high = matrix.astype(jnp.bfloat16)
    return high, (matrix - high.astype(jnp.float32)).astype(jnp.bfloat16)


def wide_dot(left, right):
    return jnp.dot(left, right, preferred_element_type=jnp.float32)


def wide_dot_nt(left, right):
    return lax.dot_general(
        left, right, (((1,), (1,)), ((), ())), preferred_element_type=jnp.float32
    )


def split_dot(left, right):
    left_high, left_low = left
    right_high, right_low = right
    return wide_dot(
        jnp.concatenate([left_high, left_high, left_low], axis=1),
        jnp.concatenate([right_high, right_low, right_high], axis=0),
    )


def split_dot_nt(left, right):
    left_high, left_low = left
    right_high, right_low = right
    return wide_dot_nt(
        jnp.concatenate([left_high, left_high, left_low], axis=1),
        jnp.concatenate([right_high, right_low, right_high], axis=1),
    )


def identity_matrix():
    return (
        lax.broadcasted_iota(jnp.int32, (M, M), 0) == lax.broadcasted_iota(jnp.int32, (M, M), 1)
    ).astype(jnp.float32)


def chunk_of(ref, array, slot, index):
    per = CHUNK // ref.shape[3]
    return ref[index * per : (index + 1) * per, array, slot].reshape(CHUNK, HD)


def store_chunk(ref, lead, index, value):
    rows = ref.shape[-2]
    per = CHUNK // rows
    ref[(slice(index * per, (index + 1) * per), *lead)] = value.reshape(per, rows, HD)


def all_tokens(ref, array, slot):
    return ref[:, array, slot].reshape(ref.shape[0] * ref.shape[3], HD)


def tokens_of(ref):
    return ref.shape[0] * ref.shape[3]


def columns(index):
    return pl.ds(pl.multiple_of(index * CHUNK, CHUNK), CHUNK)


def swap_lanes(matrix):
    return jnp.concatenate([matrix[:, HALF:], matrix[:, :HALF]], axis=1)


def thirds(rows):
    first = rows.astype(jnp.bfloat16).astype(jnp.float32)
    second = (rows - first).astype(jnp.bfloat16).astype(jnp.float32)
    return jnp.concatenate([first, second, rows - first - second], axis=0)


def joined_thirds(rows):
    count = rows.shape[0] // 3
    return rows[:count] + (rows[count : 2 * count] + rows[2 * count :])


def held_shape(kind, shape):
    return shape[1:] if kind in SLOTS else shape


def pieces_of(kind, shape):
    if kind == LEAD:
        return [(index,) for index in range(shape[0])]
    if kind == GROUPS:
        per = CHUNK // shape[-2]
        return [(slice(place, place + per),) for place in range(0, shape[0], per)]
    return [()]


def window(ref, piece):
    place = tuple(
        pl.ds(part.start, part.stop - part.start) if isinstance(part, slice) else part
        for part in piece
    )
    return ref.at[place] if place else ref


class Staged:
    def __init__(self, names, kinds, outer, inner, done, outward):
        self.refs = SimpleNamespace(**dict(zip(names, inner)))
        self.copies, self.order = [], []
        count = 0
        steps = []
        for place, (kind, home, held) in enumerate(zip(kinds, outer, inner)):
            home = home.at[kind - SLOTS[0]] if kind in SLOTS else home
            copies = {}
            for step, piece in enumerate(pieces_of(kind, held.shape)):
                ends = (window(held, piece), window(home, piece))
                source, target = ends if outward else ends[::-1]
                key = tuple(
                    part.start if isinstance(part, slice) else part for part in piece
                )
                copies[key] = pltpu.make_async_copy(source, target, done.at[count])
                steps.append((step if kind != WHOLE else -1, place, key))
                count += 1
            self.copies.append(copies)
        self.inner = inner
        self.order = sorted(steps, key=lambda item: item[:2])
        self.started, self.waited = set(), set()

    def place_of(self, ref):
        return next(index for index, held in enumerate(self.inner) if held is ref)

    def start(self, ref=None, *key):
        chosen = [
            (place, name)
            for _, place, name in self.order
            if (ref is None or place == self.place_of(ref)) and (not key or name == key)
        ]
        for item in chosen:
            if item not in self.started:
                self.started.add(item)
                self.copies[item[0]][item[1]].start()

    def wait(self, ref=None, *key):
        chosen = [
            (place, name)
            for _, place, name in self.order
            if (ref is None or place == self.place_of(ref)) and (not key or name == key)
        ]
        for item in chosen:
            if item not in self.waited:
                self.waited.add(item)
                self.copies[item[0]][item[1]].wait()


def staged_call(compute, inputs, outputs, flops, extra=(), after=(), in_place=False):
    names_in, names_out = tuple(inputs), tuple(outputs)
    kinds_in = [x[1] if isinstance(x, tuple) else WHOLE for x in inputs.values()]
    kinds_out = [x[1] if isinstance(x, tuple) else WHOLE for x in outputs.values()]
    operands = tuple(x[0] if isinstance(x, tuple) else x for x in inputs.values())
    shapes = tuple(x[0] if isinstance(x, tuple) else x for x in outputs.values())
    n_in, n_out, n_after = len(operands), len(shapes), len(after)
    moved = sum(x.size * x.dtype.itemsize for x in (*operands, *shapes))
    anywhere = pl.BlockSpec(memory_space=pl.ANY)

    def count(kinds, arrays):
        return sum(len(pieces_of(kind, x.shape)) for kind, x in zip(kinds, arrays))

    def kernel(*refs):
        sources, refs = refs[:n_in], refs[n_in + n_after :]
        homes, refs = refs[:n_out], refs[n_out:]
        held_in, held_out = refs[:n_in], refs[n_in : n_in + n_out]
        *scratch, in_done, out_done = refs[n_in + n_out :]
        reads = Staged(names_in, kinds_in, sources, held_in, in_done, False)
        writes = Staged(names_out, kinds_out, homes, held_out, out_done, True)
        reads.start()
        compute(reads.refs, writes.refs, reads.wait, writes.start, *scratch)
        reads.wait()
        writes.start()
        writes.wait()

    results = pl.pallas_call(
        kernel,
        out_shape=shapes,
        in_specs=[anywhere] * (n_in + n_after),
        out_specs=(anywhere,) * n_out,
        scratch_shapes=[
            *(
                pltpu.VMEM(held_shape(kind, x.shape), x.dtype)
                for kind, x in zip((*kinds_in, *kinds_out), (*operands, *shapes))
            ),
            *extra,
            pltpu.SemaphoreType.DMA((count(kinds_in, operands),)),
            pltpu.SemaphoreType.DMA((count(kinds_out, shapes),)),
        ],
        compiler_params=pltpu.CompilerParams(vmem_limit_bytes=VMEM_LIMIT),
        cost_estimate=pl.CostEstimate(
            flops=int(flops * 10**9), bytes_accessed=moved, transcendentals=0
        ),
    )(*operands, *after)
    return SimpleNamespace(**dict(zip(outputs, results)))


def low(*shape):
    return jax.ShapeDtypeStruct(shape, jnp.bfloat16)


def wide(*shape):
    return jax.ShapeDtypeStruct(shape, jnp.float32)


def pack_kernel(half_ref, first_ref, second_ref, out_ref, rows_s, packed_s, in_done, out_done):
    half = half_ref[0]
    pairs = out_ref.shape[0]
    group = pairs // PACK_GROUPS
    span = 2 * HD
    reads, writes = [], []
    for index in range(PACK_GROUPS):
        for array, ref in enumerate((first_ref, second_ref)):
            place = pl.ds(index * group * span, group * span)
            reads.append(
                pltpu.make_async_copy(
                    ref.at[:, place], rows_s.at[array, :, place], in_done.at[array, index]
                )
            )
        place = pl.ds(index * group, group)
        writes.append(
            pltpu.make_async_copy(packed_s.at[place], out_ref.at[place], out_done.at[index])
        )
    for copy in reads:
        copy.start()
    for index in range(PACK_GROUPS):
        for array in range(2):
            reads[2 * index + array].wait()
            for pair in range(index * group, (index + 1) * group):
                start = pair * span
                packed_s[pair, array, half] = rows_s[array, :, start : start + HD]
                packed_s[pair, array, 1 - half] = rows_s[array, :, start + HD : start + span]
        writes[index].start()
    for copy in writes:
        copy.wait()


def unpack_kernel(half_ref, packed_ref, first_ref, second_ref, rows_s, out_done):
    half = half_ref[0]
    pairs = packed_ref.shape[0]
    group = pairs // PACK_GROUPS
    span = 2 * HD
    writes = []
    for index in range(PACK_GROUPS):
        for array, ref in enumerate((first_ref, second_ref)):
            for pair in range(index * group, (index + 1) * group):
                start = pair * span
                rows_s[array, :, start : start + HD] = packed_ref[pair, array, half]
                rows_s[array, :, start + HD : start + span] = packed_ref[pair, array, 1 - half]
            place = pl.ds(index * group * span, group * span)
            write = pltpu.make_async_copy(
                rows_s.at[array, :, place], ref.at[:, place], out_done.at[array, index]
            )
            write.start()
            writes.append(write)
    for copy in writes:
        copy.wait()


def layout_call(kernel, half, operands, out_shape, scratch, in_space, limit):
    anywhere = pl.BlockSpec(memory_space=pl.ANY)
    moved = 2 * sum(x.size * x.dtype.itemsize for x in operands)
    return pl.pallas_call(
        kernel,
        out_shape=out_shape,
        in_specs=[pl.BlockSpec(memory_space=pltpu.SMEM)]
        + [pl.BlockSpec(memory_space=in_space)] * len(operands),
        out_specs=jax.tree.map(lambda _: anywhere, out_shape),
        scratch_shapes=scratch,
        compiler_params=pltpu.CompilerParams(vmem_limit_bytes=limit),
        cost_estimate=pl.CostEstimate(flops=0, bytes_accessed=moved, transcendentals=0),
    )(half, *operands)


def pack(half, first, second):
    rows, width = first.shape
    shape = low(width // (2 * HD), 2, 2, rows, HD)
    scratch = [
        pltpu.VMEM((2, rows, width), jnp.bfloat16),
        pltpu.VMEM(shape.shape, jnp.bfloat16),
        pltpu.SemaphoreType.DMA((2, PACK_GROUPS)),
        pltpu.SemaphoreType.DMA((PACK_GROUPS,)),
    ]
    return layout_call(
        pack_kernel, half, (first, second), shape, scratch, pl.ANY, VMEM_LIMIT
    )


def unpack(half, packed):
    pairs, _, _, rows, _ = packed.shape
    shape = low(rows, pairs * 2 * HD)
    scratch = [
        pltpu.VMEM((2, *shape.shape), jnp.bfloat16),
        pltpu.SemaphoreType.DMA((2, PACK_GROUPS)),
    ]
    return layout_call(
        unpack_kernel, half, (packed,), (shape, shape), scratch, pltpu.VMEM, SMALL_LIMIT
    )


def landmark_kernel(qk_ref, marks_ref):
    tokens = tokens_of(qk_ref)
    segment_len = tokens // HALF
    per = CHUNK // segment_len
    member = (
        lax.broadcasted_iota(jnp.int32, (per, CHUNK), 1) // segment_len
        == lax.broadcasted_iota(jnp.int32, (per, CHUNK), 0)
    ).astype(jnp.bfloat16)
    kinds = [(slot, array) for slot in range(2) for array in range(2)]
    for index in range(tokens // CHUNK):
        parts = [chunk_of(qk_ref, array, slot, index) for slot, array in kinds]
        summed = wide_dot(member, jnp.concatenate(parts, axis=1))
        mean = (summed / segment_len).astype(jnp.bfloat16)
        for place, (slot, array) in enumerate(kinds):
            marks_ref[slot, array, index * per : (index + 1) * per] = mean[
                :, place * HD : (place + 1) * HD
            ]


def landmarks_of(qk):
    held = pl.BlockSpec(memory_space=pltpu.VMEM)
    return pl.pallas_call(
        landmark_kernel,
        out_shape=low(2, 2, HALF, HD),
        in_specs=[held],
        out_specs=held,
        compiler_params=pltpu.CompilerParams(vmem_limit_bytes=SMALL_LIMIT),
        cost_estimate=pl.CostEstimate(
            flops=2 * 10**8, bytes_accessed=qk.size * 2, transcendentals=0
        ),
    )(qk)


def sweep_forward(power_s, iterate_s, saved, sweep, work):
    pair_ref, weight_ref, growth_ref = saved
    power = power_s[...]
    power_high, power_low = halves(power)
    square = split_dot((power_high, power_low), (power_high, power_low))
    next(work)()
    square_halves = halves(square)
    pair = (
        jnp.concatenate([power_high, square_halves[0]], axis=0),
        jnp.concatenate([power_low, square_halves[1]], axis=0),
    )
    pair_ref[sweep, 0], pair_ref[sweep, 1] = pair
    higher = split_dot(pair, square_halves)
    next(work)()
    cube, fourth = higher[:M], higher[M:]
    weight = halves(0.25 * (13.0 * identity_matrix() - 15.0 * power + 7.0 * square - cube))
    power_s[...] = 0.25 * (13.0 * power - 15.0 * square + 7.0 * cube - fourth)
    weight_ref[sweep, 0], weight_ref[sweep, 1] = weight
    iterate = halves(iterate_s[...])
    growth_ref[sweep, 0], growth_ref[sweep, 1] = iterate[0][M:], iterate[1][M:]
    iterate_s[...] = split_dot(iterate, weight)


def probability_compute(ins, outs, need, put, power_s, iterate_s):
    need()
    qk_ref = ins.qk
    chunks = tokens_of(qk_ref) // CHUNK
    score_scale = HD ** (-0.5)
    for slot in range(2):
        for array in range(2):
            outs.marks[slot, array] = jnp.concatenate(
                [ins.mine[slot, array], ins.theirs[1 - slot, array]], axis=0
            )
    put(outs.marks)
    landmark_q, landmark_k = outs.marks[0, 0], outs.marks[0, 1]
    mark_score = wide_dot_nt(landmark_q, landmark_k) * score_scale
    mark_exp = jnp.exp(mark_score - jnp.max(mark_score, axis=1, keepdims=True))
    mark_prob = mark_exp / jnp.sum(mark_exp, axis=1, keepdims=True)
    outs.mark_prob[...] = mark_prob
    factor = 1.0 / jnp.max(jnp.sum(mark_prob, axis=0, keepdims=True), axis=1, keepdims=True)
    outs.factor[...] = jnp.broadcast_to(factor, outs.factor.shape)
    mark_halves = halves(mark_prob)
    power_s[...] = split_dot_nt(mark_halves, mark_halves) * factor
    iterate_s[0:M] = mark_prob.T * factor
    iterate_s[M:] = identity_matrix()
    tops, totals = [[], []], [[], []]

    def scores(slot, index):
        query_chunk, key_chunk = (chunk_of(qk_ref, array, slot, index) for array in range(2))
        place = slice(index * CHUNK, (index + 1) * CHUNK)
        outs.turned[slot, 0, :, place] = query_chunk.T
        outs.turned[slot, 1, :, place] = key_chunk.T
        score = wide_dot_nt(query_chunk, outs.marks[slot, 1]) * score_scale
        grown = jnp.exp(score - jnp.max(score, axis=1, keepdims=True))
        prob = grown * (1.0 / jnp.sum(grown, axis=1, keepdims=True))
        outs.token_prob[slot, place] = prob
        outs.token_low[slot, place] = prob.astype(jnp.bfloat16)
        key_score = wide_dot_nt(key_chunk, outs.marks[slot, 0]) * score_scale
        outs.key_exp[slot, place] = key_score
        tops[slot].append(jnp.max(key_score, axis=0, keepdims=True))

    def grow(slot, index):
        if index == 0:
            tops[slot] = functools.reduce(jnp.maximum, tops[slot])
        place = slice(index * CHUNK, (index + 1) * CHUNK)
        grown = jnp.exp(outs.key_exp[slot, place] - tops[slot])
        outs.key_exp[slot, place] = grown
        outs.key_low[slot, place] = grown.astype(jnp.bfloat16)
        totals[slot].append(jnp.sum(grown, axis=0, keepdims=True))

    def several(unit, pairs):
        for slot, index in pairs:
            unit(slot, index)

    pairs = [(slot, index) for slot in range(2) for index in range(chunks)]
    work = iter(
        [functools.partial(several, scores, [pair]) for pair in pairs]
        + [
            functools.partial(several, grow, pairs[first : first + 2])
            for first in range(0, len(pairs), 2)
        ]
    )
    saved = (outs.pair, outs.weight, outs.growth)
    for sweep in range(PINV_ITERS):
        sweep_forward(power_s, iterate_s, saved, sweep, work)
        for ref in saved:
            put(ref, sweep)
        if sweep == 3:
            for ref in (outs.token_low, outs.token_prob, outs.turned):
                put(ref)
    put(outs.key_low)
    put(outs.key_exp)
    outs.inverse[0], outs.inverse[1] = halves(iterate_s[0:M])
    outs.last_growth[0], outs.last_growth[1] = halves(iterate_s[M:])
    stats = [x for slot in range(2) for x in (tops[slot], sum(totals[slot][1:], totals[slot][0]))]
    outs.stats[0:4] = jnp.concatenate(stats, axis=0)
    outs.stats[4:8] = jnp.zeros((4, M), jnp.float32)


def partial_compute(ins, outs, need, put):
    need(ins.vg)
    turned = [[all_tokens(ins.vg, array, slot).T for array in range(2)] for slot in range(2)]
    need()
    rows = thirds(ins.stats[0:4])
    outs.send[2 * HD :] = jnp.concatenate([rows, jnp.zeros((4, M), jnp.float32)], axis=0).astype(
        jnp.bfloat16
    )
    for slot, home in ((1, outs.send), (0, outs.keep)):
        home[0:HD] = wide_dot(turned[slot][0], ins.key_low[slot]).astype(home.dtype)
        home[HD : 2 * HD] = wide_dot(turned[slot][1], ins.token_low[slot]).astype(home.dtype)
        put(home)


def mixing_compute(ins, outs, need, put):
    need()
    got = ins.got[...].astype(jnp.float32)
    others = swap_lanes(joined_thirds(got[2 * HD : 2 * HD + 12]))
    scales = []
    for slot in range(2):
        own_max, own_total = ins.stats[2 * slot : 2 * slot + 1], ins.stats[2 * slot + 1 : 2 * slot + 2]
        other = 1 - slot
        other_max, other_total = others[2 * other : 2 * other + 1], others[2 * other + 1 : 2 * other + 2]
        key_max = jnp.maximum(own_max, other_max)
        own_factor, other_factor = jnp.exp(own_max - key_max), jnp.exp(other_max - key_max)
        inverse_total = 1.0 / (own_total * own_factor + other_total * other_factor)
        scales.append((own_factor * inverse_total, other_factor * inverse_total))
    outs.scales[...] = jnp.concatenate(
        [scales[0][0], scales[1][0], jnp.zeros((6, M), jnp.float32)], axis=0
    )
    landmark_values = ins.keep[0:HD] * scales[0][0] + swap_lanes(got[0:HD]) * scales[0][1]
    mixing_grad = ins.keep[HD : 2 * HD] + swap_lanes(got[HD : 2 * HD])
    inverse = (ins.inverse[0], ins.inverse[1])
    outs.share[0:HD] = split_dot_nt(halves(landmark_values), inverse).astype(jnp.bfloat16)
    values_low = split_dot(halves(mixing_grad), inverse).astype(jnp.bfloat16)
    outs.share[HD : 2 * HD] = values_low
    row_total = jnp.sum(values_low.astype(jnp.float32) * landmark_values, axis=0, keepdims=True)
    outs.share[2 * HD :] = jnp.concatenate(
        [thirds(row_total), jnp.zeros((13, M), jnp.float32)], axis=0
    ).astype(jnp.bfloat16)
    put(outs.share)
    outs.mixing_grad[...] = mixing_grad
    outs.mark_values[...] = landmark_values


def several(*units):
    for unit in units:
        unit()


def out_units(ins, slot, out_ref, lead, share):
    mixing_low, values_low, _ = share
    scale = ins.scales[slot : slot + 1]

    def token_side(index):
        place = slice(index * CHUNK, (index + 1) * CHUNK)
        attended = wide_dot_nt(ins.token_low[place], mixing_low)
        store_chunk(out_ref, (0, *lead), index, attended.astype(jnp.bfloat16))

    def key_side(index):
        place = slice(index * CHUNK, (index + 1) * CHUNK)
        key_plow = (ins.key_exp[place] * scale).astype(jnp.bfloat16)
        value_gradient = wide_dot_nt(key_plow, values_low)
        store_chunk(out_ref, (1, *lead), index, value_gradient.astype(jnp.bfloat16))

    chunks = ins.token_low.shape[0] // CHUNK
    return [
        functools.partial(unit, index) for unit in (token_side, key_side) for index in range(chunks)
    ]


def gradient_units(ins, slot, direct_ref, share):
    score_scale = HD ** (-0.5)
    mixing_low, values_low, row_total = share
    query_sums, key_sums = [], []
    scale = ins.scales[slot : slot + 1]

    def token_side(index):
        place = slice(index * CHUNK, (index + 1) * CHUNK)
        prob = ins.token_prob[slot, place]
        token_grad = wide_dot(chunk_of(ins.vg, 1, slot, index), mixing_low)
        token_sgrad = (
            prob * (token_grad - jnp.sum(token_grad * prob, axis=1, keepdims=True))
        ).astype(jnp.bfloat16)
        direct_ref[slot, 0, place] = wide_dot(token_sgrad, ins.marks[slot, 1]) * score_scale
        key_sums.append(wide_dot(ins.turned[slot, 0, :, place], token_sgrad))

    def key_side(index):
        place = slice(index * CHUNK, (index + 1) * CHUNK)
        key_prob = ins.key_exp[slot, place] * scale
        key_dgrad = wide_dot(chunk_of(ins.vg, 0, slot, index), values_low)
        key_sgrad = (key_prob * (key_dgrad - row_total)).astype(jnp.bfloat16)
        direct_ref[slot, 1, place] = wide_dot(key_sgrad, ins.marks[slot, 0]) * score_scale
        query_sums.append(wide_dot(ins.turned[slot, 1, :, place], key_sgrad))

    chunks = tokens_of(ins.vg) // CHUNK
    units = [
        functools.partial(unit, index) for index in range(chunks) for unit in (key_side, token_side)
    ]
    return units, query_sums, key_sums


def share_parts(ref, swap):
    parts = [ref[0:HD], ref[HD : 2 * HD], joined_thirds(ref[2 * HD :].astype(jnp.float32)[0:3])]
    return [swap_lanes(part) for part in parts] if swap else parts


def own_gradient_compute(ins, outs, need, put):
    for ref in (ins.mark_prob, ins.factor, ins.mixing_grad, ins.mark_values, ins.share, ins.scales):
        need(ref)
    mark_prob = ins.mark_prob[...]
    mark_halves = halves(mark_prob)
    factor = ins.factor[0:1, 0:1]
    inverse_grad = split_dot(halves(ins.mixing_grad[...].T), halves(ins.mark_values[...]))
    inverse_grad_halves = halves(inverse_grad)
    toward = split_dot(mark_halves, inverse_grad_halves) * factor
    power = 0.5 * (toward + toward.T)
    growth = None
    work = iter(out_units(ins, 0, outs.out, (), share_parts(ins.share, False)))

    def beside():
        next(work, lambda: None)()

    for sweep in range(PINV_ITERS):
        if sweep == 0:
            need(ins.token_low)
        if sweep == 2:
            need(ins.key_exp)
        for ref in (ins.pair, ins.weight, ins.growth):
            need(ref, sweep)
        pair = (ins.pair[sweep, 0], ins.pair[sweep, 1])
        first = split_dot(pair, halves(power))
        beside()
        square = first[:M] + first[:M].T
        last = sweep == PINV_ITERS - 1
        second = split_dot(tuple(x[:M] for x in pair) if last else pair, halves(square))
        beside()
        cube = first[M:].T + second[:M]
        weight = halves(0.25 * (7.0 * square - 15.0 * power - cube))
        if not last:
            fourth = second[M:] + second[M:].T
            power = 0.25 * (13.0 * power - 15.0 * square + 7.0 * cube - fourth)
        left = [ins.growth[sweep, 0], ins.growth[sweep, 0], ins.growth[sweep, 1]]
        right = [weight[0], weight[1], weight[0]]
        if growth is not None:
            grown = halves(growth)
            left += [grown[0], grown[0], grown[1]]
            right += [ins.weight[sweep, 0], ins.weight[sweep, 1], ins.weight[sweep, 0]]
        growth = wide_dot(jnp.concatenate(left, axis=1), jnp.concatenate(right, axis=0))
    for unit in work:
        unit()
    put(outs.out)
    need()
    mark_grad = factor * (
        split_dot_nt((ins.last_growth[0], ins.last_growth[1]), inverse_grad_halves)
        + split_dot(halves(growth + growth.T), mark_halves)
    )
    mark_sgrad = mark_prob * (mark_grad - jnp.sum(mark_grad * mark_prob, axis=1, keepdims=True))

    def marks_dot(left, right):
        left_high, left_low = halves(left)
        return wide_dot(
            jnp.concatenate([left_high, left_low], axis=1), jnp.concatenate([right, right], axis=0)
        )

    outs.mark_grads[0] = marks_dot(mark_sgrad, ins.marks[0, 1])
    outs.mark_grads[1] = marks_dot(mark_sgrad.T, ins.marks[0, 0])


def other_out_compute(ins, outs, need, put):
    need(ins.got_share)
    need(ins.scales)
    need(ins.token_low)
    units = out_units(ins, 1, outs.out, (1,), share_parts(ins.got_share, True))
    chunks = len(units) // 2
    several(*units[:chunks])
    need()
    several(*units[chunks:])
    outs.out[:, :, 0] = ins.own_out[...]


def gradient_compute(ins, outs, need, put):
    for ref in (ins.share, ins.got_share, ins.scales, ins.marks, ins.vg, ins.mark_grads):
        need(ref)
    marks_scale = HD ** (-0.5) / (tokens_of(ins.vg) // HALF)
    for slot in range(2):
        for ref in (ins.key_exp, ins.token_prob, ins.turned):
            need(ref, slot)
        share = share_parts(ins.got_share if slot else ins.share, bool(slot))
        units, query_sums, key_sums = gradient_units(ins, slot, outs.direct, share)
        several(*units)
        put(outs.direct, slot)
        for kind, sums in enumerate((query_sums, key_sums)):
            total = sum(sums[1:], sums[0]).T
            if slot == 0:
                total = total + ins.mark_grads[kind]
            total = total * marks_scale
            outs.near[kind, slot] = total[:HALF]
            outs.far[kind, slot] = total[HALF:].astype(jnp.bfloat16)


def finish_compute(ins, outs, need, put):
    need()
    out_ref = outs.out
    group = CHUNK // out_ref.shape[3]
    segment_len = tokens_of(out_ref) // HALF
    per = CHUNK // segment_len
    for index in range(tokens_of(out_ref) // CHUNK):
        place, start = slice(index * per, (index + 1) * per), index * CHUNK
        for slot in range(2):
            for kind in range(2):
                marks = ins.near[kind, slot, place] + ins.got_far[
                    kind, 1 - slot, place
                ].astype(jnp.float32)
                spread = jnp.broadcast_to(marks[:, None], (per, segment_len, HD))
                total = ins.direct[slot, kind, start : start + CHUNK] + spread.reshape(CHUNK, HD)
                store_chunk(out_ref, (kind, slot), index, total.astype(jnp.bfloat16))
        put(out_ref, index * group)


def exchange(packed):
    return lax.all_to_all(packed, "cube", split_axis=0, concat_axis=0, tiled=True)


def partner(array):
    return lax.ppermute(array, "half", SWAP)


def body(queries, keys, values, out_grad):
    half = lax.axis_index("half").reshape(1)
    qk, vg_packed = lax.optimization_barrier(
        (exchange(pack(half, queries, keys)), pack(half, values, out_grad))
    )
    tokens = qk.shape[0] * qk.shape[3]
    mine = landmarks_of(qk)
    theirs = partner(mine)
    vg_packed, mine = lax.optimization_barrier((vg_packed, mine))
    vg = exchange(vg_packed)
    kept = staged_call(
        probability_compute,
        dict(qk=qk, mine=mine, theirs=theirs),
        dict(
            marks=low(2, 2, M, HD),
            token_prob=wide(2, tokens, M),
            token_low=low(2, tokens, M),
            key_exp=wide(2, tokens, M),
            key_low=low(2, tokens, M),
            turned=low(2, 2, HD, tokens),
            stats=wide(8, M),
            mark_prob=wide(M, M),
            factor=wide(8, HD),
            pair=(low(PINV_ITERS, 2, 2 * M, M), LEAD),
            weight=(low(PINV_ITERS, 2, M, M), LEAD),
            growth=(low(PINV_ITERS, 2, M, M), LEAD),
            inverse=low(2, M, M),
            last_growth=low(2, M, M),
        ),
        LONG,
        extra=(pltpu.VMEM((M, M), jnp.float32), pltpu.VMEM((2 * M, M), jnp.float32)),
    )
    sums = staged_call(
        partial_compute,
        dict(vg=vg, stats=kept.stats, key_low=kept.key_low, token_low=kept.token_low),
        dict(send=low(2 * HD + 16, M), keep=wide(2 * HD, M)),
        2,
    )
    mixed = staged_call(
        mixing_compute,
        dict(got=partner(sums.send), keep=sums.keep, stats=kept.stats, inverse=kept.inverse),
        dict(
            share=low(2 * HD + 16, M),
            scales=wide(8, M),
            mixing_grad=wide(HD, M),
            mark_values=wide(HD, M),
        ),
        1,
    )
    got_share = partner(mixed.share)
    own = staged_call(
        own_gradient_compute,
        dict(
            mark_prob=kept.mark_prob,
            factor=kept.factor,
            mixing_grad=mixed.mixing_grad,
            mark_values=mixed.mark_values,
            share=mixed.share,
            scales=mixed.scales,
            token_low=(kept.token_low, SLOTS[0]),
            pair=(kept.pair, LEAD),
            weight=(kept.weight, LEAD),
            growth=(kept.growth, LEAD),
            key_exp=(kept.key_exp, SLOTS[0]),
            last_growth=kept.last_growth,
            marks=kept.marks,
        ),
        dict(out=low(qk.shape[0], 2, *qk.shape[3:]), mark_grads=wide(2, M, HD)),
        14,
    )
    first_results = staged_call(
        other_out_compute,
        dict(
            got_share=got_share,
            scales=mixed.scales,
            token_low=(kept.token_low, SLOTS[1]),
            key_exp=(kept.key_exp, SLOTS[1]),
            own_out=own.out,
        ),
        dict(out=low(*qk.shape)),
        1,
    ).out
    attended, value_gradient_array = unpack(half, exchange(first_results))
    grads = staged_call(
        gradient_compute,
        dict(
            share=mixed.share,
            got_share=got_share,
            scales=mixed.scales,
            marks=kept.marks,
            vg=vg,
            key_exp=(kept.key_exp, LEAD),
            token_prob=(kept.token_prob, LEAD),
            turned=(kept.turned, LEAD),
            mark_grads=own.mark_grads,
        ),
        dict(
            far=low(2, 2, HALF, HD),
            near=wide(2, 2, HALF, HD),
            direct=(wide(2, 2, tokens, HD), LEAD),
        ),
        LONG,
        after=(first_results,),
    )
    results = staged_call(
        finish_compute,
        dict(got_far=partner(grads.far), near=grads.near, direct=grads.direct),
        dict(out=(low(*qk.shape), GROUPS)),
        LONG,
    ).out
    query_grad, key_grad = unpack(half, exchange(results))
    return attended, query_grad, key_grad, value_gradient_array


def solution(mesh):
    whole_placement = P(("seq", "head"), None)
    halves_placement = P(("half", "cube"), None)

    def layer(queries, keys, values, out_grad):
        tokens, width = queries.shape
        own_head_each = width // HD == mesh.size and tokens == 8 * CHUNK
        if own_head_each:
            split = jax.sharding.Mesh(
                mesh.devices.reshape(2, mesh.size // 2), ("half", "cube")
            )
        return jax.shard_map(
            body if own_head_each else shared_body,
            mesh=split if own_head_each else mesh,
            in_specs=(halves_placement if own_head_each else whole_placement,) * 4,
            out_specs=(halves_placement if own_head_each else whole_placement,) * 4,
            check_vma=False,
        )(queries, keys, values, out_grad)

    return layer
```

```python
import functools
from types import SimpleNamespace

import jax
import jax.numpy as jnp
from jax import lax
from jax.experimental import pallas as pl
from jax.experimental.pallas import tpu as pltpu
from jax.sharding import PartitionSpec as P

HD = 128
M = 256
PINV_ITERS = 6
CHUNK = 256
PACK_GROUPS = 4
HALF = M // 2
SWAP = ((0, 1), (1, 0))
VMEM_LIMIT = 60 * 2**20
SMALL_LIMIT = 16 * 2**20
WHOLE, LEAD, GROUPS = range(3)
SLOTS = (10, 11)
LONG = 200


precise_setting = lax.Precision.HIGHEST


def newton_inverse(matrix):
    identity = jnp.eye(matrix.shape[0], dtype=matrix.dtype)
    factor = lax.stop_gradient(1.0 / jnp.max(jnp.sum(matrix, axis=0)))
    iterate = matrix.T * factor
    for sweep_index in range(PINV_ITERS):
        product = jnp.matmul(matrix, iterate, precision=precise_setting)
        inner_term = jnp.matmul(product, 7.0 * identity - product, precision=precise_setting)
        inner_term = jnp.matmul(product, 15.0 * identity - inner_term, precision=precise_setting)
        iterate = 0.25 * jnp.matmul(
            iterate, 13.0 * identity - inner_term, precision=precise_setting
        )
    return iterate


def share_heads(own_matrix, head_count):
    seq_index = lax.axis_index("seq")
    slot_mask = (jnp.arange(head_count, dtype=jnp.int32) == seq_index).astype(jnp.float32)
    return lax.psum(slot_mask[:, None, None] * own_matrix[None], "seq")


def shared_body(queries, keys, values, out_grad):
    query_rows, key_rows, value_rows, grad_rows = (
        lax.all_to_all(queries, "head", split_axis=1, concat_axis=0, tiled=True),
        lax.all_to_all(keys, "head", split_axis=1, concat_axis=0, tiled=True),
        lax.all_to_all(values, "head", split_axis=1, concat_axis=0, tiled=True),
        lax.all_to_all(out_grad, "head", split_axis=1, concat_axis=0, tiled=True),
    )
    tok_rows = query_rows.shape[0]
    head_count = query_rows.shape[1] // HD
    local_marks = M // lax.axis_size("seq")
    segment_len = tok_rows // local_marks
    score_scale = HD ** (-0.5)
    seq_index = lax.axis_index("seq")

    def landmark(matrix):
        summed = jnp.sum(
            matrix.reshape(local_marks, segment_len, matrix.shape[1]), axis=1, dtype=jnp.float32
        )
        return (summed / segment_len).astype(jnp.bfloat16)

    mark_queries, mark_keys = (
        lax.all_gather(landmark(query_rows), "seq", axis=0, tiled=True),
        lax.all_gather(landmark(key_rows), "seq", axis=0, tiled=True),
    )
    query_per_head = query_rows.reshape(tok_rows, head_count, HD)
    key_per_head = key_rows.reshape(tok_rows, head_count, HD)
    value_per_head = value_rows.reshape(tok_rows, head_count, HD)
    gradient_per_head = grad_rows.reshape(tok_rows, head_count, HD)
    landmark_query_heads = mark_queries.reshape(M, head_count, HD)
    landmark_key_heads = mark_keys.reshape(M, head_count, HD)
    key_score = (
        jnp.einsum(
            "pcv,gcv->cpg", landmark_query_heads, key_per_head, preferred_element_type=jnp.float32
        )
        * score_scale
    )
    key_max = lax.pmax(jnp.max(key_score, axis=-1), "seq")
    key_exp = jnp.exp(key_score - key_max[..., None])
    partial_num = jnp.einsum(
        "akq,qay->aky",
        key_exp.astype(jnp.bfloat16),
        value_per_head,
        preferred_element_type=jnp.float32,
    )
    key_total, numerator = lax.psum((jnp.sum(key_exp, axis=-1), partial_num), "seq")
    landmark_value_rows = numerator / key_total[..., None]
    token_prob = jax.nn.softmax(
        jnp.einsum(
            "jti,cti->tjc", query_per_head, landmark_key_heads, preferred_element_type=jnp.float32
        )
        * score_scale,
        axis=-1,
    )
    token_probability_lowered = token_prob.astype(jnp.bfloat16)
    mark_prob = jax.nn.softmax(
        jnp.einsum(
            "jou,iou->oji",
            landmark_query_heads,
            landmark_key_heads,
            preferred_element_type=jnp.float32,
        )
        * score_scale,
        axis=-1,
    )
    own_head = seq_index % head_count
    own_mark = lax.dynamic_index_in_dim(mark_prob, own_head, 0, keepdims=False)
    own_inverse, pull_back = jax.vjp(newton_inverse, own_mark)
    pseudo_inverse_matrix = share_heads(own_inverse, head_count)
    mixing_matrix = jnp.einsum(
        "jvy,jys->jvs", pseudo_inverse_matrix, landmark_value_rows, precision=precise_setting
    )
    mixing_matrix_lowered = mixing_matrix.astype(jnp.bfloat16)
    attended = jnp.einsum(
        "yvo,yor->vyr",
        token_probability_lowered,
        mixing_matrix_lowered,
        preferred_element_type=jnp.float32,
    ).astype(jnp.bfloat16)
    token_grad = jnp.einsum(
        "fag,aog->afo", gradient_per_head, mixing_matrix_lowered, preferred_element_type=jnp.float32
    )
    partial_mix = jnp.einsum(
        "klz,lkr->kzr",
        token_probability_lowered,
        gradient_per_head,
        preferred_element_type=jnp.float32,
    )
    mixing_matrix_gradient = lax.psum(partial_mix, "seq")
    token_score_gradient = (
        token_prob * (token_grad - jnp.sum(token_grad * token_prob, axis=-1, keepdims=True))
    ).astype(jnp.bfloat16)
    direct_qgrad = (
        jnp.einsum(
            "ufg,guc->fuc",
            token_score_gradient,
            landmark_key_heads,
            preferred_element_type=jnp.float32,
        )
        * score_scale
    )
    mark_kgrad_f = (
        jnp.einsum(
            "xgi,gxy->ixy", token_score_gradient, query_per_head, preferred_element_type=jnp.float32
        )
        * score_scale
    )
    pseudo_inverse_gradient = jnp.einsum(
        "ktu,kyu->kty", mixing_matrix_gradient, landmark_value_rows, precision=precise_setting
    )
    landmark_value_gradient = jnp.einsum(
        "lrb,lrz->lbz", pseudo_inverse_matrix, mixing_matrix_gradient, precision=precise_setting
    )
    own_igrad = lax.dynamic_index_in_dim(pseudo_inverse_gradient, own_head, 0, keepdims=False)
    (own_mgrad,) = pull_back(own_igrad)
    mark_grad = share_heads(own_mgrad, head_count)
    mark_sgrad = mark_prob * (mark_grad - jnp.sum(mark_grad * mark_prob, axis=-1, keepdims=True))
    first_mark = seq_index * local_marks
    score_gradient_rows = lax.dynamic_slice_in_dim(mark_sgrad, first_mark, local_marks, 1)
    score_gradient_columns = lax.dynamic_slice_in_dim(mark_sgrad, first_mark, local_marks, 2)
    own_qgrad_a = (
        jnp.einsum(
            "txs,ste->xte",
            score_gradient_rows,
            landmark_key_heads.astype(jnp.float32),
            precision=precise_setting,
        )
        * score_scale
    )
    own_kgrad_a = (
        jnp.einsum(
            "eaj,aev->jev",
            score_gradient_columns,
            landmark_query_heads.astype(jnp.float32),
            precision=precise_setting,
        )
        * score_scale
    )
    landmark_value_lowered = landmark_value_gradient.astype(jnp.bfloat16)
    key_prob = key_exp / key_total[..., None]
    key_probability_lowered = key_prob.astype(jnp.bfloat16)
    value_gradient_array = jnp.einsum(
        "zct,zcj->tzj",
        key_probability_lowered,
        landmark_value_lowered,
        preferred_element_type=jnp.float32,
    )
    key_direct_gradient = jnp.einsum(
        "exb,geb->exg", landmark_value_lowered, value_per_head, preferred_element_type=jnp.float32
    )
    row_total = lax.psum(jnp.sum(key_prob * key_direct_gradient, axis=-1), "seq")
    key_score_gradient = (key_prob * (key_direct_gradient - row_total[..., None])).astype(
        jnp.bfloat16
    )
    direct_kgrad = (
        jnp.einsum(
            "pbo,bpx->opx",
            key_score_gradient,
            landmark_query_heads,
            preferred_element_type=jnp.float32,
        )
        * score_scale
    )
    mark_qgrad_b = (
        jnp.einsum(
            "cbj,jcp->bcp", key_score_gradient, key_per_head, preferred_element_type=jnp.float32
        )
        * score_scale
    )
    own_kgrad_f, own_qgrad_b = (
        lax.psum_scatter(mark_kgrad_f, "seq", scatter_dimension=0, tiled=True),
        lax.psum_scatter(mark_qgrad_b, "seq", scatter_dimension=0, tiled=True),
    )
    mark_qtotal = (own_qgrad_a + own_qgrad_b) / segment_len
    mark_ktotal = (own_kgrad_a + own_kgrad_f) / segment_len
    query_grad = (
        direct_qgrad.reshape(local_marks, segment_len, head_count, HD) + mark_qtotal[:, None]
    )
    key_grad = direct_kgrad.reshape(local_marks, segment_len, head_count, HD) + mark_ktotal[:, None]
    width = head_count * HD
    results = (
        attended.reshape(tok_rows, width),
        query_grad.astype(jnp.bfloat16).reshape(tok_rows, width),
        key_grad.astype(jnp.bfloat16).reshape(tok_rows, width),
        value_gradient_array.astype(jnp.bfloat16).reshape(tok_rows, width),
    )
    attended_out, query_out, key_out, value_out = (
        lax.all_to_all(results[0], "head", split_axis=0, concat_axis=1, tiled=True),
        lax.all_to_all(results[1], "head", split_axis=0, concat_axis=1, tiled=True),
        lax.all_to_all(results[2], "head", split_axis=0, concat_axis=1, tiled=True),
        lax.all_to_all(results[3], "head", split_axis=0, concat_axis=1, tiled=True),
    )
    return (attended_out, query_out, key_out, value_out)


def halves(matrix):
    high = matrix.astype(jnp.bfloat16)
    return high, (matrix - high.astype(jnp.float32)).astype(jnp.bfloat16)


def wide_dot(left, right):
    return jnp.dot(left, right, preferred_element_type=jnp.float32)


def wide_dot_nt(left, right):
    return lax.dot_general(
        left, right, (((1,), (1,)), ((), ())), preferred_element_type=jnp.float32
    )


def split_dot(left, right):
    left_high, left_low = left
    right_high, right_low = right
    return wide_dot(
        jnp.concatenate([left_high, left_high, left_low], axis=1),
        jnp.concatenate([right_high, right_low, right_high], axis=0),
    )


def split_dot_nt(left, right):
    left_high, left_low = left
    right_high, right_low = right
    return wide_dot_nt(
        jnp.concatenate([left_high, left_high, left_low], axis=1),
        jnp.concatenate([right_high, right_low, right_high], axis=1),
    )


def identity_matrix():
    return (
        lax.broadcasted_iota(jnp.int32, (M, M), 0) == lax.broadcasted_iota(jnp.int32, (M, M), 1)
    ).astype(jnp.float32)


def chunk_of(ref, array, slot, index):
    per = CHUNK // ref.shape[3]
    return ref[index * per : (index + 1) * per, array, slot].reshape(CHUNK, HD)


def store_chunk(ref, lead, index, value):
    rows = ref.shape[-2]
    per = CHUNK // rows
    ref[(slice(index * per, (index + 1) * per), *lead)] = value.reshape(per, rows, HD)


def all_tokens(ref, array, slot):
    return ref[:, array, slot].reshape(ref.shape[0] * ref.shape[3], HD)


def tokens_of(ref):
    return ref.shape[0] * ref.shape[3]


def columns(index):
    return pl.ds(pl.multiple_of(index * CHUNK, CHUNK), CHUNK)


def swap_lanes(matrix):
    return jnp.concatenate([matrix[:, HALF:], matrix[:, :HALF]], axis=1)


def thirds(rows):
    first = rows.astype(jnp.bfloat16).astype(jnp.float32)
    second = (rows - first).astype(jnp.bfloat16).astype(jnp.float32)
    return jnp.concatenate([first, second, rows - first - second], axis=0)


def joined_thirds(rows):
    count = rows.shape[0] // 3
    return rows[:count] + (rows[count : 2 * count] + rows[2 * count :])


def held_shape(kind, shape):
    return shape[1:] if kind in SLOTS else shape


def pieces_of(kind, shape):
    if kind == LEAD:
        return [(index,) for index in range(shape[0])]
    if kind == GROUPS:
        per = CHUNK // shape[-2]
        return [(slice(place, place + per),) for place in range(0, shape[0], per)]
    return [()]


def window(ref, piece):
    place = tuple(
        pl.ds(part.start, part.stop - part.start) if isinstance(part, slice) else part
        for part in piece
    )
    return ref.at[place] if place else ref


class Staged:
    def __init__(self, names, kinds, outer, inner, done, outward):
        self.refs = SimpleNamespace(**dict(zip(names, inner)))
        self.copies, self.order = [], []
        count = 0
        steps = []
        for place, (kind, home, held) in enumerate(zip(kinds, outer, inner)):
            home = home.at[kind - SLOTS[0]] if kind in SLOTS else home
            copies = {}
            for step, piece in enumerate(pieces_of(kind, held.shape)):
                ends = (window(held, piece), window(home, piece))
                source, target = ends if outward else ends[::-1]
                key = tuple(
                    part.start if isinstance(part, slice) else part for part in piece
                )
                copies[key] = pltpu.make_async_copy(source, target, done.at[count])
                steps.append((step if kind != WHOLE else -1, place, key))
                count += 1
            self.copies.append(copies)
        self.inner = inner
        self.order = sorted(steps, key=lambda item: item[:2])
        self.started, self.waited = set(), set()

    def place_of(self, ref):
        return next(index for index, held in enumerate(self.inner) if held is ref)

    def start(self, ref=None, *key):
        chosen = [
            (place, name)
            for _, place, name in self.order
            if (ref is None or place == self.place_of(ref)) and (not key or name == key)
        ]
        for item in chosen:
            if item not in self.started:
                self.started.add(item)
                self.copies[item[0]][item[1]].start()

    def wait(self, ref=None, *key):
        chosen = [
            (place, name)
            for _, place, name in self.order
            if (ref is None or place == self.place_of(ref)) and (not key or name == key)
        ]
        for item in chosen:
            if item not in self.waited:
                self.waited.add(item)
                self.copies[item[0]][item[1]].wait()


def staged_call(compute, inputs, outputs, flops, extra=(), after=(), in_place=False):
    names_in, names_out = tuple(inputs), tuple(outputs)
    kinds_in = [x[1] if isinstance(x, tuple) else WHOLE for x in inputs.values()]
    kinds_out = [x[1] if isinstance(x, tuple) else WHOLE for x in outputs.values()]
    operands = tuple(x[0] if isinstance(x, tuple) else x for x in inputs.values())
    shapes = tuple(x[0] if isinstance(x, tuple) else x for x in outputs.values())
    n_in, n_out, n_after = len(operands), len(shapes), len(after)
    moved = sum(x.size * x.dtype.itemsize for x in (*operands, *shapes))
    anywhere = pl.BlockSpec(memory_space=pl.ANY)

    def count(kinds, arrays):
        return sum(len(pieces_of(kind, x.shape)) for kind, x in zip(kinds, arrays))

    def kernel(*refs):
        sources, refs = refs[:n_in], refs[n_in + n_after :]
        homes, refs = refs[:n_out], refs[n_out:]
        held_in, held_out = refs[:n_in], refs[n_in : n_in + n_out]
        *scratch, in_done, out_done = refs[n_in + n_out :]
        reads = Staged(names_in, kinds_in, sources, held_in, in_done, False)
        writes = Staged(names_out, kinds_out, homes, held_out, out_done, True)
        reads.start()
        compute(reads.refs, writes.refs, reads.wait, writes.start, *scratch)
        reads.wait()
        writes.start()
        writes.wait()

    results = pl.pallas_call(
        kernel,
        out_shape=shapes,
        in_specs=[anywhere] * (n_in + n_after),
        out_specs=(anywhere,) * n_out,
        scratch_shapes=[
            *(
                pltpu.VMEM(held_shape(kind, x.shape), x.dtype)
                for kind, x in zip((*kinds_in, *kinds_out), (*operands, *shapes))
            ),
            *extra,
            pltpu.SemaphoreType.DMA((count(kinds_in, operands),)),
            pltpu.SemaphoreType.DMA((count(kinds_out, shapes),)),
        ],
        compiler_params=pltpu.CompilerParams(vmem_limit_bytes=VMEM_LIMIT),
        cost_estimate=pl.CostEstimate(
            flops=int(flops * 10**9), bytes_accessed=moved, transcendentals=0
        ),
    )(*operands, *after)
    return SimpleNamespace(**dict(zip(outputs, results)))


def low(*shape):
    return jax.ShapeDtypeStruct(shape, jnp.bfloat16)


def wide(*shape):
    return jax.ShapeDtypeStruct(shape, jnp.float32)


def pack_kernel(half_ref, first_ref, second_ref, out_ref, rows_s, packed_s, in_done, out_done):
    half = half_ref[0]
    pairs = out_ref.shape[0]
    group = pairs // PACK_GROUPS
    span = 2 * HD
    reads, writes = [], []
    for index in range(PACK_GROUPS):
        for array, ref in enumerate((first_ref, second_ref)):
            place = pl.ds(index * group * span, group * span)
            reads.append(
                pltpu.make_async_copy(
                    ref.at[:, place], rows_s.at[array, :, place], in_done.at[array, index]
                )
            )
        place = pl.ds(index * group, group)
        writes.append(
            pltpu.make_async_copy(packed_s.at[place], out_ref.at[place], out_done.at[index])
        )
    for copy in reads:
        copy.start()
    for index in range(PACK_GROUPS):
        for array in range(2):
            reads[2 * index + array].wait()
            for pair in range(index * group, (index + 1) * group):
                start = pair * span
                packed_s[pair, array, half] = rows_s[array, :, start : start + HD]
                packed_s[pair, array, 1 - half] = rows_s[array, :, start + HD : start + span]
        writes[index].start()
    for copy in writes:
        copy.wait()


def unpack_kernel(half_ref, packed_ref, first_ref, second_ref, rows_s, out_done):
    half = half_ref[0]
    pairs = packed_ref.shape[0]
    group = pairs // PACK_GROUPS
    span = 2 * HD
    writes = []
    for index in range(PACK_GROUPS):
        for array, ref in enumerate((first_ref, second_ref)):
            for pair in range(index * group, (index + 1) * group):
                start = pair * span
                rows_s[array, :, start : start + HD] = packed_ref[pair, array, half]
                rows_s[array, :, start + HD : start + span] = packed_ref[pair, array, 1 - half]
            place = pl.ds(index * group * span, group * span)
            write = pltpu.make_async_copy(
                rows_s.at[array, :, place], ref.at[:, place], out_done.at[array, index]
            )
            write.start()
            writes.append(write)
    for copy in writes:
        copy.wait()


def layout_call(kernel, half, operands, out_shape, scratch, in_space, limit):
    anywhere = pl.BlockSpec(memory_space=pl.ANY)
    moved = 2 * sum(x.size * x.dtype.itemsize for x in operands)
    return pl.pallas_call(
        kernel,
        out_shape=out_shape,
        in_specs=[pl.BlockSpec(memory_space=pltpu.SMEM)]
        + [pl.BlockSpec(memory_space=in_space)] * len(operands),
        out_specs=jax.tree.map(lambda _: anywhere, out_shape),
        scratch_shapes=scratch,
        compiler_params=pltpu.CompilerParams(vmem_limit_bytes=limit),
        cost_estimate=pl.CostEstimate(flops=0, bytes_accessed=moved, transcendentals=0),
    )(half, *operands)


def pack(half, first, second):
    rows, width = first.shape
    shape = low(width // (2 * HD), 2, 2, rows, HD)
    scratch = [
        pltpu.VMEM((2, rows, width), jnp.bfloat16),
        pltpu.VMEM(shape.shape, jnp.bfloat16),
        pltpu.SemaphoreType.DMA((2, PACK_GROUPS)),
        pltpu.SemaphoreType.DMA((PACK_GROUPS,)),
    ]
    return layout_call(
        pack_kernel, half, (first, second), shape, scratch, pl.ANY, VMEM_LIMIT
    )


def unpack(half, packed):
    pairs, _, _, rows, _ = packed.shape
    shape = low(rows, pairs * 2 * HD)
    scratch = [
        pltpu.VMEM((2, *shape.shape), jnp.bfloat16),
        pltpu.SemaphoreType.DMA((2, PACK_GROUPS)),
    ]
    return layout_call(
        unpack_kernel, half, (packed,), (shape, shape), scratch, pltpu.VMEM, SMALL_LIMIT
    )


def landmark_kernel(qk_ref, marks_ref):
    tokens = tokens_of(qk_ref)
    segment_len = tokens // HALF
    per = CHUNK // segment_len
    member = (
        lax.broadcasted_iota(jnp.int32, (per, CHUNK), 1) // segment_len
        == lax.broadcasted_iota(jnp.int32, (per, CHUNK), 0)
    ).astype(jnp.bfloat16)
    kinds = [(slot, array) for slot in range(2) for array in range(2)]
    for index in range(tokens // CHUNK):
        parts = [chunk_of(qk_ref, array, slot, index) for slot, array in kinds]
        summed = wide_dot(member, jnp.concatenate(parts, axis=1))
        mean = (summed / segment_len).astype(jnp.bfloat16)
        for place, (slot, array) in enumerate(kinds):
            marks_ref[slot, array, index * per : (index + 1) * per] = mean[
                :, place * HD : (place + 1) * HD
            ]


def landmarks_of(qk):
    held = pl.BlockSpec(memory_space=pltpu.VMEM)
    return pl.pallas_call(
        landmark_kernel,
        out_shape=low(2, 2, HALF, HD),
        in_specs=[held],
        out_specs=held,
        compiler_params=pltpu.CompilerParams(vmem_limit_bytes=SMALL_LIMIT),
        cost_estimate=pl.CostEstimate(
            flops=2 * 10**8, bytes_accessed=qk.size * 2, transcendentals=0
        ),
    )(qk)


def sweep_forward(power_s, iterate_s, saved, sweep, work):
    pair_ref, weight_ref, growth_ref = saved
    power = power_s[...]
    power_high, power_low = halves(power)
    square = split_dot((power_high, power_low), (power_high, power_low))
    next(work)()
    square_halves = halves(square)
    pair = (
        jnp.concatenate([power_high, square_halves[0]], axis=0),
        jnp.concatenate([power_low, square_halves[1]], axis=0),
    )
    pair_ref[sweep, 0], pair_ref[sweep, 1] = pair
    higher = split_dot(pair, square_halves)
    next(work)()
    cube, fourth = higher[:M], higher[M:]
    weight = halves(0.25 * (13.0 * identity_matrix() - 15.0 * power + 7.0 * square - cube))
    power_s[...] = 0.25 * (13.0 * power - 15.0 * square + 7.0 * cube - fourth)
    weight_ref[sweep, 0], weight_ref[sweep, 1] = weight
    iterate = halves(iterate_s[...])
    growth_ref[sweep, 0], growth_ref[sweep, 1] = iterate[0][M:], iterate[1][M:]
    iterate_s[...] = split_dot(iterate, weight)


def probability_compute(ins, outs, need, put, power_s, iterate_s):
    need()
    qk_ref = ins.qk
    chunks = tokens_of(qk_ref) // CHUNK
    score_scale = HD ** (-0.5)
    for slot in range(2):
        for array in range(2):
            outs.marks[slot, array] = jnp.concatenate(
                [ins.mine[slot, array], ins.theirs[1 - slot, array]], axis=0
            )
    put(outs.marks)
    landmark_q, landmark_k = outs.marks[0, 0], outs.marks[0, 1]
    mark_score = wide_dot_nt(landmark_q, landmark_k) * score_scale
    mark_exp = jnp.exp(mark_score - jnp.max(mark_score, axis=1, keepdims=True))
    mark_prob = mark_exp / jnp.sum(mark_exp, axis=1, keepdims=True)
    outs.mark_prob[...] = mark_prob
    factor = 1.0 / jnp.max(jnp.sum(mark_prob, axis=0, keepdims=True), axis=1, keepdims=True)
    outs.factor[...] = jnp.broadcast_to(factor, outs.factor.shape)
    mark_halves = halves(mark_prob)
    power_s[...] = split_dot_nt(mark_halves, mark_halves) * factor
    iterate_s[0:M] = mark_prob.T * factor
    iterate_s[M:] = identity_matrix()
    tops, totals = [[], []], [[], []]

    def scores(slot, index):
        query_chunk, key_chunk = (chunk_of(qk_ref, array, slot, index) for array in range(2))
        place = slice(index * CHUNK, (index + 1) * CHUNK)
        outs.turned[slot, 0, :, place] = query_chunk.T
        outs.turned[slot, 1, :, place] = key_chunk.T
        score = wide_dot_nt(query_chunk, outs.marks[slot, 1]) * score_scale
        grown = jnp.exp(score - jnp.max(score, axis=1, keepdims=True))
        prob = grown * (1.0 / jnp.sum(grown, axis=1, keepdims=True))
        outs.token_prob[slot, place] = prob
        outs.token_low[slot, place] = prob.astype(jnp.bfloat16)
        key_score = wide_dot_nt(key_chunk, outs.marks[slot, 0]) * score_scale
        outs.key_exp[slot, place] = key_score
        tops[slot].append(jnp.max(key_score, axis=0, keepdims=True))

    def grow(slot, index):
        if index == 0:
            tops[slot] = functools.reduce(jnp.maximum, tops[slot])
        place = slice(index * CHUNK, (index + 1) * CHUNK)
        grown = jnp.exp(outs.key_exp[slot, place] - tops[slot])
        outs.key_exp[slot, place] = grown
        outs.key_low[slot, place] = grown.astype(jnp.bfloat16)
        totals[slot].append(jnp.sum(grown, axis=0, keepdims=True))

    def several(unit, pairs):
        for slot, index in pairs:
            unit(slot, index)

    pairs = [(slot, index) for slot in range(2) for index in range(chunks)]
    work = iter(
        [functools.partial(several, scores, [pair]) for pair in pairs]
        + [
            functools.partial(several, grow, pairs[first : first + 2])
            for first in range(0, len(pairs), 2)
        ]
    )
    saved = (outs.pair, outs.weight, outs.growth)
    for sweep in range(PINV_ITERS):
        sweep_forward(power_s, iterate_s, saved, sweep, work)
        for ref in saved:
            put(ref, sweep)
        if sweep == 3:
            for ref in (outs.token_low, outs.token_prob, outs.turned):
                put(ref)
    put(outs.key_low)
    put(outs.key_exp)
    outs.inverse[0], outs.inverse[1] = halves(iterate_s[0:M])
    outs.last_growth[0], outs.last_growth[1] = halves(iterate_s[M:])
    stats = [x for slot in range(2) for x in (tops[slot], sum(totals[slot][1:], totals[slot][0]))]
    outs.stats[0:4] = jnp.concatenate(stats, axis=0)
    outs.stats[4:8] = jnp.zeros((4, M), jnp.float32)


def partial_compute(ins, outs, need, put):
    need(ins.vg)
    turned = [[all_tokens(ins.vg, array, slot).T for array in range(2)] for slot in range(2)]
    need()
    rows = thirds(ins.stats[0:4])
    outs.send[2 * HD :] = jnp.concatenate([rows, jnp.zeros((4, M), jnp.float32)], axis=0).astype(
        jnp.bfloat16
    )
    for slot, home in ((1, outs.send), (0, outs.keep)):
        home[0:HD] = wide_dot(turned[slot][0], ins.key_low[slot]).astype(home.dtype)
        home[HD : 2 * HD] = wide_dot(turned[slot][1], ins.token_low[slot]).astype(home.dtype)
        put(home)


def mixing_compute(ins, outs, need, put):
    need()
    got = ins.got[...].astype(jnp.float32)
    others = swap_lanes(joined_thirds(got[2 * HD : 2 * HD + 12]))
    scales = []
    for slot in range(2):
        own_max, own_total = ins.stats[2 * slot : 2 * slot + 1], ins.stats[2 * slot + 1 : 2 * slot + 2]
        other = 1 - slot
        other_max, other_total = others[2 * other : 2 * other + 1], others[2 * other + 1 : 2 * other + 2]
        key_max = jnp.maximum(own_max, other_max)
        own_factor, other_factor = jnp.exp(own_max - key_max), jnp.exp(other_max - key_max)
        inverse_total = 1.0 / (own_total * own_factor + other_total * other_factor)
        scales.append((own_factor * inverse_total, other_factor * inverse_total))
    outs.scales[...] = jnp.concatenate(
        [scales[0][0], scales[1][0], jnp.zeros((6, M), jnp.float32)], axis=0
    )
    landmark_values = ins.keep[0:HD] * scales[0][0] + swap_lanes(got[0:HD]) * scales[0][1]
    mixing_grad = ins.keep[HD : 2 * HD] + swap_lanes(got[HD : 2 * HD])
    inverse = (ins.inverse[0], ins.inverse[1])
    outs.share[0:HD] = split_dot_nt(halves(landmark_values), inverse).astype(jnp.bfloat16)
    values_low = split_dot(halves(mixing_grad), inverse).astype(jnp.bfloat16)
    outs.share[HD : 2 * HD] = values_low
    row_total = jnp.sum(values_low.astype(jnp.float32) * landmark_values, axis=0, keepdims=True)
    outs.share[2 * HD :] = jnp.concatenate(
        [thirds(row_total), jnp.zeros((13, M), jnp.float32)], axis=0
    ).astype(jnp.bfloat16)
    put(outs.share)
    outs.mixing_grad[...] = mixing_grad
    outs.mark_values[...] = landmark_values


def several(*units):
    for unit in units:
        unit()


def out_units(ins, slot, out_ref, lead, share):
    mixing_low, values_low, _ = share
    scale = ins.scales[slot : slot + 1]

    def token_side(index):
        place = slice(index * CHUNK, (index + 1) * CHUNK)
        attended = wide_dot_nt(ins.token_low[place], mixing_low)
        store_chunk(out_ref, (0, *lead), index, attended.astype(jnp.bfloat16))

    def key_side(index):
        place = slice(index * CHUNK, (index + 1) * CHUNK)
        key_plow = (ins.key_exp[place] * scale).astype(jnp.bfloat16)
        value_gradient = wide_dot_nt(key_plow, values_low)
        store_chunk(out_ref, (1, *lead), index, value_gradient.astype(jnp.bfloat16))

    chunks = ins.token_low.shape[0] // CHUNK
    return [
        functools.partial(unit, index) for unit in (token_side, key_side) for index in range(chunks)
    ]


def gradient_units(ins, slot, direct_ref, share):
    score_scale = HD ** (-0.5)
    mixing_low, values_low, row_total = share
    query_sums, key_sums = [], []
    scale = ins.scales[slot : slot + 1]

    def token_side(index):
        place = slice(index * CHUNK, (index + 1) * CHUNK)
        prob = ins.token_prob[slot, place]
        token_grad = wide_dot(chunk_of(ins.vg, 1, slot, index), mixing_low)
        token_sgrad = (
            prob * (token_grad - jnp.sum(token_grad * prob, axis=1, keepdims=True))
        ).astype(jnp.bfloat16)
        direct_ref[slot, 0, place] = wide_dot(token_sgrad, ins.marks[slot, 1]) * score_scale
        key_sums.append(wide_dot(ins.turned[slot, 0, :, place], token_sgrad))

    def key_side(index):
        place = slice(index * CHUNK, (index + 1) * CHUNK)
        key_prob = ins.key_exp[slot, place] * scale
        key_dgrad = wide_dot(chunk_of(ins.vg, 0, slot, index), values_low)
        key_sgrad = (key_prob * (key_dgrad - row_total)).astype(jnp.bfloat16)
        direct_ref[slot, 1, place] = wide_dot(key_sgrad, ins.marks[slot, 0]) * score_scale
        query_sums.append(wide_dot(ins.turned[slot, 1, :, place], key_sgrad))

    chunks = tokens_of(ins.vg) // CHUNK
    units = [
        functools.partial(unit, index) for index in range(chunks) for unit in (key_side, token_side)
    ]
    return units, query_sums, key_sums


def share_parts(ref, swap):
    parts = [ref[0:HD], ref[HD : 2 * HD], joined_thirds(ref[2 * HD :].astype(jnp.float32)[0:3])]
    return [swap_lanes(part) for part in parts] if swap else parts


def own_gradient_compute(ins, outs, need, put):
    for ref in (ins.mark_prob, ins.factor, ins.mixing_grad, ins.mark_values, ins.share, ins.scales):
        need(ref)
    mark_prob = ins.mark_prob[...]
    mark_halves = halves(mark_prob)
    factor = ins.factor[0:1, 0:1]
    inverse_grad = split_dot(halves(ins.mixing_grad[...].T), halves(ins.mark_values[...]))
    inverse_grad_halves = halves(inverse_grad)
    toward = split_dot(mark_halves, inverse_grad_halves) * factor
    power = 0.5 * (toward + toward.T)
    growth = None
    work = iter(out_units(ins, 0, outs.out, (), share_parts(ins.share, False)))

    def beside():
        next(work, lambda: None)()

    for sweep in range(PINV_ITERS):
        if sweep == 0:
            need(ins.token_low)
        if sweep == 2:
            need(ins.key_exp)
        for ref in (ins.pair, ins.weight, ins.growth):
            need(ref, sweep)
        pair = (ins.pair[sweep, 0], ins.pair[sweep, 1])
        first = split_dot(pair, halves(power))
        beside()
        square = first[:M] + first[:M].T
        last = sweep == PINV_ITERS - 1
        second = split_dot(tuple(x[:M] for x in pair) if last else pair, halves(square))
        beside()
        cube = first[M:].T + second[:M]
        weight = halves(0.25 * (7.0 * square - 15.0 * power - cube))
        if not last:
            fourth = second[M:] + second[M:].T
            power = 0.25 * (13.0 * power - 15.0 * square + 7.0 * cube - fourth)
        left = [ins.growth[sweep, 0], ins.growth[sweep, 0], ins.growth[sweep, 1]]
        right = [weight[0], weight[1], weight[0]]
        if growth is not None:
            grown = halves(growth)
            left += [grown[0], grown[0], grown[1]]
            right += [ins.weight[sweep, 0], ins.weight[sweep, 1], ins.weight[sweep, 0]]
        growth = wide_dot(jnp.concatenate(left, axis=1), jnp.concatenate(right, axis=0))
    for unit in work:
        unit()
    put(outs.out)
    need()
    mark_grad = factor * (
        split_dot_nt((ins.last_growth[0], ins.last_growth[1]), inverse_grad_halves)
        + split_dot(halves(growth + growth.T), mark_halves)
    )
    mark_sgrad = mark_prob * (mark_grad - jnp.sum(mark_grad * mark_prob, axis=1, keepdims=True))

    def marks_dot(left, right):
        left_high, left_low = halves(left)
        return wide_dot(
            jnp.concatenate([left_high, left_low], axis=1), jnp.concatenate([right, right], axis=0)
        )

    outs.mark_grads[0] = marks_dot(mark_sgrad, ins.marks[0, 1])
    outs.mark_grads[1] = marks_dot(mark_sgrad.T, ins.marks[0, 0])


def other_out_compute(ins, outs, need, put):
    need(ins.got_share)
    need(ins.scales)
    need(ins.token_low)
    units = out_units(ins, 1, outs.out, (1,), share_parts(ins.got_share, True))
    chunks = len(units) // 2
    several(*units[:chunks])
    need()
    several(*units[chunks:])
    outs.out[:, :, 0] = ins.own_out[...]


def gradient_compute(ins, outs, need, put):
    for ref in (ins.share, ins.got_share, ins.scales, ins.marks, ins.vg, ins.mark_grads):
        need(ref)
    marks_scale = HD ** (-0.5) / (tokens_of(ins.vg) // HALF)
    for slot in range(2):
        for ref in (ins.key_exp, ins.token_prob, ins.turned):
            need(ref, slot)
        share = share_parts(ins.got_share if slot else ins.share, bool(slot))
        units, query_sums, key_sums = gradient_units(ins, slot, outs.direct, share)
        several(*units)
        put(outs.direct, slot)
        for kind, sums in enumerate((query_sums, key_sums)):
            total = sum(sums[1:], sums[0]).T
            if slot == 0:
                total = total + ins.mark_grads[kind]
            total = total * marks_scale
            outs.near[kind, slot] = total[:HALF]
            outs.far[kind, slot] = total[HALF:].astype(jnp.bfloat16)


def finish_compute(ins, outs, need, put):
    need()
    out_ref = outs.out
    group = CHUNK // out_ref.shape[3]
    segment_len = tokens_of(out_ref) // HALF
    per = CHUNK // segment_len
    for index in range(tokens_of(out_ref) // CHUNK):
        place, start = slice(index * per, (index + 1) * per), index * CHUNK
        for slot in range(2):
            for kind in range(2):
                marks = ins.near[kind, slot, place] + ins.got_far[
                    kind, 1 - slot, place
                ].astype(jnp.float32)
                spread = jnp.broadcast_to(marks[:, None], (per, segment_len, HD))
                total = ins.direct[slot, kind, start : start + CHUNK] + spread.reshape(CHUNK, HD)
                store_chunk(out_ref, (kind, slot), index, total.astype(jnp.bfloat16))
        put(out_ref, index * group)


def exchange(packed):
    return lax.all_to_all(packed, "cube", split_axis=0, concat_axis=0, tiled=True)


def partner(array):
    return lax.ppermute(array, "half", SWAP)


def body(queries, keys, values, out_grad):
    half = lax.axis_index("half").reshape(1)
    qk, vg_packed = lax.optimization_barrier(
        (exchange(pack(half, queries, keys)), pack(half, values, out_grad))
    )
    tokens = qk.shape[0] * qk.shape[3]
    mine = landmarks_of(qk)
    theirs = partner(mine)
    vg_packed, mine = lax.optimization_barrier((vg_packed, mine))
    vg = exchange(vg_packed)
    kept = staged_call(
        probability_compute,
        dict(qk=qk, mine=mine, theirs=theirs),
        dict(
            marks=low(2, 2, M, HD),
            token_prob=wide(2, tokens, M),
            token_low=low(2, tokens, M),
            key_exp=wide(2, tokens, M),
            key_low=low(2, tokens, M),
            turned=low(2, 2, HD, tokens),
            stats=wide(8, M),
            mark_prob=wide(M, M),
            factor=wide(8, HD),
            pair=(low(PINV_ITERS, 2, 2 * M, M), LEAD),
            weight=(low(PINV_ITERS, 2, M, M), LEAD),
            growth=(low(PINV_ITERS, 2, M, M), LEAD),
            inverse=low(2, M, M),
            last_growth=low(2, M, M),
        ),
        LONG,
        extra=(pltpu.VMEM((M, M), jnp.float32), pltpu.VMEM((2 * M, M), jnp.float32)),
    )
    sums = staged_call(
        partial_compute,
        dict(vg=vg, stats=kept.stats, key_low=kept.key_low, token_low=kept.token_low),
        dict(send=low(2 * HD + 16, M), keep=wide(2 * HD, M)),
        2,
    )
    mixed = staged_call(
        mixing_compute,
        dict(got=partner(sums.send), keep=sums.keep, stats=kept.stats, inverse=kept.inverse),
        dict(
            share=low(2 * HD + 16, M),
            scales=wide(8, M),
            mixing_grad=wide(HD, M),
            mark_values=wide(HD, M),
        ),
        1,
    )
    got_share = partner(mixed.share)
    own = staged_call(
        own_gradient_compute,
        dict(
            mark_prob=kept.mark_prob,
            factor=kept.factor,
            mixing_grad=mixed.mixing_grad,
            mark_values=mixed.mark_values,
            share=mixed.share,
            scales=mixed.scales,
            token_low=(kept.token_low, SLOTS[0]),
            pair=(kept.pair, LEAD),
            weight=(kept.weight, LEAD),
            growth=(kept.growth, LEAD),
            key_exp=(kept.key_exp, SLOTS[0]),
            last_growth=kept.last_growth,
            marks=kept.marks,
        ),
        dict(out=low(qk.shape[0], 2, *qk.shape[3:]), mark_grads=wide(2, M, HD)),
        14,
    )
    first_results = staged_call(
        other_out_compute,
        dict(
            got_share=got_share,
            scales=mixed.scales,
            token_low=(kept.token_low, SLOTS[1]),
            key_exp=(kept.key_exp, SLOTS[1]),
            own_out=own.out,
        ),
        dict(out=low(*qk.shape)),
        1,
    ).out
    attended, value_gradient_array = unpack(half, exchange(first_results))
    grads = staged_call(
        gradient_compute,
        dict(
            share=mixed.share,
            got_share=got_share,
            scales=mixed.scales,
            marks=kept.marks,
            vg=vg,
            key_exp=(kept.key_exp, LEAD),
            token_prob=(kept.token_prob, LEAD),
            turned=(kept.turned, LEAD),
            mark_grads=own.mark_grads,
        ),
        dict(
            far=low(2, 2, HALF, HD),
            near=wide(2, 2, HALF, HD),
            direct=(wide(2, 2, tokens, HD), LEAD),
        ),
        LONG,
        after=(first_results,),
    )
    results = staged_call(
        finish_compute,
        dict(got_far=partner(grads.far), near=grads.near, direct=grads.direct),
        dict(out=(low(*qk.shape), GROUPS)),
        0.1,
    ).out
    query_grad, key_grad = unpack(half, exchange(results))
    return attended, query_grad, key_grad, value_gradient_array


def solution(mesh):
    whole_placement = P(("seq", "head"), None)
    halves_placement = P(("half", "cube"), None)

    def layer(queries, keys, values, out_grad):
        tokens, width = queries.shape
        own_head_each = width // HD == mesh.size and tokens == 8 * CHUNK
        if own_head_each:
            split = jax.sharding.Mesh(
                mesh.devices.reshape(2, mesh.size // 2), ("half", "cube")
            )
        return jax.shard_map(
            body if own_head_each else shared_body,
            mesh=split if own_head_each else mesh,
            in_specs=(halves_placement if own_head_each else whole_placement,) * 4,
            out_specs=(halves_placement if own_head_each else whole_placement,) * 4,
            check_vma=False,
        )(queries, keys, values, out_grad)

    return layer
```

```python
import functools
from types import SimpleNamespace

import jax
import jax.numpy as jnp
from jax import lax
from jax.experimental import pallas as pl
from jax.experimental.pallas import tpu as pltpu
from jax.sharding import PartitionSpec as P

HD = 128
M = 256
PINV_ITERS = 6
CHUNK = 256
PACK_GROUPS = 4
HALF = M // 2
SWAP = ((0, 1), (1, 0))
VMEM_LIMIT = 60 * 2**20
SMALL_LIMIT = 16 * 2**20
WHOLE, LEAD, GROUPS, BLOCKS = range(4)
SLOTS = (10, 11)
LONG = 200
EARLY_SWEEPS = PINV_ITERS // 2


precise_setting = lax.Precision.HIGHEST


def newton_inverse(matrix):
    identity = jnp.eye(matrix.shape[0], dtype=matrix.dtype)
    factor = lax.stop_gradient(1.0 / jnp.max(jnp.sum(matrix, axis=0)))
    iterate = matrix.T * factor
    for sweep_index in range(PINV_ITERS):
        product = jnp.matmul(matrix, iterate, precision=precise_setting)
        inner_term = jnp.matmul(product, 7.0 * identity - product, precision=precise_setting)
        inner_term = jnp.matmul(product, 15.0 * identity - inner_term, precision=precise_setting)
        iterate = 0.25 * jnp.matmul(
            iterate, 13.0 * identity - inner_term, precision=precise_setting
        )
    return iterate


def share_heads(own_matrix, head_count):
    seq_index = lax.axis_index("seq")
    slot_mask = (jnp.arange(head_count, dtype=jnp.int32) == seq_index).astype(jnp.float32)
    return lax.psum(slot_mask[:, None, None] * own_matrix[None], "seq")


def shared_body(queries, keys, values, out_grad):
    query_rows, key_rows, value_rows, grad_rows = (
        lax.all_to_all(queries, "head", split_axis=1, concat_axis=0, tiled=True),
        lax.all_to_all(keys, "head", split_axis=1, concat_axis=0, tiled=True),
        lax.all_to_all(values, "head", split_axis=1, concat_axis=0, tiled=True),
        lax.all_to_all(out_grad, "head", split_axis=1, concat_axis=0, tiled=True),
    )
    tok_rows = query_rows.shape[0]
    head_count = query_rows.shape[1] // HD
    local_marks = M // lax.axis_size("seq")
    segment_len = tok_rows // local_marks
    score_scale = HD ** (-0.5)
    seq_index = lax.axis_index("seq")

    def landmark(matrix):
        summed = jnp.sum(
            matrix.reshape(local_marks, segment_len, matrix.shape[1]), axis=1, dtype=jnp.float32
        )
        return (summed / segment_len).astype(jnp.bfloat16)

    mark_queries, mark_keys = (
        lax.all_gather(landmark(query_rows), "seq", axis=0, tiled=True),
        lax.all_gather(landmark(key_rows), "seq", axis=0, tiled=True),
    )
    query_per_head = query_rows.reshape(tok_rows, head_count, HD)
    key_per_head = key_rows.reshape(tok_rows, head_count, HD)
    value_per_head = value_rows.reshape(tok_rows, head_count, HD)
    gradient_per_head = grad_rows.reshape(tok_rows, head_count, HD)
    landmark_query_heads = mark_queries.reshape(M, head_count, HD)
    landmark_key_heads = mark_keys.reshape(M, head_count, HD)
    key_score = (
        jnp.einsum(
            "pcv,gcv->cpg", landmark_query_heads, key_per_head, preferred_element_type=jnp.float32
        )
        * score_scale
    )
    key_max = lax.pmax(jnp.max(key_score, axis=-1), "seq")
    key_exp = jnp.exp(key_score - key_max[..., None])
    partial_num = jnp.einsum(
        "akq,qay->aky",
        key_exp.astype(jnp.bfloat16),
        value_per_head,
        preferred_element_type=jnp.float32,
    )
    key_total, numerator = lax.psum((jnp.sum(key_exp, axis=-1), partial_num), "seq")
    landmark_value_rows = numerator / key_total[..., None]
    token_prob = jax.nn.softmax(
        jnp.einsum(
            "jti,cti->tjc", query_per_head, landmark_key_heads, preferred_element_type=jnp.float32
        )
        * score_scale,
        axis=-1,
    )
    token_probability_lowered = token_prob.astype(jnp.bfloat16)
    mark_prob = jax.nn.softmax(
        jnp.einsum(
            "jou,iou->oji",
            landmark_query_heads,
            landmark_key_heads,
            preferred_element_type=jnp.float32,
        )
        * score_scale,
        axis=-1,
    )
    own_head = seq_index % head_count
    own_mark = lax.dynamic_index_in_dim(mark_prob, own_head, 0, keepdims=False)
    own_inverse, pull_back = jax.vjp(newton_inverse, own_mark)
    pseudo_inverse_matrix = share_heads(own_inverse, head_count)
    mixing_matrix = jnp.einsum(
        "jvy,jys->jvs", pseudo_inverse_matrix, landmark_value_rows, precision=precise_setting
    )
    mixing_matrix_lowered = mixing_matrix.astype(jnp.bfloat16)
    attended = jnp.einsum(
        "yvo,yor->vyr",
        token_probability_lowered,
        mixing_matrix_lowered,
        preferred_element_type=jnp.float32,
    ).astype(jnp.bfloat16)
    token_grad = jnp.einsum(
        "fag,aog->afo", gradient_per_head, mixing_matrix_lowered, preferred_element_type=jnp.float32
    )
    partial_mix = jnp.einsum(
        "klz,lkr->kzr",
        token_probability_lowered,
        gradient_per_head,
        preferred_element_type=jnp.float32,
    )
    mixing_matrix_gradient = lax.psum(partial_mix, "seq")
    token_score_gradient = (
        token_prob * (token_grad - jnp.sum(token_grad * token_prob, axis=-1, keepdims=True))
    ).astype(jnp.bfloat16)
    direct_qgrad = (
        jnp.einsum(
            "ufg,guc->fuc",
            token_score_gradient,
            landmark_key_heads,
            preferred_element_type=jnp.float32,
        )
        * score_scale
    )
    mark_kgrad_f = (
        jnp.einsum(
            "xgi,gxy->ixy", token_score_gradient, query_per_head, preferred_element_type=jnp.float32
        )
        * score_scale
    )
    pseudo_inverse_gradient = jnp.einsum(
        "ktu,kyu->kty", mixing_matrix_gradient, landmark_value_rows, precision=precise_setting
    )
    landmark_value_gradient = jnp.einsum(
        "lrb,lrz->lbz", pseudo_inverse_matrix, mixing_matrix_gradient, precision=precise_setting
    )
    own_igrad = lax.dynamic_index_in_dim(pseudo_inverse_gradient, own_head, 0, keepdims=False)
    (own_mgrad,) = pull_back(own_igrad)
    mark_grad = share_heads(own_mgrad, head_count)
    mark_sgrad = mark_prob * (mark_grad - jnp.sum(mark_grad * mark_prob, axis=-1, keepdims=True))
    first_mark = seq_index * local_marks
    score_gradient_rows = lax.dynamic_slice_in_dim(mark_sgrad, first_mark, local_marks, 1)
    score_gradient_columns = lax.dynamic_slice_in_dim(mark_sgrad, first_mark, local_marks, 2)
    own_qgrad_a = (
        jnp.einsum(
            "txs,ste->xte",
            score_gradient_rows,
            landmark_key_heads.astype(jnp.float32),
            precision=precise_setting,
        )
        * score_scale
    )
    own_kgrad_a = (
        jnp.einsum(
            "eaj,aev->jev",
            score_gradient_columns,
            landmark_query_heads.astype(jnp.float32),
            precision=precise_setting,
        )
        * score_scale
    )
    landmark_value_lowered = landmark_value_gradient.astype(jnp.bfloat16)
    key_prob = key_exp / key_total[..., None]
    key_probability_lowered = key_prob.astype(jnp.bfloat16)
    value_gradient_array = jnp.einsum(
        "zct,zcj->tzj",
        key_probability_lowered,
        landmark_value_lowered,
        preferred_element_type=jnp.float32,
    )
    key_direct_gradient = jnp.einsum(
        "exb,geb->exg", landmark_value_lowered, value_per_head, preferred_element_type=jnp.float32
    )
    row_total = lax.psum(jnp.sum(key_prob * key_direct_gradient, axis=-1), "seq")
    key_score_gradient = (key_prob * (key_direct_gradient - row_total[..., None])).astype(
        jnp.bfloat16
    )
    direct_kgrad = (
        jnp.einsum(
            "pbo,bpx->opx",
            key_score_gradient,
            landmark_query_heads,
            preferred_element_type=jnp.float32,
        )
        * score_scale
    )
    mark_qgrad_b = (
        jnp.einsum(
            "cbj,jcp->bcp", key_score_gradient, key_per_head, preferred_element_type=jnp.float32
        )
        * score_scale
    )
    own_kgrad_f, own_qgrad_b = (
        lax.psum_scatter(mark_kgrad_f, "seq", scatter_dimension=0, tiled=True),
        lax.psum_scatter(mark_qgrad_b, "seq", scatter_dimension=0, tiled=True),
    )
    mark_qtotal = (own_qgrad_a + own_qgrad_b) / segment_len
    mark_ktotal = (own_kgrad_a + own_kgrad_f) / segment_len
    query_grad = (
        direct_qgrad.reshape(local_marks, segment_len, head_count, HD) + mark_qtotal[:, None]
    )
    key_grad = direct_kgrad.reshape(local_marks, segment_len, head_count, HD) + mark_ktotal[:, None]
    width = head_count * HD
    results = (
        attended.reshape(tok_rows, width),
        query_grad.astype(jnp.bfloat16).reshape(tok_rows, width),
        key_grad.astype(jnp.bfloat16).reshape(tok_rows, width),
        value_gradient_array.astype(jnp.bfloat16).reshape(tok_rows, width),
    )
    attended_out, query_out, key_out, value_out = (
        lax.all_to_all(results[0], "head", split_axis=0, concat_axis=1, tiled=True),
        lax.all_to_all(results[1], "head", split_axis=0, concat_axis=1, tiled=True),
        lax.all_to_all(results[2], "head", split_axis=0, concat_axis=1, tiled=True),
        lax.all_to_all(results[3], "head", split_axis=0, concat_axis=1, tiled=True),
    )
    return (attended_out, query_out, key_out, value_out)


def halves(matrix):
    high = matrix.astype(jnp.bfloat16)
    return high, (matrix - high.astype(jnp.float32)).astype(jnp.bfloat16)


def wide_dot(left, right):
    return jnp.dot(left, right, preferred_element_type=jnp.float32)


def wide_dot_nt(left, right):
    return lax.dot_general(
        left, right, (((1,), (1,)), ((), ())), preferred_element_type=jnp.float32
    )


def split_dot(left, right):
    left_high, left_low = left
    right_high, right_low = right
    return wide_dot(
        jnp.concatenate([left_high, left_high, left_low], axis=1),
        jnp.concatenate([right_high, right_low, right_high], axis=0),
    )


def split_dot_nt(left, right):
    left_high, left_low = left
    right_high, right_low = right
    return wide_dot_nt(
        jnp.concatenate([left_high, left_high, left_low], axis=1),
        jnp.concatenate([right_high, right_low, right_high], axis=1),
    )


def identity_matrix():
    return (
        lax.broadcasted_iota(jnp.int32, (M, M), 0) == lax.broadcasted_iota(jnp.int32, (M, M), 1)
    ).astype(jnp.float32)


def chunk_of(ref, array, slot, index):
    per = CHUNK // ref.shape[3]
    return ref[index * per : (index + 1) * per, array, slot].reshape(CHUNK, HD)


def store_chunk(ref, lead, index, value):
    rows = ref.shape[-2]
    per = CHUNK // rows
    ref[(slice(index * per, (index + 1) * per), *lead)] = value.reshape(per, rows, HD)


def all_tokens(ref, array, slot):
    return ref[:, array, slot].reshape(ref.shape[0] * ref.shape[3], HD)


def tokens_of(ref):
    return ref.shape[0] * ref.shape[3]


def columns(index):
    return pl.ds(pl.multiple_of(index * CHUNK, CHUNK), CHUNK)


def swap_lanes(matrix):
    return jnp.concatenate([matrix[:, HALF:], matrix[:, :HALF]], axis=1)


def thirds(rows):
    first = rows.astype(jnp.bfloat16).astype(jnp.float32)
    second = (rows - first).astype(jnp.bfloat16).astype(jnp.float32)
    return jnp.concatenate([first, second, rows - first - second], axis=0)


def joined_thirds(rows):
    count = rows.shape[0] // 3
    return rows[:count] + (rows[count : 2 * count] + rows[2 * count :])


def held_shape(kind, shape):
    return shape[1:] if kind in SLOTS else shape


def pieces_of(kind, shape):
    if kind == LEAD:
        return [(index,) for index in range(shape[0])]
    if kind == BLOCKS:
        return [
            (first, second, slice(place, place + 2 * CHUNK))
            for place in range(0, shape[2], 2 * CHUNK)
            for first in range(shape[0])
            for second in range(shape[1])
        ]
    if kind == GROUPS:
        per = CHUNK // shape[-2]
        return [(slice(place, place + per),) for place in range(0, shape[0], per)]
    return [()]


def window(ref, piece):
    place = tuple(
        pl.ds(part.start, part.stop - part.start) if isinstance(part, slice) else part
        for part in piece
    )
    return ref.at[place] if place else ref


class Staged:
    def __init__(self, names, kinds, outer, inner, done, outward):
        self.refs = SimpleNamespace(**dict(zip(names, inner)))
        self.copies, self.order = [], []
        count = 0
        steps = []
        for place, (kind, home, held) in enumerate(zip(kinds, outer, inner)):
            home = home.at[kind - SLOTS[0]] if kind in SLOTS else home
            copies = {}
            for step, piece in enumerate(pieces_of(kind, held.shape)):
                ends = (window(held, piece), window(home, piece))
                source, target = ends if outward else ends[::-1]
                key = tuple(
                    part.start if isinstance(part, slice) else part for part in piece
                )
                copies[key] = pltpu.make_async_copy(source, target, done.at[count])
                steps.append((step if kind != WHOLE else -1, place, key))
                count += 1
            self.copies.append(copies)
        self.inner = inner
        self.order = sorted(steps, key=lambda item: item[:2])
        self.started, self.waited = set(), set()

    def place_of(self, ref):
        return next(index for index, held in enumerate(self.inner) if held is ref)

    def start(self, ref=None, *key):
        chosen = [
            (place, name)
            for _, place, name in self.order
            if (ref is None or place == self.place_of(ref)) and (not key or name == key)
        ]
        for item in chosen:
            if item not in self.started:
                self.started.add(item)
                self.copies[item[0]][item[1]].start()

    def wait(self, ref=None, *key):
        chosen = [
            (place, name)
            for _, place, name in self.order
            if (ref is None or place == self.place_of(ref)) and (not key or name == key)
        ]
        for item in chosen:
            if item not in self.waited:
                self.waited.add(item)
                self.copies[item[0]][item[1]].wait()


def staged_call(compute, inputs, outputs, flops, extra=(), after=(), in_place=False):
    names_in, names_out = tuple(inputs), tuple(outputs)
    kinds_in = [x[1] if isinstance(x, tuple) else WHOLE for x in inputs.values()]
    kinds_out = [x[1] if isinstance(x, tuple) else WHOLE for x in outputs.values()]
    operands = tuple(x[0] if isinstance(x, tuple) else x for x in inputs.values())
    shapes = tuple(x[0] if isinstance(x, tuple) else x for x in outputs.values())
    n_in, n_out, n_after = len(operands), len(shapes), len(after)
    moved = sum(x.size * x.dtype.itemsize for x in (*operands, *shapes))
    anywhere = pl.BlockSpec(memory_space=pl.ANY)

    def count(kinds, arrays):
        return sum(len(pieces_of(kind, x.shape)) for kind, x in zip(kinds, arrays))

    def kernel(*refs):
        sources, refs = refs[:n_in], refs[n_in + n_after :]
        homes, refs = refs[:n_out], refs[n_out:]
        held_in, held_out = refs[:n_in], refs[n_in : n_in + n_out]
        *scratch, in_done, out_done = refs[n_in + n_out :]
        reads = Staged(names_in, kinds_in, sources, held_in, in_done, False)
        writes = Staged(names_out, kinds_out, homes, held_out, out_done, True)
        reads.start()
        compute(reads.refs, writes.refs, reads.wait, writes.start, *scratch)
        reads.wait()
        writes.start()
        writes.wait()

    results = pl.pallas_call(
        kernel,
        out_shape=shapes,
        in_specs=[anywhere] * (n_in + n_after),
        out_specs=(anywhere,) * n_out,
        scratch_shapes=[
            *(
                pltpu.VMEM(held_shape(kind, x.shape), x.dtype)
                for kind, x in zip((*kinds_in, *kinds_out), (*operands, *shapes))
            ),
            *extra,
            pltpu.SemaphoreType.DMA((count(kinds_in, operands),)),
            pltpu.SemaphoreType.DMA((count(kinds_out, shapes),)),
        ],
        compiler_params=pltpu.CompilerParams(vmem_limit_bytes=VMEM_LIMIT),
        cost_estimate=pl.CostEstimate(
            flops=int(flops * 10**9), bytes_accessed=moved, transcendentals=0
        ),
    )(*operands, *after)
    return SimpleNamespace(**dict(zip(outputs, results)))


def low(*shape):
    return jax.ShapeDtypeStruct(shape, jnp.bfloat16)


def wide(*shape):
    return jax.ShapeDtypeStruct(shape, jnp.float32)


def pack_kernel(half_ref, first_ref, second_ref, out_ref, rows_s, packed_s, in_done, out_done):
    half = half_ref[0]
    pairs = out_ref.shape[0]
    group = pairs // PACK_GROUPS
    span = 2 * HD
    reads, writes = [], []
    for index in range(PACK_GROUPS):
        for array, ref in enumerate((first_ref, second_ref)):
            place = pl.ds(index * group * span, group * span)
            reads.append(
                pltpu.make_async_copy(
                    ref.at[:, place], rows_s.at[array, :, place], in_done.at[array, index]
                )
            )
        place = pl.ds(index * group, group)
        writes.append(
            pltpu.make_async_copy(packed_s.at[place], out_ref.at[place], out_done.at[index])
        )
    for copy in reads:
        copy.start()
    for index in range(PACK_GROUPS):
        for array in range(2):
            reads[2 * index + array].wait()
            for pair in range(index * group, (index + 1) * group):
                start = pair * span
                packed_s[pair, array, half] = rows_s[array, :, start : start + HD]
                packed_s[pair, array, 1 - half] = rows_s[array, :, start + HD : start + span]
        writes[index].start()
    for copy in writes:
        copy.wait()


def unpack_kernel(half_ref, packed_ref, first_ref, second_ref, rows_s, out_done):
    half = half_ref[0]
    pairs = packed_ref.shape[0]
    group = pairs // PACK_GROUPS
    span = 2 * HD
    writes = []
    for index in range(PACK_GROUPS):
        for array, ref in enumerate((first_ref, second_ref)):
            for pair in range(index * group, (index + 1) * group):
                start = pair * span
                rows_s[array, :, start : start + HD] = packed_ref[pair, array, half]
                rows_s[array, :, start + HD : start + span] = packed_ref[pair, array, 1 - half]
            place = pl.ds(index * group * span, group * span)
            write = pltpu.make_async_copy(
                rows_s.at[array, :, place], ref.at[:, place], out_done.at[array, index]
            )
            write.start()
            writes.append(write)
    for copy in writes:
        copy.wait()


def layout_call(kernel, half, operands, out_shape, scratch, in_space, limit):
    anywhere = pl.BlockSpec(memory_space=pl.ANY)
    moved = 2 * sum(x.size * x.dtype.itemsize for x in operands)
    return pl.pallas_call(
        kernel,
        out_shape=out_shape,
        in_specs=[pl.BlockSpec(memory_space=pltpu.SMEM)]
        + [pl.BlockSpec(memory_space=in_space)] * len(operands),
        out_specs=jax.tree.map(lambda _: anywhere, out_shape),
        scratch_shapes=scratch,
        compiler_params=pltpu.CompilerParams(vmem_limit_bytes=limit),
        cost_estimate=pl.CostEstimate(flops=0, bytes_accessed=moved, transcendentals=0),
    )(half, *operands)


def pack(half, first, second):
    rows, width = first.shape
    shape = low(width // (2 * HD), 2, 2, rows, HD)
    scratch = [
        pltpu.VMEM((2, rows, width), jnp.bfloat16),
        pltpu.VMEM(shape.shape, jnp.bfloat16),
        pltpu.SemaphoreType.DMA((2, PACK_GROUPS)),
        pltpu.SemaphoreType.DMA((PACK_GROUPS,)),
    ]
    return layout_call(
        pack_kernel, half, (first, second), shape, scratch, pl.ANY, VMEM_LIMIT
    )


def unpack(half, packed):
    pairs, _, _, rows, _ = packed.shape
    shape = low(rows, pairs * 2 * HD)
    scratch = [
        pltpu.VMEM((2, *shape.shape), jnp.bfloat16),
        pltpu.SemaphoreType.DMA((2, PACK_GROUPS)),
    ]
    return layout_call(
        unpack_kernel, half, (packed,), (shape, shape), scratch, pltpu.VMEM, SMALL_LIMIT
    )


def landmark_kernel(qk_ref, marks_ref):
    tokens = tokens_of(qk_ref)
    segment_len = tokens // HALF
    per = CHUNK // segment_len
    member = (
        lax.broadcasted_iota(jnp.int32, (per, CHUNK), 1) // segment_len
        == lax.broadcasted_iota(jnp.int32, (per, CHUNK), 0)
    ).astype(jnp.bfloat16)
    kinds = [(slot, array) for slot in range(2) for array in range(2)]
    for index in range(tokens // CHUNK):
        parts = [chunk_of(qk_ref, array, slot, index) for slot, array in kinds]
        summed = wide_dot(member, jnp.concatenate(parts, axis=1))
        mean = (summed / segment_len).astype(jnp.bfloat16)
        for place, (slot, array) in enumerate(kinds):
            marks_ref[slot, array, index * per : (index + 1) * per] = mean[
                :, place * HD : (place + 1) * HD
            ]


def landmarks_of(qk):
    held = pl.BlockSpec(memory_space=pltpu.VMEM)
    return pl.pallas_call(
        landmark_kernel,
        out_shape=low(2, 2, HALF, HD),
        in_specs=[held],
        out_specs=held,
        compiler_params=pltpu.CompilerParams(vmem_limit_bytes=SMALL_LIMIT),
        cost_estimate=pl.CostEstimate(
            flops=2 * 10**8, bytes_accessed=qk.size * 2, transcendentals=0
        ),
    )(qk)


def sweep_forward(power_s, iterate_s, saved, sweep, work):
    pair_ref, weight_ref, growth_ref = saved
    power = power_s[...]
    power_high, power_low = halves(power)
    square = split_dot((power_high, power_low), (power_high, power_low))
    next(work)()
    square_halves = halves(square)
    pair = (
        jnp.concatenate([power_high, square_halves[0]], axis=0),
        jnp.concatenate([power_low, square_halves[1]], axis=0),
    )
    pair_ref[sweep, 0], pair_ref[sweep, 1] = pair
    higher = split_dot(pair, square_halves)
    next(work)()
    cube, fourth = higher[:M], higher[M:]
    weight = halves(0.25 * (13.0 * identity_matrix() - 15.0 * power + 7.0 * square - cube))
    power_s[...] = 0.25 * (13.0 * power - 15.0 * square + 7.0 * cube - fourth)
    weight_ref[sweep, 0], weight_ref[sweep, 1] = weight
    iterate = halves(iterate_s[...])
    growth_ref[sweep, 0], growth_ref[sweep, 1] = iterate[0][M:], iterate[1][M:]
    iterate_s[...] = split_dot(iterate, weight)


def probability_compute(ins, outs, need, put, power_s, iterate_s):
    need()
    qk_ref = ins.qk
    chunks = tokens_of(qk_ref) // CHUNK
    score_scale = HD ** (-0.5)
    for slot in range(2):
        for array in range(2):
            outs.marks[slot, array] = jnp.concatenate(
                [ins.mine[slot, array], ins.theirs[1 - slot, array]], axis=0
            )
    put(outs.marks)
    landmark_q, landmark_k = outs.marks[0, 0], outs.marks[0, 1]
    mark_score = wide_dot_nt(landmark_q, landmark_k) * score_scale
    mark_exp = jnp.exp(mark_score - jnp.max(mark_score, axis=1, keepdims=True))
    mark_prob = mark_exp / jnp.sum(mark_exp, axis=1, keepdims=True)
    outs.mark_prob[...] = mark_prob
    factor = 1.0 / jnp.max(jnp.sum(mark_prob, axis=0, keepdims=True), axis=1, keepdims=True)
    outs.factor[...] = jnp.broadcast_to(factor, outs.factor.shape)
    mark_halves = halves(mark_prob)
    power_s[...] = split_dot_nt(mark_halves, mark_halves) * factor
    iterate_s[0:M] = mark_prob.T * factor
    iterate_s[M:] = identity_matrix()
    tops, totals = [[], []], [[], []]

    def scores(slot, index):
        query_chunk, key_chunk = (chunk_of(qk_ref, array, slot, index) for array in range(2))
        place = slice(index * CHUNK, (index + 1) * CHUNK)
        outs.turned[slot, 0, :, place] = query_chunk.T
        outs.turned[slot, 1, :, place] = key_chunk.T
        score = wide_dot_nt(query_chunk, outs.marks[slot, 1]) * score_scale
        grown = jnp.exp(score - jnp.max(score, axis=1, keepdims=True))
        prob = grown * (1.0 / jnp.sum(grown, axis=1, keepdims=True))
        outs.token_prob[slot, place] = prob
        outs.token_low[slot, place] = prob.astype(jnp.bfloat16)
        key_score = wide_dot_nt(key_chunk, outs.marks[slot, 0]) * score_scale
        outs.key_exp[slot, place] = key_score
        tops[slot].append(jnp.max(key_score, axis=0, keepdims=True))

    def grow(slot, index):
        if index == 0:
            tops[slot] = functools.reduce(jnp.maximum, tops[slot])
        place = slice(index * CHUNK, (index + 1) * CHUNK)
        grown = jnp.exp(outs.key_exp[slot, place] - tops[slot])
        outs.key_exp[slot, place] = grown
        outs.key_low[slot, place] = grown.astype(jnp.bfloat16)
        totals[slot].append(jnp.sum(grown, axis=0, keepdims=True))

    def several(unit, pairs):
        for slot, index in pairs:
            unit(slot, index)

    pairs = [(slot, index) for slot in range(2) for index in range(chunks)]
    work = iter(
        [functools.partial(several, scores, [pair]) for pair in pairs]
        + [
            functools.partial(several, grow, pairs[first : first + 2])
            for first in range(0, len(pairs), 2)
        ]
    )
    for sweep in range(PINV_ITERS):
        first = sweep < EARLY_SWEEPS
        place = sweep if first else sweep - EARLY_SWEEPS
        saved = (
            (outs.pair_a, outs.weight_a, outs.growth_a)
            if first
            else (outs.pair_b, outs.weight_b, outs.growth_b)
        )
        sweep_forward(power_s, iterate_s, saved, place, work)
        for ref in saved:
            put(ref, place)
        if sweep == 3:
            for ref in (outs.token_low, outs.token_prob, outs.turned):
                put(ref)
    put(outs.key_low)
    put(outs.key_exp)
    outs.inverse[0], outs.inverse[1] = halves(iterate_s[0:M])
    outs.last_growth[0], outs.last_growth[1] = halves(iterate_s[M:])
    stats = [x for slot in range(2) for x in (tops[slot], sum(totals[slot][1:], totals[slot][0]))]
    outs.stats[0:4] = jnp.concatenate(stats, axis=0)
    outs.stats[4:8] = jnp.zeros((4, M), jnp.float32)


def partial_compute(ins, outs, need, put):
    need(ins.vg)
    turned = [[all_tokens(ins.vg, array, slot).T for array in range(2)] for slot in range(2)]
    need()
    rows = thirds(ins.stats[0:4])
    outs.send[2 * HD :] = jnp.concatenate([rows, jnp.zeros((4, M), jnp.float32)], axis=0).astype(
        jnp.bfloat16
    )
    for slot, home in ((1, outs.send), (0, outs.keep)):
        home[0:HD] = wide_dot(turned[slot][0], ins.key_low[slot]).astype(home.dtype)
        home[HD : 2 * HD] = wide_dot(turned[slot][1], ins.token_low[slot]).astype(home.dtype)
        put(home)


def mixing_compute(ins, outs, need, put):
    need()
    got = ins.got[...].astype(jnp.float32)
    others = swap_lanes(joined_thirds(got[2 * HD : 2 * HD + 12]))
    scales = []
    for slot in range(2):
        own_max, own_total = ins.stats[2 * slot : 2 * slot + 1], ins.stats[2 * slot + 1 : 2 * slot + 2]
        other = 1 - slot
        other_max, other_total = others[2 * other : 2 * other + 1], others[2 * other + 1 : 2 * other + 2]
        key_max = jnp.maximum(own_max, other_max)
        own_factor, other_factor = jnp.exp(own_max - key_max), jnp.exp(other_max - key_max)
        inverse_total = 1.0 / (own_total * own_factor + other_total * other_factor)
        scales.append((own_factor * inverse_total, other_factor * inverse_total))
    outs.scales[...] = jnp.concatenate(
        [scales[0][0], scales[1][0], jnp.zeros((6, M), jnp.float32)], axis=0
    )
    landmark_values = ins.keep[0:HD] * scales[0][0] + swap_lanes(got[0:HD]) * scales[0][1]
    mixing_grad = ins.keep[HD : 2 * HD] + swap_lanes(got[HD : 2 * HD])
    inverse = (ins.inverse[0], ins.inverse[1])
    outs.share[0:HD] = split_dot_nt(halves(landmark_values), inverse).astype(jnp.bfloat16)
    values_low = split_dot(halves(mixing_grad), inverse).astype(jnp.bfloat16)
    outs.share[HD : 2 * HD] = values_low
    row_total = jnp.sum(values_low.astype(jnp.float32) * landmark_values, axis=0, keepdims=True)
    outs.share[2 * HD :] = jnp.concatenate(
        [thirds(row_total), jnp.zeros((13, M), jnp.float32)], axis=0
    ).astype(jnp.bfloat16)
    put(outs.share)
    outs.mixing_grad[...] = mixing_grad
    outs.mark_values[...] = landmark_values


def several(*units):
    for unit in units:
        unit()


def out_units(ins, slot, out_ref, lead, share):
    mixing_low, values_low, _ = share
    scale = ins.scales[slot : slot + 1]

    def token_side(index):
        place = slice(index * CHUNK, (index + 1) * CHUNK)
        attended = wide_dot_nt(ins.token_low[place], mixing_low)
        store_chunk(out_ref, (0, *lead), index, attended.astype(jnp.bfloat16))

    def key_side(index):
        place = slice(index * CHUNK, (index + 1) * CHUNK)
        key_plow = (ins.key_exp[place] * scale).astype(jnp.bfloat16)
        value_gradient = wide_dot_nt(key_plow, values_low)
        store_chunk(out_ref, (1, *lead), index, value_gradient.astype(jnp.bfloat16))

    chunks = ins.token_low.shape[0] // CHUNK
    return [
        functools.partial(unit, index) for unit in (token_side, key_side) for index in range(chunks)
    ]


def gradient_units(ins, slot, direct_ref, share):
    score_scale = HD ** (-0.5)
    mixing_low, values_low, row_total = share
    query_sums, key_sums = [], []
    scale = ins.scales[slot : slot + 1]

    def token_side(index):
        place = slice(index * CHUNK, (index + 1) * CHUNK)
        prob = ins.token_prob[slot, place]
        token_grad = wide_dot(chunk_of(ins.vg, 1, slot, index), mixing_low)
        token_sgrad = (
            prob * (token_grad - jnp.sum(token_grad * prob, axis=1, keepdims=True))
        ).astype(jnp.bfloat16)
        direct_ref[slot, 0, place] = wide_dot(token_sgrad, ins.marks[slot, 1]) * score_scale
        key_sums.append(wide_dot(ins.turned[slot, 0, :, place], token_sgrad))

    def key_side(index):
        place = slice(index * CHUNK, (index + 1) * CHUNK)
        key_prob = ins.key_exp[slot, place] * scale
        key_dgrad = wide_dot(chunk_of(ins.vg, 0, slot, index), values_low)
        key_sgrad = (key_prob * (key_dgrad - row_total)).astype(jnp.bfloat16)
        direct_ref[slot, 1, place] = wide_dot(key_sgrad, ins.marks[slot, 0]) * score_scale
        query_sums.append(wide_dot(ins.turned[slot, 1, :, place], key_sgrad))

    chunks = tokens_of(ins.vg) // CHUNK
    units = [
        functools.partial(unit, index) for index in range(chunks) for unit in (key_side, token_side)
    ]
    return units, query_sums, key_sums


def share_parts(ref, swap):
    parts = [ref[0:HD], ref[HD : 2 * HD], joined_thirds(ref[2 * HD :].astype(jnp.float32)[0:3])]
    return [swap_lanes(part) for part in parts] if swap else parts


def gradient_sweep(state, saved, place, beside, last):
    power, growth = state
    pair_ref, weight_ref, growth_ref = saved
    pair = (pair_ref[place, 0], pair_ref[place, 1])
    first = split_dot(pair, halves(power))
    beside()
    square = first[:M] + first[:M].T
    second = split_dot(tuple(x[:M] for x in pair) if last else pair, halves(square))
    beside()
    cube = first[M:].T + second[:M]
    weight = halves(0.25 * (7.0 * square - 15.0 * power - cube))
    if not last:
        fourth = second[M:] + second[M:].T
        power = 0.25 * (13.0 * power - 15.0 * square + 7.0 * cube - fourth)
    left = [growth_ref[place, 0], growth_ref[place, 0], growth_ref[place, 1]]
    right = [weight[0], weight[1], weight[0]]
    if growth is not None:
        grown = halves(growth)
        left += [grown[0], grown[0], grown[1]]
        right += [weight_ref[place, 0], weight_ref[place, 1], weight_ref[place, 0]]
    growth = wide_dot(jnp.concatenate(left, axis=1), jnp.concatenate(right, axis=0))
    return power, growth


def own_gradient_compute(ins, outs, need, put):
    for ref in (ins.mark_prob, ins.factor, ins.mixing_grad, ins.mark_values, ins.share, ins.scales):
        need(ref)
    inverse_grad = split_dot(halves(ins.mixing_grad[...].T), halves(ins.mark_values[...]))
    inverse_grad_halves = halves(inverse_grad)
    outs.inverse_grad[0], outs.inverse_grad[1] = inverse_grad_halves
    toward = split_dot(halves(ins.mark_prob[...]), inverse_grad_halves) * ins.factor[0:1, 0:1]
    state = (0.5 * (toward + toward.T), None)
    units = out_units(ins, 0, outs.out, (), share_parts(ins.share, False))
    work = iter([units[index : index + 2] for index in range(0, len(units), 2)])
    saved = (ins.pair, ins.weight, ins.growth)

    def beside():
        several(*next(work, ()))

    for sweep in range(EARLY_SWEEPS):
        if sweep == 0:
            need(ins.token_low)
        if sweep == 1:
            need(ins.key_exp)
        for ref in saved:
            need(ref, sweep)
        state = gradient_sweep(state, saved, sweep, beside, False)
    outs.state[0], outs.state[1] = state


def other_out_compute(ins, outs, need, put):
    need(ins.got_share)
    need(ins.scales)
    need(ins.token_low)
    units = out_units(ins, 1, outs.out, (1,), share_parts(ins.got_share, True))
    chunks = len(units) // 2
    several(*units[:chunks])
    need()
    several(*units[chunks:])
    outs.out[:, :, 0] = ins.own_out[...]


def gradient_compute(ins, outs, need, put):
    for ref in (ins.state, ins.share, ins.got_share, ins.scales, ins.marks, ins.vg):
        need(ref)
    sides = []
    for slot in range(2):
        share = share_parts(ins.got_share if slot else ins.share, bool(slot))
        sides.append(gradient_units(ins, slot, outs.direct, share))
    units = sides[0][0] + sides[1][0]
    sweeps = PINV_ITERS - EARLY_SWEEPS
    span = -(-len(units) // (2 * sweeps))
    work = iter([units[index : index + span] for index in range(0, len(units), span)])
    saved = (ins.pair, ins.weight, ins.growth)
    state = (ins.state[0], ins.state[1])

    def beside():
        several(*next(work, ()))

    for sweep in range(sweeps):
        if sweep < 2:
            for ref in (ins.key_exp, ins.token_prob, ins.turned):
                need(ref, sweep)
        for ref in saved:
            need(ref, sweep)
        state = gradient_sweep(state, saved, sweep, beside, sweep == sweeps - 1)
    put(outs.direct)
    need()
    growth = state[1]
    mark_prob = ins.mark_prob[...]
    mark_grad = ins.factor[0:1, 0:1] * (
        split_dot_nt(
            (ins.last_growth[0], ins.last_growth[1]), (ins.inverse_grad[0], ins.inverse_grad[1])
        )
        + split_dot(halves(growth + growth.T), halves(mark_prob))
    )
    mark_sgrad = mark_prob * (mark_grad - jnp.sum(mark_grad * mark_prob, axis=1, keepdims=True))

    def marks_dot(left, right):
        left_high, left_low = halves(left)
        return wide_dot(
            jnp.concatenate([left_high, left_low], axis=1), jnp.concatenate([right, right], axis=0)
        )

    own_marks = (
        marks_dot(mark_sgrad, ins.marks[0, 1]),
        marks_dot(mark_sgrad.T, ins.marks[0, 0]),
    )
    marks_scale = HD ** (-0.5) / (tokens_of(ins.vg) // HALF)
    for slot, (_, query_sums, key_sums) in enumerate(sides):
        for kind, sums in enumerate((query_sums, key_sums)):
            total = sum(sums[1:], sums[0]).T
            if slot == 0:
                total = total + own_marks[kind]
            total = total * marks_scale
            outs.far[kind, slot] = total[HALF:].astype(jnp.bfloat16)
            outs.near[kind, slot] = total[:HALF]
    put(outs.far)


def finish_compute(ins, outs, need, put):
    need(ins.near)
    need(ins.got_far)
    out_ref = outs.out
    group = CHUNK // out_ref.shape[3]
    segment_len = tokens_of(out_ref) // HALF
    per = CHUNK // segment_len
    for index in range(tokens_of(out_ref) // CHUNK):
        place, start = slice(index * per, (index + 1) * per), index * CHUNK
        for slot in range(2):
            for kind in range(2):
                if index % 2 == 0:
                    need(ins.direct, slot, kind, start)
                marks = ins.near[kind, slot, place] + ins.got_far[
                    kind, 1 - slot, place
                ].astype(jnp.float32)
                spread = jnp.broadcast_to(marks[:, None], (per, segment_len, HD))
                total = ins.direct[slot, kind, start : start + CHUNK] + spread.reshape(CHUNK, HD)
                store_chunk(out_ref, (kind, slot), index, total.astype(jnp.bfloat16))
        put(out_ref, index * group)


def exchange(packed):
    return lax.all_to_all(packed, "cube", split_axis=0, concat_axis=0, tiled=True)


def partner(array):
    return lax.ppermute(array, "half", SWAP)


def body(queries, keys, values, out_grad):
    half = lax.axis_index("half").reshape(1)
    qk, vg_packed = lax.optimization_barrier(
        (exchange(pack(half, queries, keys)), pack(half, values, out_grad))
    )
    tokens = qk.shape[0] * qk.shape[3]
    mine = landmarks_of(qk)
    theirs = partner(mine)
    vg_packed, mine = lax.optimization_barrier((vg_packed, mine))
    vg = exchange(vg_packed)
    kept = staged_call(
        probability_compute,
        dict(qk=qk, mine=mine, theirs=theirs),
        dict(
            marks=low(2, 2, M, HD),
            token_prob=wide(2, tokens, M),
            token_low=low(2, tokens, M),
            key_exp=wide(2, tokens, M),
            key_low=low(2, tokens, M),
            turned=low(2, 2, HD, tokens),
            stats=wide(8, M),
            mark_prob=wide(M, M),
            factor=wide(8, HD),
            pair_a=(low(EARLY_SWEEPS, 2, 2 * M, M), LEAD),
            weight_a=(low(EARLY_SWEEPS, 2, M, M), LEAD),
            growth_a=(low(EARLY_SWEEPS, 2, M, M), LEAD),
            pair_b=(low(PINV_ITERS - EARLY_SWEEPS, 2, 2 * M, M), LEAD),
            weight_b=(low(PINV_ITERS - EARLY_SWEEPS, 2, M, M), LEAD),
            growth_b=(low(PINV_ITERS - EARLY_SWEEPS, 2, M, M), LEAD),
            inverse=low(2, M, M),
            last_growth=low(2, M, M),
        ),
        LONG,
        extra=(pltpu.VMEM((M, M), jnp.float32), pltpu.VMEM((2 * M, M), jnp.float32)),
    )
    sums = staged_call(
        partial_compute,
        dict(vg=vg, stats=kept.stats, key_low=kept.key_low, token_low=kept.token_low),
        dict(send=low(2 * HD + 16, M), keep=wide(2 * HD, M)),
        2,
    )
    mixed = staged_call(
        mixing_compute,
        dict(got=partner(sums.send), keep=sums.keep, stats=kept.stats, inverse=kept.inverse),
        dict(
            share=low(2 * HD + 16, M),
            scales=wide(8, M),
            mixing_grad=wide(HD, M),
            mark_values=wide(HD, M),
        ),
        1,
    )
    got_share = partner(mixed.share)
    own = staged_call(
        own_gradient_compute,
        dict(
            mark_prob=kept.mark_prob,
            factor=kept.factor,
            mixing_grad=mixed.mixing_grad,
            mark_values=mixed.mark_values,
            share=mixed.share,
            scales=mixed.scales,
            token_low=(kept.token_low, SLOTS[0]),
            pair=(kept.pair_a, LEAD),
            weight=(kept.weight_a, LEAD),
            growth=(kept.growth_a, LEAD),
            key_exp=(kept.key_exp, SLOTS[0]),
        ),
        dict(
            out=low(qk.shape[0], 2, *qk.shape[3:]),
            state=wide(2, M, M),
            inverse_grad=low(2, M, M),
        ),
        8,
    )
    first_results = staged_call(
        other_out_compute,
        dict(
            got_share=got_share,
            scales=mixed.scales,
            token_low=(kept.token_low, SLOTS[1]),
            key_exp=(kept.key_exp, SLOTS[1]),
            own_out=own.out,
        ),
        dict(out=low(*qk.shape)),
        1,
    ).out
    attended, value_gradient_array = unpack(half, exchange(first_results))
    grads = staged_call(
        gradient_compute,
        dict(
            state=own.state,
            share=mixed.share,
            got_share=got_share,
            scales=mixed.scales,
            marks=kept.marks,
            vg=vg,
            pair=(kept.pair_b, LEAD),
            weight=(kept.weight_b, LEAD),
            growth=(kept.growth_b, LEAD),
            key_exp=(kept.key_exp, LEAD),
            token_prob=(kept.token_prob, LEAD),
            turned=(kept.turned, LEAD),
            inverse_grad=own.inverse_grad,
            last_growth=kept.last_growth,
            mark_prob=kept.mark_prob,
            factor=kept.factor,
        ),
        dict(
            far=low(2, 2, HALF, HD),
            near=wide(2, 2, HALF, HD),
            direct=(wide(2, 2, tokens, HD), LEAD),
        ),
        LONG,
        after=(first_results,),
    )
    results = staged_call(
        finish_compute,
        dict(got_far=partner(grads.far), near=grads.near, direct=(grads.direct, BLOCKS)),
        dict(out=(low(*qk.shape), GROUPS)),
        0.1,
    ).out
    query_grad, key_grad = unpack(half, exchange(results))
    return attended, query_grad, key_grad, value_gradient_array


def solution(mesh):
    whole_placement = P(("seq", "head"), None)
    halves_placement = P(("half", "cube"), None)

    def layer(queries, keys, values, out_grad):
        tokens, width = queries.shape
        own_head_each = width // HD == mesh.size and tokens == 8 * CHUNK
        if own_head_each:
            split = jax.sharding.Mesh(
                mesh.devices.reshape(2, mesh.size // 2), ("half", "cube")
            )
        return jax.shard_map(
            body if own_head_each else shared_body,
            mesh=split if own_head_each else mesh,
            in_specs=(halves_placement if own_head_each else whole_placement,) * 4,
            out_specs=(halves_placement if own_head_each else whole_placement,) * 4,
            check_vma=False,
        )(queries, keys, values, out_grad)

    return layer
```

```python
import functools
from types import SimpleNamespace

import jax
import jax.numpy as jnp
from jax import lax
from jax.experimental import pallas as pl
from jax.experimental.pallas import tpu as pltpu
from jax.sharding import PartitionSpec as P

HD = 128
M = 256
PINV_ITERS = 6
CHUNK = 256
PACK_GROUPS = 4
HALF = M // 2
SWAP = ((0, 1), (1, 0))
VMEM_LIMIT = 60 * 2**20
SMALL_LIMIT = 16 * 2**20
WHOLE, LEAD, GROUPS, BLOCKS, LATE, LAST = range(6)
SLOTS = (10, 11)
LONG = 200
EARLY_SWEEPS = PINV_ITERS // 2


precise_setting = lax.Precision.HIGHEST


def newton_inverse(matrix):
    identity = jnp.eye(matrix.shape[0], dtype=matrix.dtype)
    factor = lax.stop_gradient(1.0 / jnp.max(jnp.sum(matrix, axis=0)))
    iterate = matrix.T * factor
    for sweep_index in range(PINV_ITERS):
        product = jnp.matmul(matrix, iterate, precision=precise_setting)
        inner_term = jnp.matmul(product, 7.0 * identity - product, precision=precise_setting)
        inner_term = jnp.matmul(product, 15.0 * identity - inner_term, precision=precise_setting)
        iterate = 0.25 * jnp.matmul(
            iterate, 13.0 * identity - inner_term, precision=precise_setting
        )
    return iterate


def share_heads(own_matrix, head_count):
    seq_index = lax.axis_index("seq")
    slot_mask = (jnp.arange(head_count, dtype=jnp.int32) == seq_index).astype(jnp.float32)
    return lax.psum(slot_mask[:, None, None] * own_matrix[None], "seq")


def shared_body(queries, keys, values, out_grad):
    query_rows, key_rows, value_rows, grad_rows = (
        lax.all_to_all(queries, "head", split_axis=1, concat_axis=0, tiled=True),
        lax.all_to_all(keys, "head", split_axis=1, concat_axis=0, tiled=True),
        lax.all_to_all(values, "head", split_axis=1, concat_axis=0, tiled=True),
        lax.all_to_all(out_grad, "head", split_axis=1, concat_axis=0, tiled=True),
    )
    tok_rows = query_rows.shape[0]
    head_count = query_rows.shape[1] // HD
    local_marks = M // lax.axis_size("seq")
    segment_len = tok_rows // local_marks
    score_scale = HD ** (-0.5)
    seq_index = lax.axis_index("seq")

    def landmark(matrix):
        summed = jnp.sum(
            matrix.reshape(local_marks, segment_len, matrix.shape[1]), axis=1, dtype=jnp.float32
        )
        return (summed / segment_len).astype(jnp.bfloat16)

    mark_queries, mark_keys = (
        lax.all_gather(landmark(query_rows), "seq", axis=0, tiled=True),
        lax.all_gather(landmark(key_rows), "seq", axis=0, tiled=True),
    )
    query_per_head = query_rows.reshape(tok_rows, head_count, HD)
    key_per_head = key_rows.reshape(tok_rows, head_count, HD)
    value_per_head = value_rows.reshape(tok_rows, head_count, HD)
    gradient_per_head = grad_rows.reshape(tok_rows, head_count, HD)
    landmark_query_heads = mark_queries.reshape(M, head_count, HD)
    landmark_key_heads = mark_keys.reshape(M, head_count, HD)
    key_score = (
        jnp.einsum(
            "pcv,gcv->cpg", landmark_query_heads, key_per_head, preferred_element_type=jnp.float32
        )
        * score_scale
    )
    key_max = lax.pmax(jnp.max(key_score, axis=-1), "seq")
    key_exp = jnp.exp(key_score - key_max[..., None])
    partial_num = jnp.einsum(
        "akq,qay->aky",
        key_exp.astype(jnp.bfloat16),
        value_per_head,
        preferred_element_type=jnp.float32,
    )
    key_total, numerator = lax.psum((jnp.sum(key_exp, axis=-1), partial_num), "seq")
    landmark_value_rows = numerator / key_total[..., None]
    token_prob = jax.nn.softmax(
        jnp.einsum(
            "jti,cti->tjc", query_per_head, landmark_key_heads, preferred_element_type=jnp.float32
        )
        * score_scale,
        axis=-1,
    )
    token_probability_lowered = token_prob.astype(jnp.bfloat16)
    mark_prob = jax.nn.softmax(
        jnp.einsum(
            "jou,iou->oji",
            landmark_query_heads,
            landmark_key_heads,
            preferred_element_type=jnp.float32,
        )
        * score_scale,
        axis=-1,
    )
    own_head = seq_index % head_count
    own_mark = lax.dynamic_index_in_dim(mark_prob, own_head, 0, keepdims=False)
    own_inverse, pull_back = jax.vjp(newton_inverse, own_mark)
    pseudo_inverse_matrix = share_heads(own_inverse, head_count)
    mixing_matrix = jnp.einsum(
        "jvy,jys->jvs", pseudo_inverse_matrix, landmark_value_rows, precision=precise_setting
    )
    mixing_matrix_lowered = mixing_matrix.astype(jnp.bfloat16)
    attended = jnp.einsum(
        "yvo,yor->vyr",
        token_probability_lowered,
        mixing_matrix_lowered,
        preferred_element_type=jnp.float32,
    ).astype(jnp.bfloat16)
    token_grad = jnp.einsum(
        "fag,aog->afo", gradient_per_head, mixing_matrix_lowered, preferred_element_type=jnp.float32
    )
    partial_mix = jnp.einsum(
        "klz,lkr->kzr",
        token_probability_lowered,
        gradient_per_head,
        preferred_element_type=jnp.float32,
    )
    mixing_matrix_gradient = lax.psum(partial_mix, "seq")
    token_score_gradient = (
        token_prob * (token_grad - jnp.sum(token_grad * token_prob, axis=-1, keepdims=True))
    ).astype(jnp.bfloat16)
    direct_qgrad = (
        jnp.einsum(
            "ufg,guc->fuc",
            token_score_gradient,
            landmark_key_heads,
            preferred_element_type=jnp.float32,
        )
        * score_scale
    )
    mark_kgrad_f = (
        jnp.einsum(
            "xgi,gxy->ixy", token_score_gradient, query_per_head, preferred_element_type=jnp.float32
        )
        * score_scale
    )
    pseudo_inverse_gradient = jnp.einsum(
        "ktu,kyu->kty", mixing_matrix_gradient, landmark_value_rows, precision=precise_setting
    )
    landmark_value_gradient = jnp.einsum(
        "lrb,lrz->lbz", pseudo_inverse_matrix, mixing_matrix_gradient, precision=precise_setting
    )
    own_igrad = lax.dynamic_index_in_dim(pseudo_inverse_gradient, own_head, 0, keepdims=False)
    (own_mgrad,) = pull_back(own_igrad)
    mark_grad = share_heads(own_mgrad, head_count)
    mark_sgrad = mark_prob * (mark_grad - jnp.sum(mark_grad * mark_prob, axis=-1, keepdims=True))
    first_mark = seq_index * local_marks
    score_gradient_rows = lax.dynamic_slice_in_dim(mark_sgrad, first_mark, local_marks, 1)
    score_gradient_columns = lax.dynamic_slice_in_dim(mark_sgrad, first_mark, local_marks, 2)
    own_qgrad_a = (
        jnp.einsum(
            "txs,ste->xte",
            score_gradient_rows,
            landmark_key_heads.astype(jnp.float32),
            precision=precise_setting,
        )
        * score_scale
    )
    own_kgrad_a = (
        jnp.einsum(
            "eaj,aev->jev",
            score_gradient_columns,
            landmark_query_heads.astype(jnp.float32),
            precision=precise_setting,
        )
        * score_scale
    )
    landmark_value_lowered = landmark_value_gradient.astype(jnp.bfloat16)
    key_prob = key_exp / key_total[..., None]
    key_probability_lowered = key_prob.astype(jnp.bfloat16)
    value_gradient_array = jnp.einsum(
        "zct,zcj->tzj",
        key_probability_lowered,
        landmark_value_lowered,
        preferred_element_type=jnp.float32,
    )
    key_direct_gradient = jnp.einsum(
        "exb,geb->exg", landmark_value_lowered, value_per_head, preferred_element_type=jnp.float32
    )
    row_total = lax.psum(jnp.sum(key_prob * key_direct_gradient, axis=-1), "seq")
    key_score_gradient = (key_prob * (key_direct_gradient - row_total[..., None])).astype(
        jnp.bfloat16
    )
    direct_kgrad = (
        jnp.einsum(
            "pbo,bpx->opx",
            key_score_gradient,
            landmark_query_heads,
            preferred_element_type=jnp.float32,
        )
        * score_scale
    )
    mark_qgrad_b = (
        jnp.einsum(
            "cbj,jcp->bcp", key_score_gradient, key_per_head, preferred_element_type=jnp.float32
        )
        * score_scale
    )
    own_kgrad_f, own_qgrad_b = (
        lax.psum_scatter(mark_kgrad_f, "seq", scatter_dimension=0, tiled=True),
        lax.psum_scatter(mark_qgrad_b, "seq", scatter_dimension=0, tiled=True),
    )
    mark_qtotal = (own_qgrad_a + own_qgrad_b) / segment_len
    mark_ktotal = (own_kgrad_a + own_kgrad_f) / segment_len
    query_grad = (
        direct_qgrad.reshape(local_marks, segment_len, head_count, HD) + mark_qtotal[:, None]
    )
    key_grad = direct_kgrad.reshape(local_marks, segment_len, head_count, HD) + mark_ktotal[:, None]
    width = head_count * HD
    results = (
        attended.reshape(tok_rows, width),
        query_grad.astype(jnp.bfloat16).reshape(tok_rows, width),
        key_grad.astype(jnp.bfloat16).reshape(tok_rows, width),
        value_gradient_array.astype(jnp.bfloat16).reshape(tok_rows, width),
    )
    attended_out, query_out, key_out, value_out = (
        lax.all_to_all(results[0], "head", split_axis=0, concat_axis=1, tiled=True),
        lax.all_to_all(results[1], "head", split_axis=0, concat_axis=1, tiled=True),
        lax.all_to_all(results[2], "head", split_axis=0, concat_axis=1, tiled=True),
        lax.all_to_all(results[3], "head", split_axis=0, concat_axis=1, tiled=True),
    )
    return (attended_out, query_out, key_out, value_out)


def halves(matrix):
    high = matrix.astype(jnp.bfloat16)
    return high, (matrix - high.astype(jnp.float32)).astype(jnp.bfloat16)


def wide_dot(left, right):
    return jnp.dot(left, right, preferred_element_type=jnp.float32)


def wide_dot_nt(left, right):
    return lax.dot_general(
        left, right, (((1,), (1,)), ((), ())), preferred_element_type=jnp.float32
    )


def split_dot(left, right):
    left_high, left_low = left
    right_high, right_low = right
    return wide_dot(
        jnp.concatenate([left_high, left_high, left_low], axis=1),
        jnp.concatenate([right_high, right_low, right_high], axis=0),
    )


def split_dot_nt(left, right):
    left_high, left_low = left
    right_high, right_low = right
    return wide_dot_nt(
        jnp.concatenate([left_high, left_high, left_low], axis=1),
        jnp.concatenate([right_high, right_low, right_high], axis=1),
    )


def identity_matrix():
    return (
        lax.broadcasted_iota(jnp.int32, (M, M), 0) == lax.broadcasted_iota(jnp.int32, (M, M), 1)
    ).astype(jnp.float32)


def chunk_of(ref, array, slot, index):
    per = CHUNK // ref.shape[3]
    return ref[index * per : (index + 1) * per, array, slot].reshape(CHUNK, HD)


def store_chunk(ref, lead, index, value):
    rows = ref.shape[-2]
    per = CHUNK // rows
    ref[(slice(index * per, (index + 1) * per), *lead)] = value.reshape(per, rows, HD)


def all_tokens(ref, array, slot):
    return ref[:, array, slot].reshape(ref.shape[0] * ref.shape[3], HD)


def tokens_of(ref):
    return ref.shape[0] * ref.shape[3]


def columns(index):
    return pl.ds(pl.multiple_of(index * CHUNK, CHUNK), CHUNK)


def swap_lanes(matrix):
    return jnp.concatenate([matrix[:, HALF:], matrix[:, :HALF]], axis=1)


def thirds(rows):
    first = rows.astype(jnp.bfloat16).astype(jnp.float32)
    second = (rows - first).astype(jnp.bfloat16).astype(jnp.float32)
    return jnp.concatenate([first, second, rows - first - second], axis=0)


def joined_thirds(rows):
    count = rows.shape[0] // 3
    return rows[:count] + (rows[count : 2 * count] + rows[2 * count :])


def held_shape(kind, shape):
    return shape[1:] if kind in SLOTS else shape


def pieces_of(kind, shape):
    if kind == LEAD:
        return [(index,) for index in range(shape[0])]
    if kind == BLOCKS:
        return [
            (first, second, slice(place, place + 2 * CHUNK))
            for place in range(0, shape[2], 2 * CHUNK)
            for first in range(shape[0])
            for second in range(shape[1])
        ]
    if kind == GROUPS:
        per = CHUNK // shape[-2]
        return [(slice(place, place + per),) for place in range(0, shape[0], per)]
    return [()]


def window(ref, piece):
    place = tuple(
        pl.ds(part.start, part.stop - part.start) if isinstance(part, slice) else part
        for part in piece
    )
    return ref.at[place] if place else ref


class Staged:
    def __init__(self, names, kinds, outer, inner, done, outward):
        self.refs = SimpleNamespace(**dict(zip(names, inner)))
        self.copies, self.order = [], []
        count = 0
        steps = []
        for place, (kind, home, held) in enumerate(zip(kinds, outer, inner)):
            home = home.at[kind - SLOTS[0]] if kind in SLOTS else home
            copies = {}
            for step, piece in enumerate(pieces_of(kind, held.shape)):
                ends = (window(held, piece), window(home, piece))
                source, target = ends if outward else ends[::-1]
                key = tuple(
                    part.start if isinstance(part, slice) else part for part in piece
                )
                copies[key] = pltpu.make_async_copy(source, target, done.at[count])
                steps.append(({WHOLE: -1, LAST: 9}.get(kind, step), place, key))
                count += 1
            self.copies.append(copies)
        self.inner = inner
        self.order = sorted(steps, key=lambda item: item[:2])
        self.started, self.waited = set(), set()

    def place_of(self, ref):
        return next(index for index, held in enumerate(self.inner) if held is ref)

    def start(self, ref=None, *key):
        chosen = [
            (place, name)
            for _, place, name in self.order
            if (ref is None or place == self.place_of(ref)) and (not key or name == key)
        ]
        for item in chosen:
            if item not in self.started:
                self.started.add(item)
                self.copies[item[0]][item[1]].start()

    def wait(self, ref=None, *key):
        chosen = [
            (place, name)
            for _, place, name in self.order
            if (ref is None or place == self.place_of(ref)) and (not key or name == key)
        ]
        for item in chosen:
            if item not in self.waited:
                self.waited.add(item)
                self.copies[item[0]][item[1]].wait()


def staged_call(compute, inputs, outputs, flops, extra=(), after=(), in_place=False):
    names_in, names_out = tuple(inputs), tuple(outputs)
    kinds_in = [x[1] if isinstance(x, tuple) else WHOLE for x in inputs.values()]
    kinds_out = [x[1] if isinstance(x, tuple) else WHOLE for x in outputs.values()]
    operands = tuple(x[0] if isinstance(x, tuple) else x for x in inputs.values())
    shapes = tuple(x[0] if isinstance(x, tuple) else x for x in outputs.values())
    n_in, n_out, n_after = len(operands), len(shapes), len(after)
    moved = sum(x.size * x.dtype.itemsize for x in (*operands, *shapes))
    anywhere = pl.BlockSpec(memory_space=pl.ANY)

    def count(kinds, arrays):
        return sum(len(pieces_of(kind, x.shape)) for kind, x in zip(kinds, arrays))

    def kernel(*refs):
        sources, refs = refs[:n_in], refs[n_in + n_after :]
        homes, refs = refs[:n_out], refs[n_out:]
        held_in, held_out = refs[:n_in], refs[n_in : n_in + n_out]
        *scratch, in_done, out_done = refs[n_in + n_out :]
        reads = Staged(names_in, kinds_in, sources, held_in, in_done, False)
        writes = Staged(names_out, kinds_out, homes, held_out, out_done, True)
        reads.start()
        compute(reads.refs, writes.refs, reads.wait, writes.start, *scratch)
        reads.wait()
        writes.start()
        writes.wait()

    results = pl.pallas_call(
        kernel,
        out_shape=shapes,
        in_specs=[anywhere] * (n_in + n_after),
        out_specs=(anywhere,) * n_out,
        scratch_shapes=[
            *(
                pltpu.VMEM(held_shape(kind, x.shape), x.dtype)
                for kind, x in zip((*kinds_in, *kinds_out), (*operands, *shapes))
            ),
            *extra,
            pltpu.SemaphoreType.DMA((count(kinds_in, operands),)),
            pltpu.SemaphoreType.DMA((count(kinds_out, shapes),)),
        ],
        compiler_params=pltpu.CompilerParams(vmem_limit_bytes=VMEM_LIMIT),
        cost_estimate=pl.CostEstimate(
            flops=int(flops * 10**9), bytes_accessed=moved, transcendentals=0
        ),
    )(*operands, *after)
    return SimpleNamespace(**dict(zip(outputs, results)))


def low(*shape):
    return jax.ShapeDtypeStruct(shape, jnp.bfloat16)


def wide(*shape):
    return jax.ShapeDtypeStruct(shape, jnp.float32)


def pack_kernel(half_ref, first_ref, second_ref, out_ref, rows_s, packed_s, in_done, out_done):
    half = half_ref[0]
    pairs = out_ref.shape[0]
    group = pairs // PACK_GROUPS
    span = 2 * HD
    reads, writes = [], []
    for index in range(PACK_GROUPS):
        for array, ref in enumerate((first_ref, second_ref)):
            place = pl.ds(index * group * span, group * span)
            reads.append(
                pltpu.make_async_copy(
                    ref.at[:, place], rows_s.at[array, :, place], in_done.at[array, index]
                )
            )
        place = pl.ds(index * group, group)
        writes.append(
            pltpu.make_async_copy(packed_s.at[place], out_ref.at[place], out_done.at[index])
        )
    for copy in reads:
        copy.start()
    for index in range(PACK_GROUPS):
        for array in range(2):
            reads[2 * index + array].wait()
            for pair in range(index * group, (index + 1) * group):
                start = pair * span
                packed_s[pair, array, half] = rows_s[array, :, start : start + HD]
                packed_s[pair, array, 1 - half] = rows_s[array, :, start + HD : start + span]
        writes[index].start()
    for copy in writes:
        copy.wait()


def unpack_kernel(half_ref, packed_ref, first_ref, second_ref, rows_s, out_done):
    half = half_ref[0]
    pairs = packed_ref.shape[0]
    group = pairs // PACK_GROUPS
    span = 2 * HD
    writes = []
    for index in range(PACK_GROUPS):
        for array, ref in enumerate((first_ref, second_ref)):
            for pair in range(index * group, (index + 1) * group):
                start = pair * span
                rows_s[array, :, start : start + HD] = packed_ref[pair, array, half]
                rows_s[array, :, start + HD : start + span] = packed_ref[pair, array, 1 - half]
            place = pl.ds(index * group * span, group * span)
            write = pltpu.make_async_copy(
                rows_s.at[array, :, place], ref.at[:, place], out_done.at[array, index]
            )
            write.start()
            writes.append(write)
    for copy in writes:
        copy.wait()


def layout_call(kernel, half, operands, out_shape, scratch, in_space, limit):
    anywhere = pl.BlockSpec(memory_space=pl.ANY)
    moved = 2 * sum(x.size * x.dtype.itemsize for x in operands)
    return pl.pallas_call(
        kernel,
        out_shape=out_shape,
        in_specs=[pl.BlockSpec(memory_space=pltpu.SMEM)]
        + [pl.BlockSpec(memory_space=in_space)] * len(operands),
        out_specs=jax.tree.map(lambda _: anywhere, out_shape),
        scratch_shapes=scratch,
        compiler_params=pltpu.CompilerParams(vmem_limit_bytes=limit),
        cost_estimate=pl.CostEstimate(flops=0, bytes_accessed=moved, transcendentals=0),
    )(half, *operands)


def pack(half, first, second):
    rows, width = first.shape
    shape = low(width // (2 * HD), 2, 2, rows, HD)
    scratch = [
        pltpu.VMEM((2, rows, width), jnp.bfloat16),
        pltpu.VMEM(shape.shape, jnp.bfloat16),
        pltpu.SemaphoreType.DMA((2, PACK_GROUPS)),
        pltpu.SemaphoreType.DMA((PACK_GROUPS,)),
    ]
    return layout_call(
        pack_kernel, half, (first, second), shape, scratch, pl.ANY, VMEM_LIMIT
    )


def unpack(half, packed):
    pairs, _, _, rows, _ = packed.shape
    shape = low(rows, pairs * 2 * HD)
    scratch = [
        pltpu.VMEM((2, *shape.shape), jnp.bfloat16),
        pltpu.SemaphoreType.DMA((2, PACK_GROUPS)),
    ]
    return layout_call(
        unpack_kernel, half, (packed,), (shape, shape), scratch, pltpu.VMEM, SMALL_LIMIT
    )


def landmark_kernel(qk_ref, marks_ref):
    tokens = tokens_of(qk_ref)
    segment_len = tokens // HALF
    per = CHUNK // segment_len
    member = (
        lax.broadcasted_iota(jnp.int32, (per, CHUNK), 1) // segment_len
        == lax.broadcasted_iota(jnp.int32, (per, CHUNK), 0)
    ).astype(jnp.bfloat16)
    kinds = [(slot, array) for slot in range(2) for array in range(2)]
    for index in range(tokens // CHUNK):
        parts = [chunk_of(qk_ref, array, slot, index) for slot, array in kinds]
        summed = wide_dot(member, jnp.concatenate(parts, axis=1))
        mean = (summed / segment_len).astype(jnp.bfloat16)
        for place, (slot, array) in enumerate(kinds):
            marks_ref[slot, array, index * per : (index + 1) * per] = mean[
                :, place * HD : (place + 1) * HD
            ]


def landmarks_of(qk):
    held = pl.BlockSpec(memory_space=pltpu.VMEM)
    return pl.pallas_call(
        landmark_kernel,
        out_shape=low(2, 2, HALF, HD),
        in_specs=[held],
        out_specs=held,
        compiler_params=pltpu.CompilerParams(vmem_limit_bytes=SMALL_LIMIT),
        cost_estimate=pl.CostEstimate(
            flops=2 * 10**8, bytes_accessed=qk.size * 2, transcendentals=0
        ),
    )(qk)


def sweep_forward(power_s, iterate_s, saved, sweep, work):
    pair_ref, weight_ref, growth_ref = saved
    power = power_s[...]
    power_high, power_low = halves(power)
    square = split_dot((power_high, power_low), (power_high, power_low))
    next(work)()
    square_halves = halves(square)
    pair = (
        jnp.concatenate([power_high, square_halves[0]], axis=0),
        jnp.concatenate([power_low, square_halves[1]], axis=0),
    )
    pair_ref[sweep, 0], pair_ref[sweep, 1] = pair
    higher = split_dot(pair, square_halves)
    next(work)()
    cube, fourth = higher[:M], higher[M:]
    weight = halves(0.25 * (13.0 * identity_matrix() - 15.0 * power + 7.0 * square - cube))
    power_s[...] = 0.25 * (13.0 * power - 15.0 * square + 7.0 * cube - fourth)
    weight_ref[sweep, 0], weight_ref[sweep, 1] = weight
    iterate = halves(iterate_s[...])
    growth_ref[sweep, 0], growth_ref[sweep, 1] = iterate[0][M:], iterate[1][M:]
    iterate_s[...] = split_dot(iterate, weight)


def probability_compute(ins, outs, need, put, power_s, iterate_s):
    need()
    qk_ref = ins.qk
    chunks = tokens_of(qk_ref) // CHUNK
    score_scale = HD ** (-0.5)
    for slot in range(2):
        for array in range(2):
            outs.marks[slot, array] = jnp.concatenate(
                [ins.mine[slot, array], ins.theirs[1 - slot, array]], axis=0
            )
    put(outs.marks)
    landmark_q, landmark_k = outs.marks[0, 0], outs.marks[0, 1]
    mark_score = wide_dot_nt(landmark_q, landmark_k) * score_scale
    mark_exp = jnp.exp(mark_score - jnp.max(mark_score, axis=1, keepdims=True))
    mark_prob = mark_exp / jnp.sum(mark_exp, axis=1, keepdims=True)
    outs.mark_prob[...] = mark_prob
    factor = 1.0 / jnp.max(jnp.sum(mark_prob, axis=0, keepdims=True), axis=1, keepdims=True)
    outs.factor[...] = jnp.broadcast_to(factor, outs.factor.shape)
    mark_halves = halves(mark_prob)
    power_s[...] = split_dot_nt(mark_halves, mark_halves) * factor
    iterate_s[0:M] = mark_prob.T * factor
    iterate_s[M:] = identity_matrix()
    tops, totals = [[], []], [[], []]

    def scores(slot, index):
        query_chunk, key_chunk = (chunk_of(qk_ref, array, slot, index) for array in range(2))
        place = slice(index * CHUNK, (index + 1) * CHUNK)
        outs.turned[slot, 0, :, place] = query_chunk.T
        outs.turned[slot, 1, :, place] = key_chunk.T
        score = wide_dot_nt(query_chunk, outs.marks[slot, 1]) * score_scale
        grown = jnp.exp(score - jnp.max(score, axis=1, keepdims=True))
        prob = grown * (1.0 / jnp.sum(grown, axis=1, keepdims=True))
        outs.token_prob[slot, place] = prob
        outs.token_low[slot, place] = prob.astype(jnp.bfloat16)
        key_score = wide_dot_nt(key_chunk, outs.marks[slot, 0]) * score_scale
        outs.key_exp[slot, place] = key_score
        tops[slot].append(jnp.max(key_score, axis=0, keepdims=True))

    def grow(slot, index):
        if index == 0:
            tops[slot] = functools.reduce(jnp.maximum, tops[slot])
        place = slice(index * CHUNK, (index + 1) * CHUNK)
        grown = jnp.exp(outs.key_exp[slot, place] - tops[slot])
        outs.key_exp[slot, place] = grown
        outs.key_low[slot, place] = grown.astype(jnp.bfloat16)
        totals[slot].append(jnp.sum(grown, axis=0, keepdims=True))

    def several(unit, pairs):
        for slot, index in pairs:
            unit(slot, index)

    pairs = [(slot, index) for slot in range(2) for index in range(chunks)]
    work = iter(
        [functools.partial(several, scores, [pair]) for pair in pairs]
        + [
            functools.partial(several, grow, pairs[first : first + 2])
            for first in range(0, len(pairs), 2)
        ]
    )
    for sweep in range(PINV_ITERS):
        first = sweep < EARLY_SWEEPS
        place = sweep if first else sweep - EARLY_SWEEPS
        saved = (
            (outs.pair_a, outs.weight_a, outs.growth_a)
            if first
            else (outs.pair_b, outs.weight_b, outs.growth_b)
        )
        sweep_forward(power_s, iterate_s, saved, place, work)
        for ref in saved:
            put(ref, place)
        if sweep == 3:
            for ref in (outs.token_low, outs.token_prob, outs.turned):
                put(ref)
    put(outs.key_low)
    put(outs.key_exp)
    outs.inverse[0], outs.inverse[1] = halves(iterate_s[0:M])
    outs.last_growth[0], outs.last_growth[1] = halves(iterate_s[M:])
    stats = [x for slot in range(2) for x in (tops[slot], sum(totals[slot][1:], totals[slot][0]))]
    outs.stats[0:4] = jnp.concatenate(stats, axis=0)
    outs.stats[4:8] = jnp.zeros((4, M), jnp.float32)


def partial_compute(ins, outs, need, put):
    need(ins.vg)
    turned = [[all_tokens(ins.vg, array, slot).T for array in range(2)] for slot in range(2)]
    need(ins.stats)
    rows = thirds(ins.stats[0:4])
    outs.send[2 * HD :] = jnp.concatenate([rows, jnp.zeros((4, M), jnp.float32)], axis=0).astype(
        jnp.bfloat16
    )
    for slot, home in enumerate((outs.keep, outs.send)):
        need(ins.key_low, slot)
        home[0:HD] = wide_dot(turned[slot][0], ins.key_low[slot]).astype(home.dtype)
        need(ins.token_low, slot)
        home[HD : 2 * HD] = wide_dot(turned[slot][1], ins.token_low[slot]).astype(home.dtype)
        put(home)


def mixing_compute(ins, outs, need, put):
    need()
    got = ins.got[...].astype(jnp.float32)
    others = swap_lanes(joined_thirds(got[2 * HD : 2 * HD + 12]))
    scales = []
    for slot in range(2):
        own_max, own_total = ins.stats[2 * slot : 2 * slot + 1], ins.stats[2 * slot + 1 : 2 * slot + 2]
        other = 1 - slot
        other_max, other_total = others[2 * other : 2 * other + 1], others[2 * other + 1 : 2 * other + 2]
        key_max = jnp.maximum(own_max, other_max)
        own_factor, other_factor = jnp.exp(own_max - key_max), jnp.exp(other_max - key_max)
        inverse_total = 1.0 / (own_total * own_factor + other_total * other_factor)
        scales.append((own_factor * inverse_total, other_factor * inverse_total))
    outs.scales[...] = jnp.concatenate(
        [scales[0][0], scales[1][0], jnp.zeros((6, M), jnp.float32)], axis=0
    )
    landmark_values = ins.keep[0:HD] * scales[0][0] + swap_lanes(got[0:HD]) * scales[0][1]
    mixing_grad = ins.keep[HD : 2 * HD] + swap_lanes(got[HD : 2 * HD])
    inverse = (ins.inverse[0], ins.inverse[1])
    outs.share[0:HD] = split_dot_nt(halves(landmark_values), inverse).astype(jnp.bfloat16)
    values_low = split_dot(halves(mixing_grad), inverse).astype(jnp.bfloat16)
    outs.share[HD : 2 * HD] = values_low
    row_total = jnp.sum(values_low.astype(jnp.float32) * landmark_values, axis=0, keepdims=True)
    outs.share[2 * HD :] = jnp.concatenate(
        [thirds(row_total), jnp.zeros((13, M), jnp.float32)], axis=0
    ).astype(jnp.bfloat16)
    put(outs.share)
    outs.mixing_grad[...] = mixing_grad
    outs.mark_values[...] = landmark_values


def several(*units):
    for unit in units:
        unit()


def out_units(ins, slot, out_ref, lead, share):
    mixing_low, values_low, _ = share
    scale = ins.scales[slot : slot + 1]

    def token_side(index):
        place = slice(index * CHUNK, (index + 1) * CHUNK)
        attended = wide_dot_nt(ins.token_low[place], mixing_low)
        store_chunk(out_ref, (0, *lead), index, attended.astype(jnp.bfloat16))

    def key_side(index):
        place = slice(index * CHUNK, (index + 1) * CHUNK)
        key_plow = (ins.key_exp[place] * scale).astype(jnp.bfloat16)
        value_gradient = wide_dot_nt(key_plow, values_low)
        store_chunk(out_ref, (1, *lead), index, value_gradient.astype(jnp.bfloat16))

    chunks = ins.token_low.shape[0] // CHUNK
    return [
        functools.partial(unit, index) for unit in (token_side, key_side) for index in range(chunks)
    ]


def gradient_units(ins, slot, direct_ref, share):
    score_scale = HD ** (-0.5)
    mixing_low, values_low, row_total = share
    query_sums, key_sums = [], []
    scale = ins.scales[slot : slot + 1]

    def token_side(index):
        place = slice(index * CHUNK, (index + 1) * CHUNK)
        prob = ins.token_prob[slot, place]
        token_grad = wide_dot(chunk_of(ins.vg, 1, slot, index), mixing_low)
        token_sgrad = (
            prob * (token_grad - jnp.sum(token_grad * prob, axis=1, keepdims=True))
        ).astype(jnp.bfloat16)
        direct_ref[slot, 0, place] = wide_dot(token_sgrad, ins.marks[slot, 1]) * score_scale
        key_sums.append(wide_dot(ins.turned[slot, 0, :, place], token_sgrad))

    def key_side(index):
        place = slice(index * CHUNK, (index + 1) * CHUNK)
        key_prob = ins.key_exp[slot, place] * scale
        key_dgrad = wide_dot(chunk_of(ins.vg, 0, slot, index), values_low)
        key_sgrad = (key_prob * (key_dgrad - row_total)).astype(jnp.bfloat16)
        direct_ref[slot, 1, place] = wide_dot(key_sgrad, ins.marks[slot, 0]) * score_scale
        query_sums.append(wide_dot(ins.turned[slot, 1, :, place], key_sgrad))

    chunks = tokens_of(ins.vg) // CHUNK
    units = [
        [functools.partial(unit, index) for index in range(chunks)] for unit in (key_side, token_side)
    ]
    return units, query_sums, key_sums


def share_parts(ref, swap):
    parts = [ref[0:HD], ref[HD : 2 * HD], joined_thirds(ref[2 * HD :].astype(jnp.float32)[0:3])]
    return [swap_lanes(part) for part in parts] if swap else parts


def gradient_sweep(state, saved, place, beside, last):
    power, growth = state
    pair_ref, weight_ref, growth_ref = saved
    pair = (pair_ref[place, 0], pair_ref[place, 1])
    first = split_dot(pair, halves(power))
    beside()
    square = first[:M] + first[:M].T
    second = split_dot(tuple(x[:M] for x in pair) if last else pair, halves(square))
    beside()
    cube = first[M:].T + second[:M]
    weight = halves(0.25 * (7.0 * square - 15.0 * power - cube))
    if not last:
        fourth = second[M:] + second[M:].T
        power = 0.25 * (13.0 * power - 15.0 * square + 7.0 * cube - fourth)
    left = [growth_ref[place, 0], growth_ref[place, 0], growth_ref[place, 1]]
    right = [weight[0], weight[1], weight[0]]
    if growth is not None:
        grown = halves(growth)
        left += [grown[0], grown[0], grown[1]]
        right += [weight_ref[place, 0], weight_ref[place, 1], weight_ref[place, 0]]
    growth = wide_dot(jnp.concatenate(left, axis=1), jnp.concatenate(right, axis=0))
    return power, growth


def own_gradient_compute(ins, outs, need, put):
    for ref in (ins.mark_prob, ins.factor, ins.mixing_grad, ins.mark_values, ins.share, ins.scales):
        need(ref)
    inverse_grad = split_dot(halves(ins.mixing_grad[...].T), halves(ins.mark_values[...]))
    inverse_grad_halves = halves(inverse_grad)
    outs.inverse_grad[0], outs.inverse_grad[1] = inverse_grad_halves
    toward = split_dot(halves(ins.mark_prob[...]), inverse_grad_halves) * ins.factor[0:1, 0:1]
    state = (0.5 * (toward + toward.T), None)
    units = out_units(ins, 0, outs.out, (), share_parts(ins.share, False))
    work = iter([units[index : index + 2] for index in range(0, len(units), 2)])
    saved = (ins.pair, ins.weight, ins.growth)

    def beside():
        several(*next(work, ()))

    for sweep in range(EARLY_SWEEPS):
        if sweep == 0:
            need(ins.token_low)
        if sweep == 1:
            need(ins.key_exp)
        for ref in saved:
            need(ref, sweep)
        state = gradient_sweep(state, saved, sweep, beside, False)
    outs.state[0], outs.state[1] = state


def other_out_compute(ins, outs, need, put):
    for ref in (ins.got_share, ins.scales, ins.token_low):
        need(ref)
    units = out_units(ins, 1, outs.out, (1,), share_parts(ins.got_share, True))
    chunks = len(units) // 2
    several(*units[:chunks])
    need()
    group = CHUNK // outs.out.shape[3]
    for index, unit in enumerate(units[chunks:]):
        unit()
        place = slice(index * group, (index + 1) * group)
        outs.out[place, :, 0] = ins.own_out[place]
        put(outs.out, index * group)


def gradient_compute(ins, outs, need, put):
    for ref in (ins.state, ins.share, ins.got_share, ins.scales, ins.marks):
        need(ref)
    sides = []
    for slot in range(2):
        share = share_parts(ins.got_share if slot else ins.share, bool(slot))
        sides.append(gradient_units(ins, slot, outs.direct, share))
    units = [
        (slot, kind, unit)
        for slot in range(2)
        for kind, side in enumerate(sides[slot][0])
        for unit in side
    ]
    sweeps = PINV_ITERS - EARLY_SWEEPS
    span = -(-len(units) // (2 * sweeps))
    work = iter([units[index : index + span] for index in range(0, len(units), span)])
    saved = (ins.pair, ins.weight, ins.growth)
    state = (ins.state[0], ins.state[1])

    def beside():
        for slot, kind, unit in next(work, ()):
            need(ins.vg)
            need(ins.turned, slot)
            need(ins.token_prob if kind else ins.key_exp, slot)
            unit()

    for sweep in range(sweeps):
        for ref in saved:
            need(ref, sweep)
        state = gradient_sweep(state, saved, sweep, beside, sweep == sweeps - 1)
    put(outs.direct)
    need()
    growth = state[1]
    mark_prob = ins.mark_prob[...]
    mark_grad = ins.factor[0:1, 0:1] * (
        split_dot_nt(
            (ins.last_growth[0], ins.last_growth[1]), (ins.inverse_grad[0], ins.inverse_grad[1])
        )
        + split_dot(halves(growth + growth.T), halves(mark_prob))
    )
    mark_sgrad = mark_prob * (mark_grad - jnp.sum(mark_grad * mark_prob, axis=1, keepdims=True))

    def marks_dot(left, right):
        left_high, left_low = halves(left)
        return wide_dot(
            jnp.concatenate([left_high, left_low], axis=1), jnp.concatenate([right, right], axis=0)
        )

    own_marks = (
        marks_dot(mark_sgrad, ins.marks[0, 1]),
        marks_dot(mark_sgrad.T, ins.marks[0, 0]),
    )
    marks_scale = HD ** (-0.5) / (tokens_of(ins.vg) // HALF)
    for slot, (_, query_sums, key_sums) in enumerate(sides):
        for kind, sums in enumerate((query_sums, key_sums)):
            total = sum(sums[1:], sums[0]).T
            if slot == 0:
                total = total + own_marks[kind]
            total = total * marks_scale
            outs.far[kind, slot] = total[HALF:].astype(jnp.bfloat16)
            outs.near[kind, slot] = total[:HALF]
    put(outs.far)


def finish_compute(ins, outs, need, put):
    need(ins.near)
    need(ins.got_far)
    out_ref = outs.out
    group = CHUNK // out_ref.shape[3]
    segment_len = tokens_of(out_ref) // HALF
    per = CHUNK // segment_len
    for index in range(tokens_of(out_ref) // CHUNK):
        place, start = slice(index * per, (index + 1) * per), index * CHUNK
        for slot in range(2):
            for kind in range(2):
                if index % 2 == 0:
                    need(ins.direct, slot, kind, start)
                marks = ins.near[kind, slot, place] + ins.got_far[
                    kind, 1 - slot, place
                ].astype(jnp.float32)
                spread = jnp.broadcast_to(marks[:, None], (per, segment_len, HD))
                total = ins.direct[slot, kind, start : start + CHUNK] + spread.reshape(CHUNK, HD)
                store_chunk(out_ref, (kind, slot), index, total.astype(jnp.bfloat16))
        put(out_ref, index * group)


def exchange(packed):
    return lax.all_to_all(packed, "cube", split_axis=0, concat_axis=0, tiled=True)


def partner(array):
    return lax.ppermute(array, "half", SWAP)


def body(queries, keys, values, out_grad):
    half = lax.axis_index("half").reshape(1)
    qk, vg_packed = lax.optimization_barrier(
        (exchange(pack(half, queries, keys)), pack(half, values, out_grad))
    )
    tokens = qk.shape[0] * qk.shape[3]
    mine = landmarks_of(qk)
    theirs = partner(mine)
    vg_packed, mine = lax.optimization_barrier((vg_packed, mine))
    vg = exchange(vg_packed)
    kept = staged_call(
        probability_compute,
        dict(qk=qk, mine=mine, theirs=theirs),
        dict(
            marks=low(2, 2, M, HD),
            token_prob=wide(2, tokens, M),
            token_low=low(2, tokens, M),
            key_exp=wide(2, tokens, M),
            key_low=low(2, tokens, M),
            turned=low(2, 2, HD, tokens),
            stats=wide(8, M),
            mark_prob=wide(M, M),
            factor=wide(8, HD),
            pair_a=(low(EARLY_SWEEPS, 2, 2 * M, M), LEAD),
            weight_a=(low(EARLY_SWEEPS, 2, M, M), LEAD),
            growth_a=(low(EARLY_SWEEPS, 2, M, M), LEAD),
            pair_b=(low(PINV_ITERS - EARLY_SWEEPS, 2, 2 * M, M), LEAD),
            weight_b=(low(PINV_ITERS - EARLY_SWEEPS, 2, M, M), LEAD),
            growth_b=(low(PINV_ITERS - EARLY_SWEEPS, 2, M, M), LEAD),
            inverse=low(2, M, M),
            last_growth=low(2, M, M),
        ),
        LONG,
        extra=(pltpu.VMEM((M, M), jnp.float32), pltpu.VMEM((2 * M, M), jnp.float32)),
    )
    sums = staged_call(
        partial_compute,
        dict(
            vg=vg,
            stats=kept.stats,
            key_low=(kept.key_low, LEAD),
            token_low=(kept.token_low, LEAD),
        ),
        dict(send=low(2 * HD + 16, M), keep=wide(2 * HD, M)),
        2,
    )
    mixed = staged_call(
        mixing_compute,
        dict(got=partner(sums.send), keep=sums.keep, stats=kept.stats, inverse=kept.inverse),
        dict(
            share=low(2 * HD + 16, M),
            scales=wide(8, M),
            mixing_grad=wide(HD, M),
            mark_values=wide(HD, M),
        ),
        1,
    )
    got_share = partner(mixed.share)
    own = staged_call(
        own_gradient_compute,
        dict(
            mark_prob=kept.mark_prob,
            factor=kept.factor,
            mixing_grad=mixed.mixing_grad,
            mark_values=mixed.mark_values,
            share=mixed.share,
            scales=mixed.scales,
            token_low=(kept.token_low, SLOTS[0]),
            pair=(kept.pair_a, LEAD),
            weight=(kept.weight_a, LEAD),
            growth=(kept.growth_a, LEAD),
            key_exp=(kept.key_exp, SLOTS[0]),
        ),
        dict(
            out=low(qk.shape[0], 2, *qk.shape[3:]),
            state=wide(2, M, M),
            inverse_grad=low(2, M, M),
        ),
        8,
    )
    first_results = staged_call(
        other_out_compute,
        dict(
            got_share=got_share,
            scales=mixed.scales,
            token_low=(kept.token_low, SLOTS[1]),
            key_exp=(kept.key_exp, SLOTS[1]),
            own_out=own.out,
        ),
        dict(out=(low(*qk.shape), GROUPS)),
        1,
    ).out
    attended, value_gradient_array = unpack(half, exchange(first_results))
    grads = staged_call(
        gradient_compute,
        dict(
            state=own.state,
            share=mixed.share,
            got_share=got_share,
            scales=mixed.scales,
            marks=kept.marks,
            pair=(kept.pair_b, LEAD),
            weight=(kept.weight_b, LEAD),
            growth=(kept.growth_b, LEAD),
            vg=(vg, LATE),
            key_exp=(kept.key_exp, LEAD),
            turned=(kept.turned, LEAD),
            token_prob=(kept.token_prob, LEAD),
            inverse_grad=(own.inverse_grad, LAST),
            last_growth=(kept.last_growth, LAST),
            mark_prob=(kept.mark_prob, LAST),
            factor=(kept.factor, LAST),
        ),
        dict(
            far=low(2, 2, HALF, HD),
            near=wide(2, 2, HALF, HD),
            direct=(wide(2, 2, tokens, HD), LEAD),
        ),
        LONG,
        after=(first_results,),
    )
    results = staged_call(
        finish_compute,
        dict(got_far=partner(grads.far), near=grads.near, direct=(grads.direct, BLOCKS)),
        dict(out=(low(*qk.shape), GROUPS)),
        0.1,
    ).out
    query_grad, key_grad = unpack(half, exchange(results))
    return attended, query_grad, key_grad, value_gradient_array


def solution(mesh):
    whole_placement = P(("seq", "head"), None)
    halves_placement = P(("half", "cube"), None)

    def layer(queries, keys, values, out_grad):
        tokens, width = queries.shape
        own_head_each = width // HD == mesh.size and tokens == 8 * CHUNK
        if own_head_each:
            split = jax.sharding.Mesh(
                mesh.devices.reshape(2, mesh.size // 2), ("half", "cube")
            )
        return jax.shard_map(
            body if own_head_each else shared_body,
            mesh=split if own_head_each else mesh,
            in_specs=(halves_placement if own_head_each else whole_placement,) * 4,
            out_specs=(halves_placement if own_head_each else whole_placement,) * 4,
            check_vma=False,
        )(queries, keys, values, out_grad)

    return layer
```

```python
import functools
from types import SimpleNamespace

import jax
import jax.numpy as jnp
from jax import lax
from jax.experimental import pallas as pl
from jax.experimental.pallas import tpu as pltpu
from jax.sharding import PartitionSpec as P

HD = 128
M = 256
PINV_ITERS = 6
CHUNK = 256
PACK_GROUPS = 4
HALF = M // 2
SWAP = ((0, 1), (1, 0))
VMEM_LIMIT = 60 * 2**20
SMALL_LIMIT = 16 * 2**20
WHOLE, LEAD, GROUPS, BLOCKS, LATE, LAST = range(6)
SLOTS = (10, 11)
LONG = 200
EARLY_SWEEPS = PINV_ITERS // 2


precise_setting = lax.Precision.HIGHEST


def newton_inverse(matrix):
    identity = jnp.eye(matrix.shape[0], dtype=matrix.dtype)
    factor = lax.stop_gradient(1.0 / jnp.max(jnp.sum(matrix, axis=0)))
    iterate = matrix.T * factor
    for sweep_index in range(PINV_ITERS):
        product = jnp.matmul(matrix, iterate, precision=precise_setting)
        inner_term = jnp.matmul(product, 7.0 * identity - product, precision=precise_setting)
        inner_term = jnp.matmul(product, 15.0 * identity - inner_term, precision=precise_setting)
        iterate = 0.25 * jnp.matmul(
            iterate, 13.0 * identity - inner_term, precision=precise_setting
        )
    return iterate


def share_heads(own_matrix, head_count):
    seq_index = lax.axis_index("seq")
    slot_mask = (jnp.arange(head_count, dtype=jnp.int32) == seq_index).astype(jnp.float32)
    return lax.psum(slot_mask[:, None, None] * own_matrix[None], "seq")


def shared_body(queries, keys, values, out_grad):
    query_rows, key_rows, value_rows, grad_rows = (
        lax.all_to_all(queries, "head", split_axis=1, concat_axis=0, tiled=True),
        lax.all_to_all(keys, "head", split_axis=1, concat_axis=0, tiled=True),
        lax.all_to_all(values, "head", split_axis=1, concat_axis=0, tiled=True),
        lax.all_to_all(out_grad, "head", split_axis=1, concat_axis=0, tiled=True),
    )
    tok_rows = query_rows.shape[0]
    head_count = query_rows.shape[1] // HD
    local_marks = M // lax.axis_size("seq")
    segment_len = tok_rows // local_marks
    score_scale = HD ** (-0.5)
    seq_index = lax.axis_index("seq")

    def landmark(matrix):
        summed = jnp.sum(
            matrix.reshape(local_marks, segment_len, matrix.shape[1]), axis=1, dtype=jnp.float32
        )
        return (summed / segment_len).astype(jnp.bfloat16)

    mark_queries, mark_keys = (
        lax.all_gather(landmark(query_rows), "seq", axis=0, tiled=True),
        lax.all_gather(landmark(key_rows), "seq", axis=0, tiled=True),
    )
    query_per_head = query_rows.reshape(tok_rows, head_count, HD)
    key_per_head = key_rows.reshape(tok_rows, head_count, HD)
    value_per_head = value_rows.reshape(tok_rows, head_count, HD)
    gradient_per_head = grad_rows.reshape(tok_rows, head_count, HD)
    landmark_query_heads = mark_queries.reshape(M, head_count, HD)
    landmark_key_heads = mark_keys.reshape(M, head_count, HD)
    key_score = (
        jnp.einsum(
            "pcv,gcv->cpg", landmark_query_heads, key_per_head, preferred_element_type=jnp.float32
        )
        * score_scale
    )
    key_max = lax.pmax(jnp.max(key_score, axis=-1), "seq")
    key_exp = jnp.exp(key_score - key_max[..., None])
    partial_num = jnp.einsum(
        "akq,qay->aky",
        key_exp.astype(jnp.bfloat16),
        value_per_head,
        preferred_element_type=jnp.float32,
    )
    key_total, numerator = lax.psum((jnp.sum(key_exp, axis=-1), partial_num), "seq")
    landmark_value_rows = numerator / key_total[..., None]
    token_prob = jax.nn.softmax(
        jnp.einsum(
            "jti,cti->tjc", query_per_head, landmark_key_heads, preferred_element_type=jnp.float32
        )
        * score_scale,
        axis=-1,
    )
    token_probability_lowered = token_prob.astype(jnp.bfloat16)
    mark_prob = jax.nn.softmax(
        jnp.einsum(
            "jou,iou->oji",
            landmark_query_heads,
            landmark_key_heads,
            preferred_element_type=jnp.float32,
        )
        * score_scale,
        axis=-1,
    )
    own_head = seq_index % head_count
    own_mark = lax.dynamic_index_in_dim(mark_prob, own_head, 0, keepdims=False)
    own_inverse, pull_back = jax.vjp(newton_inverse, own_mark)
    pseudo_inverse_matrix = share_heads(own_inverse, head_count)
    mixing_matrix = jnp.einsum(
        "jvy,jys->jvs", pseudo_inverse_matrix, landmark_value_rows, precision=precise_setting
    )
    mixing_matrix_lowered = mixing_matrix.astype(jnp.bfloat16)
    attended = jnp.einsum(
        "yvo,yor->vyr",
        token_probability_lowered,
        mixing_matrix_lowered,
        preferred_element_type=jnp.float32,
    ).astype(jnp.bfloat16)
    token_grad = jnp.einsum(
        "fag,aog->afo", gradient_per_head, mixing_matrix_lowered, preferred_element_type=jnp.float32
    )
    partial_mix = jnp.einsum(
        "klz,lkr->kzr",
        token_probability_lowered,
        gradient_per_head,
        preferred_element_type=jnp.float32,
    )
    mixing_matrix_gradient = lax.psum(partial_mix, "seq")
    token_score_gradient = (
        token_prob * (token_grad - jnp.sum(token_grad * token_prob, axis=-1, keepdims=True))
    ).astype(jnp.bfloat16)
    direct_qgrad = (
        jnp.einsum(
            "ufg,guc->fuc",
            token_score_gradient,
            landmark_key_heads,
            preferred_element_type=jnp.float32,
        )
        * score_scale
    )
    mark_kgrad_f = (
        jnp.einsum(
            "xgi,gxy->ixy", token_score_gradient, query_per_head, preferred_element_type=jnp.float32
        )
        * score_scale
    )
    pseudo_inverse_gradient = jnp.einsum(
        "ktu,kyu->kty", mixing_matrix_gradient, landmark_value_rows, precision=precise_setting
    )
    landmark_value_gradient = jnp.einsum(
        "lrb,lrz->lbz", pseudo_inverse_matrix, mixing_matrix_gradient, precision=precise_setting
    )
    own_igrad = lax.dynamic_index_in_dim(pseudo_inverse_gradient, own_head, 0, keepdims=False)
    (own_mgrad,) = pull_back(own_igrad)
    mark_grad = share_heads(own_mgrad, head_count)
    mark_sgrad = mark_prob * (mark_grad - jnp.sum(mark_grad * mark_prob, axis=-1, keepdims=True))
    first_mark = seq_index * local_marks
    score_gradient_rows = lax.dynamic_slice_in_dim(mark_sgrad, first_mark, local_marks, 1)
    score_gradient_columns = lax.dynamic_slice_in_dim(mark_sgrad, first_mark, local_marks, 2)
    own_qgrad_a = (
        jnp.einsum(
            "txs,ste->xte",
            score_gradient_rows,
            landmark_key_heads.astype(jnp.float32),
            precision=precise_setting,
        )
        * score_scale
    )
    own_kgrad_a = (
        jnp.einsum(
            "eaj,aev->jev",
            score_gradient_columns,
            landmark_query_heads.astype(jnp.float32),
            precision=precise_setting,
        )
        * score_scale
    )
    landmark_value_lowered = landmark_value_gradient.astype(jnp.bfloat16)
    key_prob = key_exp / key_total[..., None]
    key_probability_lowered = key_prob.astype(jnp.bfloat16)
    value_gradient_array = jnp.einsum(
        "zct,zcj->tzj",
        key_probability_lowered,
        landmark_value_lowered,
        preferred_element_type=jnp.float32,
    )
    key_direct_gradient = jnp.einsum(
        "exb,geb->exg", landmark_value_lowered, value_per_head, preferred_element_type=jnp.float32
    )
    row_total = lax.psum(jnp.sum(key_prob * key_direct_gradient, axis=-1), "seq")
    key_score_gradient = (key_prob * (key_direct_gradient - row_total[..., None])).astype(
        jnp.bfloat16
    )
    direct_kgrad = (
        jnp.einsum(
            "pbo,bpx->opx",
            key_score_gradient,
            landmark_query_heads,
            preferred_element_type=jnp.float32,
        )
        * score_scale
    )
    mark_qgrad_b = (
        jnp.einsum(
            "cbj,jcp->bcp", key_score_gradient, key_per_head, preferred_element_type=jnp.float32
        )
        * score_scale
    )
    own_kgrad_f, own_qgrad_b = (
        lax.psum_scatter(mark_kgrad_f, "seq", scatter_dimension=0, tiled=True),
        lax.psum_scatter(mark_qgrad_b, "seq", scatter_dimension=0, tiled=True),
    )
    mark_qtotal = (own_qgrad_a + own_qgrad_b) / segment_len
    mark_ktotal = (own_kgrad_a + own_kgrad_f) / segment_len
    query_grad = (
        direct_qgrad.reshape(local_marks, segment_len, head_count, HD) + mark_qtotal[:, None]
    )
    key_grad = direct_kgrad.reshape(local_marks, segment_len, head_count, HD) + mark_ktotal[:, None]
    width = head_count * HD
    results = (
        attended.reshape(tok_rows, width),
        query_grad.astype(jnp.bfloat16).reshape(tok_rows, width),
        key_grad.astype(jnp.bfloat16).reshape(tok_rows, width),
        value_gradient_array.astype(jnp.bfloat16).reshape(tok_rows, width),
    )
    attended_out, query_out, key_out, value_out = (
        lax.all_to_all(results[0], "head", split_axis=0, concat_axis=1, tiled=True),
        lax.all_to_all(results[1], "head", split_axis=0, concat_axis=1, tiled=True),
        lax.all_to_all(results[2], "head", split_axis=0, concat_axis=1, tiled=True),
        lax.all_to_all(results[3], "head", split_axis=0, concat_axis=1, tiled=True),
    )
    return (attended_out, query_out, key_out, value_out)


def halves(matrix):
    high = matrix.astype(jnp.bfloat16)
    return high, (matrix - high.astype(jnp.float32)).astype(jnp.bfloat16)


def wide_dot(left, right):
    return jnp.dot(left, right, preferred_element_type=jnp.float32)


def wide_dot_nt(left, right):
    return lax.dot_general(
        left, right, (((1,), (1,)), ((), ())), preferred_element_type=jnp.float32
    )


def split_dot(left, right):
    left_high, left_low = left
    right_high, right_low = right
    return wide_dot(
        jnp.concatenate([left_high, left_high, left_low], axis=1),
        jnp.concatenate([right_high, right_low, right_high], axis=0),
    )


def split_dot_nt(left, right):
    left_high, left_low = left
    right_high, right_low = right
    return wide_dot_nt(
        jnp.concatenate([left_high, left_high, left_low], axis=1),
        jnp.concatenate([right_high, right_low, right_high], axis=1),
    )


def identity_matrix():
    return (
        lax.broadcasted_iota(jnp.int32, (M, M), 0) == lax.broadcasted_iota(jnp.int32, (M, M), 1)
    ).astype(jnp.float32)


def chunk_of(ref, array, slot, index):
    per = CHUNK // ref.shape[3]
    return ref[index * per : (index + 1) * per, array, slot].reshape(CHUNK, HD)


def store_chunk(ref, lead, index, value):
    rows = ref.shape[-2]
    per = CHUNK // rows
    ref[(slice(index * per, (index + 1) * per), *lead)] = value.reshape(per, rows, HD)


def all_tokens(ref, array, slot):
    return ref[:, array, slot].reshape(ref.shape[0] * ref.shape[3], HD)


def tokens_of(ref):
    return ref.shape[0] * ref.shape[3]


def columns(index):
    return pl.ds(pl.multiple_of(index * CHUNK, CHUNK), CHUNK)


def swap_lanes(matrix):
    return jnp.concatenate([matrix[:, HALF:], matrix[:, :HALF]], axis=1)


def thirds(rows):
    first = rows.astype(jnp.bfloat16).astype(jnp.float32)
    second = (rows - first).astype(jnp.bfloat16).astype(jnp.float32)
    return jnp.concatenate([first, second, rows - first - second], axis=0)


def joined_thirds(rows):
    count = rows.shape[0] // 3
    return rows[:count] + (rows[count : 2 * count] + rows[2 * count :])


def held_shape(kind, shape):
    return shape[1:] if kind in SLOTS else shape


def pieces_of(kind, shape):
    if kind == LEAD:
        return [(index,) for index in range(shape[0])]
    if kind == BLOCKS:
        return [
            (first, second, slice(place, place + 2 * CHUNK))
            for place in range(0, shape[2], 2 * CHUNK)
            for first in range(shape[0])
            for second in range(shape[1])
        ]
    if kind == GROUPS:
        per = CHUNK // shape[-2]
        return [(slice(place, place + per),) for place in range(0, shape[0], per)]
    return [()]


def window(ref, piece):
    place = tuple(
        pl.ds(part.start, part.stop - part.start) if isinstance(part, slice) else part
        for part in piece
    )
    return ref.at[place] if place else ref


class Staged:
    def __init__(self, names, kinds, outer, inner, done, outward):
        self.refs = SimpleNamespace(**dict(zip(names, inner)))
        self.copies, self.order = [], []
        count = 0
        steps = []
        for place, (kind, home, held) in enumerate(zip(kinds, outer, inner)):
            home = home.at[kind - SLOTS[0]] if kind in SLOTS else home
            copies = {}
            for step, piece in enumerate(pieces_of(kind, held.shape)):
                ends = (window(held, piece), window(home, piece))
                source, target = ends if outward else ends[::-1]
                key = tuple(
                    part.start if isinstance(part, slice) else part for part in piece
                )
                copies[key] = pltpu.make_async_copy(source, target, done.at[count])
                steps.append(({WHOLE: -1, LAST: 9}.get(kind, step), place, key))
                count += 1
            self.copies.append(copies)
        self.inner = inner
        self.order = sorted(steps, key=lambda item: item[:2])
        self.started, self.waited = set(), set()

    def place_of(self, ref):
        return next(index for index, held in enumerate(self.inner) if held is ref)

    def start(self, ref=None, *key):
        chosen = [
            (place, name)
            for _, place, name in self.order
            if (ref is None or place == self.place_of(ref)) and (not key or name == key)
        ]
        for item in chosen:
            if item not in self.started:
                self.started.add(item)
                self.copies[item[0]][item[1]].start()

    def wait(self, ref=None, *key):
        chosen = [
            (place, name)
            for _, place, name in self.order
            if (ref is None or place == self.place_of(ref)) and (not key or name == key)
        ]
        for item in chosen:
            if item not in self.waited:
                self.waited.add(item)
                self.copies[item[0]][item[1]].wait()


def staged_call(compute, inputs, outputs, flops, extra=(), after=(), in_place=False):
    names_in, names_out = tuple(inputs), tuple(outputs)
    kinds_in = [x[1] if isinstance(x, tuple) else WHOLE for x in inputs.values()]
    kinds_out = [x[1] if isinstance(x, tuple) else WHOLE for x in outputs.values()]
    operands = tuple(x[0] if isinstance(x, tuple) else x for x in inputs.values())
    shapes = tuple(x[0] if isinstance(x, tuple) else x for x in outputs.values())
    n_in, n_out, n_after = len(operands), len(shapes), len(after)
    moved = sum(x.size * x.dtype.itemsize for x in (*operands, *shapes))
    anywhere = pl.BlockSpec(memory_space=pl.ANY)

    def count(kinds, arrays):
        return sum(len(pieces_of(kind, x.shape)) for kind, x in zip(kinds, arrays))

    def kernel(*refs):
        sources, refs = refs[:n_in], refs[n_in + n_after :]
        homes, refs = refs[:n_out], refs[n_out:]
        held_in, held_out = refs[:n_in], refs[n_in : n_in + n_out]
        *scratch, in_done, out_done = refs[n_in + n_out :]
        reads = Staged(names_in, kinds_in, sources, held_in, in_done, False)
        writes = Staged(names_out, kinds_out, homes, held_out, out_done, True)
        reads.start()
        compute(reads.refs, writes.refs, reads.wait, writes.start, *scratch)
        reads.wait()
        writes.start()
        writes.wait()

    results = pl.pallas_call(
        kernel,
        out_shape=shapes,
        in_specs=[anywhere] * (n_in + n_after),
        out_specs=(anywhere,) * n_out,
        scratch_shapes=[
            *(
                pltpu.VMEM(held_shape(kind, x.shape), x.dtype)
                for kind, x in zip((*kinds_in, *kinds_out), (*operands, *shapes))
            ),
            *extra,
            pltpu.SemaphoreType.DMA((count(kinds_in, operands),)),
            pltpu.SemaphoreType.DMA((count(kinds_out, shapes),)),
        ],
        compiler_params=pltpu.CompilerParams(vmem_limit_bytes=VMEM_LIMIT),
        cost_estimate=pl.CostEstimate(
            flops=int(flops * 10**9), bytes_accessed=moved, transcendentals=0
        ),
    )(*operands, *after)
    return SimpleNamespace(**dict(zip(outputs, results)))


def low(*shape):
    return jax.ShapeDtypeStruct(shape, jnp.bfloat16)


def wide(*shape):
    return jax.ShapeDtypeStruct(shape, jnp.float32)


def pack_kernel(half_ref, first_ref, second_ref, out_ref, rows_s, packed_s, in_done, out_done):
    half = half_ref[0]
    pairs = out_ref.shape[0]
    group = pairs // PACK_GROUPS
    span = 2 * HD
    reads, writes = [], []
    for index in range(PACK_GROUPS):
        for array, ref in enumerate((first_ref, second_ref)):
            place = pl.ds(index * group * span, group * span)
            reads.append(
                pltpu.make_async_copy(
                    ref.at[:, place], rows_s.at[array, :, place], in_done.at[array, index]
                )
            )
        place = pl.ds(index * group, group)
        writes.append(
            pltpu.make_async_copy(packed_s.at[place], out_ref.at[place], out_done.at[index])
        )
    for copy in reads:
        copy.start()
    for index in range(PACK_GROUPS):
        for array in range(2):
            reads[2 * index + array].wait()
            for pair in range(index * group, (index + 1) * group):
                start = pair * span
                packed_s[pair, array, half] = rows_s[array, :, start : start + HD]
                packed_s[pair, array, 1 - half] = rows_s[array, :, start + HD : start + span]
        writes[index].start()
    for copy in writes:
        copy.wait()


def unpack_kernel(half_ref, packed_ref, first_ref, second_ref, rows_s, out_done):
    half = half_ref[0]
    pairs = packed_ref.shape[0]
    group = pairs // PACK_GROUPS
    span = 2 * HD
    writes = []
    for index in range(PACK_GROUPS):
        for array, ref in enumerate((first_ref, second_ref)):
            for pair in range(index * group, (index + 1) * group):
                start = pair * span
                rows_s[array, :, start : start + HD] = packed_ref[pair, array, half]
                rows_s[array, :, start + HD : start + span] = packed_ref[pair, array, 1 - half]
            place = pl.ds(index * group * span, group * span)
            write = pltpu.make_async_copy(
                rows_s.at[array, :, place], ref.at[:, place], out_done.at[array, index]
            )
            write.start()
            writes.append(write)
    for copy in writes:
        copy.wait()


def layout_call(kernel, half, operands, out_shape, scratch, in_space, limit):
    anywhere = pl.BlockSpec(memory_space=pl.ANY)
    moved = 2 * sum(x.size * x.dtype.itemsize for x in operands)
    return pl.pallas_call(
        kernel,
        out_shape=out_shape,
        in_specs=[pl.BlockSpec(memory_space=pltpu.SMEM)]
        + [pl.BlockSpec(memory_space=in_space)] * len(operands),
        out_specs=jax.tree.map(lambda _: anywhere, out_shape),
        scratch_shapes=scratch,
        compiler_params=pltpu.CompilerParams(vmem_limit_bytes=limit),
        cost_estimate=pl.CostEstimate(flops=0, bytes_accessed=moved, transcendentals=0),
    )(half, *operands)


def pack(half, first, second):
    rows, width = first.shape
    shape = low(width // (2 * HD), 2, 2, rows, HD)
    scratch = [
        pltpu.VMEM((2, rows, width), jnp.bfloat16),
        pltpu.VMEM(shape.shape, jnp.bfloat16),
        pltpu.SemaphoreType.DMA((2, PACK_GROUPS)),
        pltpu.SemaphoreType.DMA((PACK_GROUPS,)),
    ]
    return layout_call(
        pack_kernel, half, (first, second), shape, scratch, pl.ANY, VMEM_LIMIT
    )


def unpack(half, packed):
    pairs, _, _, rows, _ = packed.shape
    shape = low(rows, pairs * 2 * HD)
    scratch = [
        pltpu.VMEM((2, *shape.shape), jnp.bfloat16),
        pltpu.SemaphoreType.DMA((2, PACK_GROUPS)),
    ]
    return layout_call(
        unpack_kernel, half, (packed,), (shape, shape), scratch, pltpu.VMEM, SMALL_LIMIT
    )


def landmark_kernel(qk_ref, marks_ref):
    tokens = tokens_of(qk_ref)
    segment_len = tokens // HALF
    per = CHUNK // segment_len
    member = (
        lax.broadcasted_iota(jnp.int32, (per, CHUNK), 1) // segment_len
        == lax.broadcasted_iota(jnp.int32, (per, CHUNK), 0)
    ).astype(jnp.bfloat16)
    kinds = [(slot, array) for slot in range(2) for array in range(2)]
    for index in range(tokens // CHUNK):
        parts = [chunk_of(qk_ref, array, slot, index) for slot, array in kinds]
        summed = wide_dot(member, jnp.concatenate(parts, axis=1))
        mean = (summed / segment_len).astype(jnp.bfloat16)
        for place, (slot, array) in enumerate(kinds):
            marks_ref[slot, array, index * per : (index + 1) * per] = mean[
                :, place * HD : (place + 1) * HD
            ]


def landmarks_of(qk):
    held = pl.BlockSpec(memory_space=pltpu.VMEM)
    return pl.pallas_call(
        landmark_kernel,
        out_shape=low(2, 2, HALF, HD),
        in_specs=[held],
        out_specs=held,
        compiler_params=pltpu.CompilerParams(vmem_limit_bytes=SMALL_LIMIT),
        cost_estimate=pl.CostEstimate(
            flops=2 * 10**8, bytes_accessed=qk.size * 2, transcendentals=0
        ),
    )(qk)


def sweep_forward(power_s, iterate_s, saved, sweep, work):
    pair_ref, weight_ref, growth_ref = saved
    power = power_s[...]
    power_high, power_low = halves(power)
    square = split_dot((power_high, power_low), (power_high, power_low))
    next(work)()
    square_halves = halves(square)
    pair = (
        jnp.concatenate([power_high, square_halves[0]], axis=0),
        jnp.concatenate([power_low, square_halves[1]], axis=0),
    )
    pair_ref[sweep, 0], pair_ref[sweep, 1] = pair
    higher = split_dot(pair, square_halves)
    next(work)()
    cube, fourth = higher[:M], higher[M:]
    weight = halves(0.25 * (13.0 * identity_matrix() - 15.0 * power + 7.0 * square - cube))
    power_s[...] = 0.25 * (13.0 * power - 15.0 * square + 7.0 * cube - fourth)
    weight_ref[sweep, 0], weight_ref[sweep, 1] = weight
    iterate = halves(iterate_s[...])
    growth_ref[sweep, 0], growth_ref[sweep, 1] = iterate[0][M:], iterate[1][M:]
    iterate_s[...] = split_dot(iterate, weight)


def probability_compute(ins, outs, need, put, power_s, iterate_s):
    need()
    qk_ref = ins.qk
    chunks = tokens_of(qk_ref) // CHUNK
    score_scale = HD ** (-0.5)
    for slot in range(2):
        for array in range(2):
            outs.marks[slot, array] = jnp.concatenate(
                [ins.mine[slot, array], ins.theirs[1 - slot, array]], axis=0
            )
    put(outs.marks)
    landmark_q, landmark_k = outs.marks[0, 0], outs.marks[0, 1]
    mark_score = wide_dot_nt(landmark_q, landmark_k) * score_scale
    mark_exp = jnp.exp(mark_score - jnp.max(mark_score, axis=1, keepdims=True))
    mark_prob = mark_exp / jnp.sum(mark_exp, axis=1, keepdims=True)
    outs.mark_prob[...] = mark_prob
    factor = 1.0 / jnp.max(jnp.sum(mark_prob, axis=0, keepdims=True), axis=1, keepdims=True)
    outs.factor[...] = jnp.broadcast_to(factor, outs.factor.shape)
    mark_halves = halves(mark_prob)
    power_s[...] = split_dot_nt(mark_halves, mark_halves) * factor
    iterate_s[0:M] = mark_prob.T * factor
    iterate_s[M:] = identity_matrix()
    tops, totals = [[], []], [[], []]

    def scores(slot, index):
        query_chunk, key_chunk = (chunk_of(qk_ref, array, slot, index) for array in range(2))
        place = slice(index * CHUNK, (index + 1) * CHUNK)
        outs.turned[slot, 0, :, place] = query_chunk.T
        outs.turned[slot, 1, :, place] = key_chunk.T
        score = wide_dot_nt(query_chunk, outs.marks[slot, 1]) * score_scale
        grown = jnp.exp(score - jnp.max(score, axis=1, keepdims=True))
        prob = grown * (1.0 / jnp.sum(grown, axis=1, keepdims=True))
        outs.token_prob[slot, place] = prob
        outs.token_low[slot, place] = prob.astype(jnp.bfloat16)
        key_score = wide_dot_nt(key_chunk, outs.marks[slot, 0]) * score_scale
        outs.key_exp[slot, place] = key_score
        tops[slot].append(jnp.max(key_score, axis=0, keepdims=True))

    def grow(slot, index):
        if index == 0:
            tops[slot] = functools.reduce(jnp.maximum, tops[slot])
        place = slice(index * CHUNK, (index + 1) * CHUNK)
        grown = jnp.exp(outs.key_exp[slot, place] - tops[slot])
        outs.key_exp[slot, place] = grown
        outs.key_low[slot, place] = grown.astype(jnp.bfloat16)
        totals[slot].append(jnp.sum(grown, axis=0, keepdims=True))

    def several(unit, pairs):
        for slot, index in pairs:
            unit(slot, index)

    pairs = [(slot, index) for slot in range(2) for index in range(chunks)]
    work = iter(
        [functools.partial(several, scores, [pair]) for pair in pairs]
        + [
            functools.partial(several, grow, pairs[first : first + 2])
            for first in range(0, len(pairs), 2)
        ]
    )
    for sweep in range(PINV_ITERS):
        first = sweep < EARLY_SWEEPS
        place = sweep if first else sweep - EARLY_SWEEPS
        saved = (
            (outs.pair_a, outs.weight_a, outs.growth_a)
            if first
            else (outs.pair_b, outs.weight_b, outs.growth_b)
        )
        sweep_forward(power_s, iterate_s, saved, place, work)
        for ref in saved:
            put(ref, place)
        if sweep == 3:
            for ref in (outs.token_low, outs.token_prob, outs.turned):
                put(ref)
    put(outs.key_low)
    put(outs.key_exp)
    outs.inverse[0], outs.inverse[1] = halves(iterate_s[0:M])
    outs.last_growth[0], outs.last_growth[1] = halves(iterate_s[M:])
    stats = [x for slot in range(2) for x in (tops[slot], sum(totals[slot][1:], totals[slot][0]))]
    outs.stats[0:4] = jnp.concatenate(stats, axis=0)
    outs.stats[4:8] = jnp.zeros((4, M), jnp.float32)


def partial_compute(ins, outs, need, put):
    need(ins.vg)
    turned = [[all_tokens(ins.vg, array, slot).T for array in range(2)] for slot in range(2)]
    need(ins.stats)
    rows = thirds(ins.stats[0:4])
    outs.send[2 * HD :] = jnp.concatenate([rows, jnp.zeros((4, M), jnp.float32)], axis=0).astype(
        jnp.bfloat16
    )
    for slot, home in enumerate((outs.keep, outs.send)):
        need(ins.key_low, slot)
        home[0:HD] = wide_dot(turned[slot][0], ins.key_low[slot]).astype(home.dtype)
        need(ins.token_low, slot)
        home[HD : 2 * HD] = wide_dot(turned[slot][1], ins.token_low[slot]).astype(home.dtype)
        put(home)


def mixing_kernel(got_ref, keep_ref, stats_ref, inverse_ref, share_ref, mix_ref):
    got = got_ref[...].astype(jnp.float32)
    others = swap_lanes(joined_thirds(got[2 * HD : 2 * HD + 12]))
    scales = []
    for slot in range(2):
        own, other = 2 * slot, 2 * (1 - slot)
        own_max, own_total = stats_ref[own : own + 1], stats_ref[own + 1 : own + 2]
        other_max, other_total = others[other : other + 1], others[other + 1 : other + 2]
        key_max = jnp.maximum(own_max, other_max)
        own_factor, other_factor = jnp.exp(own_max - key_max), jnp.exp(other_max - key_max)
        inverse_total = 1.0 / (own_total * own_factor + other_total * other_factor)
        scales.append((own_factor * inverse_total, other_factor * inverse_total))
    landmark_values = keep_ref[0:HD] * scales[0][0] + swap_lanes(got[0:HD]) * scales[0][1]
    mixing_grad = keep_ref[HD : 2 * HD] + swap_lanes(got[HD : 2 * HD])
    inverse = (inverse_ref[0], inverse_ref[1])
    mixing_low = split_dot_nt(halves(landmark_values), inverse).astype(jnp.bfloat16)
    values_low = split_dot(halves(mixing_grad), inverse).astype(jnp.bfloat16)
    row_total = jnp.sum(values_low.astype(jnp.float32) * landmark_values, axis=0, keepdims=True)
    share_ref[0:HD] = mixing_low
    share_ref[HD : 2 * HD] = values_low
    share_ref[2 * HD :] = jnp.concatenate(
        [thirds(row_total), jnp.zeros((13, M), jnp.float32)], axis=0
    ).astype(jnp.bfloat16)
    mix_ref[0:HD] = mixing_low.astype(jnp.float32)
    mix_ref[HD : 2 * HD] = values_low.astype(jnp.float32)
    mix_ref[2 * HD : 2 * HD + 8] = jnp.concatenate(
        [row_total, scales[0][0], scales[1][0], jnp.zeros((5, M), jnp.float32)], axis=0
    )
    mix_ref[2 * HD + 8 : 3 * HD + 8] = mixing_grad
    mix_ref[3 * HD + 8 :] = landmark_values


def joined_sums(*operands):
    held = pl.BlockSpec(memory_space=pltpu.VMEM)
    return pl.pallas_call(
        mixing_kernel,
        out_shape=(low(2 * HD + 16, M), wide(4 * HD + 8, M)),
        in_specs=[held] * len(operands),
        out_specs=(held, held),
        compiler_params=pltpu.CompilerParams(vmem_limit_bytes=SMALL_LIMIT),
        cost_estimate=pl.CostEstimate(flops=2 * 10**8, bytes_accessed=2**20, transcendentals=0),
    )(*operands)


def several(*units):
    for unit in units:
        unit()


def out_units(ins, slot, out_ref, lead, share):
    mixing_low, values_low, _ = share
    scale = ins.mix[2 * HD + 1 + slot : 2 * HD + 2 + slot]

    def token_side(index):
        place = slice(index * CHUNK, (index + 1) * CHUNK)
        attended = wide_dot_nt(ins.token_low[place], mixing_low)
        store_chunk(out_ref, (0, *lead), index, attended.astype(jnp.bfloat16))

    def key_side(index):
        place = slice(index * CHUNK, (index + 1) * CHUNK)
        key_plow = (ins.key_exp[place] * scale).astype(jnp.bfloat16)
        value_gradient = wide_dot_nt(key_plow, values_low)
        store_chunk(out_ref, (1, *lead), index, value_gradient.astype(jnp.bfloat16))

    chunks = ins.token_low.shape[0] // CHUNK
    return [
        functools.partial(unit, index) for unit in (token_side, key_side) for index in range(chunks)
    ]


def gradient_units(ins, slot, direct_ref, share):
    score_scale = HD ** (-0.5)
    mixing_low, values_low, row_total = share
    query_sums, key_sums = [], []
    scale = ins.mix[2 * HD + 1 + slot : 2 * HD + 2 + slot]

    def token_side(index):
        place = slice(index * CHUNK, (index + 1) * CHUNK)
        prob = ins.token_prob[slot, place]
        token_grad = wide_dot(chunk_of(ins.vg, 1, slot, index), mixing_low)
        token_sgrad = (
            prob * (token_grad - jnp.sum(token_grad * prob, axis=1, keepdims=True))
        ).astype(jnp.bfloat16)
        direct_ref[slot, 0, place] = wide_dot(token_sgrad, ins.marks[slot, 1]) * score_scale
        key_sums.append(wide_dot(ins.turned[slot, 0, :, place], token_sgrad))

    def key_side(index):
        place = slice(index * CHUNK, (index + 1) * CHUNK)
        key_prob = ins.key_exp[slot, place] * scale
        key_dgrad = wide_dot(chunk_of(ins.vg, 0, slot, index), values_low)
        key_sgrad = (key_prob * (key_dgrad - row_total)).astype(jnp.bfloat16)
        direct_ref[slot, 1, place] = wide_dot(key_sgrad, ins.marks[slot, 0]) * score_scale
        query_sums.append(wide_dot(ins.turned[slot, 1, :, place], key_sgrad))

    chunks = tokens_of(ins.vg) // CHUNK
    units = [
        [functools.partial(unit, index) for index in range(chunks)] for unit in (key_side, token_side)
    ]
    return units, query_sums, key_sums


def own_parts(ref):
    return (
        ref[0:HD].astype(jnp.bfloat16),
        ref[HD : 2 * HD].astype(jnp.bfloat16),
        ref[2 * HD : 2 * HD + 1],
    )


def other_parts(ref):
    parts = (ref[0:HD], ref[HD : 2 * HD], joined_thirds(ref[2 * HD :].astype(jnp.float32)[0:3]))
    return [swap_lanes(part) for part in parts]


def gradient_sweep(state, saved, place, beside, last):
    power, growth = state
    pair_ref, weight_ref, growth_ref = saved
    pair = (pair_ref[place, 0], pair_ref[place, 1])
    first = split_dot(pair, halves(power))
    beside()
    square = first[:M] + first[:M].T
    second = split_dot(tuple(x[:M] for x in pair) if last else pair, halves(square))
    beside()
    cube = first[M:].T + second[:M]
    weight = halves(0.25 * (7.0 * square - 15.0 * power - cube))
    if not last:
        fourth = second[M:] + second[M:].T
        power = 0.25 * (13.0 * power - 15.0 * square + 7.0 * cube - fourth)
    left = [growth_ref[place, 0], growth_ref[place, 0], growth_ref[place, 1]]
    right = [weight[0], weight[1], weight[0]]
    if growth is not None:
        grown = halves(growth)
        left += [grown[0], grown[0], grown[1]]
        right += [weight_ref[place, 0], weight_ref[place, 1], weight_ref[place, 0]]
    growth = wide_dot(jnp.concatenate(left, axis=1), jnp.concatenate(right, axis=0))
    return power, growth


def own_gradient_compute(ins, outs, need, put):
    for ref in (ins.mark_prob, ins.factor, ins.mix):
        need(ref)
    inverse_grad = split_dot(
        halves(ins.mix[2 * HD + 8 : 3 * HD + 8].T), halves(ins.mix[3 * HD + 8 :])
    )
    inverse_grad_halves = halves(inverse_grad)
    outs.inverse_grad[0], outs.inverse_grad[1] = inverse_grad_halves
    toward = split_dot(halves(ins.mark_prob[...]), inverse_grad_halves) * ins.factor[0:1, 0:1]
    state = (0.5 * (toward + toward.T), None)
    units = out_units(ins, 0, outs.out, (), own_parts(ins.mix))
    work = iter([units[index : index + 2] for index in range(0, len(units), 2)])
    saved = (ins.pair, ins.weight, ins.growth)

    def beside():
        several(*next(work, ()))

    for sweep in range(EARLY_SWEEPS):
        if sweep == 0:
            need(ins.token_low)
        if sweep == 1:
            need(ins.key_exp)
        for ref in saved:
            need(ref, sweep)
        state = gradient_sweep(state, saved, sweep, beside, False)
    outs.state[0], outs.state[1] = state


def other_out_compute(ins, outs, need, put):
    for ref in (ins.got_share, ins.mix, ins.token_low):
        need(ref)
    units = out_units(ins, 1, outs.out, (1,), other_parts(ins.got_share))
    chunks = len(units) // 2
    several(*units[:chunks])
    need()
    group = CHUNK // outs.out.shape[3]
    for index, unit in enumerate(units[chunks:]):
        unit()
        place = slice(index * group, (index + 1) * group)
        outs.out[place, :, 0] = ins.own_out[place]
        put(outs.out, index * group)


def gradient_compute(ins, outs, need, put):
    for ref in (ins.state, ins.mix, ins.got_share, ins.marks):
        need(ref)
    sides = []
    for slot in range(2):
        share = other_parts(ins.got_share) if slot else own_parts(ins.mix)
        sides.append(gradient_units(ins, slot, outs.direct, share))
    units = [
        (slot, kind, unit)
        for slot in range(2)
        for kind, side in enumerate(sides[slot][0])
        for unit in side
    ]
    sweeps = PINV_ITERS - EARLY_SWEEPS
    span = -(-len(units) // (2 * sweeps))
    work = iter([units[index : index + span] for index in range(0, len(units), span)])
    saved = (ins.pair, ins.weight, ins.growth)
    state = (ins.state[0], ins.state[1])

    def beside():
        for slot, kind, unit in next(work, ()):
            need(ins.vg)
            need(ins.turned, slot)
            need(ins.token_prob if kind else ins.key_exp, slot)
            unit()

    for sweep in range(sweeps):
        for ref in saved:
            need(ref, sweep)
        state = gradient_sweep(state, saved, sweep, beside, sweep == sweeps - 1)
    put(outs.direct)
    need()
    growth = state[1]
    mark_prob = ins.mark_prob[...]
    mark_grad = ins.factor[0:1, 0:1] * (
        split_dot_nt(
            (ins.last_growth[0], ins.last_growth[1]), (ins.inverse_grad[0], ins.inverse_grad[1])
        )
        + split_dot(halves(growth + growth.T), halves(mark_prob))
    )
    mark_sgrad = mark_prob * (mark_grad - jnp.sum(mark_grad * mark_prob, axis=1, keepdims=True))

    def marks_dot(left, right):
        left_high, left_low = halves(left)
        return wide_dot(
            jnp.concatenate([left_high, left_low], axis=1), jnp.concatenate([right, right], axis=0)
        )

    own_marks = (
        marks_dot(mark_sgrad, ins.marks[0, 1]),
        marks_dot(mark_sgrad.T, ins.marks[0, 0]),
    )
    marks_scale = HD ** (-0.5) / (tokens_of(ins.vg) // HALF)
    for slot, (_, query_sums, key_sums) in enumerate(sides):
        for kind, sums in enumerate((query_sums, key_sums)):
            total = sum(sums[1:], sums[0]).T
            if slot == 0:
                total = total + own_marks[kind]
            total = total * marks_scale
            outs.far[kind, slot] = total[HALF:].astype(jnp.bfloat16)
            outs.near[kind, slot] = total[:HALF]
    put(outs.far)


def finish_compute(ins, outs, need, put):
    need(ins.near)
    need(ins.got_far)
    out_ref = outs.out
    group = CHUNK // out_ref.shape[3]
    segment_len = tokens_of(out_ref) // HALF
    per = CHUNK // segment_len
    for index in range(tokens_of(out_ref) // CHUNK):
        place, start = slice(index * per, (index + 1) * per), index * CHUNK
        for slot in range(2):
            for kind in range(2):
                if index % 2 == 0:
                    need(ins.direct, slot, kind, start)
                marks = ins.near[kind, slot, place] + ins.got_far[
                    kind, 1 - slot, place
                ].astype(jnp.float32)
                spread = jnp.broadcast_to(marks[:, None], (per, segment_len, HD))
                total = ins.direct[slot, kind, start : start + CHUNK] + spread.reshape(CHUNK, HD)
                store_chunk(out_ref, (kind, slot), index, total.astype(jnp.bfloat16))
        put(out_ref, index * group)


def exchange(packed):
    return lax.all_to_all(packed, "cube", split_axis=0, concat_axis=0, tiled=True)


def partner(array):
    return lax.ppermute(array, "half", SWAP)


def body(queries, keys, values, out_grad):
    half = lax.axis_index("half").reshape(1)
    qk, vg_packed = lax.optimization_barrier(
        (exchange(pack(half, queries, keys)), pack(half, values, out_grad))
    )
    tokens = qk.shape[0] * qk.shape[3]
    mine = landmarks_of(qk)
    theirs = partner(mine)
    vg_packed, mine = lax.optimization_barrier((vg_packed, mine))
    vg = exchange(vg_packed)
    kept = staged_call(
        probability_compute,
        dict(qk=qk, mine=mine, theirs=theirs),
        dict(
            marks=low(2, 2, M, HD),
            token_prob=wide(2, tokens, M),
            token_low=low(2, tokens, M),
            key_exp=wide(2, tokens, M),
            key_low=low(2, tokens, M),
            turned=low(2, 2, HD, tokens),
            stats=wide(8, M),
            mark_prob=wide(M, M),
            factor=wide(8, HD),
            pair_a=(low(EARLY_SWEEPS, 2, 2 * M, M), LEAD),
            weight_a=(low(EARLY_SWEEPS, 2, M, M), LEAD),
            growth_a=(low(EARLY_SWEEPS, 2, M, M), LEAD),
            pair_b=(low(PINV_ITERS - EARLY_SWEEPS, 2, 2 * M, M), LEAD),
            weight_b=(low(PINV_ITERS - EARLY_SWEEPS, 2, M, M), LEAD),
            growth_b=(low(PINV_ITERS - EARLY_SWEEPS, 2, M, M), LEAD),
            inverse=low(2, M, M),
            last_growth=low(2, M, M),
        ),
        LONG,
        extra=(pltpu.VMEM((M, M), jnp.float32), pltpu.VMEM((2 * M, M), jnp.float32)),
    )
    sums = staged_call(
        partial_compute,
        dict(
            vg=vg,
            stats=kept.stats,
            key_low=(kept.key_low, LEAD),
            token_low=(kept.token_low, LEAD),
        ),
        dict(send=low(2 * HD + 16, M), keep=wide(2 * HD, M)),
        2,
    )
    share, mix = joined_sums(partner(sums.send), sums.keep, kept.stats, kept.inverse)
    got_share = partner(share)
    own = staged_call(
        own_gradient_compute,
        dict(
            mark_prob=kept.mark_prob,
            factor=kept.factor,
            mix=mix,
            token_low=(kept.token_low, SLOTS[0]),
            pair=(kept.pair_a, LEAD),
            weight=(kept.weight_a, LEAD),
            growth=(kept.growth_a, LEAD),
            key_exp=(kept.key_exp, SLOTS[0]),
        ),
        dict(
            out=low(qk.shape[0], 2, *qk.shape[3:]),
            state=wide(2, M, M),
            inverse_grad=low(2, M, M),
        ),
        8,
    )
    first_results = staged_call(
        other_out_compute,
        dict(
            got_share=got_share,
            mix=mix,
            token_low=(kept.token_low, SLOTS[1]),
            key_exp=(kept.key_exp, SLOTS[1]),
            own_out=own.out,
        ),
        dict(out=(low(*qk.shape), GROUPS)),
        1,
    ).out
    attended, value_gradient_array = unpack(half, exchange(first_results))
    grads = staged_call(
        gradient_compute,
        dict(
            state=own.state,
            got_share=got_share,
            mix=mix,
            marks=kept.marks,
            pair=(kept.pair_b, LEAD),
            weight=(kept.weight_b, LEAD),
            growth=(kept.growth_b, LEAD),
            vg=(vg, LATE),
            key_exp=(kept.key_exp, LEAD),
            turned=(kept.turned, LEAD),
            token_prob=(kept.token_prob, LEAD),
            inverse_grad=(own.inverse_grad, LAST),
            last_growth=(kept.last_growth, LAST),
            mark_prob=(kept.mark_prob, LAST),
            factor=(kept.factor, LAST),
        ),
        dict(
            far=low(2, 2, HALF, HD),
            near=wide(2, 2, HALF, HD),
            direct=(wide(2, 2, tokens, HD), LEAD),
        ),
        LONG,
        after=(first_results,),
    )
    results = staged_call(
        finish_compute,
        dict(got_far=partner(grads.far), near=grads.near, direct=(grads.direct, BLOCKS)),
        dict(out=(low(*qk.shape), GROUPS)),
        0.1,
    ).out
    query_grad, key_grad = unpack(half, exchange(results))
    return attended, query_grad, key_grad, value_gradient_array


def solution(mesh):
    whole_placement = P(("seq", "head"), None)
    halves_placement = P(("half", "cube"), None)

    def layer(queries, keys, values, out_grad):
        tokens, width = queries.shape
        own_head_each = width // HD == mesh.size and tokens == 8 * CHUNK
        if own_head_each:
            split = jax.sharding.Mesh(
                mesh.devices.reshape(2, mesh.size // 2), ("half", "cube")
            )
        return jax.shard_map(
            body if own_head_each else shared_body,
            mesh=split if own_head_each else mesh,
            in_specs=(halves_placement if own_head_each else whole_placement,) * 4,
            out_specs=(halves_placement if own_head_each else whole_placement,) * 4,
            check_vma=False,
        )(queries, keys, values, out_grad)

    return layer
```

```python
import functools
from types import SimpleNamespace

import jax
import jax.numpy as jnp
from jax import lax
from jax.experimental import pallas as pl
from jax.experimental.pallas import tpu as pltpu
from jax.sharding import PartitionSpec as P

HD = 128
M = 256
PINV_ITERS = 6
CHUNK = 256
PACK_GROUPS = 4
HALF = M // 2
SWAP = ((0, 1), (1, 0))
VMEM_LIMIT = 60 * 2**20
SMALL_LIMIT = 16 * 2**20
WHOLE, LEAD, GROUPS, BLOCKS, LATE, LAST = range(6)
SLOTS = (10, 11)
LONG = 200
EARLY_SWEEPS = PINV_ITERS // 2


precise_setting = lax.Precision.HIGHEST


def newton_inverse(matrix):
    identity = jnp.eye(matrix.shape[0], dtype=matrix.dtype)
    factor = lax.stop_gradient(1.0 / jnp.max(jnp.sum(matrix, axis=0)))
    iterate = matrix.T * factor
    for sweep_index in range(PINV_ITERS):
        product = jnp.matmul(matrix, iterate, precision=precise_setting)
        inner_term = jnp.matmul(product, 7.0 * identity - product, precision=precise_setting)
        inner_term = jnp.matmul(product, 15.0 * identity - inner_term, precision=precise_setting)
        iterate = 0.25 * jnp.matmul(
            iterate, 13.0 * identity - inner_term, precision=precise_setting
        )
    return iterate


def share_heads(own_matrix, head_count):
    seq_index = lax.axis_index("seq")
    slot_mask = (jnp.arange(head_count, dtype=jnp.int32) == seq_index).astype(jnp.float32)
    return lax.psum(slot_mask[:, None, None] * own_matrix[None], "seq")


def shared_body(queries, keys, values, out_grad):
    query_rows, key_rows, value_rows, grad_rows = (
        lax.all_to_all(queries, "head", split_axis=1, concat_axis=0, tiled=True),
        lax.all_to_all(keys, "head", split_axis=1, concat_axis=0, tiled=True),
        lax.all_to_all(values, "head", split_axis=1, concat_axis=0, tiled=True),
        lax.all_to_all(out_grad, "head", split_axis=1, concat_axis=0, tiled=True),
    )
    tok_rows = query_rows.shape[0]
    head_count = query_rows.shape[1] // HD
    local_marks = M // lax.axis_size("seq")
    segment_len = tok_rows // local_marks
    score_scale = HD ** (-0.5)
    seq_index = lax.axis_index("seq")

    def landmark(matrix):
        summed = jnp.sum(
            matrix.reshape(local_marks, segment_len, matrix.shape[1]), axis=1, dtype=jnp.float32
        )
        return (summed / segment_len).astype(jnp.bfloat16)

    mark_queries, mark_keys = (
        lax.all_gather(landmark(query_rows), "seq", axis=0, tiled=True),
        lax.all_gather(landmark(key_rows), "seq", axis=0, tiled=True),
    )
    query_per_head = query_rows.reshape(tok_rows, head_count, HD)
    key_per_head = key_rows.reshape(tok_rows, head_count, HD)
    value_per_head = value_rows.reshape(tok_rows, head_count, HD)
    gradient_per_head = grad_rows.reshape(tok_rows, head_count, HD)
    landmark_query_heads = mark_queries.reshape(M, head_count, HD)
    landmark_key_heads = mark_keys.reshape(M, head_count, HD)
    key_score = (
        jnp.einsum(
            "pcv,gcv->cpg", landmark_query_heads, key_per_head, preferred_element_type=jnp.float32
        )
        * score_scale
    )
    key_max = lax.pmax(jnp.max(key_score, axis=-1), "seq")
    key_exp = jnp.exp(key_score - key_max[..., None])
    partial_num = jnp.einsum(
        "akq,qay->aky",
        key_exp.astype(jnp.bfloat16),
        value_per_head,
        preferred_element_type=jnp.float32,
    )
    key_total, numerator = lax.psum((jnp.sum(key_exp, axis=-1), partial_num), "seq")
    landmark_value_rows = numerator / key_total[..., None]
    token_prob = jax.nn.softmax(
        jnp.einsum(
            "jti,cti->tjc", query_per_head, landmark_key_heads, preferred_element_type=jnp.float32
        )
        * score_scale,
        axis=-1,
    )
    token_probability_lowered = token_prob.astype(jnp.bfloat16)
    mark_prob = jax.nn.softmax(
        jnp.einsum(
            "jou,iou->oji",
            landmark_query_heads,
            landmark_key_heads,
            preferred_element_type=jnp.float32,
        )
        * score_scale,
        axis=-1,
    )
    own_head = seq_index % head_count
    own_mark = lax.dynamic_index_in_dim(mark_prob, own_head, 0, keepdims=False)
    own_inverse, pull_back = jax.vjp(newton_inverse, own_mark)
    pseudo_inverse_matrix = share_heads(own_inverse, head_count)
    mixing_matrix = jnp.einsum(
        "jvy,jys->jvs", pseudo_inverse_matrix, landmark_value_rows, precision=precise_setting
    )
    mixing_matrix_lowered = mixing_matrix.astype(jnp.bfloat16)
    attended = jnp.einsum(
        "yvo,yor->vyr",
        token_probability_lowered,
        mixing_matrix_lowered,
        preferred_element_type=jnp.float32,
    ).astype(jnp.bfloat16)
    token_grad = jnp.einsum(
        "fag,aog->afo", gradient_per_head, mixing_matrix_lowered, preferred_element_type=jnp.float32
    )
    partial_mix = jnp.einsum(
        "klz,lkr->kzr",
        token_probability_lowered,
        gradient_per_head,
        preferred_element_type=jnp.float32,
    )
    mixing_matrix_gradient = lax.psum(partial_mix, "seq")
    token_score_gradient = (
        token_prob * (token_grad - jnp.sum(token_grad * token_prob, axis=-1, keepdims=True))
    ).astype(jnp.bfloat16)
    direct_qgrad = (
        jnp.einsum(
            "ufg,guc->fuc",
            token_score_gradient,
            landmark_key_heads,
            preferred_element_type=jnp.float32,
        )
        * score_scale
    )
    mark_kgrad_f = (
        jnp.einsum(
            "xgi,gxy->ixy", token_score_gradient, query_per_head, preferred_element_type=jnp.float32
        )
        * score_scale
    )
    pseudo_inverse_gradient = jnp.einsum(
        "ktu,kyu->kty", mixing_matrix_gradient, landmark_value_rows, precision=precise_setting
    )
    landmark_value_gradient = jnp.einsum(
        "lrb,lrz->lbz", pseudo_inverse_matrix, mixing_matrix_gradient, precision=precise_setting
    )
    own_igrad = lax.dynamic_index_in_dim(pseudo_inverse_gradient, own_head, 0, keepdims=False)
    (own_mgrad,) = pull_back(own_igrad)
    mark_grad = share_heads(own_mgrad, head_count)
    mark_sgrad = mark_prob * (mark_grad - jnp.sum(mark_grad * mark_prob, axis=-1, keepdims=True))
    first_mark = seq_index * local_marks
    score_gradient_rows = lax.dynamic_slice_in_dim(mark_sgrad, first_mark, local_marks, 1)
    score_gradient_columns = lax.dynamic_slice_in_dim(mark_sgrad, first_mark, local_marks, 2)
    own_qgrad_a = (
        jnp.einsum(
            "txs,ste->xte",
            score_gradient_rows,
            landmark_key_heads.astype(jnp.float32),
            precision=precise_setting,
        )
        * score_scale
    )
    own_kgrad_a = (
        jnp.einsum(
            "eaj,aev->jev",
            score_gradient_columns,
            landmark_query_heads.astype(jnp.float32),
            precision=precise_setting,
        )
        * score_scale
    )
    landmark_value_lowered = landmark_value_gradient.astype(jnp.bfloat16)
    key_prob = key_exp / key_total[..., None]
    key_probability_lowered = key_prob.astype(jnp.bfloat16)
    value_gradient_array = jnp.einsum(
        "zct,zcj->tzj",
        key_probability_lowered,
        landmark_value_lowered,
        preferred_element_type=jnp.float32,
    )
    key_direct_gradient = jnp.einsum(
        "exb,geb->exg", landmark_value_lowered, value_per_head, preferred_element_type=jnp.float32
    )
    row_total = lax.psum(jnp.sum(key_prob * key_direct_gradient, axis=-1), "seq")
    key_score_gradient = (key_prob * (key_direct_gradient - row_total[..., None])).astype(
        jnp.bfloat16
    )
    direct_kgrad = (
        jnp.einsum(
            "pbo,bpx->opx",
            key_score_gradient,
            landmark_query_heads,
            preferred_element_type=jnp.float32,
        )
        * score_scale
    )
    mark_qgrad_b = (
        jnp.einsum(
            "cbj,jcp->bcp", key_score_gradient, key_per_head, preferred_element_type=jnp.float32
        )
        * score_scale
    )
    own_kgrad_f, own_qgrad_b = (
        lax.psum_scatter(mark_kgrad_f, "seq", scatter_dimension=0, tiled=True),
        lax.psum_scatter(mark_qgrad_b, "seq", scatter_dimension=0, tiled=True),
    )
    mark_qtotal = (own_qgrad_a + own_qgrad_b) / segment_len
    mark_ktotal = (own_kgrad_a + own_kgrad_f) / segment_len
    query_grad = (
        direct_qgrad.reshape(local_marks, segment_len, head_count, HD) + mark_qtotal[:, None]
    )
    key_grad = direct_kgrad.reshape(local_marks, segment_len, head_count, HD) + mark_ktotal[:, None]
    width = head_count * HD
    results = (
        attended.reshape(tok_rows, width),
        query_grad.astype(jnp.bfloat16).reshape(tok_rows, width),
        key_grad.astype(jnp.bfloat16).reshape(tok_rows, width),
        value_gradient_array.astype(jnp.bfloat16).reshape(tok_rows, width),
    )
    attended_out, query_out, key_out, value_out = (
        lax.all_to_all(results[0], "head", split_axis=0, concat_axis=1, tiled=True),
        lax.all_to_all(results[1], "head", split_axis=0, concat_axis=1, tiled=True),
        lax.all_to_all(results[2], "head", split_axis=0, concat_axis=1, tiled=True),
        lax.all_to_all(results[3], "head", split_axis=0, concat_axis=1, tiled=True),
    )
    return (attended_out, query_out, key_out, value_out)


def halves(matrix):
    high = matrix.astype(jnp.bfloat16)
    return high, (matrix - high.astype(jnp.float32)).astype(jnp.bfloat16)


def wide_dot(left, right):
    return jnp.dot(left, right, preferred_element_type=jnp.float32)


def wide_dot_nt(left, right):
    return lax.dot_general(
        left, right, (((1,), (1,)), ((), ())), preferred_element_type=jnp.float32
    )


def split_dot(left, right):
    left_high, left_low = left
    right_high, right_low = right
    return wide_dot(
        jnp.concatenate([left_high, left_high, left_low], axis=1),
        jnp.concatenate([right_high, right_low, right_high], axis=0),
    )


def split_dot_nt(left, right):
    left_high, left_low = left
    right_high, right_low = right
    return wide_dot_nt(
        jnp.concatenate([left_high, left_high, left_low], axis=1),
        jnp.concatenate([right_high, right_low, right_high], axis=1),
    )


def identity_matrix():
    return (
        lax.broadcasted_iota(jnp.int32, (M, M), 0) == lax.broadcasted_iota(jnp.int32, (M, M), 1)
    ).astype(jnp.float32)


def chunk_of(ref, array, slot, index):
    per = CHUNK // ref.shape[3]
    return ref[index * per : (index + 1) * per, array, slot].reshape(CHUNK, HD)


def store_chunk(ref, lead, index, value):
    rows = ref.shape[-2]
    per = CHUNK // rows
    ref[(slice(index * per, (index + 1) * per), *lead)] = value.reshape(per, rows, HD)


def all_tokens(ref, array, slot):
    return ref[:, array, slot].reshape(ref.shape[0] * ref.shape[3], HD)


def tokens_of(ref):
    return ref.shape[0] * ref.shape[3]


def columns(index):
    return pl.ds(pl.multiple_of(index * CHUNK, CHUNK), CHUNK)


def swap_lanes(matrix):
    return jnp.concatenate([matrix[:, HALF:], matrix[:, :HALF]], axis=1)


def thirds(rows):
    first = rows.astype(jnp.bfloat16).astype(jnp.float32)
    second = (rows - first).astype(jnp.bfloat16).astype(jnp.float32)
    return jnp.concatenate([first, second, rows - first - second], axis=0)


def joined_thirds(rows):
    count = rows.shape[0] // 3
    return rows[:count] + (rows[count : 2 * count] + rows[2 * count :])


def held_shape(kind, shape):
    return shape[1:] if kind in SLOTS else shape


def pieces_of(kind, shape):
    if kind == LEAD:
        return [(index,) for index in range(shape[0])]
    if kind == BLOCKS:
        return [
            (first, second, slice(place, place + 2 * CHUNK))
            for place in range(0, shape[2], 2 * CHUNK)
            for first in range(shape[0])
            for second in range(shape[1])
        ]
    if kind == GROUPS:
        per = CHUNK // shape[-2]
        return [(slice(place, place + per),) for place in range(0, shape[0], per)]
    return [()]


def window(ref, piece):
    place = tuple(
        pl.ds(part.start, part.stop - part.start) if isinstance(part, slice) else part
        for part in piece
    )
    return ref.at[place] if place else ref


class Staged:
    def __init__(self, names, kinds, outer, inner, done, outward):
        self.refs = SimpleNamespace(**dict(zip(names, inner)))
        self.copies, self.order = [], []
        count = 0
        steps = []
        for place, (kind, home, held) in enumerate(zip(kinds, outer, inner)):
            home = home.at[kind - SLOTS[0]] if kind in SLOTS else home
            copies = {}
            for step, piece in enumerate(pieces_of(kind, held.shape)):
                ends = (window(held, piece), window(home, piece))
                source, target = ends if outward else ends[::-1]
                key = tuple(
                    part.start if isinstance(part, slice) else part for part in piece
                )
                copies[key] = pltpu.make_async_copy(source, target, done.at[count])
                steps.append(({WHOLE: -1, LAST: 9}.get(kind, step), place, key))
                count += 1
            self.copies.append(copies)
        self.inner = inner
        self.order = sorted(steps, key=lambda item: item[:2])
        self.started, self.waited = set(), set()

    def place_of(self, ref):
        return next(index for index, held in enumerate(self.inner) if held is ref)

    def start(self, ref=None, *key):
        chosen = [
            (place, name)
            for _, place, name in self.order
            if (ref is None or place == self.place_of(ref)) and (not key or name == key)
        ]
        for item in chosen:
            if item not in self.started:
                self.started.add(item)
                self.copies[item[0]][item[1]].start()

    def wait(self, ref=None, *key):
        chosen = [
            (place, name)
            for _, place, name in self.order
            if (ref is None or place == self.place_of(ref)) and (not key or name == key)
        ]
        for item in chosen:
            if item not in self.waited:
                self.waited.add(item)
                self.copies[item[0]][item[1]].wait()


def staged_call(compute, inputs, outputs, flops, extra=(), after=(), in_place=False):
    names_in, names_out = tuple(inputs), tuple(outputs)
    kinds_in = [x[1] if isinstance(x, tuple) else WHOLE for x in inputs.values()]
    kinds_out = [x[1] if isinstance(x, tuple) else WHOLE for x in outputs.values()]
    operands = tuple(x[0] if isinstance(x, tuple) else x for x in inputs.values())
    shapes = tuple(x[0] if isinstance(x, tuple) else x for x in outputs.values())
    n_in, n_out, n_after = len(operands), len(shapes), len(after)
    moved = sum(x.size * x.dtype.itemsize for x in (*operands, *shapes))
    anywhere = pl.BlockSpec(memory_space=pl.ANY)

    def count(kinds, arrays):
        return sum(len(pieces_of(kind, x.shape)) for kind, x in zip(kinds, arrays))

    def kernel(*refs):
        sources, refs = refs[:n_in], refs[n_in + n_after :]
        homes, refs = refs[:n_out], refs[n_out:]
        held_in, held_out = refs[:n_in], refs[n_in : n_in + n_out]
        *scratch, in_done, out_done = refs[n_in + n_out :]
        reads = Staged(names_in, kinds_in, sources, held_in, in_done, False)
        writes = Staged(names_out, kinds_out, homes, held_out, out_done, True)
        reads.start()
        compute(reads.refs, writes.refs, reads.wait, writes.start, *scratch)
        reads.wait()
        writes.start()
        writes.wait()

    results = pl.pallas_call(
        kernel,
        out_shape=shapes,
        in_specs=[anywhere] * (n_in + n_after),
        out_specs=(anywhere,) * n_out,
        scratch_shapes=[
            *(
                pltpu.VMEM(held_shape(kind, x.shape), x.dtype)
                for kind, x in zip((*kinds_in, *kinds_out), (*operands, *shapes))
            ),
            *extra,
            pltpu.SemaphoreType.DMA((count(kinds_in, operands),)),
            pltpu.SemaphoreType.DMA((count(kinds_out, shapes),)),
        ],
        compiler_params=pltpu.CompilerParams(vmem_limit_bytes=VMEM_LIMIT),
        cost_estimate=pl.CostEstimate(
            flops=int(flops * 10**9), bytes_accessed=moved, transcendentals=0
        ),
    )(*operands, *after)
    return SimpleNamespace(**dict(zip(outputs, results)))


def low(*shape):
    return jax.ShapeDtypeStruct(shape, jnp.bfloat16)


def wide(*shape):
    return jax.ShapeDtypeStruct(shape, jnp.float32)


def pack_kernel(half_ref, first_ref, second_ref, out_ref, rows_s, packed_s, in_done, out_done):
    half = half_ref[0]
    pairs = out_ref.shape[0]
    group = pairs // PACK_GROUPS
    span = 2 * HD
    reads, writes = [], []
    for index in range(PACK_GROUPS):
        for array, ref in enumerate((first_ref, second_ref)):
            place = pl.ds(index * group * span, group * span)
            reads.append(
                pltpu.make_async_copy(
                    ref.at[:, place], rows_s.at[array, :, place], in_done.at[array, index]
                )
            )
        place = pl.ds(index * group, group)
        writes.append(
            pltpu.make_async_copy(packed_s.at[place], out_ref.at[place], out_done.at[index])
        )
    for copy in reads:
        copy.start()
    for index in range(PACK_GROUPS):
        for array in range(2):
            reads[2 * index + array].wait()
            for pair in range(index * group, (index + 1) * group):
                start = pair * span
                packed_s[pair, array, half] = rows_s[array, :, start : start + HD]
                packed_s[pair, array, 1 - half] = rows_s[array, :, start + HD : start + span]
        writes[index].start()
    for copy in writes:
        copy.wait()


def unpack_kernel(half_ref, packed_ref, first_ref, second_ref, rows_s, out_done):
    half = half_ref[0]
    pairs = packed_ref.shape[0]
    group = pairs // PACK_GROUPS
    span = 2 * HD
    writes = []
    for index in range(PACK_GROUPS):
        for array, ref in enumerate((first_ref, second_ref)):
            for pair in range(index * group, (index + 1) * group):
                start = pair * span
                rows_s[array, :, start : start + HD] = packed_ref[pair, array, half]
                rows_s[array, :, start + HD : start + span] = packed_ref[pair, array, 1 - half]
            place = pl.ds(index * group * span, group * span)
            write = pltpu.make_async_copy(
                rows_s.at[array, :, place], ref.at[:, place], out_done.at[array, index]
            )
            write.start()
            writes.append(write)
    for copy in writes:
        copy.wait()


def layout_call(kernel, half, operands, out_shape, scratch, in_space, limit):
    anywhere = pl.BlockSpec(memory_space=pl.ANY)
    moved = 2 * sum(x.size * x.dtype.itemsize for x in operands)
    return pl.pallas_call(
        kernel,
        out_shape=out_shape,
        in_specs=[pl.BlockSpec(memory_space=pltpu.SMEM)]
        + [pl.BlockSpec(memory_space=in_space)] * len(operands),
        out_specs=jax.tree.map(lambda _: anywhere, out_shape),
        scratch_shapes=scratch,
        compiler_params=pltpu.CompilerParams(vmem_limit_bytes=limit),
        cost_estimate=pl.CostEstimate(flops=0, bytes_accessed=moved, transcendentals=0),
    )(half, *operands)


def pack(half, first, second):
    rows, width = first.shape
    shape = low(width // (2 * HD), 2, 2, rows, HD)
    scratch = [
        pltpu.VMEM((2, rows, width), jnp.bfloat16),
        pltpu.VMEM(shape.shape, jnp.bfloat16),
        pltpu.SemaphoreType.DMA((2, PACK_GROUPS)),
        pltpu.SemaphoreType.DMA((PACK_GROUPS,)),
    ]
    return layout_call(
        pack_kernel, half, (first, second), shape, scratch, pl.ANY, VMEM_LIMIT
    )


def unpack(half, packed):
    pairs, _, _, rows, _ = packed.shape
    shape = low(rows, pairs * 2 * HD)
    scratch = [
        pltpu.VMEM((2, *shape.shape), jnp.bfloat16),
        pltpu.SemaphoreType.DMA((2, PACK_GROUPS)),
    ]
    return layout_call(
        unpack_kernel, half, (packed,), (shape, shape), scratch, pltpu.VMEM, SMALL_LIMIT
    )


def landmark_kernel(qk_ref, marks_ref):
    tokens = tokens_of(qk_ref)
    segment_len = tokens // HALF
    per = CHUNK // segment_len
    member = (
        lax.broadcasted_iota(jnp.int32, (per, CHUNK), 1) // segment_len
        == lax.broadcasted_iota(jnp.int32, (per, CHUNK), 0)
    ).astype(jnp.bfloat16)
    kinds = [(slot, array) for slot in range(2) for array in range(2)]
    for index in range(tokens // CHUNK):
        parts = [chunk_of(qk_ref, array, slot, index) for slot, array in kinds]
        summed = wide_dot(member, jnp.concatenate(parts, axis=1))
        mean = (summed / segment_len).astype(jnp.bfloat16)
        for place, (slot, array) in enumerate(kinds):
            marks_ref[slot, array, index * per : (index + 1) * per] = mean[
                :, place * HD : (place + 1) * HD
            ]


def landmarks_of(qk):
    held = pl.BlockSpec(memory_space=pltpu.VMEM)
    return pl.pallas_call(
        landmark_kernel,
        out_shape=low(2, 2, HALF, HD),
        in_specs=[held],
        out_specs=held,
        compiler_params=pltpu.CompilerParams(vmem_limit_bytes=SMALL_LIMIT),
        cost_estimate=pl.CostEstimate(
            flops=2 * 10**8, bytes_accessed=qk.size * 2, transcendentals=0
        ),
    )(qk)


def sweep_forward(power_s, iterate_s, saved, sweep, work):
    pair_ref, weight_ref, growth_ref = saved
    power = power_s[...]
    power_high, power_low = halves(power)
    square = split_dot((power_high, power_low), (power_high, power_low))
    next(work)()
    square_halves = halves(square)
    pair = (
        jnp.concatenate([power_high, square_halves[0]], axis=0),
        jnp.concatenate([power_low, square_halves[1]], axis=0),
    )
    pair_ref[sweep, 0], pair_ref[sweep, 1] = pair
    higher = split_dot(pair, square_halves)
    next(work)()
    cube, fourth = higher[:M], higher[M:]
    weight = halves(0.25 * (13.0 * identity_matrix() - 15.0 * power + 7.0 * square - cube))
    power_s[...] = 0.25 * (13.0 * power - 15.0 * square + 7.0 * cube - fourth)
    weight_ref[sweep, 0], weight_ref[sweep, 1] = weight
    iterate = halves(iterate_s[...])
    growth_ref[sweep, 0], growth_ref[sweep, 1] = iterate[0][M:], iterate[1][M:]
    iterate_s[...] = split_dot(iterate, weight)


def probability_compute(ins, outs, need, put, power_s, iterate_s):
    need()
    qk_ref = ins.qk
    chunks = tokens_of(qk_ref) // CHUNK
    score_scale = HD ** (-0.5)
    for slot in range(2):
        for array in range(2):
            outs.marks[slot, array] = jnp.concatenate(
                [ins.mine[slot, array], ins.theirs[1 - slot, array]], axis=0
            )
    put(outs.marks)
    landmark_q, landmark_k = outs.marks[0, 0], outs.marks[0, 1]
    mark_score = wide_dot_nt(landmark_q, landmark_k) * score_scale
    mark_exp = jnp.exp(mark_score - jnp.max(mark_score, axis=1, keepdims=True))
    mark_prob = mark_exp / jnp.sum(mark_exp, axis=1, keepdims=True)
    outs.mark_prob[...] = mark_prob
    factor = 1.0 / jnp.max(jnp.sum(mark_prob, axis=0, keepdims=True), axis=1, keepdims=True)
    outs.factor[...] = jnp.broadcast_to(factor, outs.factor.shape)
    mark_halves = halves(mark_prob)
    power_s[...] = split_dot_nt(mark_halves, mark_halves) * factor
    iterate_s[0:M] = mark_prob.T * factor
    iterate_s[M:] = identity_matrix()
    tops, totals = [[], []], [[], []]

    def scores(slot, index):
        query_chunk, key_chunk = (chunk_of(qk_ref, array, slot, index) for array in range(2))
        place = slice(index * CHUNK, (index + 1) * CHUNK)
        outs.turned[slot, 0, :, place] = query_chunk.T
        outs.turned[slot, 1, :, place] = key_chunk.T
        score = wide_dot_nt(query_chunk, outs.marks[slot, 1]) * score_scale
        grown = jnp.exp(score - jnp.max(score, axis=1, keepdims=True))
        prob = grown * (1.0 / jnp.sum(grown, axis=1, keepdims=True))
        outs.token_prob[slot, place] = prob
        outs.token_low[slot, place] = prob.astype(jnp.bfloat16)
        key_score = wide_dot_nt(key_chunk, outs.marks[slot, 0]) * score_scale
        outs.key_exp[slot, place] = key_score
        tops[slot].append(jnp.max(key_score, axis=0, keepdims=True))

    def grow(slot, index):
        if index == 0:
            tops[slot] = functools.reduce(jnp.maximum, tops[slot])
        place = slice(index * CHUNK, (index + 1) * CHUNK)
        grown = jnp.exp(outs.key_exp[slot, place] - tops[slot])
        outs.key_exp[slot, place] = grown
        outs.key_low[slot, place] = grown.astype(jnp.bfloat16)
        totals[slot].append(jnp.sum(grown, axis=0, keepdims=True))

    def several(unit, pairs):
        for slot, index in pairs:
            unit(slot, index)

    pairs = [(slot, index) for slot in range(2) for index in range(chunks)]
    work = iter(
        [functools.partial(several, scores, [pair]) for pair in pairs]
        + [
            functools.partial(several, grow, pairs[first : first + 2])
            for first in range(0, len(pairs), 2)
        ]
    )
    for sweep in range(PINV_ITERS):
        first = sweep < EARLY_SWEEPS
        place = sweep if first else sweep - EARLY_SWEEPS
        saved = (
            (outs.pair_a, outs.weight_a, outs.growth_a)
            if first
            else (outs.pair_b, outs.weight_b, outs.growth_b)
        )
        sweep_forward(power_s, iterate_s, saved, place, work)
        for ref in saved:
            put(ref, place)
        if sweep == 3:
            for ref in (outs.token_low, outs.token_prob, outs.turned):
                put(ref)
    put(outs.key_low)
    put(outs.key_exp)
    outs.inverse[0], outs.inverse[1] = halves(iterate_s[0:M])
    outs.last_growth[0], outs.last_growth[1] = halves(iterate_s[M:])
    stats = [x for slot in range(2) for x in (tops[slot], sum(totals[slot][1:], totals[slot][0]))]
    outs.stats[0:4] = jnp.concatenate(stats, axis=0)
    outs.stats[4:8] = jnp.zeros((4, M), jnp.float32)


def partial_compute(ins, outs, need, put):
    need(ins.vg)
    turned = [[all_tokens(ins.vg, array, slot).T for array in range(2)] for slot in range(2)]
    need(ins.stats)
    rows = thirds(ins.stats[0:4])
    outs.send[2 * HD :] = jnp.concatenate([rows, jnp.zeros((4, M), jnp.float32)], axis=0).astype(
        jnp.bfloat16
    )
    for slot, home in enumerate((outs.keep, outs.send)):
        need(ins.key_low, slot)
        home[0:HD] = wide_dot(turned[slot][0], ins.key_low[slot]).astype(home.dtype)
        need(ins.token_low, slot)
        home[HD : 2 * HD] = wide_dot(turned[slot][1], ins.token_low[slot]).astype(home.dtype)
        put(home)


def mixing_kernel(got_ref, keep_ref, stats_ref, inverse_ref, share_ref, mix_ref):
    got = got_ref[...].astype(jnp.float32)
    others = swap_lanes(joined_thirds(got[2 * HD : 2 * HD + 12]))
    scales = []
    for slot in range(2):
        own, other = 2 * slot, 2 * (1 - slot)
        own_max, own_total = stats_ref[own : own + 1], stats_ref[own + 1 : own + 2]
        other_max, other_total = others[other : other + 1], others[other + 1 : other + 2]
        key_max = jnp.maximum(own_max, other_max)
        own_factor, other_factor = jnp.exp(own_max - key_max), jnp.exp(other_max - key_max)
        inverse_total = 1.0 / (own_total * own_factor + other_total * other_factor)
        scales.append((own_factor * inverse_total, other_factor * inverse_total))
    landmark_values = keep_ref[0:HD] * scales[0][0] + swap_lanes(got[0:HD]) * scales[0][1]
    mixing_grad = keep_ref[HD : 2 * HD] + swap_lanes(got[HD : 2 * HD])
    inverse = (inverse_ref[0], inverse_ref[1])
    mixing_low = split_dot_nt(halves(landmark_values), inverse).astype(jnp.bfloat16)
    values_low = split_dot(halves(mixing_grad), inverse).astype(jnp.bfloat16)
    row_total = jnp.sum(values_low.astype(jnp.float32) * landmark_values, axis=0, keepdims=True)
    share_ref[0:HD] = mixing_low
    share_ref[HD : 2 * HD] = values_low
    share_ref[2 * HD :] = jnp.concatenate(
        [thirds(row_total), jnp.zeros((13, M), jnp.float32)], axis=0
    ).astype(jnp.bfloat16)
    mix_ref[0:HD] = mixing_low.astype(jnp.float32)
    mix_ref[HD : 2 * HD] = values_low.astype(jnp.float32)
    mix_ref[2 * HD : 2 * HD + 8] = jnp.concatenate(
        [row_total, scales[0][0], scales[1][0], jnp.zeros((5, M), jnp.float32)], axis=0
    )
    mix_ref[2 * HD + 8 : 3 * HD + 8] = mixing_grad
    mix_ref[3 * HD + 8 :] = landmark_values


def joined_sums(*operands):
    held = pl.BlockSpec(memory_space=pltpu.VMEM)
    return pl.pallas_call(
        mixing_kernel,
        out_shape=(low(2 * HD + 16, M), wide(4 * HD + 8, M)),
        in_specs=[held] * len(operands),
        out_specs=(held, held),
        compiler_params=pltpu.CompilerParams(vmem_limit_bytes=SMALL_LIMIT),
        cost_estimate=pl.CostEstimate(flops=2 * 10**8, bytes_accessed=2**20, transcendentals=0),
    )(*operands)


def several(*units):
    for unit in units:
        unit()


def out_units(ins, slot, out_ref, lead, share):
    mixing_low, values_low, _ = share
    scale = ins.mix[2 * HD + 1 + slot : 2 * HD + 2 + slot]

    def token_side(index):
        place = slice(index * CHUNK, (index + 1) * CHUNK)
        attended = wide_dot_nt(ins.token_low[place], mixing_low)
        store_chunk(out_ref, (0, *lead), index, attended.astype(jnp.bfloat16))

    def key_side(index):
        place = slice(index * CHUNK, (index + 1) * CHUNK)
        key_plow = (ins.key_exp[place] * scale).astype(jnp.bfloat16)
        value_gradient = wide_dot_nt(key_plow, values_low)
        store_chunk(out_ref, (1, *lead), index, value_gradient.astype(jnp.bfloat16))

    chunks = ins.token_low.shape[0] // CHUNK
    return [
        functools.partial(unit, index) for unit in (token_side, key_side) for index in range(chunks)
    ]


def gradient_units(ins, slot, direct_ref, share):
    score_scale = HD ** (-0.5)
    mixing_low, values_low, row_total = share
    query_sums, key_sums = [], []
    scale = ins.mix[2 * HD + 1 + slot : 2 * HD + 2 + slot]

    def token_side(index):
        place = slice(index * CHUNK, (index + 1) * CHUNK)
        prob = ins.token_prob[slot, place]
        token_grad = wide_dot(chunk_of(ins.vg, 1, slot, index), mixing_low)
        token_sgrad = (
            prob * (token_grad - jnp.sum(token_grad * prob, axis=1, keepdims=True))
        ).astype(jnp.bfloat16)
        direct_ref[slot, 0, place] = wide_dot(token_sgrad, ins.marks[slot, 1]) * score_scale
        key_sums.append(wide_dot(ins.turned[slot, 0, :, place], token_sgrad))

    def key_side(index):
        place = slice(index * CHUNK, (index + 1) * CHUNK)
        key_prob = ins.key_exp[slot, place] * scale
        key_dgrad = wide_dot(chunk_of(ins.vg, 0, slot, index), values_low)
        key_sgrad = (key_prob * (key_dgrad - row_total)).astype(jnp.bfloat16)
        direct_ref[slot, 1, place] = wide_dot(key_sgrad, ins.marks[slot, 0]) * score_scale
        query_sums.append(wide_dot(ins.turned[slot, 1, :, place], key_sgrad))

    chunks = tokens_of(ins.vg) // CHUNK
    units = [
        [functools.partial(unit, index) for index in range(chunks)] for unit in (key_side, token_side)
    ]
    return units, query_sums, key_sums


def own_parts(ref):
    return (
        ref[0:HD].astype(jnp.bfloat16),
        ref[HD : 2 * HD].astype(jnp.bfloat16),
        ref[2 * HD : 2 * HD + 1],
    )


def other_parts(ref):
    parts = (ref[0:HD], ref[HD : 2 * HD], joined_thirds(ref[2 * HD :].astype(jnp.float32)[0:3]))
    return [swap_lanes(part) for part in parts]


def gradient_sweep(state, saved, place, beside, last):
    power, growth = state
    pair_ref, weight_ref, growth_ref = saved
    pair = (pair_ref[place, 0], pair_ref[place, 1])
    first = split_dot(pair, halves(power))
    beside()
    square = first[:M] + first[:M].T
    second = split_dot(tuple(x[:M] for x in pair) if last else pair, halves(square))
    beside()
    cube = first[M:].T + second[:M]
    weight = halves(0.25 * (7.0 * square - 15.0 * power - cube))
    if not last:
        fourth = second[M:] + second[M:].T
        power = 0.25 * (13.0 * power - 15.0 * square + 7.0 * cube - fourth)
    left = [growth_ref[place, 0], growth_ref[place, 0], growth_ref[place, 1]]
    right = [weight[0], weight[1], weight[0]]
    if growth is not None:
        grown = halves(growth)
        left += [grown[0], grown[0], grown[1]]
        right += [weight_ref[place, 0], weight_ref[place, 1], weight_ref[place, 0]]
    growth = wide_dot(jnp.concatenate(left, axis=1), jnp.concatenate(right, axis=0))
    return power, growth


def own_gradient_compute(ins, outs, need, put):
    for ref in (ins.mark_prob, ins.factor, ins.mix):
        need(ref)
    inverse_grad = split_dot(
        halves(ins.mix[2 * HD + 8 : 3 * HD + 8].T), halves(ins.mix[3 * HD + 8 :])
    )
    inverse_grad_halves = halves(inverse_grad)
    outs.inverse_grad[0], outs.inverse_grad[1] = inverse_grad_halves
    toward = split_dot(halves(ins.mark_prob[...]), inverse_grad_halves) * ins.factor[0:1, 0:1]
    state = (0.5 * (toward + toward.T), None)
    units = out_units(ins, 0, outs.out, (), own_parts(ins.mix))
    work = iter([units[index : index + 2] for index in range(0, len(units), 2)])
    saved = (ins.pair, ins.weight, ins.growth)

    def beside():
        several(*next(work, ()))

    for sweep in range(EARLY_SWEEPS):
        if sweep == 0:
            need(ins.token_low)
        if sweep == 1:
            need(ins.key_exp)
        for ref in saved:
            need(ref, sweep)
        state = gradient_sweep(state, saved, sweep, beside, False)
    outs.state[0], outs.state[1] = state


def other_out_compute(ins, outs, need, put):
    for ref in (ins.got_share, ins.mix, ins.token_low):
        need(ref)
    units = out_units(ins, 1, outs.out, (1,), other_parts(ins.got_share))
    chunks = len(units) // 2
    several(*units[:chunks])
    need()
    group = CHUNK // outs.out.shape[3]
    for index, unit in enumerate(units[chunks:]):
        unit()
        place = slice(index * group, (index + 1) * group)
        outs.out[place, :, 0] = ins.own_out[place]
        put(outs.out, index * group)


def gradient_compute(ins, outs, need, put):
    for ref in (ins.state, ins.mix, ins.got_share, ins.marks):
        need(ref)
    sides = []
    for slot in range(2):
        share = other_parts(ins.got_share) if slot else own_parts(ins.mix)
        sides.append(gradient_units(ins, slot, outs.direct, share))
    units = [
        (slot, kind, unit)
        for slot in range(2)
        for kind, side in enumerate(sides[slot][0])
        for unit in side
    ]
    sweeps = PINV_ITERS - EARLY_SWEEPS
    span = -(-len(units) // (2 * sweeps))
    work = iter([units[index : index + span] for index in range(0, len(units), span)])
    saved = (ins.pair, ins.weight, ins.growth)
    state = (ins.state[0], ins.state[1])

    def beside():
        for slot, kind, unit in next(work, ()):
            need(ins.vg)
            need(ins.turned, slot)
            need(ins.token_prob if kind else ins.key_exp, slot)
            unit()

    for sweep in range(sweeps):
        for ref in saved:
            need(ref, sweep)
        state = gradient_sweep(state, saved, sweep, beside, sweep == sweeps - 1)
    put(outs.direct)
    need()
    growth = state[1]
    mark_prob = ins.mark_prob[...]
    mark_grad = ins.factor[0:1, 0:1] * (
        split_dot_nt(
            (ins.last_growth[0], ins.last_growth[1]), (ins.inverse_grad[0], ins.inverse_grad[1])
        )
        + split_dot(halves(growth + growth.T), halves(mark_prob))
    )
    mark_sgrad = mark_prob * (mark_grad - jnp.sum(mark_grad * mark_prob, axis=1, keepdims=True))

    def marks_dot(left, right):
        left_high, left_low = halves(left)
        return wide_dot(
            jnp.concatenate([left_high, left_low], axis=1), jnp.concatenate([right, right], axis=0)
        )

    own_marks = (
        marks_dot(mark_sgrad, ins.marks[0, 1]),
        marks_dot(mark_sgrad.T, ins.marks[0, 0]),
    )
    marks_scale = HD ** (-0.5) / (tokens_of(ins.vg) // HALF)
    for slot, (_, query_sums, key_sums) in enumerate(sides):
        for kind, sums in enumerate((query_sums, key_sums)):
            total = sum(sums[1:], sums[0]).T
            if slot == 0:
                total = total + own_marks[kind]
            total = total * marks_scale
            outs.far[kind, slot] = total[HALF:].astype(jnp.bfloat16)
            outs.near[kind, slot] = total[:HALF]
    put(outs.far)


def finish_kernel(far_ref, near_ref, direct_ref, home, out_ref, done):
    tokens = tokens_of(out_ref)
    group = CHUNK // out_ref.shape[3]
    segment_len = tokens // HALF
    per = CHUNK // segment_len
    writes = []
    for index in range(tokens // CHUNK):
        place, start = slice(index * per, (index + 1) * per), index * CHUNK
        for slot in range(2):
            for kind in range(2):
                marks = near_ref[kind, slot, place] + far_ref[kind, 1 - slot, place].astype(
                    jnp.float32
                )
                spread = jnp.broadcast_to(marks[:, None], (per, segment_len, HD))
                total = direct_ref[slot, kind, start : start + CHUNK] + spread.reshape(CHUNK, HD)
                store_chunk(out_ref, (kind, slot), index, total.astype(jnp.bfloat16))
        ends = pl.ds(index * group, group)
        write = pltpu.make_async_copy(out_ref.at[ends], home.at[ends], done.at[index])
        write.start()
        writes.append(write)
    for write in writes:
        write.wait()


def finished(shape, *operands):
    held = pl.BlockSpec(memory_space=pltpu.VMEM)
    return pl.pallas_call(
        finish_kernel,
        out_shape=shape,
        in_specs=[held] * len(operands),
        out_specs=pl.BlockSpec(memory_space=pl.ANY),
        scratch_shapes=[
            pltpu.VMEM(shape.shape, shape.dtype),
            pltpu.SemaphoreType.DMA((shape.shape[0] * shape.shape[3] // CHUNK,)),
        ],
        compiler_params=pltpu.CompilerParams(vmem_limit_bytes=SMALL_LIMIT),
        cost_estimate=pl.CostEstimate(flops=10**8, bytes_accessed=2**20, transcendentals=0),
    )(*operands)


def exchange(packed):
    return lax.all_to_all(packed, "cube", split_axis=0, concat_axis=0, tiled=True)


def partner(array):
    return lax.ppermute(array, "half", SWAP)


def body(queries, keys, values, out_grad):
    half = lax.axis_index("half").reshape(1)
    qk, vg_packed = lax.optimization_barrier(
        (exchange(pack(half, queries, keys)), pack(half, values, out_grad))
    )
    tokens = qk.shape[0] * qk.shape[3]
    mine = landmarks_of(qk)
    theirs = partner(mine)
    vg_packed, mine = lax.optimization_barrier((vg_packed, mine))
    vg = exchange(vg_packed)
    kept = staged_call(
        probability_compute,
        dict(qk=qk, mine=mine, theirs=theirs),
        dict(
            marks=low(2, 2, M, HD),
            token_prob=wide(2, tokens, M),
            token_low=low(2, tokens, M),
            key_exp=wide(2, tokens, M),
            key_low=low(2, tokens, M),
            turned=low(2, 2, HD, tokens),
            stats=wide(8, M),
            mark_prob=wide(M, M),
            factor=wide(8, HD),
            pair_a=(low(EARLY_SWEEPS, 2, 2 * M, M), LEAD),
            weight_a=(low(EARLY_SWEEPS, 2, M, M), LEAD),
            growth_a=(low(EARLY_SWEEPS, 2, M, M), LEAD),
            pair_b=(low(PINV_ITERS - EARLY_SWEEPS, 2, 2 * M, M), LEAD),
            weight_b=(low(PINV_ITERS - EARLY_SWEEPS, 2, M, M), LEAD),
            growth_b=(low(PINV_ITERS - EARLY_SWEEPS, 2, M, M), LEAD),
            inverse=low(2, M, M),
            last_growth=low(2, M, M),
        ),
        LONG,
        extra=(pltpu.VMEM((M, M), jnp.float32), pltpu.VMEM((2 * M, M), jnp.float32)),
    )
    sums = staged_call(
        partial_compute,
        dict(
            vg=vg,
            stats=kept.stats,
            key_low=(kept.key_low, LEAD),
            token_low=(kept.token_low, LEAD),
        ),
        dict(send=low(2 * HD + 16, M), keep=wide(2 * HD, M)),
        2,
    )
    share, mix = joined_sums(partner(sums.send), sums.keep, kept.stats, kept.inverse)
    got_share = partner(share)
    own = staged_call(
        own_gradient_compute,
        dict(
            mark_prob=kept.mark_prob,
            factor=kept.factor,
            mix=mix,
            token_low=(kept.token_low, SLOTS[0]),
            pair=(kept.pair_a, LEAD),
            weight=(kept.weight_a, LEAD),
            growth=(kept.growth_a, LEAD),
            key_exp=(kept.key_exp, SLOTS[0]),
        ),
        dict(
            out=low(qk.shape[0], 2, *qk.shape[3:]),
            state=wide(2, M, M),
            inverse_grad=low(2, M, M),
        ),
        8,
    )
    first_results = staged_call(
        other_out_compute,
        dict(
            got_share=got_share,
            mix=mix,
            token_low=(kept.token_low, SLOTS[1]),
            key_exp=(kept.key_exp, SLOTS[1]),
            own_out=own.out,
        ),
        dict(out=(low(*qk.shape), GROUPS)),
        1,
    ).out
    attended, value_gradient_array = unpack(half, exchange(first_results))
    grads = staged_call(
        gradient_compute,
        dict(
            state=own.state,
            got_share=got_share,
            mix=mix,
            marks=kept.marks,
            pair=(kept.pair_b, LEAD),
            weight=(kept.weight_b, LEAD),
            growth=(kept.growth_b, LEAD),
            vg=(vg, LATE),
            key_exp=(kept.key_exp, LEAD),
            turned=(kept.turned, LEAD),
            token_prob=(kept.token_prob, LEAD),
            inverse_grad=(own.inverse_grad, LAST),
            last_growth=(kept.last_growth, LAST),
            mark_prob=(kept.mark_prob, LAST),
            factor=(kept.factor, LAST),
        ),
        dict(
            far=low(2, 2, HALF, HD),
            near=wide(2, 2, HALF, HD),
            direct=(wide(2, 2, tokens, HD), LEAD),
        ),
        LONG,
        after=(first_results,),
    )
    results = finished(low(*qk.shape), partner(grads.far), grads.near, grads.direct)
    query_grad, key_grad = unpack(half, exchange(results))
    return attended, query_grad, key_grad, value_gradient_array


def solution(mesh):
    whole_placement = P(("seq", "head"), None)
    halves_placement = P(("half", "cube"), None)

    def layer(queries, keys, values, out_grad):
        tokens, width = queries.shape
        own_head_each = width // HD == mesh.size and tokens == 8 * CHUNK
        if own_head_each:
            split = jax.sharding.Mesh(
                mesh.devices.reshape(2, mesh.size // 2), ("half", "cube")
            )
        return jax.shard_map(
            body if own_head_each else shared_body,
            mesh=split if own_head_each else mesh,
            in_specs=(halves_placement if own_head_each else whole_placement,) * 4,
            out_specs=(halves_placement if own_head_each else whole_placement,) * 4,
            check_vma=False,
        )(queries, keys, values, out_grad)

    return layer
```

```python
import functools
from types import SimpleNamespace

import jax
import jax.numpy as jnp
from jax import lax
from jax.experimental import pallas as pl
from jax.experimental.pallas import tpu as pltpu
from jax.sharding import PartitionSpec as P

HD = 128
M = 256
PINV_ITERS = 6
CHUNK = 256
PACK_GROUPS = 4
HALF = M // 2
SWAP = ((0, 1), (1, 0))
VMEM_LIMIT = 60 * 2**20
SMALL_LIMIT = 16 * 2**20
WHOLE, LEAD, GROUPS, BLOCKS, LATE, LAST = range(6)
SLOTS = (10, 11)
TOP = 12
LONG = 200
EARLY_SWEEPS = PINV_ITERS // 2


precise_setting = lax.Precision.HIGHEST


def newton_inverse(matrix):
    identity = jnp.eye(matrix.shape[0], dtype=matrix.dtype)
    factor = lax.stop_gradient(1.0 / jnp.max(jnp.sum(matrix, axis=0)))
    iterate = matrix.T * factor
    for sweep_index in range(PINV_ITERS):
        product = jnp.matmul(matrix, iterate, precision=precise_setting)
        inner_term = jnp.matmul(product, 7.0 * identity - product, precision=precise_setting)
        inner_term = jnp.matmul(product, 15.0 * identity - inner_term, precision=precise_setting)
        iterate = 0.25 * jnp.matmul(
            iterate, 13.0 * identity - inner_term, precision=precise_setting
        )
    return iterate


def share_heads(own_matrix, head_count):
    seq_index = lax.axis_index("seq")
    slot_mask = (jnp.arange(head_count, dtype=jnp.int32) == seq_index).astype(jnp.float32)
    return lax.psum(slot_mask[:, None, None] * own_matrix[None], "seq")


def shared_body(queries, keys, values, out_grad):
    query_rows, key_rows, value_rows, grad_rows = (
        lax.all_to_all(queries, "head", split_axis=1, concat_axis=0, tiled=True),
        lax.all_to_all(keys, "head", split_axis=1, concat_axis=0, tiled=True),
        lax.all_to_all(values, "head", split_axis=1, concat_axis=0, tiled=True),
        lax.all_to_all(out_grad, "head", split_axis=1, concat_axis=0, tiled=True),
    )
    tok_rows = query_rows.shape[0]
    head_count = query_rows.shape[1] // HD
    local_marks = M // lax.axis_size("seq")
    segment_len = tok_rows // local_marks
    score_scale = HD ** (-0.5)
    seq_index = lax.axis_index("seq")

    def landmark(matrix):
        summed = jnp.sum(
            matrix.reshape(local_marks, segment_len, matrix.shape[1]), axis=1, dtype=jnp.float32
        )
        return (summed / segment_len).astype(jnp.bfloat16)

    mark_queries, mark_keys = (
        lax.all_gather(landmark(query_rows), "seq", axis=0, tiled=True),
        lax.all_gather(landmark(key_rows), "seq", axis=0, tiled=True),
    )
    query_per_head = query_rows.reshape(tok_rows, head_count, HD)
    key_per_head = key_rows.reshape(tok_rows, head_count, HD)
    value_per_head = value_rows.reshape(tok_rows, head_count, HD)
    gradient_per_head = grad_rows.reshape(tok_rows, head_count, HD)
    landmark_query_heads = mark_queries.reshape(M, head_count, HD)
    landmark_key_heads = mark_keys.reshape(M, head_count, HD)
    key_score = (
        jnp.einsum(
            "pcv,gcv->cpg", landmark_query_heads, key_per_head, preferred_element_type=jnp.float32
        )
        * score_scale
    )
    key_max = lax.pmax(jnp.max(key_score, axis=-1), "seq")
    key_exp = jnp.exp(key_score - key_max[..., None])
    partial_num = jnp.einsum(
        "akq,qay->aky",
        key_exp.astype(jnp.bfloat16),
        value_per_head,
        preferred_element_type=jnp.float32,
    )
    key_total, numerator = lax.psum((jnp.sum(key_exp, axis=-1), partial_num), "seq")
    landmark_value_rows = numerator / key_total[..., None]
    token_prob = jax.nn.softmax(
        jnp.einsum(
            "jti,cti->tjc", query_per_head, landmark_key_heads, preferred_element_type=jnp.float32
        )
        * score_scale,
        axis=-1,
    )
    token_probability_lowered = token_prob.astype(jnp.bfloat16)
    mark_prob = jax.nn.softmax(
        jnp.einsum(
            "jou,iou->oji",
            landmark_query_heads,
            landmark_key_heads,
            preferred_element_type=jnp.float32,
        )
        * score_scale,
        axis=-1,
    )
    own_head = seq_index % head_count
    own_mark = lax.dynamic_index_in_dim(mark_prob, own_head, 0, keepdims=False)
    own_inverse, pull_back = jax.vjp(newton_inverse, own_mark)
    pseudo_inverse_matrix = share_heads(own_inverse, head_count)
    mixing_matrix = jnp.einsum(
        "jvy,jys->jvs", pseudo_inverse_matrix, landmark_value_rows, precision=precise_setting
    )
    mixing_matrix_lowered = mixing_matrix.astype(jnp.bfloat16)
    attended = jnp.einsum(
        "yvo,yor->vyr",
        token_probability_lowered,
        mixing_matrix_lowered,
        preferred_element_type=jnp.float32,
    ).astype(jnp.bfloat16)
    token_grad = jnp.einsum(
        "fag,aog->afo", gradient_per_head, mixing_matrix_lowered, preferred_element_type=jnp.float32
    )
    partial_mix = jnp.einsum(
        "klz,lkr->kzr",
        token_probability_lowered,
        gradient_per_head,
        preferred_element_type=jnp.float32,
    )
    mixing_matrix_gradient = lax.psum(partial_mix, "seq")
    token_score_gradient = (
        token_prob * (token_grad - jnp.sum(token_grad * token_prob, axis=-1, keepdims=True))
    ).astype(jnp.bfloat16)
    direct_qgrad = (
        jnp.einsum(
            "ufg,guc->fuc",
            token_score_gradient,
            landmark_key_heads,
            preferred_element_type=jnp.float32,
        )
        * score_scale
    )
    mark_kgrad_f = (
        jnp.einsum(
            "xgi,gxy->ixy", token_score_gradient, query_per_head, preferred_element_type=jnp.float32
        )
        * score_scale
    )
    pseudo_inverse_gradient = jnp.einsum(
        "ktu,kyu->kty", mixing_matrix_gradient, landmark_value_rows, precision=precise_setting
    )
    landmark_value_gradient = jnp.einsum(
        "lrb,lrz->lbz", pseudo_inverse_matrix, mixing_matrix_gradient, precision=precise_setting
    )
    own_igrad = lax.dynamic_index_in_dim(pseudo_inverse_gradient, own_head, 0, keepdims=False)
    (own_mgrad,) = pull_back(own_igrad)
    mark_grad = share_heads(own_mgrad, head_count)
    mark_sgrad = mark_prob * (mark_grad - jnp.sum(mark_grad * mark_prob, axis=-1, keepdims=True))
    first_mark = seq_index * local_marks
    score_gradient_rows = lax.dynamic_slice_in_dim(mark_sgrad, first_mark, local_marks, 1)
    score_gradient_columns = lax.dynamic_slice_in_dim(mark_sgrad, first_mark, local_marks, 2)
    own_qgrad_a = (
        jnp.einsum(
            "txs,ste->xte",
            score_gradient_rows,
            landmark_key_heads.astype(jnp.float32),
            precision=precise_setting,
        )
        * score_scale
    )
    own_kgrad_a = (
        jnp.einsum(
            "eaj,aev->jev",
            score_gradient_columns,
            landmark_query_heads.astype(jnp.float32),
            precision=precise_setting,
        )
        * score_scale
    )
    landmark_value_lowered = landmark_value_gradient.astype(jnp.bfloat16)
    key_prob = key_exp / key_total[..., None]
    key_probability_lowered = key_prob.astype(jnp.bfloat16)
    value_gradient_array = jnp.einsum(
        "zct,zcj->tzj",
        key_probability_lowered,
        landmark_value_lowered,
        preferred_element_type=jnp.float32,
    )
    key_direct_gradient = jnp.einsum(
        "exb,geb->exg", landmark_value_lowered, value_per_head, preferred_element_type=jnp.float32
    )
    row_total = lax.psum(jnp.sum(key_prob * key_direct_gradient, axis=-1), "seq")
    key_score_gradient = (key_prob * (key_direct_gradient - row_total[..., None])).astype(
        jnp.bfloat16
    )
    direct_kgrad = (
        jnp.einsum(
            "pbo,bpx->opx",
            key_score_gradient,
            landmark_query_heads,
            preferred_element_type=jnp.float32,
        )
        * score_scale
    )
    mark_qgrad_b = (
        jnp.einsum(
            "cbj,jcp->bcp", key_score_gradient, key_per_head, preferred_element_type=jnp.float32
        )
        * score_scale
    )
    own_kgrad_f, own_qgrad_b = (
        lax.psum_scatter(mark_kgrad_f, "seq", scatter_dimension=0, tiled=True),
        lax.psum_scatter(mark_qgrad_b, "seq", scatter_dimension=0, tiled=True),
    )
    mark_qtotal = (own_qgrad_a + own_qgrad_b) / segment_len
    mark_ktotal = (own_kgrad_a + own_kgrad_f) / segment_len
    query_grad = (
        direct_qgrad.reshape(local_marks, segment_len, head_count, HD) + mark_qtotal[:, None]
    )
    key_grad = direct_kgrad.reshape(local_marks, segment_len, head_count, HD) + mark_ktotal[:, None]
    width = head_count * HD
    results = (
        attended.reshape(tok_rows, width),
        query_grad.astype(jnp.bfloat16).reshape(tok_rows, width),
        key_grad.astype(jnp.bfloat16).reshape(tok_rows, width),
        value_gradient_array.astype(jnp.bfloat16).reshape(tok_rows, width),
    )
    attended_out, query_out, key_out, value_out = (
        lax.all_to_all(results[0], "head", split_axis=0, concat_axis=1, tiled=True),
        lax.all_to_all(results[1], "head", split_axis=0, concat_axis=1, tiled=True),
        lax.all_to_all(results[2], "head", split_axis=0, concat_axis=1, tiled=True),
        lax.all_to_all(results[3], "head", split_axis=0, concat_axis=1, tiled=True),
    )
    return (attended_out, query_out, key_out, value_out)


def halves(matrix):
    high = matrix.astype(jnp.bfloat16)
    return high, (matrix - high.astype(jnp.float32)).astype(jnp.bfloat16)


def wide_dot(left, right):
    return jnp.dot(left, right, preferred_element_type=jnp.float32)


def wide_dot_nt(left, right):
    return lax.dot_general(
        left, right, (((1,), (1,)), ((), ())), preferred_element_type=jnp.float32
    )


def split_dot(left, right):
    left_high, left_low = left
    right_high, right_low = right
    return wide_dot(
        jnp.concatenate([left_high, left_high, left_low], axis=1),
        jnp.concatenate([right_high, right_low, right_high], axis=0),
    )


def split_dot_nt(left, right):
    left_high, left_low = left
    right_high, right_low = right
    return wide_dot_nt(
        jnp.concatenate([left_high, left_high, left_low], axis=1),
        jnp.concatenate([right_high, right_low, right_high], axis=1),
    )


def identity_matrix():
    return (
        lax.broadcasted_iota(jnp.int32, (M, M), 0) == lax.broadcasted_iota(jnp.int32, (M, M), 1)
    ).astype(jnp.float32)


def chunk_of(ref, array, slot, index):
    per = CHUNK // ref.shape[3]
    return ref[index * per : (index + 1) * per, array, slot].reshape(CHUNK, HD)


def store_chunk(ref, lead, index, value):
    rows = ref.shape[-2]
    per = CHUNK // rows
    ref[(slice(index * per, (index + 1) * per), *lead)] = value.reshape(per, rows, HD)


def all_tokens(ref, array, slot):
    return ref[:, array, slot].reshape(ref.shape[0] * ref.shape[3], HD)


def tokens_of(ref):
    return ref.shape[0] * ref.shape[3]


def columns(index):
    return pl.ds(pl.multiple_of(index * CHUNK, CHUNK), CHUNK)


def swap_lanes(matrix):
    return jnp.concatenate([matrix[:, HALF:], matrix[:, :HALF]], axis=1)


def thirds(rows):
    first = rows.astype(jnp.bfloat16).astype(jnp.float32)
    second = (rows - first).astype(jnp.bfloat16).astype(jnp.float32)
    return jnp.concatenate([first, second, rows - first - second], axis=0)


def joined_thirds(rows):
    count = rows.shape[0] // 3
    return rows[:count] + (rows[count : 2 * count] + rows[2 * count :])


def held_shape(kind, shape):
    if kind == TOP:
        return (2 * HD + 8, *shape[1:])
    return shape[1:] if kind in SLOTS else shape


def pieces_of(kind, shape):
    if kind == LEAD:
        return [(index,) for index in range(shape[0])]
    if kind == BLOCKS:
        return [
            (first, second, slice(place, place + 2 * CHUNK))
            for place in range(0, shape[2], 2 * CHUNK)
            for first in range(shape[0])
            for second in range(shape[1])
        ]
    if kind == GROUPS:
        per = CHUNK // shape[-2]
        return [(slice(place, place + per),) for place in range(0, shape[0], per)]
    return [()]


def window(ref, piece):
    place = tuple(
        pl.ds(part.start, part.stop - part.start) if isinstance(part, slice) else part
        for part in piece
    )
    return ref.at[place] if place else ref


class Staged:
    def __init__(self, names, kinds, outer, inner, done, outward):
        self.refs = SimpleNamespace(**dict(zip(names, inner)))
        self.copies, self.order = [], []
        count = 0
        steps = []
        for place, (kind, home, held) in enumerate(zip(kinds, outer, inner)):
            home = home.at[kind - SLOTS[0]] if kind in SLOTS else home
            home = home.at[pl.ds(0, 2 * HD + 8)] if kind == TOP else home
            copies = {}
            for step, piece in enumerate(pieces_of(kind, held.shape)):
                ends = (window(held, piece), window(home, piece))
                source, target = ends if outward else ends[::-1]
                key = tuple(
                    part.start if isinstance(part, slice) else part for part in piece
                )
                copies[key] = pltpu.make_async_copy(source, target, done.at[count])
                steps.append(({WHOLE: -1, TOP: -1, LAST: 9}.get(kind, step), place, key))
                count += 1
            self.copies.append(copies)
        self.inner = inner
        self.order = sorted(steps, key=lambda item: item[:2])
        self.started, self.waited = set(), set()

    def place_of(self, ref):
        return next(index for index, held in enumerate(self.inner) if held is ref)

    def start(self, ref=None, *key):
        chosen = [
            (place, name)
            for _, place, name in self.order
            if (ref is None or place == self.place_of(ref)) and (not key or name == key)
        ]
        for item in chosen:
            if item not in self.started:
                self.started.add(item)
                self.copies[item[0]][item[1]].start()

    def wait(self, ref=None, *key):
        chosen = [
            (place, name)
            for _, place, name in self.order
            if (ref is None or place == self.place_of(ref)) and (not key or name == key)
        ]
        for item in chosen:
            if item not in self.waited:
                self.waited.add(item)
                self.copies[item[0]][item[1]].wait()


def staged_call(compute, inputs, outputs, flops, extra=(), after=(), in_place=False):
    names_in, names_out = tuple(inputs), tuple(outputs)
    kinds_in = [x[1] if isinstance(x, tuple) else WHOLE for x in inputs.values()]
    kinds_out = [x[1] if isinstance(x, tuple) else WHOLE for x in outputs.values()]
    operands = tuple(x[0] if isinstance(x, tuple) else x for x in inputs.values())
    shapes = tuple(x[0] if isinstance(x, tuple) else x for x in outputs.values())
    n_in, n_out, n_after = len(operands), len(shapes), len(after)
    moved = sum(x.size * x.dtype.itemsize for x in (*operands, *shapes))
    anywhere = pl.BlockSpec(memory_space=pl.ANY)

    def count(kinds, arrays):
        return sum(len(pieces_of(kind, x.shape)) for kind, x in zip(kinds, arrays))

    def kernel(*refs):
        sources, refs = refs[:n_in], refs[n_in + n_after :]
        homes, refs = refs[:n_out], refs[n_out:]
        held_in, held_out = refs[:n_in], refs[n_in : n_in + n_out]
        *scratch, in_done, out_done = refs[n_in + n_out :]
        reads = Staged(names_in, kinds_in, sources, held_in, in_done, False)
        writes = Staged(names_out, kinds_out, homes, held_out, out_done, True)
        reads.start()
        compute(reads.refs, writes.refs, reads.wait, writes.start, *scratch)
        reads.wait()
        writes.start()
        writes.wait()

    results = pl.pallas_call(
        kernel,
        out_shape=shapes,
        in_specs=[anywhere] * (n_in + n_after),
        out_specs=(anywhere,) * n_out,
        scratch_shapes=[
            *(
                pltpu.VMEM(held_shape(kind, x.shape), x.dtype)
                for kind, x in zip((*kinds_in, *kinds_out), (*operands, *shapes))
            ),
            *extra,
            pltpu.SemaphoreType.DMA((count(kinds_in, operands),)),
            pltpu.SemaphoreType.DMA((count(kinds_out, shapes),)),
        ],
        compiler_params=pltpu.CompilerParams(vmem_limit_bytes=VMEM_LIMIT),
        cost_estimate=pl.CostEstimate(
            flops=int(flops * 10**9), bytes_accessed=moved, transcendentals=0
        ),
    )(*operands, *after)
    return SimpleNamespace(**dict(zip(outputs, results)))


def low(*shape):
    return jax.ShapeDtypeStruct(shape, jnp.bfloat16)


def wide(*shape):
    return jax.ShapeDtypeStruct(shape, jnp.float32)


def pack_kernel(half_ref, first_ref, second_ref, out_ref, rows_s, packed_s, in_done, out_done):
    half = half_ref[0]
    pairs = out_ref.shape[0]
    group = pairs // PACK_GROUPS
    span = 2 * HD
    reads, writes = [], []
    for index in range(PACK_GROUPS):
        for array, ref in enumerate((first_ref, second_ref)):
            place = pl.ds(index * group * span, group * span)
            reads.append(
                pltpu.make_async_copy(
                    ref.at[:, place], rows_s.at[array, :, place], in_done.at[array, index]
                )
            )
        place = pl.ds(index * group, group)
        writes.append(
            pltpu.make_async_copy(packed_s.at[place], out_ref.at[place], out_done.at[index])
        )
    for copy in reads:
        copy.start()
    for index in range(PACK_GROUPS):
        for array in range(2):
            reads[2 * index + array].wait()
            for pair in range(index * group, (index + 1) * group):
                start = pair * span
                packed_s[pair, array, half] = rows_s[array, :, start : start + HD]
                packed_s[pair, array, 1 - half] = rows_s[array, :, start + HD : start + span]
        writes[index].start()
    for copy in writes:
        copy.wait()


def unpack_kernel(half_ref, packed_ref, first_ref, second_ref, rows_s, out_done):
    half = half_ref[0]
    pairs = packed_ref.shape[0]
    group = pairs // PACK_GROUPS
    span = 2 * HD
    writes = []
    for index in range(PACK_GROUPS):
        for array, ref in enumerate((first_ref, second_ref)):
            for pair in range(index * group, (index + 1) * group):
                start = pair * span
                rows_s[array, :, start : start + HD] = packed_ref[pair, array, half]
                rows_s[array, :, start + HD : start + span] = packed_ref[pair, array, 1 - half]
            place = pl.ds(index * group * span, group * span)
            write = pltpu.make_async_copy(
                rows_s.at[array, :, place], ref.at[:, place], out_done.at[array, index]
            )
            write.start()
            writes.append(write)
    for copy in writes:
        copy.wait()


def layout_call(kernel, half, operands, out_shape, scratch, in_space, limit):
    anywhere = pl.BlockSpec(memory_space=pl.ANY)
    moved = 2 * sum(x.size * x.dtype.itemsize for x in operands)
    return pl.pallas_call(
        kernel,
        out_shape=out_shape,
        in_specs=[pl.BlockSpec(memory_space=pltpu.SMEM)]
        + [pl.BlockSpec(memory_space=in_space)] * len(operands),
        out_specs=jax.tree.map(lambda _: anywhere, out_shape),
        scratch_shapes=scratch,
        compiler_params=pltpu.CompilerParams(vmem_limit_bytes=limit),
        cost_estimate=pl.CostEstimate(flops=0, bytes_accessed=moved, transcendentals=0),
    )(half, *operands)


def pack(half, first, second):
    rows, width = first.shape
    shape = low(width // (2 * HD), 2, 2, rows, HD)
    scratch = [
        pltpu.VMEM((2, rows, width), jnp.bfloat16),
        pltpu.VMEM(shape.shape, jnp.bfloat16),
        pltpu.SemaphoreType.DMA((2, PACK_GROUPS)),
        pltpu.SemaphoreType.DMA((PACK_GROUPS,)),
    ]
    return layout_call(
        pack_kernel, half, (first, second), shape, scratch, pl.ANY, VMEM_LIMIT
    )


def unpack(half, packed):
    pairs, _, _, rows, _ = packed.shape
    shape = low(rows, pairs * 2 * HD)
    scratch = [
        pltpu.VMEM((2, *shape.shape), jnp.bfloat16),
        pltpu.SemaphoreType.DMA((2, PACK_GROUPS)),
    ]
    return layout_call(
        unpack_kernel, half, (packed,), (shape, shape), scratch, pltpu.VMEM, SMALL_LIMIT
    )


def landmark_kernel(qk_ref, marks_ref):
    tokens = tokens_of(qk_ref)
    segment_len = tokens // HALF
    per = CHUNK // segment_len
    member = (
        lax.broadcasted_iota(jnp.int32, (per, CHUNK), 1) // segment_len
        == lax.broadcasted_iota(jnp.int32, (per, CHUNK), 0)
    ).astype(jnp.bfloat16)
    kinds = [(slot, array) for slot in range(2) for array in range(2)]
    for index in range(tokens // CHUNK):
        parts = [chunk_of(qk_ref, array, slot, index) for slot, array in kinds]
        summed = wide_dot(member, jnp.concatenate(parts, axis=1))
        mean = (summed / segment_len).astype(jnp.bfloat16)
        for place, (slot, array) in enumerate(kinds):
            marks_ref[slot, array, index * per : (index + 1) * per] = mean[
                :, place * HD : (place + 1) * HD
            ]


def landmarks_of(qk):
    held = pl.BlockSpec(memory_space=pltpu.VMEM)
    return pl.pallas_call(
        landmark_kernel,
        out_shape=low(2, 2, HALF, HD),
        in_specs=[held],
        out_specs=held,
        compiler_params=pltpu.CompilerParams(vmem_limit_bytes=SMALL_LIMIT),
        cost_estimate=pl.CostEstimate(
            flops=2 * 10**8, bytes_accessed=qk.size * 2, transcendentals=0
        ),
    )(qk)


def sweep_forward(power_s, iterate_s, saved, sweep, work):
    pair_ref, weight_ref, growth_ref = saved
    power = power_s[...]
    power_high, power_low = halves(power)
    square = split_dot((power_high, power_low), (power_high, power_low))
    next(work)()
    square_halves = halves(square)
    pair = (
        jnp.concatenate([power_high, square_halves[0]], axis=0),
        jnp.concatenate([power_low, square_halves[1]], axis=0),
    )
    pair_ref[sweep, 0], pair_ref[sweep, 1] = pair
    higher = split_dot(pair, square_halves)
    next(work)()
    cube, fourth = higher[:M], higher[M:]
    weight = halves(0.25 * (13.0 * identity_matrix() - 15.0 * power + 7.0 * square - cube))
    power_s[...] = 0.25 * (13.0 * power - 15.0 * square + 7.0 * cube - fourth)
    weight_ref[sweep, 0], weight_ref[sweep, 1] = weight
    iterate = halves(iterate_s[...])
    growth_ref[sweep, 0], growth_ref[sweep, 1] = iterate[0][M:], iterate[1][M:]
    iterate_s[...] = split_dot(iterate, weight)


def probability_compute(ins, outs, need, put, power_s, iterate_s):
    need()
    qk_ref = ins.qk
    chunks = tokens_of(qk_ref) // CHUNK
    score_scale = HD ** (-0.5)
    for slot in range(2):
        for array in range(2):
            outs.marks[slot, array] = jnp.concatenate(
                [ins.mine[slot, array], ins.theirs[1 - slot, array]], axis=0
            )
    put(outs.marks)
    landmark_q, landmark_k = outs.marks[0, 0], outs.marks[0, 1]
    mark_score = wide_dot_nt(landmark_q, landmark_k) * score_scale
    mark_exp = jnp.exp(mark_score - jnp.max(mark_score, axis=1, keepdims=True))
    mark_prob = mark_exp / jnp.sum(mark_exp, axis=1, keepdims=True)
    outs.mark_prob[...] = mark_prob
    factor = 1.0 / jnp.max(jnp.sum(mark_prob, axis=0, keepdims=True), axis=1, keepdims=True)
    outs.factor[...] = jnp.broadcast_to(factor, outs.factor.shape)
    mark_halves = halves(mark_prob)
    power_s[...] = split_dot_nt(mark_halves, mark_halves) * factor
    iterate_s[0:M] = mark_prob.T * factor
    iterate_s[M:] = identity_matrix()
    tops, totals = [[], []], [[], []]

    def scores(slot, index):
        query_chunk, key_chunk = (chunk_of(qk_ref, array, slot, index) for array in range(2))
        place = slice(index * CHUNK, (index + 1) * CHUNK)
        outs.turned[slot, 0, :, place] = query_chunk.T
        outs.turned[slot, 1, :, place] = key_chunk.T
        score = wide_dot_nt(query_chunk, outs.marks[slot, 1]) * score_scale
        grown = jnp.exp(score - jnp.max(score, axis=1, keepdims=True))
        prob = grown * (1.0 / jnp.sum(grown, axis=1, keepdims=True))
        outs.token_prob[slot, place] = prob
        outs.token_low[slot, place] = prob.astype(jnp.bfloat16)
        key_score = wide_dot_nt(key_chunk, outs.marks[slot, 0]) * score_scale
        outs.key_exp[slot, place] = key_score
        tops[slot].append(jnp.max(key_score, axis=0, keepdims=True))

    def grow(slot, index):
        if index == 0:
            tops[slot] = functools.reduce(jnp.maximum, tops[slot])
        place = slice(index * CHUNK, (index + 1) * CHUNK)
        grown = jnp.exp(outs.key_exp[slot, place] - tops[slot])
        outs.key_exp[slot, place] = grown
        outs.key_low[slot, place] = grown.astype(jnp.bfloat16)
        totals[slot].append(jnp.sum(grown, axis=0, keepdims=True))

    def several(unit, pairs):
        for slot, index in pairs:
            unit(slot, index)

    pairs = [(slot, index) for slot in range(2) for index in range(chunks)]
    work = iter(
        [functools.partial(several, scores, [pair]) for pair in pairs]
        + [
            functools.partial(several, grow, pairs[first : first + 2])
            for first in range(0, len(pairs), 2)
        ]
    )
    for sweep in range(PINV_ITERS):
        first = sweep < EARLY_SWEEPS
        place = sweep if first else sweep - EARLY_SWEEPS
        saved = (
            (outs.pair_a, outs.weight_a, outs.growth_a)
            if first
            else (outs.pair_b, outs.weight_b, outs.growth_b)
        )
        sweep_forward(power_s, iterate_s, saved, place, work)
        for ref in saved:
            put(ref, place)
        if sweep == 3:
            for ref in (outs.token_low, outs.token_prob, outs.turned):
                put(ref)
    put(outs.key_low)
    put(outs.key_exp)
    outs.inverse[0], outs.inverse[1] = halves(iterate_s[0:M])
    outs.last_growth[0], outs.last_growth[1] = halves(iterate_s[M:])
    stats = [x for slot in range(2) for x in (tops[slot], sum(totals[slot][1:], totals[slot][0]))]
    outs.stats[0:4] = jnp.concatenate(stats, axis=0)
    outs.stats[4:8] = jnp.zeros((4, M), jnp.float32)


def partial_compute(ins, outs, need, put):
    need(ins.vg)
    turned = [[all_tokens(ins.vg, array, slot).T for array in range(2)] for slot in range(2)]
    need(ins.stats)
    rows = thirds(ins.stats[0:4])
    outs.send[2 * HD :] = jnp.concatenate([rows, jnp.zeros((4, M), jnp.float32)], axis=0).astype(
        jnp.bfloat16
    )
    for slot, home in enumerate((outs.keep, outs.send)):
        need(ins.key_low, slot)
        home[0:HD] = wide_dot(turned[slot][0], ins.key_low[slot]).astype(home.dtype)
        need(ins.token_low, slot)
        home[HD : 2 * HD] = wide_dot(turned[slot][1], ins.token_low[slot]).astype(home.dtype)
        put(home)


def mixing_kernel(got_ref, keep_ref, stats_ref, inverse_ref, share_ref, mix_ref):
    got = got_ref[...].astype(jnp.float32)
    others = swap_lanes(joined_thirds(got[2 * HD : 2 * HD + 12]))
    scales = []
    for slot in range(2):
        own, other = 2 * slot, 2 * (1 - slot)
        own_max, own_total = stats_ref[own : own + 1], stats_ref[own + 1 : own + 2]
        other_max, other_total = others[other : other + 1], others[other + 1 : other + 2]
        key_max = jnp.maximum(own_max, other_max)
        own_factor, other_factor = jnp.exp(own_max - key_max), jnp.exp(other_max - key_max)
        inverse_total = 1.0 / (own_total * own_factor + other_total * other_factor)
        scales.append((own_factor * inverse_total, other_factor * inverse_total))
    landmark_values = keep_ref[0:HD] * scales[0][0] + swap_lanes(got[0:HD]) * scales[0][1]
    mixing_grad = keep_ref[HD : 2 * HD] + swap_lanes(got[HD : 2 * HD])
    inverse = (inverse_ref[0], inverse_ref[1])
    mixing_low = split_dot_nt(halves(landmark_values), inverse).astype(jnp.bfloat16)
    values_low = split_dot(halves(mixing_grad), inverse).astype(jnp.bfloat16)
    row_total = jnp.sum(values_low.astype(jnp.float32) * landmark_values, axis=0, keepdims=True)
    share_ref[0:HD] = mixing_low
    share_ref[HD : 2 * HD] = values_low
    share_ref[2 * HD :] = jnp.concatenate(
        [thirds(row_total), jnp.zeros((13, M), jnp.float32)], axis=0
    ).astype(jnp.bfloat16)
    mix_ref[0:HD] = mixing_low.astype(jnp.float32)
    mix_ref[HD : 2 * HD] = values_low.astype(jnp.float32)
    mix_ref[2 * HD : 2 * HD + 8] = jnp.concatenate(
        [row_total, scales[0][0], scales[1][0], jnp.zeros((5, M), jnp.float32)], axis=0
    )
    mix_ref[2 * HD + 8 : 3 * HD + 8] = mixing_grad
    mix_ref[3 * HD + 8 :] = landmark_values


def joined_sums(*operands):
    held = pl.BlockSpec(memory_space=pltpu.VMEM)
    return pl.pallas_call(
        mixing_kernel,
        out_shape=(low(2 * HD + 16, M), wide(4 * HD + 8, M)),
        in_specs=[held] * len(operands),
        out_specs=(held, held),
        compiler_params=pltpu.CompilerParams(vmem_limit_bytes=SMALL_LIMIT),
        cost_estimate=pl.CostEstimate(flops=2 * 10**8, bytes_accessed=2**20, transcendentals=0),
    )(*operands)


def several(*units):
    for unit in units:
        unit()


def out_units(ins, slot, out_ref, lead, share):
    mixing_low, values_low, _ = share
    scale = ins.mix[2 * HD + 1 + slot : 2 * HD + 2 + slot]

    def token_side(index):
        place = slice(index * CHUNK, (index + 1) * CHUNK)
        attended = wide_dot_nt(ins.token_low[place], mixing_low)
        store_chunk(out_ref, (0, *lead), index, attended.astype(jnp.bfloat16))

    def key_side(index):
        place = slice(index * CHUNK, (index + 1) * CHUNK)
        key_plow = (ins.key_exp[place] * scale).astype(jnp.bfloat16)
        value_gradient = wide_dot_nt(key_plow, values_low)
        store_chunk(out_ref, (1, *lead), index, value_gradient.astype(jnp.bfloat16))

    chunks = ins.token_low.shape[0] // CHUNK
    return [
        functools.partial(unit, index) for unit in (token_side, key_side) for index in range(chunks)
    ]


def gradient_units(ins, slot, direct_ref, share):
    score_scale = HD ** (-0.5)
    mixing_low, values_low, row_total = share
    query_sums, key_sums = [], []
    scale = ins.mix[2 * HD + 1 + slot : 2 * HD + 2 + slot]

    def token_side(index):
        place = slice(index * CHUNK, (index + 1) * CHUNK)
        prob = ins.token_prob[slot, place]
        token_grad = wide_dot(chunk_of(ins.vg, 1, slot, index), mixing_low)
        token_sgrad = (
            prob * (token_grad - jnp.sum(token_grad * prob, axis=1, keepdims=True))
        ).astype(jnp.bfloat16)
        direct_ref[slot, 0, place] = wide_dot(token_sgrad, ins.marks[slot, 1]) * score_scale
        key_sums.append(wide_dot(ins.turned[slot, 0, :, place], token_sgrad))

    def key_side(index):
        place = slice(index * CHUNK, (index + 1) * CHUNK)
        key_prob = ins.key_exp[slot, place] * scale
        key_dgrad = wide_dot(chunk_of(ins.vg, 0, slot, index), values_low)
        key_sgrad = (key_prob * (key_dgrad - row_total)).astype(jnp.bfloat16)
        direct_ref[slot, 1, place] = wide_dot(key_sgrad, ins.marks[slot, 0]) * score_scale
        query_sums.append(wide_dot(ins.turned[slot, 1, :, place], key_sgrad))

    chunks = tokens_of(ins.vg) // CHUNK
    units = [
        [functools.partial(unit, index) for index in range(chunks)] for unit in (key_side, token_side)
    ]
    return units, query_sums, key_sums


def own_parts(ref):
    return (
        ref[0:HD].astype(jnp.bfloat16),
        ref[HD : 2 * HD].astype(jnp.bfloat16),
        ref[2 * HD : 2 * HD + 1],
    )


def other_parts(ref):
    parts = (ref[0:HD], ref[HD : 2 * HD], joined_thirds(ref[2 * HD :].astype(jnp.float32)[0:3]))
    return [swap_lanes(part) for part in parts]


def gradient_sweep(state, saved, place, beside, last):
    power, growth = state
    pair_ref, weight_ref, growth_ref = saved
    pair = (pair_ref[place, 0], pair_ref[place, 1])
    first = split_dot(pair, halves(power))
    beside()
    square = first[:M] + first[:M].T
    second = split_dot(tuple(x[:M] for x in pair) if last else pair, halves(square))
    beside()
    cube = first[M:].T + second[:M]
    weight = halves(0.25 * (7.0 * square - 15.0 * power - cube))
    if not last:
        fourth = second[M:] + second[M:].T
        power = 0.25 * (13.0 * power - 15.0 * square + 7.0 * cube - fourth)
    left = [growth_ref[place, 0], growth_ref[place, 0], growth_ref[place, 1]]
    right = [weight[0], weight[1], weight[0]]
    if growth is not None:
        grown = halves(growth)
        left += [grown[0], grown[0], grown[1]]
        right += [weight_ref[place, 0], weight_ref[place, 1], weight_ref[place, 0]]
    growth = wide_dot(jnp.concatenate(left, axis=1), jnp.concatenate(right, axis=0))
    return power, growth


def own_gradient_compute(ins, outs, need, put):
    for ref in (ins.mark_prob, ins.factor, ins.mix):
        need(ref)
    inverse_grad = split_dot(
        halves(ins.mix[2 * HD + 8 : 3 * HD + 8].T), halves(ins.mix[3 * HD + 8 :])
    )
    inverse_grad_halves = halves(inverse_grad)
    outs.inverse_grad[0], outs.inverse_grad[1] = inverse_grad_halves
    toward = split_dot(halves(ins.mark_prob[...]), inverse_grad_halves) * ins.factor[0:1, 0:1]
    state = (0.5 * (toward + toward.T), None)
    units = out_units(ins, 0, outs.out, (), own_parts(ins.mix))
    work = iter([units[index : index + 2] for index in range(0, len(units), 2)])
    saved = (ins.pair, ins.weight, ins.growth)

    def beside():
        several(*next(work, ()))

    for sweep in range(EARLY_SWEEPS):
        if sweep == 0:
            need(ins.token_low)
        if sweep == 1:
            need(ins.key_exp)
        for ref in saved:
            need(ref, sweep)
        state = gradient_sweep(state, saved, sweep, beside, False)
    outs.state[0], outs.state[1] = state


def other_out_compute(ins, outs, need, put):
    for ref in (ins.got_share, ins.mix, ins.token_low):
        need(ref)
    units = out_units(ins, 1, outs.out, (1,), other_parts(ins.got_share))
    chunks = len(units) // 2
    several(*units[:chunks])
    need()
    group = CHUNK // outs.out.shape[3]
    for index, unit in enumerate(units[chunks:]):
        unit()
        place = slice(index * group, (index + 1) * group)
        outs.out[place, :, 0] = ins.own_out[place]
        put(outs.out, index * group)


def gradient_compute(ins, outs, need, put):
    for ref in (ins.state, ins.mix, ins.got_share, ins.marks):
        need(ref)
    sides = []
    for slot in range(2):
        share = other_parts(ins.got_share) if slot else own_parts(ins.mix)
        sides.append(gradient_units(ins, slot, outs.direct, share))
    units = [
        (slot, kind, unit)
        for slot in range(2)
        for kind, side in enumerate(sides[slot][0])
        for unit in side
    ]
    sweeps = PINV_ITERS - EARLY_SWEEPS
    span = -(-len(units) // (2 * sweeps - 1))
    work = iter([()] + [units[index : index + span] for index in range(0, len(units), span)])
    saved = (ins.pair, ins.weight, ins.growth)
    state = (ins.state[0], ins.state[1])

    def beside():
        for slot, kind, unit in next(work, ()):
            need(ins.vg)
            need(ins.turned, slot)
            need(ins.token_prob if kind else ins.key_exp, slot)
            unit()

    for sweep in range(sweeps):
        for ref in saved:
            need(ref, sweep)
        if sweep == sweeps - 1:
            need(ins.last_growth)
            need(ins.inverse_grad)
            need(ins.mark_prob)
            direct_part = split_dot_nt(
                (ins.last_growth[0], ins.last_growth[1]),
                (ins.inverse_grad[0], ins.inverse_grad[1]),
            )
            mark_prob = ins.mark_prob[...]
            mark_halves = halves(mark_prob)
        state = gradient_sweep(state, saved, sweep, beside, sweep == sweeps - 1)
    put(outs.direct)
    need()
    growth = state[1]
    mark_grad = ins.factor[0:1, 0:1] * (
        direct_part + split_dot(halves(growth + growth.T), mark_halves)
    )
    mark_sgrad = mark_prob * (mark_grad - jnp.sum(mark_grad * mark_prob, axis=1, keepdims=True))

    def marks_dot(left, right):
        left_high, left_low = halves(left)
        return wide_dot(
            jnp.concatenate([left_high, left_low], axis=1), jnp.concatenate([right, right], axis=0)
        )

    own_marks = (
        marks_dot(mark_sgrad, ins.marks[0, 1]),
        marks_dot(mark_sgrad.T, ins.marks[0, 0]),
    )
    marks_scale = HD ** (-0.5) / (tokens_of(ins.vg) // HALF)
    for slot, (_, query_sums, key_sums) in enumerate(sides):
        for kind, sums in enumerate((query_sums, key_sums)):
            total = sum(sums[1:], sums[0]).T
            if slot == 0:
                total = total + own_marks[kind]
            total = total * marks_scale
            outs.far[kind, slot] = total[HALF:].astype(jnp.bfloat16)
            outs.near[kind, slot] = total[:HALF]
    put(outs.far)


def finish_compute(ins, outs, need, put):
    need(ins.near)
    need(ins.got_far)
    out_ref = outs.out
    group = CHUNK // out_ref.shape[3]
    segment_len = tokens_of(out_ref) // HALF
    per = CHUNK // segment_len
    for index in range(tokens_of(out_ref) // CHUNK):
        place, start = slice(index * per, (index + 1) * per), index * CHUNK
        for slot in range(2):
            for kind in range(2):
                if index % 2 == 0:
                    need(ins.direct, slot, kind, start)
                marks = ins.near[kind, slot, place] + ins.got_far[
                    kind, 1 - slot, place
                ].astype(jnp.float32)
                spread = jnp.broadcast_to(marks[:, None], (per, segment_len, HD))
                total = ins.direct[slot, kind, start : start + CHUNK] + spread.reshape(CHUNK, HD)
                store_chunk(out_ref, (kind, slot), index, total.astype(jnp.bfloat16))
        put(out_ref, index * group)


def exchange(packed):
    return lax.all_to_all(packed, "cube", split_axis=0, concat_axis=0, tiled=True)


def partner(array):
    return lax.ppermute(array, "half", SWAP)


def body(queries, keys, values, out_grad):
    half = lax.axis_index("half").reshape(1)
    qk, vg_packed = lax.optimization_barrier(
        (exchange(pack(half, queries, keys)), pack(half, values, out_grad))
    )
    tokens = qk.shape[0] * qk.shape[3]
    mine = landmarks_of(qk)
    theirs = partner(mine)
    vg_packed, mine = lax.optimization_barrier((vg_packed, mine))
    vg = exchange(vg_packed)
    kept = staged_call(
        probability_compute,
        dict(qk=qk, mine=mine, theirs=theirs),
        dict(
            marks=low(2, 2, M, HD),
            token_prob=wide(2, tokens, M),
            token_low=low(2, tokens, M),
            key_exp=wide(2, tokens, M),
            key_low=low(2, tokens, M),
            turned=low(2, 2, HD, tokens),
            stats=wide(8, M),
            mark_prob=wide(M, M),
            factor=wide(8, HD),
            pair_a=(low(EARLY_SWEEPS, 2, 2 * M, M), LEAD),
            weight_a=(low(EARLY_SWEEPS, 2, M, M), LEAD),
            growth_a=(low(EARLY_SWEEPS, 2, M, M), LEAD),
            pair_b=(low(PINV_ITERS - EARLY_SWEEPS, 2, 2 * M, M), LEAD),
            weight_b=(low(PINV_ITERS - EARLY_SWEEPS, 2, M, M), LEAD),
            growth_b=(low(PINV_ITERS - EARLY_SWEEPS, 2, M, M), LEAD),
            inverse=low(2, M, M),
            last_growth=low(2, M, M),
        ),
        LONG,
        extra=(pltpu.VMEM((M, M), jnp.float32), pltpu.VMEM((2 * M, M), jnp.float32)),
    )
    sums = staged_call(
        partial_compute,
        dict(
            vg=vg,
            stats=kept.stats,
            key_low=(kept.key_low, LEAD),
            token_low=(kept.token_low, LEAD),
        ),
        dict(send=low(2 * HD + 16, M), keep=wide(2 * HD, M)),
        2,
    )
    share, mix = joined_sums(partner(sums.send), sums.keep, kept.stats, kept.inverse)
    got_share = partner(share)
    own = staged_call(
        own_gradient_compute,
        dict(
            mark_prob=kept.mark_prob,
            factor=kept.factor,
            mix=mix,
            token_low=(kept.token_low, SLOTS[0]),
            pair=(kept.pair_a, LEAD),
            weight=(kept.weight_a, LEAD),
            growth=(kept.growth_a, LEAD),
            key_exp=(kept.key_exp, SLOTS[0]),
        ),
        dict(
            out=low(qk.shape[0], 2, *qk.shape[3:]),
            state=wide(2, M, M),
            inverse_grad=low(2, M, M),
        ),
        8,
    )
    first_results = staged_call(
        other_out_compute,
        dict(
            got_share=got_share,
            mix=(mix, TOP),
            token_low=(kept.token_low, SLOTS[1]),
            key_exp=(kept.key_exp, SLOTS[1]),
            own_out=own.out,
        ),
        dict(out=(low(*qk.shape), GROUPS)),
        1,
    ).out
    attended, value_gradient_array = unpack(half, exchange(first_results))
    grads = staged_call(
        gradient_compute,
        dict(
            state=own.state,
            got_share=got_share,
            mix=(mix, TOP),
            marks=kept.marks,
            pair=(kept.pair_b, LEAD),
            weight=(kept.weight_b, LEAD),
            growth=(kept.growth_b, LEAD),
            vg=(vg, LATE),
            key_exp=(kept.key_exp, LEAD),
            turned=(kept.turned, LEAD),
            token_prob=(kept.token_prob, LEAD),
            inverse_grad=(own.inverse_grad, LAST),
            last_growth=(kept.last_growth, LAST),
            mark_prob=(kept.mark_prob, LAST),
            factor=(kept.factor, LAST),
        ),
        dict(
            far=low(2, 2, HALF, HD),
            near=wide(2, 2, HALF, HD),
            direct=(wide(2, 2, tokens, HD), LEAD),
        ),
        LONG,
        after=(first_results,),
    )
    results = staged_call(
        finish_compute,
        dict(got_far=partner(grads.far), near=grads.near, direct=(grads.direct, BLOCKS)),
        dict(out=(low(*qk.shape), GROUPS)),
        0.1,
    ).out
    query_grad, key_grad = unpack(half, exchange(results))
    return attended, query_grad, key_grad, value_gradient_array


def solution(mesh):
    whole_placement = P(("seq", "head"), None)
    halves_placement = P(("half", "cube"), None)

    def layer(queries, keys, values, out_grad):
        tokens, width = queries.shape
        own_head_each = width // HD == mesh.size and tokens == 8 * CHUNK
        if own_head_each:
            split = jax.sharding.Mesh(
                mesh.devices.reshape(2, mesh.size // 2), ("half", "cube")
            )
        return jax.shard_map(
            body if own_head_each else shared_body,
            mesh=split if own_head_each else mesh,
            in_specs=(halves_placement if own_head_each else whole_placement,) * 4,
            out_specs=(halves_placement if own_head_each else whole_placement,) * 4,
            check_vma=False,
        )(queries, keys, values, out_grad)

    return layer
```

```python
import functools
from types import SimpleNamespace

import jax
import jax.numpy as jnp
from jax import lax
from jax.experimental import pallas as pl
from jax.experimental.pallas import tpu as pltpu
from jax.sharding import PartitionSpec as P

HD = 128
M = 256
PINV_ITERS = 6
CHUNK = 256
PACK_GROUPS = 4
HALF = M // 2
SWAP = ((0, 1), (1, 0))
VMEM_LIMIT = 60 * 2**20
SMALL_LIMIT = 16 * 2**20
WHOLE, LEAD, GROUPS, BLOCKS, LATE, LAST = range(6)
SLOTS = (10, 11)
TOP = 12
SIDES = (20, 21)
LONG = 200
EARLY_SWEEPS = PINV_ITERS // 2


precise_setting = lax.Precision.HIGHEST


def newton_inverse(matrix):
    identity = jnp.eye(matrix.shape[0], dtype=matrix.dtype)
    factor = lax.stop_gradient(1.0 / jnp.max(jnp.sum(matrix, axis=0)))
    iterate = matrix.T * factor
    for sweep_index in range(PINV_ITERS):
        product = jnp.matmul(matrix, iterate, precision=precise_setting)
        inner_term = jnp.matmul(product, 7.0 * identity - product, precision=precise_setting)
        inner_term = jnp.matmul(product, 15.0 * identity - inner_term, precision=precise_setting)
        iterate = 0.25 * jnp.matmul(
            iterate, 13.0 * identity - inner_term, precision=precise_setting
        )
    return iterate


def share_heads(own_matrix, head_count):
    seq_index = lax.axis_index("seq")
    slot_mask = (jnp.arange(head_count, dtype=jnp.int32) == seq_index).astype(jnp.float32)
    return lax.psum(slot_mask[:, None, None] * own_matrix[None], "seq")


def shared_body(queries, keys, values, out_grad):
    query_rows, key_rows, value_rows, grad_rows = (
        lax.all_to_all(queries, "head", split_axis=1, concat_axis=0, tiled=True),
        lax.all_to_all(keys, "head", split_axis=1, concat_axis=0, tiled=True),
        lax.all_to_all(values, "head", split_axis=1, concat_axis=0, tiled=True),
        lax.all_to_all(out_grad, "head", split_axis=1, concat_axis=0, tiled=True),
    )
    tok_rows = query_rows.shape[0]
    head_count = query_rows.shape[1] // HD
    local_marks = M // lax.axis_size("seq")
    segment_len = tok_rows // local_marks
    score_scale = HD ** (-0.5)
    seq_index = lax.axis_index("seq")

    def landmark(matrix):
        summed = jnp.sum(
            matrix.reshape(local_marks, segment_len, matrix.shape[1]), axis=1, dtype=jnp.float32
        )
        return (summed / segment_len).astype(jnp.bfloat16)

    mark_queries, mark_keys = (
        lax.all_gather(landmark(query_rows), "seq", axis=0, tiled=True),
        lax.all_gather(landmark(key_rows), "seq", axis=0, tiled=True),
    )
    query_per_head = query_rows.reshape(tok_rows, head_count, HD)
    key_per_head = key_rows.reshape(tok_rows, head_count, HD)
    value_per_head = value_rows.reshape(tok_rows, head_count, HD)
    gradient_per_head = grad_rows.reshape(tok_rows, head_count, HD)
    landmark_query_heads = mark_queries.reshape(M, head_count, HD)
    landmark_key_heads = mark_keys.reshape(M, head_count, HD)
    key_score = (
        jnp.einsum(
            "pcv,gcv->cpg", landmark_query_heads, key_per_head, preferred_element_type=jnp.float32
        )
        * score_scale
    )
    key_max = lax.pmax(jnp.max(key_score, axis=-1), "seq")
    key_exp = jnp.exp(key_score - key_max[..., None])
    partial_num = jnp.einsum(
        "akq,qay->aky",
        key_exp.astype(jnp.bfloat16),
        value_per_head,
        preferred_element_type=jnp.float32,
    )
    key_total, numerator = lax.psum((jnp.sum(key_exp, axis=-1), partial_num), "seq")
    landmark_value_rows = numerator / key_total[..., None]
    token_prob = jax.nn.softmax(
        jnp.einsum(
            "jti,cti->tjc", query_per_head, landmark_key_heads, preferred_element_type=jnp.float32
        )
        * score_scale,
        axis=-1,
    )
    token_probability_lowered = token_prob.astype(jnp.bfloat16)
    mark_prob = jax.nn.softmax(
        jnp.einsum(
            "jou,iou->oji",
            landmark_query_heads,
            landmark_key_heads,
            preferred_element_type=jnp.float32,
        )
        * score_scale,
        axis=-1,
    )
    own_head = seq_index % head_count
    own_mark = lax.dynamic_index_in_dim(mark_prob, own_head, 0, keepdims=False)
    own_inverse, pull_back = jax.vjp(newton_inverse, own_mark)
    pseudo_inverse_matrix = share_heads(own_inverse, head_count)
    mixing_matrix = jnp.einsum(
        "jvy,jys->jvs", pseudo_inverse_matrix, landmark_value_rows, precision=precise_setting
    )
    mixing_matrix_lowered = mixing_matrix.astype(jnp.bfloat16)
    attended = jnp.einsum(
        "yvo,yor->vyr",
        token_probability_lowered,
        mixing_matrix_lowered,
        preferred_element_type=jnp.float32,
    ).astype(jnp.bfloat16)
    token_grad = jnp.einsum(
        "fag,aog->afo", gradient_per_head, mixing_matrix_lowered, preferred_element_type=jnp.float32
    )
    partial_mix = jnp.einsum(
        "klz,lkr->kzr",
        token_probability_lowered,
        gradient_per_head,
        preferred_element_type=jnp.float32,
    )
    mixing_matrix_gradient = lax.psum(partial_mix, "seq")
    token_score_gradient = (
        token_prob * (token_grad - jnp.sum(token_grad * token_prob, axis=-1, keepdims=True))
    ).astype(jnp.bfloat16)
    direct_qgrad = (
        jnp.einsum(
            "ufg,guc->fuc",
            token_score_gradient,
            landmark_key_heads,
            preferred_element_type=jnp.float32,
        )
        * score_scale
    )
    mark_kgrad_f = (
        jnp.einsum(
            "xgi,gxy->ixy", token_score_gradient, query_per_head, preferred_element_type=jnp.float32
        )
        * score_scale
    )
    pseudo_inverse_gradient = jnp.einsum(
        "ktu,kyu->kty", mixing_matrix_gradient, landmark_value_rows, precision=precise_setting
    )
    landmark_value_gradient = jnp.einsum(
        "lrb,lrz->lbz", pseudo_inverse_matrix, mixing_matrix_gradient, precision=precise_setting
    )
    own_igrad = lax.dynamic_index_in_dim(pseudo_inverse_gradient, own_head, 0, keepdims=False)
    (own_mgrad,) = pull_back(own_igrad)
    mark_grad = share_heads(own_mgrad, head_count)
    mark_sgrad = mark_prob * (mark_grad - jnp.sum(mark_grad * mark_prob, axis=-1, keepdims=True))
    first_mark = seq_index * local_marks
    score_gradient_rows = lax.dynamic_slice_in_dim(mark_sgrad, first_mark, local_marks, 1)
    score_gradient_columns = lax.dynamic_slice_in_dim(mark_sgrad, first_mark, local_marks, 2)
    own_qgrad_a = (
        jnp.einsum(
            "txs,ste->xte",
            score_gradient_rows,
            landmark_key_heads.astype(jnp.float32),
            precision=precise_setting,
        )
        * score_scale
    )
    own_kgrad_a = (
        jnp.einsum(
            "eaj,aev->jev",
            score_gradient_columns,
            landmark_query_heads.astype(jnp.float32),
            precision=precise_setting,
        )
        * score_scale
    )
    landmark_value_lowered = landmark_value_gradient.astype(jnp.bfloat16)
    key_prob = key_exp / key_total[..., None]
    key_probability_lowered = key_prob.astype(jnp.bfloat16)
    value_gradient_array = jnp.einsum(
        "zct,zcj->tzj",
        key_probability_lowered,
        landmark_value_lowered,
        preferred_element_type=jnp.float32,
    )
    key_direct_gradient = jnp.einsum(
        "exb,geb->exg", landmark_value_lowered, value_per_head, preferred_element_type=jnp.float32
    )
    row_total = lax.psum(jnp.sum(key_prob * key_direct_gradient, axis=-1), "seq")
    key_score_gradient = (key_prob * (key_direct_gradient - row_total[..., None])).astype(
        jnp.bfloat16
    )
    direct_kgrad = (
        jnp.einsum(
            "pbo,bpx->opx",
            key_score_gradient,
            landmark_query_heads,
            preferred_element_type=jnp.float32,
        )
        * score_scale
    )
    mark_qgrad_b = (
        jnp.einsum(
            "cbj,jcp->bcp", key_score_gradient, key_per_head, preferred_element_type=jnp.float32
        )
        * score_scale
    )
    own_kgrad_f, own_qgrad_b = (
        lax.psum_scatter(mark_kgrad_f, "seq", scatter_dimension=0, tiled=True),
        lax.psum_scatter(mark_qgrad_b, "seq", scatter_dimension=0, tiled=True),
    )
    mark_qtotal = (own_qgrad_a + own_qgrad_b) / segment_len
    mark_ktotal = (own_kgrad_a + own_kgrad_f) / segment_len
    query_grad = (
        direct_qgrad.reshape(local_marks, segment_len, head_count, HD) + mark_qtotal[:, None]
    )
    key_grad = direct_kgrad.reshape(local_marks, segment_len, head_count, HD) + mark_ktotal[:, None]
    width = head_count * HD
    results = (
        attended.reshape(tok_rows, width),
        query_grad.astype(jnp.bfloat16).reshape(tok_rows, width),
        key_grad.astype(jnp.bfloat16).reshape(tok_rows, width),
        value_gradient_array.astype(jnp.bfloat16).reshape(tok_rows, width),
    )
    attended_out, query_out, key_out, value_out = (
        lax.all_to_all(results[0], "head", split_axis=0, concat_axis=1, tiled=True),
        lax.all_to_all(results[1], "head", split_axis=0, concat_axis=1, tiled=True),
        lax.all_to_all(results[2], "head", split_axis=0, concat_axis=1, tiled=True),
        lax.all_to_all(results[3], "head", split_axis=0, concat_axis=1, tiled=True),
    )
    return (attended_out, query_out, key_out, value_out)


def halves(matrix):
    high = matrix.astype(jnp.bfloat16)
    return high, (matrix - high.astype(jnp.float32)).astype(jnp.bfloat16)


def wide_dot(left, right):
    return jnp.dot(left, right, preferred_element_type=jnp.float32)


def wide_dot_nt(left, right):
    return lax.dot_general(
        left, right, (((1,), (1,)), ((), ())), preferred_element_type=jnp.float32
    )


def split_dot(left, right):
    left_high, left_low = left
    right_high, right_low = right
    return wide_dot(
        jnp.concatenate([left_high, left_high, left_low], axis=1),
        jnp.concatenate([right_high, right_low, right_high], axis=0),
    )


def split_dot_nt(left, right):
    left_high, left_low = left
    right_high, right_low = right
    return wide_dot_nt(
        jnp.concatenate([left_high, left_high, left_low], axis=1),
        jnp.concatenate([right_high, right_low, right_high], axis=1),
    )


def identity_matrix():
    return (
        lax.broadcasted_iota(jnp.int32, (M, M), 0) == lax.broadcasted_iota(jnp.int32, (M, M), 1)
    ).astype(jnp.float32)


def chunk_of(ref, array, slot, index):
    per = CHUNK // ref.shape[3]
    return ref[index * per : (index + 1) * per, array, slot].reshape(CHUNK, HD)


def store_chunk(ref, lead, index, value):
    rows = ref.shape[-2]
    per = CHUNK // rows
    ref[(slice(index * per, (index + 1) * per), *lead)] = value.reshape(per, rows, HD)


def all_tokens(ref, array, slot):
    return ref[:, array, slot].reshape(ref.shape[0] * ref.shape[3], HD)


def tokens_of(ref):
    return ref.shape[0] * ref.shape[3]


def columns(index):
    return pl.ds(pl.multiple_of(index * CHUNK, CHUNK), CHUNK)


def swap_lanes(matrix):
    return jnp.concatenate([matrix[:, HALF:], matrix[:, :HALF]], axis=1)


def thirds(rows):
    first = rows.astype(jnp.bfloat16).astype(jnp.float32)
    second = (rows - first).astype(jnp.bfloat16).astype(jnp.float32)
    return jnp.concatenate([first, second, rows - first - second], axis=0)


def joined_thirds(rows):
    count = rows.shape[0] // 3
    return rows[:count] + (rows[count : 2 * count] + rows[2 * count :])


def held_shape(kind, shape):
    if kind == TOP:
        return (2 * HD + 8, *shape[1:])
    if kind in SIDES:
        return (shape[0], *shape[2:])
    return shape[1:] if kind in SLOTS else shape


def pieces_of(kind, shape):
    if kind == LEAD:
        return [(index,) for index in range(shape[0])]
    if kind == BLOCKS:
        return [
            (first, second, slice(place, place + 2 * CHUNK))
            for place in range(0, shape[2], 2 * CHUNK)
            for first in range(shape[0])
            for second in range(shape[1])
        ]
    if kind == GROUPS:
        per = CHUNK // shape[-2]
        return [(slice(place, place + per),) for place in range(0, shape[0], per)]
    return [()]


def window(ref, piece):
    place = tuple(
        pl.ds(part.start, part.stop - part.start) if isinstance(part, slice) else part
        for part in piece
    )
    return ref.at[place] if place else ref


class Staged:
    def __init__(self, names, kinds, outer, inner, done, outward):
        self.refs = SimpleNamespace(**dict(zip(names, inner)))
        self.copies, self.order = [], []
        count = 0
        steps = []
        for place, (kind, home, held) in enumerate(zip(kinds, outer, inner)):
            home = home.at[kind - SLOTS[0]] if kind in SLOTS else home
            home = home.at[pl.ds(0, 2 * HD + 8)] if kind == TOP else home
            home = home.at[:, kind - SIDES[0]] if kind in SIDES else home
            copies = {}
            for step, piece in enumerate(pieces_of(kind, held.shape)):
                ends = (window(held, piece), window(home, piece))
                source, target = ends if outward else ends[::-1]
                key = tuple(
                    part.start if isinstance(part, slice) else part for part in piece
                )
                copies[key] = pltpu.make_async_copy(source, target, done.at[count])
                steps.append(({WHOLE: -1, TOP: -1, LAST: 9}.get(kind, step), place, key))
                count += 1
            self.copies.append(copies)
        self.inner = inner
        self.order = sorted(steps, key=lambda item: item[:2])
        self.started, self.waited = set(), set()

    def place_of(self, ref):
        return next(index for index, held in enumerate(self.inner) if held is ref)

    def start(self, ref=None, *key):
        chosen = [
            (place, name)
            for _, place, name in self.order
            if (ref is None or place == self.place_of(ref)) and (not key or name == key)
        ]
        for item in chosen:
            if item not in self.started:
                self.started.add(item)
                self.copies[item[0]][item[1]].start()

    def wait(self, ref=None, *key):
        chosen = [
            (place, name)
            for _, place, name in self.order
            if (ref is None or place == self.place_of(ref)) and (not key or name == key)
        ]
        for item in chosen:
            if item not in self.waited:
                self.waited.add(item)
                self.copies[item[0]][item[1]].wait()


def staged_call(compute, inputs, outputs, flops, extra=(), after=(), in_place=False):
    names_in, names_out = tuple(inputs), tuple(outputs)
    kinds_in = [x[1] if isinstance(x, tuple) else WHOLE for x in inputs.values()]
    kinds_out = [x[1] if isinstance(x, tuple) else WHOLE for x in outputs.values()]
    operands = tuple(x[0] if isinstance(x, tuple) else x for x in inputs.values())
    shapes = tuple(x[0] if isinstance(x, tuple) else x for x in outputs.values())
    n_in, n_out, n_after = len(operands), len(shapes), len(after)
    moved = sum(x.size * x.dtype.itemsize for x in (*operands, *shapes))
    anywhere = pl.BlockSpec(memory_space=pl.ANY)

    def count(kinds, arrays):
        return sum(len(pieces_of(kind, x.shape)) for kind, x in zip(kinds, arrays))

    def kernel(*refs):
        sources, refs = refs[:n_in], refs[n_in + n_after :]
        homes, refs = refs[:n_out], refs[n_out:]
        held_in, held_out = refs[:n_in], refs[n_in : n_in + n_out]
        *scratch, in_done, out_done = refs[n_in + n_out :]
        reads = Staged(names_in, kinds_in, sources, held_in, in_done, False)
        writes = Staged(names_out, kinds_out, homes, held_out, out_done, True)
        reads.start()
        compute(reads.refs, writes.refs, reads.wait, writes.start, *scratch)
        reads.wait()
        writes.start()
        writes.wait()

    results = pl.pallas_call(
        kernel,
        out_shape=shapes,
        in_specs=[anywhere] * (n_in + n_after),
        out_specs=(anywhere,) * n_out,
        scratch_shapes=[
            *(
                pltpu.VMEM(held_shape(kind, x.shape), x.dtype)
                for kind, x in zip((*kinds_in, *kinds_out), (*operands, *shapes))
            ),
            *extra,
            pltpu.SemaphoreType.DMA((count(kinds_in, operands),)),
            pltpu.SemaphoreType.DMA((count(kinds_out, shapes),)),
        ],
        compiler_params=pltpu.CompilerParams(vmem_limit_bytes=VMEM_LIMIT),
        cost_estimate=pl.CostEstimate(
            flops=int(flops * 10**9), bytes_accessed=moved, transcendentals=0
        ),
    )(*operands, *after)
    return SimpleNamespace(**dict(zip(outputs, results)))


def low(*shape):
    return jax.ShapeDtypeStruct(shape, jnp.bfloat16)


def wide(*shape):
    return jax.ShapeDtypeStruct(shape, jnp.float32)


def pack_kernel(half_ref, first_ref, second_ref, out_ref, rows_s, packed_s, in_done, out_done):
    half = half_ref[0]
    pairs = out_ref.shape[0]
    group = pairs // PACK_GROUPS
    span = 2 * HD
    reads, writes = [], []
    for index in range(PACK_GROUPS):
        for array, ref in enumerate((first_ref, second_ref)):
            place = pl.ds(index * group * span, group * span)
            reads.append(
                pltpu.make_async_copy(
                    ref.at[:, place], rows_s.at[array, :, place], in_done.at[array, index]
                )
            )
        place = pl.ds(index * group, group)
        writes.append(
            pltpu.make_async_copy(packed_s.at[place], out_ref.at[place], out_done.at[index])
        )
    for copy in reads:
        copy.start()
    for index in range(PACK_GROUPS):
        for array in range(2):
            reads[2 * index + array].wait()
            for pair in range(index * group, (index + 1) * group):
                start = pair * span
                packed_s[pair, array, half] = rows_s[array, :, start : start + HD]
                packed_s[pair, array, 1 - half] = rows_s[array, :, start + HD : start + span]
        writes[index].start()
    for copy in writes:
        copy.wait()


def unpack_kernel(half_ref, packed_ref, first_ref, second_ref, rows_s, out_done):
    half = half_ref[0]
    pairs = packed_ref.shape[0]
    group = pairs // PACK_GROUPS
    span = 2 * HD
    writes = []
    for index in range(PACK_GROUPS):
        for array, ref in enumerate((first_ref, second_ref)):
            for pair in range(index * group, (index + 1) * group):
                start = pair * span
                rows_s[array, :, start : start + HD] = packed_ref[pair, array, half]
                rows_s[array, :, start + HD : start + span] = packed_ref[pair, array, 1 - half]
            place = pl.ds(index * group * span, group * span)
            write = pltpu.make_async_copy(
                rows_s.at[array, :, place], ref.at[:, place], out_done.at[array, index]
            )
            write.start()
            writes.append(write)
    for copy in writes:
        copy.wait()


def layout_call(kernel, half, operands, out_shape, scratch, in_space, limit):
    anywhere = pl.BlockSpec(memory_space=pl.ANY)
    moved = 2 * sum(x.size * x.dtype.itemsize for x in operands)
    return pl.pallas_call(
        kernel,
        out_shape=out_shape,
        in_specs=[pl.BlockSpec(memory_space=pltpu.SMEM)]
        + [pl.BlockSpec(memory_space=in_space)] * len(operands),
        out_specs=jax.tree.map(lambda _: anywhere, out_shape),
        scratch_shapes=scratch,
        compiler_params=pltpu.CompilerParams(vmem_limit_bytes=limit),
        cost_estimate=pl.CostEstimate(flops=0, bytes_accessed=moved, transcendentals=0),
    )(half, *operands)


def pack(half, first, second):
    rows, width = first.shape
    shape = low(width // (2 * HD), 2, 2, rows, HD)
    scratch = [
        pltpu.VMEM((2, rows, width), jnp.bfloat16),
        pltpu.VMEM(shape.shape, jnp.bfloat16),
        pltpu.SemaphoreType.DMA((2, PACK_GROUPS)),
        pltpu.SemaphoreType.DMA((PACK_GROUPS,)),
    ]
    return layout_call(
        pack_kernel, half, (first, second), shape, scratch, pl.ANY, VMEM_LIMIT
    )


def unpack(half, packed):
    pairs, _, _, rows, _ = packed.shape
    shape = low(rows, pairs * 2 * HD)
    scratch = [
        pltpu.VMEM((2, *shape.shape), jnp.bfloat16),
        pltpu.SemaphoreType.DMA((2, PACK_GROUPS)),
    ]
    return layout_call(
        unpack_kernel, half, (packed,), (shape, shape), scratch, pltpu.VMEM, SMALL_LIMIT
    )


def landmark_kernel(qk_ref, marks_ref):
    tokens = tokens_of(qk_ref)
    segment_len = tokens // HALF
    per = CHUNK // segment_len
    member = (
        lax.broadcasted_iota(jnp.int32, (per, CHUNK), 1) // segment_len
        == lax.broadcasted_iota(jnp.int32, (per, CHUNK), 0)
    ).astype(jnp.bfloat16)
    kinds = [(slot, array) for slot in range(2) for array in range(2)]
    for index in range(tokens // CHUNK):
        parts = [chunk_of(qk_ref, array, slot, index) for slot, array in kinds]
        summed = wide_dot(member, jnp.concatenate(parts, axis=1))
        mean = (summed / segment_len).astype(jnp.bfloat16)
        for place, (slot, array) in enumerate(kinds):
            marks_ref[slot, array, index * per : (index + 1) * per] = mean[
                :, place * HD : (place + 1) * HD
            ]


def landmarks_of(qk):
    held = pl.BlockSpec(memory_space=pltpu.VMEM)
    return pl.pallas_call(
        landmark_kernel,
        out_shape=low(2, 2, HALF, HD),
        in_specs=[held],
        out_specs=held,
        compiler_params=pltpu.CompilerParams(vmem_limit_bytes=SMALL_LIMIT),
        cost_estimate=pl.CostEstimate(
            flops=2 * 10**8, bytes_accessed=qk.size * 2, transcendentals=0
        ),
    )(qk)


def sweep_forward(power_s, iterate_s, saved, sweep, work):
    pair_ref, weight_ref, growth_ref = saved
    power = power_s[...]
    power_high, power_low = halves(power)
    square = split_dot((power_high, power_low), (power_high, power_low))
    next(work)()
    square_halves = halves(square)
    pair = (
        jnp.concatenate([power_high, square_halves[0]], axis=0),
        jnp.concatenate([power_low, square_halves[1]], axis=0),
    )
    pair_ref[sweep, 0], pair_ref[sweep, 1] = pair
    higher = split_dot(pair, square_halves)
    next(work)()
    cube, fourth = higher[:M], higher[M:]
    weight = halves(0.25 * (13.0 * identity_matrix() - 15.0 * power + 7.0 * square - cube))
    power_s[...] = 0.25 * (13.0 * power - 15.0 * square + 7.0 * cube - fourth)
    weight_ref[sweep, 0], weight_ref[sweep, 1] = weight
    iterate = halves(iterate_s[...])
    growth_ref[sweep, 0], growth_ref[sweep, 1] = iterate[0][M:], iterate[1][M:]
    iterate_s[...] = split_dot(iterate, weight)


def probability_compute(ins, outs, need, put, power_s, iterate_s):
    need()
    qk_ref = ins.qk
    chunks = tokens_of(qk_ref) // CHUNK
    score_scale = HD ** (-0.5)
    for slot in range(2):
        for array in range(2):
            outs.marks[slot, array] = jnp.concatenate(
                [ins.mine[slot, array], ins.theirs[1 - slot, array]], axis=0
            )
    put(outs.marks)
    landmark_q, landmark_k = outs.marks[0, 0], outs.marks[0, 1]
    mark_score = wide_dot_nt(landmark_q, landmark_k) * score_scale
    mark_exp = jnp.exp(mark_score - jnp.max(mark_score, axis=1, keepdims=True))
    mark_prob = mark_exp / jnp.sum(mark_exp, axis=1, keepdims=True)
    outs.mark_prob[...] = mark_prob
    factor = 1.0 / jnp.max(jnp.sum(mark_prob, axis=0, keepdims=True), axis=1, keepdims=True)
    outs.factor[...] = jnp.broadcast_to(factor, outs.factor.shape)
    mark_halves = halves(mark_prob)
    power_s[...] = split_dot_nt(mark_halves, mark_halves) * factor
    iterate_s[0:M] = mark_prob.T * factor
    iterate_s[M:] = identity_matrix()
    tops, totals = [[], []], [[], []]

    def scores(slot, index):
        query_chunk, key_chunk = (chunk_of(qk_ref, array, slot, index) for array in range(2))
        place = slice(index * CHUNK, (index + 1) * CHUNK)
        outs.turned[slot, 0, :, place] = query_chunk.T
        outs.turned[slot, 1, :, place] = key_chunk.T
        score = wide_dot_nt(query_chunk, outs.marks[slot, 1]) * score_scale
        grown = jnp.exp(score - jnp.max(score, axis=1, keepdims=True))
        prob = grown * (1.0 / jnp.sum(grown, axis=1, keepdims=True))
        outs.token_prob[slot, place] = prob
        outs.token_low[slot, place] = prob.astype(jnp.bfloat16)
        key_score = wide_dot_nt(key_chunk, outs.marks[slot, 0]) * score_scale
        outs.key_exp[slot, place] = key_score
        tops[slot].append(jnp.max(key_score, axis=0, keepdims=True))

    def grow(slot, index):
        if index == 0:
            tops[slot] = functools.reduce(jnp.maximum, tops[slot])
        place = slice(index * CHUNK, (index + 1) * CHUNK)
        grown = jnp.exp(outs.key_exp[slot, place] - tops[slot])
        outs.key_exp[slot, place] = grown
        outs.key_low[slot, place] = grown.astype(jnp.bfloat16)
        totals[slot].append(jnp.sum(grown, axis=0, keepdims=True))

    def several(unit, pairs):
        for slot, index in pairs:
            unit(slot, index)

    pairs = [(slot, index) for slot in range(2) for index in range(chunks)]
    work = iter(
        [functools.partial(several, scores, [pair]) for pair in pairs]
        + [
            functools.partial(several, grow, pairs[first : first + 2])
            for first in range(0, len(pairs), 2)
        ]
    )
    for sweep in range(PINV_ITERS):
        first = sweep < EARLY_SWEEPS
        place = sweep if first else sweep - EARLY_SWEEPS
        saved = (
            (outs.pair_a, outs.weight_a, outs.growth_a)
            if first
            else (outs.pair_b, outs.weight_b, outs.growth_b)
        )
        sweep_forward(power_s, iterate_s, saved, place, work)
        for ref in saved:
            put(ref, place)
        if sweep == 3:
            for ref in (outs.token_low, outs.token_prob, outs.turned):
                put(ref)
    put(outs.key_low)
    put(outs.key_exp)
    outs.inverse[0], outs.inverse[1] = halves(iterate_s[0:M])
    outs.last_growth[0], outs.last_growth[1] = halves(iterate_s[M:])
    stats = [x for slot in range(2) for x in (tops[slot], sum(totals[slot][1:], totals[slot][0]))]
    outs.stats[0:4] = jnp.concatenate(stats, axis=0)
    outs.stats[4:8] = jnp.zeros((4, M), jnp.float32)


def partial_compute(ins, outs, need, put):
    need(ins.rows)
    heads, _, rows, _ = ins.rows.shape
    turned = [ins.rows[:, slot].reshape(heads * rows, HD).T for slot in range(2)]
    for slot, home in enumerate((outs.keep, outs.send)):
        need(ins.lowered, slot)
        home[0:HD] = wide_dot(turned[slot], ins.lowered[slot]).astype(home.dtype)


def stats_partial_compute(ins, outs, need, put):
    partial_compute(ins, outs, need, put)
    need(ins.stats)
    rows = thirds(ins.stats[0:4])
    outs.send[HD:] = jnp.concatenate([rows, jnp.zeros((4, M), jnp.float32)], axis=0).astype(
        jnp.bfloat16
    )


def mixing_kernel(
    got_ref, got_grad_ref, keep_ref, keep_grad_ref, stats_ref, inverse_ref, share_ref, mix_ref
):
    got = got_ref[...].astype(jnp.float32)
    others = swap_lanes(joined_thirds(got[HD : HD + 12]))
    scales = []
    for slot in range(2):
        own, other = 2 * slot, 2 * (1 - slot)
        own_max, own_total = stats_ref[own : own + 1], stats_ref[own + 1 : own + 2]
        other_max, other_total = others[other : other + 1], others[other + 1 : other + 2]
        key_max = jnp.maximum(own_max, other_max)
        own_factor, other_factor = jnp.exp(own_max - key_max), jnp.exp(other_max - key_max)
        inverse_total = 1.0 / (own_total * own_factor + other_total * other_factor)
        scales.append((own_factor * inverse_total, other_factor * inverse_total))
    landmark_values = keep_ref[...] * scales[0][0] + swap_lanes(got[0:HD]) * scales[0][1]
    mixing_grad = keep_grad_ref[...] + swap_lanes(got_grad_ref[...].astype(jnp.float32))
    inverse = (inverse_ref[0], inverse_ref[1])
    mixing_low = split_dot_nt(halves(landmark_values), inverse).astype(jnp.bfloat16)
    values_low = split_dot(halves(mixing_grad), inverse).astype(jnp.bfloat16)
    row_total = jnp.sum(values_low.astype(jnp.float32) * landmark_values, axis=0, keepdims=True)
    share_ref[0:HD] = mixing_low
    share_ref[HD : 2 * HD] = values_low
    share_ref[2 * HD :] = jnp.concatenate(
        [thirds(row_total), jnp.zeros((13, M), jnp.float32)], axis=0
    ).astype(jnp.bfloat16)
    mix_ref[0:HD] = mixing_low.astype(jnp.float32)
    mix_ref[HD : 2 * HD] = values_low.astype(jnp.float32)
    mix_ref[2 * HD : 2 * HD + 8] = jnp.concatenate(
        [row_total, scales[0][0], scales[1][0], jnp.zeros((5, M), jnp.float32)], axis=0
    )
    mix_ref[2 * HD + 8 : 3 * HD + 8] = mixing_grad
    mix_ref[3 * HD + 8 :] = landmark_values


def joined_sums(*operands):
    held = pl.BlockSpec(memory_space=pltpu.VMEM)
    return pl.pallas_call(
        mixing_kernel,
        out_shape=(low(2 * HD + 16, M), wide(4 * HD + 8, M)),
        in_specs=[held] * len(operands),
        out_specs=(held, held),
        compiler_params=pltpu.CompilerParams(vmem_limit_bytes=SMALL_LIMIT),
        cost_estimate=pl.CostEstimate(flops=2 * 10**8, bytes_accessed=2**20, transcendentals=0),
    )(*operands)


def several(*units):
    for unit in units:
        unit()


def out_units(ins, slot, out_ref, lead, share):
    mixing_low, values_low, _ = share
    scale = ins.mix[2 * HD + 1 + slot : 2 * HD + 2 + slot]

    def token_side(index):
        place = slice(index * CHUNK, (index + 1) * CHUNK)
        attended = wide_dot_nt(ins.token_low[place], mixing_low)
        store_chunk(out_ref, (0, *lead), index, attended.astype(jnp.bfloat16))

    def key_side(index):
        place = slice(index * CHUNK, (index + 1) * CHUNK)
        key_plow = (ins.key_exp[place] * scale).astype(jnp.bfloat16)
        value_gradient = wide_dot_nt(key_plow, values_low)
        store_chunk(out_ref, (1, *lead), index, value_gradient.astype(jnp.bfloat16))

    chunks = ins.token_low.shape[0] // CHUNK
    return [
        functools.partial(unit, index) for unit in (token_side, key_side) for index in range(chunks)
    ]


def gradient_units(ins, slot, direct_ref, share):
    score_scale = HD ** (-0.5)
    mixing_low, values_low, row_total = share
    query_sums, key_sums = [], []
    scale = ins.mix[2 * HD + 1 + slot : 2 * HD + 2 + slot]

    def token_side(index):
        place = slice(index * CHUNK, (index + 1) * CHUNK)
        prob = ins.token_prob[slot, place]
        token_grad = wide_dot(chunk_of(ins.vg, 1, slot, index), mixing_low)
        token_sgrad = (
            prob * (token_grad - jnp.sum(token_grad * prob, axis=1, keepdims=True))
        ).astype(jnp.bfloat16)
        direct_ref[slot, 0, place] = wide_dot(token_sgrad, ins.marks[slot, 1]) * score_scale
        key_sums.append(wide_dot(ins.turned[slot, 0, :, place], token_sgrad))

    def key_side(index):
        place = slice(index * CHUNK, (index + 1) * CHUNK)
        key_prob = ins.key_exp[slot, place] * scale
        key_dgrad = wide_dot(chunk_of(ins.vg, 0, slot, index), values_low)
        key_sgrad = (key_prob * (key_dgrad - row_total)).astype(jnp.bfloat16)
        direct_ref[slot, 1, place] = wide_dot(key_sgrad, ins.marks[slot, 0]) * score_scale
        query_sums.append(wide_dot(ins.turned[slot, 1, :, place], key_sgrad))

    chunks = tokens_of(ins.vg) // CHUNK
    units = [
        [functools.partial(unit, index) for index in range(chunks)] for unit in (key_side, token_side)
    ]
    return units, query_sums, key_sums


def own_parts(ref):
    return (
        ref[0:HD].astype(jnp.bfloat16),
        ref[HD : 2 * HD].astype(jnp.bfloat16),
        ref[2 * HD : 2 * HD + 1],
    )


def other_parts(ref):
    parts = (ref[0:HD], ref[HD : 2 * HD], joined_thirds(ref[2 * HD :].astype(jnp.float32)[0:3]))
    return [swap_lanes(part) for part in parts]


def gradient_sweep(state, saved, place, beside, last):
    power, growth = state
    pair_ref, weight_ref, growth_ref = saved
    pair = (pair_ref[place, 0], pair_ref[place, 1])
    first = split_dot(pair, halves(power))
    beside()
    square = first[:M] + first[:M].T
    second = split_dot(tuple(x[:M] for x in pair) if last else pair, halves(square))
    beside()
    cube = first[M:].T + second[:M]
    weight = halves(0.25 * (7.0 * square - 15.0 * power - cube))
    if not last:
        fourth = second[M:] + second[M:].T
        power = 0.25 * (13.0 * power - 15.0 * square + 7.0 * cube - fourth)
    left = [growth_ref[place, 0], growth_ref[place, 0], growth_ref[place, 1]]
    right = [weight[0], weight[1], weight[0]]
    if growth is not None:
        grown = halves(growth)
        left += [grown[0], grown[0], grown[1]]
        right += [weight_ref[place, 0], weight_ref[place, 1], weight_ref[place, 0]]
    growth = wide_dot(jnp.concatenate(left, axis=1), jnp.concatenate(right, axis=0))
    return power, growth


def own_gradient_compute(ins, outs, need, put):
    for ref in (ins.mark_prob, ins.factor, ins.mix):
        need(ref)
    inverse_grad = split_dot(
        halves(ins.mix[2 * HD + 8 : 3 * HD + 8].T), halves(ins.mix[3 * HD + 8 :])
    )
    inverse_grad_halves = halves(inverse_grad)
    outs.inverse_grad[0], outs.inverse_grad[1] = inverse_grad_halves
    toward = split_dot(halves(ins.mark_prob[...]), inverse_grad_halves) * ins.factor[0:1, 0:1]
    state = (0.5 * (toward + toward.T), None)
    units = out_units(ins, 0, outs.out, (), own_parts(ins.mix))
    work = iter([units[index : index + 2] for index in range(0, len(units), 2)])
    saved = (ins.pair, ins.weight, ins.growth)

    def beside():
        several(*next(work, ()))

    for sweep in range(EARLY_SWEEPS):
        if sweep == 0:
            need(ins.token_low)
        if sweep == 1:
            need(ins.key_exp)
        for ref in saved:
            need(ref, sweep)
        state = gradient_sweep(state, saved, sweep, beside, False)
    outs.state[0], outs.state[1] = state


def other_out_compute(ins, outs, need, put):
    for ref in (ins.got_share, ins.mix, ins.token_low):
        need(ref)
    units = out_units(ins, 1, outs.out, (1,), other_parts(ins.got_share))
    chunks = len(units) // 2
    several(*units[:chunks])
    need()
    group = CHUNK // outs.out.shape[3]
    for index, unit in enumerate(units[chunks:]):
        unit()
        place = slice(index * group, (index + 1) * group)
        outs.out[place, :, 0] = ins.own_out[place]
        put(outs.out, index * group)


def gradient_compute(ins, outs, need, put):
    for ref in (ins.state, ins.mix, ins.got_share, ins.marks):
        need(ref)
    sides = []
    for slot in range(2):
        share = other_parts(ins.got_share) if slot else own_parts(ins.mix)
        sides.append(gradient_units(ins, slot, outs.direct, share))
    units = [
        (slot, kind, unit)
        for slot in range(2)
        for kind, side in enumerate(sides[slot][0])
        for unit in side
    ]
    sweeps = PINV_ITERS - EARLY_SWEEPS
    span = -(-len(units) // (2 * sweeps - 1))
    work = iter([()] + [units[index : index + span] for index in range(0, len(units), span)])
    saved = (ins.pair, ins.weight, ins.growth)
    state = (ins.state[0], ins.state[1])

    def beside():
        for slot, kind, unit in next(work, ()):
            need(ins.vg)
            need(ins.turned, slot)
            need(ins.token_prob if kind else ins.key_exp, slot)
            unit()

    for sweep in range(sweeps):
        for ref in saved:
            need(ref, sweep)
        if sweep == sweeps - 1:
            need(ins.last_growth)
            need(ins.inverse_grad)
            need(ins.mark_prob)
            direct_part = split_dot_nt(
                (ins.last_growth[0], ins.last_growth[1]),
                (ins.inverse_grad[0], ins.inverse_grad[1]),
            )
            mark_prob = ins.mark_prob[...]
            mark_halves = halves(mark_prob)
        state = gradient_sweep(state, saved, sweep, beside, sweep == sweeps - 1)
    put(outs.direct)
    need()
    growth = state[1]
    mark_grad = ins.factor[0:1, 0:1] * (
        direct_part + split_dot(halves(growth + growth.T), mark_halves)
    )
    mark_sgrad = mark_prob * (mark_grad - jnp.sum(mark_grad * mark_prob, axis=1, keepdims=True))

    def marks_dot(left, right):
        left_high, left_low = halves(left)
        return wide_dot(
            jnp.concatenate([left_high, left_low], axis=1), jnp.concatenate([right, right], axis=0)
        )

    own_marks = (
        marks_dot(mark_sgrad, ins.marks[0, 1]),
        marks_dot(mark_sgrad.T, ins.marks[0, 0]),
    )
    marks_scale = HD ** (-0.5) / (tokens_of(ins.vg) // HALF)
    for slot, (_, query_sums, key_sums) in enumerate(sides):
        for kind, sums in enumerate((query_sums, key_sums)):
            total = sum(sums[1:], sums[0]).T
            if slot == 0:
                total = total + own_marks[kind]
            total = total * marks_scale
            outs.far[kind, slot] = total[HALF:].astype(jnp.bfloat16)
            outs.near[kind, slot] = total[:HALF]
    put(outs.far)


def finish_compute(ins, outs, need, put):
    need(ins.near)
    need(ins.got_far)
    out_ref = outs.out
    group = CHUNK // out_ref.shape[3]
    segment_len = tokens_of(out_ref) // HALF
    per = CHUNK // segment_len
    for index in range(tokens_of(out_ref) // CHUNK):
        place, start = slice(index * per, (index + 1) * per), index * CHUNK
        for slot in range(2):
            for kind in range(2):
                if index % 2 == 0:
                    need(ins.direct, slot, kind, start)
                marks = ins.near[kind, slot, place] + ins.got_far[
                    kind, 1 - slot, place
                ].astype(jnp.float32)
                spread = jnp.broadcast_to(marks[:, None], (per, segment_len, HD))
                total = ins.direct[slot, kind, start : start + CHUNK] + spread.reshape(CHUNK, HD)
                store_chunk(out_ref, (kind, slot), index, total.astype(jnp.bfloat16))
        put(out_ref, index * group)


def exchange(packed):
    return lax.all_to_all(packed, "cube", split_axis=0, concat_axis=0, tiled=True)


def partner(array):
    return lax.ppermute(array, "half", SWAP)


def body(queries, keys, values, out_grad):
    half = lax.axis_index("half").reshape(1)
    qk, vg_packed = lax.optimization_barrier(
        (exchange(pack(half, queries, keys)), pack(half, values, out_grad))
    )
    tokens = qk.shape[0] * qk.shape[3]
    mine = landmarks_of(qk)
    theirs = partner(mine)
    vg_packed, mine = lax.optimization_barrier((vg_packed, mine))
    vg = exchange(vg_packed)
    kept = staged_call(
        probability_compute,
        dict(qk=qk, mine=mine, theirs=theirs),
        dict(
            marks=low(2, 2, M, HD),
            token_prob=wide(2, tokens, M),
            token_low=low(2, tokens, M),
            key_exp=wide(2, tokens, M),
            key_low=low(2, tokens, M),
            turned=low(2, 2, HD, tokens),
            stats=wide(8, M),
            mark_prob=wide(M, M),
            factor=wide(8, HD),
            pair_a=(low(EARLY_SWEEPS, 2, 2 * M, M), LEAD),
            weight_a=(low(EARLY_SWEEPS, 2, M, M), LEAD),
            growth_a=(low(EARLY_SWEEPS, 2, M, M), LEAD),
            pair_b=(low(PINV_ITERS - EARLY_SWEEPS, 2, 2 * M, M), LEAD),
            weight_b=(low(PINV_ITERS - EARLY_SWEEPS, 2, M, M), LEAD),
            growth_b=(low(PINV_ITERS - EARLY_SWEEPS, 2, M, M), LEAD),
            inverse=low(2, M, M),
            last_growth=low(2, M, M),
        ),
        LONG,
        extra=(pltpu.VMEM((M, M), jnp.float32), pltpu.VMEM((2 * M, M), jnp.float32)),
    )
    sums = staged_call(
        stats_partial_compute,
        dict(rows=(vg, SIDES[0]), lowered=(kept.key_low, LEAD), stats=kept.stats),
        dict(send=low(HD + 16, M), keep=wide(HD, M)),
        1,
    )
    got = partner(sums.send)
    grad_sums = staged_call(
        partial_compute,
        dict(rows=(vg, SIDES[1]), lowered=(kept.token_low, LEAD)),
        dict(send=low(HD, M), keep=wide(HD, M)),
        1,
        after=(sums.keep,),
    )
    share, mix = joined_sums(
        got, partner(grad_sums.send), sums.keep, grad_sums.keep, kept.stats, kept.inverse
    )
    got_share = partner(share)
    own = staged_call(
        own_gradient_compute,
        dict(
            mark_prob=kept.mark_prob,
            factor=kept.factor,
            mix=mix,
            token_low=(kept.token_low, SLOTS[0]),
            pair=(kept.pair_a, LEAD),
            weight=(kept.weight_a, LEAD),
            growth=(kept.growth_a, LEAD),
            key_exp=(kept.key_exp, SLOTS[0]),
        ),
        dict(
            out=low(qk.shape[0], 2, *qk.shape[3:]),
            state=wide(2, M, M),
            inverse_grad=low(2, M, M),
        ),
        8,
    )
    first_results = staged_call(
        other_out_compute,
        dict(
            got_share=got_share,
            mix=(mix, TOP),
            token_low=(kept.token_low, SLOTS[1]),
            key_exp=(kept.key_exp, SLOTS[1]),
            own_out=own.out,
        ),
        dict(out=(low(*qk.shape), GROUPS)),
        1,
    ).out
    attended, value_gradient_array = unpack(half, exchange(first_results))
    grads = staged_call(
        gradient_compute,
        dict(
            state=own.state,
            got_share=got_share,
            mix=(mix, TOP),
            marks=kept.marks,
            pair=(kept.pair_b, LEAD),
            weight=(kept.weight_b, LEAD),
            growth=(kept.growth_b, LEAD),
            vg=(vg, LATE),
            key_exp=(kept.key_exp, LEAD),
            turned=(kept.turned, LEAD),
            token_prob=(kept.token_prob, LEAD),
            inverse_grad=(own.inverse_grad, LAST),
            last_growth=(kept.last_growth, LAST),
            mark_prob=(kept.mark_prob, LAST),
            factor=(kept.factor, LAST),
        ),
        dict(
            far=low(2, 2, HALF, HD),
            near=wide(2, 2, HALF, HD),
            direct=(wide(2, 2, tokens, HD), LEAD),
        ),
        LONG,
        after=(first_results,),
    )
    results = staged_call(
        finish_compute,
        dict(got_far=partner(grads.far), near=grads.near, direct=(grads.direct, BLOCKS)),
        dict(out=(low(*qk.shape), GROUPS)),
        0.1,
    ).out
    query_grad, key_grad = unpack(half, exchange(results))
    return attended, query_grad, key_grad, value_gradient_array


def solution(mesh):
    whole_placement = P(("seq", "head"), None)
    halves_placement = P(("half", "cube"), None)

    def layer(queries, keys, values, out_grad):
        tokens, width = queries.shape
        own_head_each = width // HD == mesh.size and tokens == 8 * CHUNK
        if own_head_each:
            split = jax.sharding.Mesh(
                mesh.devices.reshape(2, mesh.size // 2), ("half", "cube")
            )
        return jax.shard_map(
            body if own_head_each else shared_body,
            mesh=split if own_head_each else mesh,
            in_specs=(halves_placement if own_head_each else whole_placement,) * 4,
            out_specs=(halves_placement if own_head_each else whole_placement,) * 4,
            check_vma=False,
        )(queries, keys, values, out_grad)

    return layer
```

```python
import functools
from types import SimpleNamespace

import jax
import jax.numpy as jnp
from jax import lax
from jax.experimental import pallas as pl
from jax.experimental.pallas import tpu as pltpu
from jax.sharding import PartitionSpec as P

HD = 128
M = 256
PINV_ITERS = 6
CHUNK = 256
PACK_GROUPS = 4
HALF = M // 2
SWAP = ((0, 1), (1, 0))
VMEM_LIMIT = 60 * 2**20
SMALL_LIMIT = 16 * 2**20
WHOLE, LEAD, GROUPS, BLOCKS, LATE, LAST = range(6)
SLOTS = (10, 11)
TOP = 12
SIDES = (20, 21)
LONG = 200
SPAN = 2 * CHUNK
EARLY_SWEEPS = PINV_ITERS // 2


precise_setting = lax.Precision.HIGHEST


def newton_inverse(matrix):
    identity = jnp.eye(matrix.shape[0], dtype=matrix.dtype)
    factor = lax.stop_gradient(1.0 / jnp.max(jnp.sum(matrix, axis=0)))
    iterate = matrix.T * factor
    for sweep_index in range(PINV_ITERS):
        product = jnp.matmul(matrix, iterate, precision=precise_setting)
        inner_term = jnp.matmul(product, 7.0 * identity - product, precision=precise_setting)
        inner_term = jnp.matmul(product, 15.0 * identity - inner_term, precision=precise_setting)
        iterate = 0.25 * jnp.matmul(
            iterate, 13.0 * identity - inner_term, precision=precise_setting
        )
    return iterate


def share_heads(own_matrix, head_count):
    seq_index = lax.axis_index("seq")
    slot_mask = (jnp.arange(head_count, dtype=jnp.int32) == seq_index).astype(jnp.float32)
    return lax.psum(slot_mask[:, None, None] * own_matrix[None], "seq")


def shared_body(queries, keys, values, out_grad):
    query_rows, key_rows, value_rows, grad_rows = (
        lax.all_to_all(queries, "head", split_axis=1, concat_axis=0, tiled=True),
        lax.all_to_all(keys, "head", split_axis=1, concat_axis=0, tiled=True),
        lax.all_to_all(values, "head", split_axis=1, concat_axis=0, tiled=True),
        lax.all_to_all(out_grad, "head", split_axis=1, concat_axis=0, tiled=True),
    )
    tok_rows = query_rows.shape[0]
    head_count = query_rows.shape[1] // HD
    local_marks = M // lax.axis_size("seq")
    segment_len = tok_rows // local_marks
    score_scale = HD ** (-0.5)
    seq_index = lax.axis_index("seq")

    def landmark(matrix):
        summed = jnp.sum(
            matrix.reshape(local_marks, segment_len, matrix.shape[1]), axis=1, dtype=jnp.float32
        )
        return (summed / segment_len).astype(jnp.bfloat16)

    mark_queries, mark_keys = (
        lax.all_gather(landmark(query_rows), "seq", axis=0, tiled=True),
        lax.all_gather(landmark(key_rows), "seq", axis=0, tiled=True),
    )
    query_per_head = query_rows.reshape(tok_rows, head_count, HD)
    key_per_head = key_rows.reshape(tok_rows, head_count, HD)
    value_per_head = value_rows.reshape(tok_rows, head_count, HD)
    gradient_per_head = grad_rows.reshape(tok_rows, head_count, HD)
    landmark_query_heads = mark_queries.reshape(M, head_count, HD)
    landmark_key_heads = mark_keys.reshape(M, head_count, HD)
    key_score = (
        jnp.einsum(
            "pcv,gcv->cpg", landmark_query_heads, key_per_head, preferred_element_type=jnp.float32
        )
        * score_scale
    )
    key_max = lax.pmax(jnp.max(key_score, axis=-1), "seq")
    key_exp = jnp.exp(key_score - key_max[..., None])
    partial_num = jnp.einsum(
        "akq,qay->aky",
        key_exp.astype(jnp.bfloat16),
        value_per_head,
        preferred_element_type=jnp.float32,
    )
    key_total, numerator = lax.psum((jnp.sum(key_exp, axis=-1), partial_num), "seq")
    landmark_value_rows = numerator / key_total[..., None]
    token_prob = jax.nn.softmax(
        jnp.einsum(
            "jti,cti->tjc", query_per_head, landmark_key_heads, preferred_element_type=jnp.float32
        )
        * score_scale,
        axis=-1,
    )
    token_probability_lowered = token_prob.astype(jnp.bfloat16)
    mark_prob = jax.nn.softmax(
        jnp.einsum(
            "jou,iou->oji",
            landmark_query_heads,
            landmark_key_heads,
            preferred_element_type=jnp.float32,
        )
        * score_scale,
        axis=-1,
    )
    own_head = seq_index % head_count
    own_mark = lax.dynamic_index_in_dim(mark_prob, own_head, 0, keepdims=False)
    own_inverse, pull_back = jax.vjp(newton_inverse, own_mark)
    pseudo_inverse_matrix = share_heads(own_inverse, head_count)
    mixing_matrix = jnp.einsum(
        "jvy,jys->jvs", pseudo_inverse_matrix, landmark_value_rows, precision=precise_setting
    )
    mixing_matrix_lowered = mixing_matrix.astype(jnp.bfloat16)
    attended = jnp.einsum(
        "yvo,yor->vyr",
        token_probability_lowered,
        mixing_matrix_lowered,
        preferred_element_type=jnp.float32,
    ).astype(jnp.bfloat16)
    token_grad = jnp.einsum(
        "fag,aog->afo", gradient_per_head, mixing_matrix_lowered, preferred_element_type=jnp.float32
    )
    partial_mix = jnp.einsum(
        "klz,lkr->kzr",
        token_probability_lowered,
        gradient_per_head,
        preferred_element_type=jnp.float32,
    )
    mixing_matrix_gradient = lax.psum(partial_mix, "seq")
    token_score_gradient = (
        token_prob * (token_grad - jnp.sum(token_grad * token_prob, axis=-1, keepdims=True))
    ).astype(jnp.bfloat16)
    direct_qgrad = (
        jnp.einsum(
            "ufg,guc->fuc",
            token_score_gradient,
            landmark_key_heads,
            preferred_element_type=jnp.float32,
        )
        * score_scale
    )
    mark_kgrad_f = (
        jnp.einsum(
            "xgi,gxy->ixy", token_score_gradient, query_per_head, preferred_element_type=jnp.float32
        )
        * score_scale
    )
    pseudo_inverse_gradient = jnp.einsum(
        "ktu,kyu->kty", mixing_matrix_gradient, landmark_value_rows, precision=precise_setting
    )
    landmark_value_gradient = jnp.einsum(
        "lrb,lrz->lbz", pseudo_inverse_matrix, mixing_matrix_gradient, precision=precise_setting
    )
    own_igrad = lax.dynamic_index_in_dim(pseudo_inverse_gradient, own_head, 0, keepdims=False)
    (own_mgrad,) = pull_back(own_igrad)
    mark_grad = share_heads(own_mgrad, head_count)
    mark_sgrad = mark_prob * (mark_grad - jnp.sum(mark_grad * mark_prob, axis=-1, keepdims=True))
    first_mark = seq_index * local_marks
    score_gradient_rows = lax.dynamic_slice_in_dim(mark_sgrad, first_mark, local_marks, 1)
    score_gradient_columns = lax.dynamic_slice_in_dim(mark_sgrad, first_mark, local_marks, 2)
    own_qgrad_a = (
        jnp.einsum(
            "txs,ste->xte",
            score_gradient_rows,
            landmark_key_heads.astype(jnp.float32),
            precision=precise_setting,
        )
        * score_scale
    )
    own_kgrad_a = (
        jnp.einsum(
            "eaj,aev->jev",
            score_gradient_columns,
            landmark_query_heads.astype(jnp.float32),
            precision=precise_setting,
        )
        * score_scale
    )
    landmark_value_lowered = landmark_value_gradient.astype(jnp.bfloat16)
    key_prob = key_exp / key_total[..., None]
    key_probability_lowered = key_prob.astype(jnp.bfloat16)
    value_gradient_array = jnp.einsum(
        "zct,zcj->tzj",
        key_probability_lowered,
        landmark_value_lowered,
        preferred_element_type=jnp.float32,
    )
    key_direct_gradient = jnp.einsum(
        "exb,geb->exg", landmark_value_lowered, value_per_head, preferred_element_type=jnp.float32
    )
    row_total = lax.psum(jnp.sum(key_prob * key_direct_gradient, axis=-1), "seq")
    key_score_gradient = (key_prob * (key_direct_gradient - row_total[..., None])).astype(
        jnp.bfloat16
    )
    direct_kgrad = (
        jnp.einsum(
            "pbo,bpx->opx",
            key_score_gradient,
            landmark_query_heads,
            preferred_element_type=jnp.float32,
        )
        * score_scale
    )
    mark_qgrad_b = (
        jnp.einsum(
            "cbj,jcp->bcp", key_score_gradient, key_per_head, preferred_element_type=jnp.float32
        )
        * score_scale
    )
    own_kgrad_f, own_qgrad_b = (
        lax.psum_scatter(mark_kgrad_f, "seq", scatter_dimension=0, tiled=True),
        lax.psum_scatter(mark_qgrad_b, "seq", scatter_dimension=0, tiled=True),
    )
    mark_qtotal = (own_qgrad_a + own_qgrad_b) / segment_len
    mark_ktotal = (own_kgrad_a + own_kgrad_f) / segment_len
    query_grad = (
        direct_qgrad.reshape(local_marks, segment_len, head_count, HD) + mark_qtotal[:, None]
    )
    key_grad = direct_kgrad.reshape(local_marks, segment_len, head_count, HD) + mark_ktotal[:, None]
    width = head_count * HD
    results = (
        attended.reshape(tok_rows, width),
        query_grad.astype(jnp.bfloat16).reshape(tok_rows, width),
        key_grad.astype(jnp.bfloat16).reshape(tok_rows, width),
        value_gradient_array.astype(jnp.bfloat16).reshape(tok_rows, width),
    )
    attended_out, query_out, key_out, value_out = (
        lax.all_to_all(results[0], "head", split_axis=0, concat_axis=1, tiled=True),
        lax.all_to_all(results[1], "head", split_axis=0, concat_axis=1, tiled=True),
        lax.all_to_all(results[2], "head", split_axis=0, concat_axis=1, tiled=True),
        lax.all_to_all(results[3], "head", split_axis=0, concat_axis=1, tiled=True),
    )
    return (attended_out, query_out, key_out, value_out)


def halves(matrix):
    high = matrix.astype(jnp.bfloat16)
    return high, (matrix - high.astype(jnp.float32)).astype(jnp.bfloat16)


def wide_dot(left, right):
    return jnp.dot(left, right, preferred_element_type=jnp.float32)


def wide_dot_nt(left, right):
    return lax.dot_general(
        left, right, (((1,), (1,)), ((), ())), preferred_element_type=jnp.float32
    )


def split_dot(left, right):
    left_high, left_low = left
    right_high, right_low = right
    return wide_dot(
        jnp.concatenate([left_high, left_high, left_low], axis=1),
        jnp.concatenate([right_high, right_low, right_high], axis=0),
    )


def split_dot_nt(left, right):
    left_high, left_low = left
    right_high, right_low = right
    return wide_dot_nt(
        jnp.concatenate([left_high, left_high, left_low], axis=1),
        jnp.concatenate([right_high, right_low, right_high], axis=1),
    )


def identity_matrix():
    return (
        lax.broadcasted_iota(jnp.int32, (M, M), 0) == lax.broadcasted_iota(jnp.int32, (M, M), 1)
    ).astype(jnp.float32)


def chunk_of(ref, array, slot, index, size=CHUNK):
    per = size // ref.shape[3]
    return ref[index * per : (index + 1) * per, array, slot].reshape(size, HD)


def store_chunk(ref, lead, index, value):
    rows = ref.shape[-2]
    per = value.shape[0] // rows
    ref[(slice(index * per, (index + 1) * per), *lead)] = value.reshape(per, rows, HD)


def all_tokens(ref, array, slot):
    return ref[:, array, slot].reshape(ref.shape[0] * ref.shape[3], HD)


def tokens_of(ref):
    return ref.shape[0] * ref.shape[3]


def columns(index):
    return pl.ds(pl.multiple_of(index * CHUNK, CHUNK), CHUNK)


def swap_lanes(matrix):
    return jnp.concatenate([matrix[:, HALF:], matrix[:, :HALF]], axis=1)


def thirds(rows):
    first = rows.astype(jnp.bfloat16).astype(jnp.float32)
    second = (rows - first).astype(jnp.bfloat16).astype(jnp.float32)
    return jnp.concatenate([first, second, rows - first - second], axis=0)


def joined_thirds(rows):
    count = rows.shape[0] // 3
    return rows[:count] + (rows[count : 2 * count] + rows[2 * count :])


def held_shape(kind, shape):
    if kind == TOP:
        return (2 * HD + 8, *shape[1:])
    if kind in SIDES:
        return (shape[0], *shape[2:])
    return shape[1:] if kind in SLOTS else shape


def pieces_of(kind, shape):
    if kind == LEAD:
        return [(index,) for index in range(shape[0])]
    if kind == BLOCKS:
        return [
            (first, second, slice(place, place + 2 * CHUNK))
            for place in range(0, shape[2], 2 * CHUNK)
            for first in range(shape[0])
            for second in range(shape[1])
        ]
    if kind == GROUPS:
        per = CHUNK // shape[-2]
        return [(slice(place, place + per),) for place in range(0, shape[0], per)]
    return [()]


def window(ref, piece):
    place = tuple(
        pl.ds(part.start, part.stop - part.start) if isinstance(part, slice) else part
        for part in piece
    )
    return ref.at[place] if place else ref


class Staged:
    def __init__(self, names, kinds, outer, inner, done, outward):
        self.refs = SimpleNamespace(**dict(zip(names, inner)))
        self.copies, self.order = [], []
        count = 0
        steps = []
        for place, (kind, home, held) in enumerate(zip(kinds, outer, inner)):
            home = home.at[kind - SLOTS[0]] if kind in SLOTS else home
            home = home.at[pl.ds(0, 2 * HD + 8)] if kind == TOP else home
            home = home.at[:, kind - SIDES[0]] if kind in SIDES else home
            copies = {}
            for step, piece in enumerate(pieces_of(kind, held.shape)):
                ends = (window(held, piece), window(home, piece))
                source, target = ends if outward else ends[::-1]
                key = tuple(
                    part.start if isinstance(part, slice) else part for part in piece
                )
                copies[key] = pltpu.make_async_copy(source, target, done.at[count])
                steps.append(({WHOLE: -1, TOP: -1, LAST: 9}.get(kind, step), place, key))
                count += 1
            self.copies.append(copies)
        self.inner = inner
        self.order = sorted(steps, key=lambda item: item[:2])
        self.started, self.waited = set(), set()

    def place_of(self, ref):
        return next(index for index, held in enumerate(self.inner) if held is ref)

    def start(self, ref=None, *key):
        chosen = [
            (place, name)
            for _, place, name in self.order
            if (ref is None or place == self.place_of(ref)) and (not key or name == key)
        ]
        for item in chosen:
            if item not in self.started:
                self.started.add(item)
                self.copies[item[0]][item[1]].start()

    def wait(self, ref=None, *key):
        chosen = [
            (place, name)
            for _, place, name in self.order
            if (ref is None or place == self.place_of(ref)) and (not key or name == key)
        ]
        for item in chosen:
            if item not in self.waited:
                self.waited.add(item)
                self.copies[item[0]][item[1]].wait()


def staged_call(compute, inputs, outputs, flops, extra=(), after=(), in_place=False):
    names_in, names_out = tuple(inputs), tuple(outputs)
    kinds_in = [x[1] if isinstance(x, tuple) else WHOLE for x in inputs.values()]
    kinds_out = [x[1] if isinstance(x, tuple) else WHOLE for x in outputs.values()]
    operands = tuple(x[0] if isinstance(x, tuple) else x for x in inputs.values())
    shapes = tuple(x[0] if isinstance(x, tuple) else x for x in outputs.values())
    n_in, n_out, n_after = len(operands), len(shapes), len(after)
    moved = sum(x.size * x.dtype.itemsize for x in (*operands, *shapes))
    anywhere = pl.BlockSpec(memory_space=pl.ANY)

    def count(kinds, arrays):
        return sum(len(pieces_of(kind, x.shape)) for kind, x in zip(kinds, arrays))

    def kernel(*refs):
        sources, refs = refs[:n_in], refs[n_in + n_after :]
        homes, refs = refs[:n_out], refs[n_out:]
        held_in, held_out = refs[:n_in], refs[n_in : n_in + n_out]
        *scratch, in_done, out_done = refs[n_in + n_out :]
        reads = Staged(names_in, kinds_in, sources, held_in, in_done, False)
        writes = Staged(names_out, kinds_out, homes, held_out, out_done, True)
        reads.start()
        compute(reads.refs, writes.refs, reads.wait, writes.start, *scratch)
        reads.wait()
        writes.start()
        writes.wait()

    results = pl.pallas_call(
        kernel,
        out_shape=shapes,
        in_specs=[anywhere] * (n_in + n_after),
        out_specs=(anywhere,) * n_out,
        scratch_shapes=[
            *(
                pltpu.VMEM(held_shape(kind, x.shape), x.dtype)
                for kind, x in zip((*kinds_in, *kinds_out), (*operands, *shapes))
            ),
            *extra,
            pltpu.SemaphoreType.DMA((count(kinds_in, operands),)),
            pltpu.SemaphoreType.DMA((count(kinds_out, shapes),)),
        ],
        compiler_params=pltpu.CompilerParams(vmem_limit_bytes=VMEM_LIMIT),
        cost_estimate=pl.CostEstimate(
            flops=int(flops * 10**9), bytes_accessed=moved, transcendentals=0
        ),
    )(*operands, *after)
    return SimpleNamespace(**dict(zip(outputs, results)))


def low(*shape):
    return jax.ShapeDtypeStruct(shape, jnp.bfloat16)


def wide(*shape):
    return jax.ShapeDtypeStruct(shape, jnp.float32)


def pack_kernel(half_ref, first_ref, second_ref, out_ref, rows_s, packed_s, in_done, out_done):
    half = half_ref[0]
    pairs = out_ref.shape[0]
    group = pairs // PACK_GROUPS
    span = 2 * HD
    reads, writes = [], []
    for index in range(PACK_GROUPS):
        for array, ref in enumerate((first_ref, second_ref)):
            place = pl.ds(index * group * span, group * span)
            reads.append(
                pltpu.make_async_copy(
                    ref.at[:, place], rows_s.at[array, :, place], in_done.at[array, index]
                )
            )
        place = pl.ds(index * group, group)
        writes.append(
            pltpu.make_async_copy(packed_s.at[place], out_ref.at[place], out_done.at[index])
        )
    for copy in reads:
        copy.start()
    for index in range(PACK_GROUPS):
        for array in range(2):
            reads[2 * index + array].wait()
            for pair in range(index * group, (index + 1) * group):
                start = pair * span
                packed_s[pair, array, half] = rows_s[array, :, start : start + HD]
                packed_s[pair, array, 1 - half] = rows_s[array, :, start + HD : start + span]
        writes[index].start()
    for copy in writes:
        copy.wait()


def unpack_kernel(half_ref, packed_ref, first_ref, second_ref, rows_s, out_done):
    half = half_ref[0]
    pairs = packed_ref.shape[0]
    group = pairs // PACK_GROUPS
    span = 2 * HD
    writes = []
    for index in range(PACK_GROUPS):
        for array, ref in enumerate((first_ref, second_ref)):
            for pair in range(index * group, (index + 1) * group):
                start = pair * span
                rows_s[array, :, start : start + HD] = packed_ref[pair, array, half]
                rows_s[array, :, start + HD : start + span] = packed_ref[pair, array, 1 - half]
            place = pl.ds(index * group * span, group * span)
            write = pltpu.make_async_copy(
                rows_s.at[array, :, place], ref.at[:, place], out_done.at[array, index]
            )
            write.start()
            writes.append(write)
    for copy in writes:
        copy.wait()


def layout_call(kernel, half, operands, out_shape, scratch, in_space, limit):
    anywhere = pl.BlockSpec(memory_space=pl.ANY)
    moved = 2 * sum(x.size * x.dtype.itemsize for x in operands)
    return pl.pallas_call(
        kernel,
        out_shape=out_shape,
        in_specs=[pl.BlockSpec(memory_space=pltpu.SMEM)]
        + [pl.BlockSpec(memory_space=in_space)] * len(operands),
        out_specs=jax.tree.map(lambda _: anywhere, out_shape),
        scratch_shapes=scratch,
        compiler_params=pltpu.CompilerParams(vmem_limit_bytes=limit),
        cost_estimate=pl.CostEstimate(flops=0, bytes_accessed=moved, transcendentals=0),
    )(half, *operands)


def pack(half, first, second):
    rows, width = first.shape
    shape = low(width // (2 * HD), 2, 2, rows, HD)
    scratch = [
        pltpu.VMEM((2, rows, width), jnp.bfloat16),
        pltpu.VMEM(shape.shape, jnp.bfloat16),
        pltpu.SemaphoreType.DMA((2, PACK_GROUPS)),
        pltpu.SemaphoreType.DMA((PACK_GROUPS,)),
    ]
    return layout_call(
        pack_kernel, half, (first, second), shape, scratch, pl.ANY, VMEM_LIMIT
    )


def unpack(half, packed):
    pairs, _, _, rows, _ = packed.shape
    shape = low(rows, pairs * 2 * HD)
    scratch = [
        pltpu.VMEM((2, *shape.shape), jnp.bfloat16),
        pltpu.SemaphoreType.DMA((2, PACK_GROUPS)),
    ]
    return layout_call(
        unpack_kernel, half, (packed,), (shape, shape), scratch, pltpu.VMEM, SMALL_LIMIT
    )


def landmark_kernel(qk_ref, marks_ref):
    tokens = tokens_of(qk_ref)
    segment_len = tokens // HALF
    per = CHUNK // segment_len
    member = (
        lax.broadcasted_iota(jnp.int32, (per, CHUNK), 1) // segment_len
        == lax.broadcasted_iota(jnp.int32, (per, CHUNK), 0)
    ).astype(jnp.bfloat16)
    kinds = [(slot, array) for slot in range(2) for array in range(2)]
    for index in range(tokens // CHUNK):
        parts = [chunk_of(qk_ref, array, slot, index) for slot, array in kinds]
        summed = wide_dot(member, jnp.concatenate(parts, axis=1))
        mean = (summed / segment_len).astype(jnp.bfloat16)
        for place, (slot, array) in enumerate(kinds):
            marks_ref[slot, array, index * per : (index + 1) * per] = mean[
                :, place * HD : (place + 1) * HD
            ]


def landmarks_of(qk):
    held = pl.BlockSpec(memory_space=pltpu.VMEM)
    return pl.pallas_call(
        landmark_kernel,
        out_shape=low(2, 2, HALF, HD),
        in_specs=[held],
        out_specs=held,
        compiler_params=pltpu.CompilerParams(vmem_limit_bytes=SMALL_LIMIT),
        cost_estimate=pl.CostEstimate(
            flops=2 * 10**8, bytes_accessed=qk.size * 2, transcendentals=0
        ),
    )(qk)


def sweep_forward(power_s, iterate_s, saved, sweep, work):
    pair_ref, weight_ref, growth_ref = saved
    power = power_s[...]
    power_high, power_low = halves(power)
    square = split_dot((power_high, power_low), (power_high, power_low))
    next(work)()
    square_halves = halves(square)
    pair = (
        jnp.concatenate([power_high, square_halves[0]], axis=0),
        jnp.concatenate([power_low, square_halves[1]], axis=0),
    )
    pair_ref[sweep, 0], pair_ref[sweep, 1] = pair
    higher = split_dot(pair, square_halves)
    next(work)()
    cube, fourth = higher[:M], higher[M:]
    weight = halves(0.25 * (13.0 * identity_matrix() - 15.0 * power + 7.0 * square - cube))
    power_s[...] = 0.25 * (13.0 * power - 15.0 * square + 7.0 * cube - fourth)
    weight_ref[sweep, 0], weight_ref[sweep, 1] = weight
    iterate = halves(iterate_s[...])
    growth_ref[sweep, 0], growth_ref[sweep, 1] = iterate[0][M:], iterate[1][M:]
    iterate_s[...] = split_dot(iterate, weight)


def probability_compute(ins, outs, need, put, power_s, iterate_s):
    need()
    qk_ref = ins.qk
    chunks = tokens_of(qk_ref) // CHUNK
    score_scale = HD ** (-0.5)
    for slot in range(2):
        for array in range(2):
            outs.marks[slot, array] = jnp.concatenate(
                [ins.mine[slot, array], ins.theirs[1 - slot, array]], axis=0
            )
    put(outs.marks)
    landmark_q, landmark_k = outs.marks[0, 0], outs.marks[0, 1]
    mark_score = wide_dot_nt(landmark_q, landmark_k) * score_scale
    mark_exp = jnp.exp(mark_score - jnp.max(mark_score, axis=1, keepdims=True))
    mark_prob = mark_exp / jnp.sum(mark_exp, axis=1, keepdims=True)
    outs.mark_prob[...] = mark_prob
    factor = 1.0 / jnp.max(jnp.sum(mark_prob, axis=0, keepdims=True), axis=1, keepdims=True)
    outs.factor[...] = jnp.broadcast_to(factor, outs.factor.shape)
    mark_halves = halves(mark_prob)
    power_s[...] = split_dot_nt(mark_halves, mark_halves) * factor
    iterate_s[0:M] = mark_prob.T * factor
    iterate_s[M:] = identity_matrix()
    tops, totals = [[], []], [[], []]

    def scores(slot, index):
        query_chunk, key_chunk = (chunk_of(qk_ref, array, slot, index) for array in range(2))
        place = slice(index * CHUNK, (index + 1) * CHUNK)
        outs.turned[slot, 0, :, place] = query_chunk.T
        outs.turned[slot, 1, :, place] = key_chunk.T
        score = wide_dot_nt(query_chunk, outs.marks[slot, 1]) * score_scale
        grown = jnp.exp(score - jnp.max(score, axis=1, keepdims=True))
        prob = grown * (1.0 / jnp.sum(grown, axis=1, keepdims=True))
        outs.token_prob[slot, place] = prob
        outs.token_low[slot, place] = prob.astype(jnp.bfloat16)
        key_score = wide_dot_nt(key_chunk, outs.marks[slot, 0]) * score_scale
        outs.key_exp[slot, place] = key_score
        tops[slot].append(jnp.max(key_score, axis=0, keepdims=True))

    def grow(slot, index):
        if index == 0:
            tops[slot] = functools.reduce(jnp.maximum, tops[slot])
        place = slice(index * CHUNK, (index + 1) * CHUNK)
        grown = jnp.exp(outs.key_exp[slot, place] - tops[slot])
        outs.key_exp[slot, place] = grown
        outs.key_low[slot, place] = grown.astype(jnp.bfloat16)
        totals[slot].append(jnp.sum(grown, axis=0, keepdims=True))

    def several(unit, pairs):
        for slot, index in pairs:
            unit(slot, index)

    pairs = [(slot, index) for slot in range(2) for index in range(chunks)]
    work = iter(
        [functools.partial(several, scores, [pair]) for pair in pairs]
        + [
            functools.partial(several, grow, pairs[first : first + 2])
            for first in range(0, len(pairs), 2)
        ]
    )
    for sweep in range(PINV_ITERS):
        first = sweep < EARLY_SWEEPS
        place = sweep if first else sweep - EARLY_SWEEPS
        saved = (
            (outs.pair_a, outs.weight_a, outs.growth_a)
            if first
            else (outs.pair_b, outs.weight_b, outs.growth_b)
        )
        sweep_forward(power_s, iterate_s, saved, place, work)
        for ref in saved:
            put(ref, place)
        if sweep == 3:
            for ref in (outs.token_low, outs.token_prob, outs.turned):
                put(ref)
    put(outs.key_low)
    put(outs.key_exp)
    outs.inverse[0], outs.inverse[1] = halves(iterate_s[0:M])
    outs.last_growth[0], outs.last_growth[1] = halves(iterate_s[M:])
    stats = [x for slot in range(2) for x in (tops[slot], sum(totals[slot][1:], totals[slot][0]))]
    outs.stats[0:4] = jnp.concatenate(stats, axis=0)
    outs.stats[4:8] = jnp.zeros((4, M), jnp.float32)


def partial_compute(ins, outs, need, put):
    need(ins.rows)
    heads, _, rows, _ = ins.rows.shape
    turned = [ins.rows[:, slot].reshape(heads * rows, HD).T for slot in range(2)]
    for slot, home in enumerate((outs.keep, outs.send)):
        need(ins.lowered, slot)
        home[0:HD] = wide_dot(turned[slot], ins.lowered[slot]).astype(home.dtype)


def stats_partial_compute(ins, outs, need, put):
    partial_compute(ins, outs, need, put)
    need(ins.stats)
    rows = thirds(ins.stats[0:4])
    outs.send[HD:] = jnp.concatenate([rows, jnp.zeros((4, M), jnp.float32)], axis=0).astype(
        jnp.bfloat16
    )


def mixing_kernel(
    got_ref, got_grad_ref, keep_ref, keep_grad_ref, stats_ref, inverse_ref, share_ref, mix_ref
):
    got = got_ref[...].astype(jnp.float32)
    others = swap_lanes(joined_thirds(got[HD : HD + 12]))
    scales = []
    for slot in range(2):
        own, other = 2 * slot, 2 * (1 - slot)
        own_max, own_total = stats_ref[own : own + 1], stats_ref[own + 1 : own + 2]
        other_max, other_total = others[other : other + 1], others[other + 1 : other + 2]
        key_max = jnp.maximum(own_max, other_max)
        own_factor, other_factor = jnp.exp(own_max - key_max), jnp.exp(other_max - key_max)
        inverse_total = 1.0 / (own_total * own_factor + other_total * other_factor)
        scales.append((own_factor * inverse_total, other_factor * inverse_total))
    landmark_values = keep_ref[...] * scales[0][0] + swap_lanes(got[0:HD]) * scales[0][1]
    mixing_grad = keep_grad_ref[...] + swap_lanes(got_grad_ref[...].astype(jnp.float32))
    inverse = (inverse_ref[0], inverse_ref[1])
    mixing_low = split_dot_nt(halves(landmark_values), inverse).astype(jnp.bfloat16)
    values_low = split_dot(halves(mixing_grad), inverse).astype(jnp.bfloat16)
    row_total = jnp.sum(values_low.astype(jnp.float32) * landmark_values, axis=0, keepdims=True)
    share_ref[0:HD] = mixing_low
    share_ref[HD : 2 * HD] = values_low
    share_ref[2 * HD :] = jnp.concatenate(
        [thirds(row_total), jnp.zeros((13, M), jnp.float32)], axis=0
    ).astype(jnp.bfloat16)
    mix_ref[0:HD] = mixing_low.astype(jnp.float32)
    mix_ref[HD : 2 * HD] = values_low.astype(jnp.float32)
    mix_ref[2 * HD : 2 * HD + 8] = jnp.concatenate(
        [row_total, scales[0][0], scales[1][0], jnp.zeros((5, M), jnp.float32)], axis=0
    )
    mix_ref[2 * HD + 8 : 3 * HD + 8] = mixing_grad
    mix_ref[3 * HD + 8 :] = landmark_values


def joined_sums(*operands):
    held = pl.BlockSpec(memory_space=pltpu.VMEM)
    return pl.pallas_call(
        mixing_kernel,
        out_shape=(low(2 * HD + 16, M), wide(4 * HD + 8, M)),
        in_specs=[held] * len(operands),
        out_specs=(held, held),
        compiler_params=pltpu.CompilerParams(vmem_limit_bytes=SMALL_LIMIT),
        cost_estimate=pl.CostEstimate(flops=2 * 10**8, bytes_accessed=2**20, transcendentals=0),
    )(*operands)


def several(*units):
    for unit in units:
        unit()


def out_units(ins, slot, out_ref, lead, share):
    mixing_low, values_low, _ = share
    scale = ins.mix[2 * HD + 1 + slot : 2 * HD + 2 + slot]

    def token_side(index):
        place = slice(index * SPAN, (index + 1) * SPAN)
        attended = wide_dot_nt(ins.token_low[place], mixing_low)
        store_chunk(out_ref, (0, *lead), index, attended.astype(jnp.bfloat16))

    def key_side(index):
        place = slice(index * SPAN, (index + 1) * SPAN)
        key_plow = (ins.key_exp[place] * scale).astype(jnp.bfloat16)
        value_gradient = wide_dot_nt(key_plow, values_low)
        store_chunk(out_ref, (1, *lead), index, value_gradient.astype(jnp.bfloat16))

    chunks = ins.token_low.shape[0] // SPAN
    return [
        functools.partial(unit, index) for unit in (token_side, key_side) for index in range(chunks)
    ]


def gradient_units(ins, slot, direct_ref, share):
    score_scale = HD ** (-0.5)
    mixing_low, values_low, row_total = share
    query_sums, key_sums = [], []
    scale = ins.mix[2 * HD + 1 + slot : 2 * HD + 2 + slot]

    def token_side(index):
        place = slice(index * SPAN, (index + 1) * SPAN)
        prob = ins.token_prob[slot, place]
        token_grad = wide_dot(chunk_of(ins.vg, 1, slot, index, SPAN), mixing_low)
        token_sgrad = (
            prob * (token_grad - jnp.sum(token_grad * prob, axis=1, keepdims=True))
        ).astype(jnp.bfloat16)
        direct_ref[slot, 0, place] = wide_dot(token_sgrad, ins.marks[slot, 1]) * score_scale
        key_sums.append(wide_dot(ins.turned[slot, 0, :, place], token_sgrad))

    def key_side(index):
        place = slice(index * SPAN, (index + 1) * SPAN)
        key_prob = ins.key_exp[slot, place] * scale
        key_dgrad = wide_dot(chunk_of(ins.vg, 0, slot, index, SPAN), values_low)
        key_sgrad = (key_prob * (key_dgrad - row_total)).astype(jnp.bfloat16)
        direct_ref[slot, 1, place] = wide_dot(key_sgrad, ins.marks[slot, 0]) * score_scale
        query_sums.append(wide_dot(ins.turned[slot, 1, :, place], key_sgrad))

    chunks = tokens_of(ins.vg) // SPAN
    units = [
        [functools.partial(unit, index) for index in range(chunks)] for unit in (key_side, token_side)
    ]
    return units, query_sums, key_sums


def own_parts(ref):
    return (
        ref[0:HD].astype(jnp.bfloat16),
        ref[HD : 2 * HD].astype(jnp.bfloat16),
        ref[2 * HD : 2 * HD + 1],
    )


def other_parts(ref):
    parts = (ref[0:HD], ref[HD : 2 * HD], joined_thirds(ref[2 * HD :].astype(jnp.float32)[0:3]))
    return [swap_lanes(part) for part in parts]


def gradient_sweep(state, saved, place, beside, last):
    power, growth = state
    pair_ref, weight_ref, growth_ref = saved
    pair = (pair_ref[place, 0], pair_ref[place, 1])
    first = split_dot(pair, halves(power))
    beside()
    square = first[:M] + first[:M].T
    second = split_dot(tuple(x[:M] for x in pair) if last else pair, halves(square))
    beside()
    cube = first[M:].T + second[:M]
    weight = halves(0.25 * (7.0 * square - 15.0 * power - cube))
    if not last:
        fourth = second[M:] + second[M:].T
        power = 0.25 * (13.0 * power - 15.0 * square + 7.0 * cube - fourth)
    left = [growth_ref[place, 0], growth_ref[place, 0], growth_ref[place, 1]]
    right = [weight[0], weight[1], weight[0]]
    if growth is not None:
        grown = halves(growth)
        left += [grown[0], grown[0], grown[1]]
        right += [weight_ref[place, 0], weight_ref[place, 1], weight_ref[place, 0]]
    growth = wide_dot(jnp.concatenate(left, axis=1), jnp.concatenate(right, axis=0))
    return power, growth


def own_gradient_compute(ins, outs, need, put):
    for ref in (ins.mark_prob, ins.factor, ins.mix):
        need(ref)
    inverse_grad = split_dot(
        halves(ins.mix[2 * HD + 8 : 3 * HD + 8].T), halves(ins.mix[3 * HD + 8 :])
    )
    inverse_grad_halves = halves(inverse_grad)
    outs.inverse_grad[0], outs.inverse_grad[1] = inverse_grad_halves
    toward = split_dot(halves(ins.mark_prob[...]), inverse_grad_halves) * ins.factor[0:1, 0:1]
    state = (0.5 * (toward + toward.T), None)
    units = out_units(ins, 0, outs.out, (), own_parts(ins.mix))
    work = iter([[unit] for unit in units])
    saved = (ins.pair, ins.weight, ins.growth)

    def beside():
        several(*next(work, ()))

    for sweep in range(EARLY_SWEEPS):
        if sweep == 0:
            need(ins.token_low)
        if sweep == 1:
            need(ins.key_exp)
        for ref in saved:
            need(ref, sweep)
        state = gradient_sweep(state, saved, sweep, beside, False)
    outs.state[0], outs.state[1] = state


def other_out_compute(ins, outs, need, put):
    for ref in (ins.got_share, ins.mix, ins.token_low):
        need(ref)
    units = out_units(ins, 1, outs.out, (1,), other_parts(ins.got_share))
    chunks = len(units) // 2
    several(*units[:chunks])
    need()
    group = SPAN // outs.out.shape[3]
    for index, unit in enumerate(units[chunks:]):
        unit()
        place = slice(index * group, (index + 1) * group)
        outs.out[place, :, 0] = ins.own_out[place]
        for start in range(index * group, (index + 1) * group, CHUNK // outs.out.shape[3]):
            put(outs.out, start)


def gradient_compute(ins, outs, need, put):
    for ref in (ins.state, ins.mix, ins.got_share, ins.marks):
        need(ref)
    sides = []
    for slot in range(2):
        share = other_parts(ins.got_share) if slot else own_parts(ins.mix)
        sides.append(gradient_units(ins, slot, outs.direct, share))
    units = [
        (slot, kind, unit)
        for slot in range(2)
        for kind, side in enumerate(sides[slot][0])
        for unit in side
    ]
    sweeps = PINV_ITERS - EARLY_SWEEPS
    span = -(-len(units) // (2 * sweeps - 1))
    work = iter([()] + [units[index : index + span] for index in range(0, len(units), span)])
    saved = (ins.pair, ins.weight, ins.growth)
    state = (ins.state[0], ins.state[1])

    def beside():
        for slot, kind, unit in next(work, ()):
            need(ins.vg)
            need(ins.turned, slot)
            need(ins.token_prob if kind else ins.key_exp, slot)
            unit()

    for sweep in range(sweeps):
        for ref in saved:
            need(ref, sweep)
        if sweep == sweeps - 1:
            need(ins.last_growth)
            need(ins.inverse_grad)
            need(ins.mark_prob)
            direct_part = split_dot_nt(
                (ins.last_growth[0], ins.last_growth[1]),
                (ins.inverse_grad[0], ins.inverse_grad[1]),
            )
            mark_prob = ins.mark_prob[...]
            mark_halves = halves(mark_prob)
        state = gradient_sweep(state, saved, sweep, beside, sweep == sweeps - 1)
    put(outs.direct)
    need()
    growth = state[1]
    mark_grad = ins.factor[0:1, 0:1] * (
        direct_part + split_dot(halves(growth + growth.T), mark_halves)
    )
    mark_sgrad = mark_prob * (mark_grad - jnp.sum(mark_grad * mark_prob, axis=1, keepdims=True))

    def marks_dot(left, right):
        left_high, left_low = halves(left)
        return wide_dot(
            jnp.concatenate([left_high, left_low], axis=1), jnp.concatenate([right, right], axis=0)
        )

    own_marks = (
        marks_dot(mark_sgrad, ins.marks[0, 1]),
        marks_dot(mark_sgrad.T, ins.marks[0, 0]),
    )
    marks_scale = HD ** (-0.5) / (tokens_of(ins.vg) // HALF)
    for slot, (_, query_sums, key_sums) in enumerate(sides):
        for kind, sums in enumerate((query_sums, key_sums)):
            total = sum(sums[1:], sums[0]).T
            if slot == 0:
                total = total + own_marks[kind]
            total = total * marks_scale
            outs.far[kind, slot] = total[HALF:].astype(jnp.bfloat16)
            outs.near[kind, slot] = total[:HALF]
    put(outs.far)


def finish_compute(ins, outs, need, put):
    need(ins.near)
    need(ins.got_far)
    out_ref = outs.out
    group = CHUNK // out_ref.shape[3]
    segment_len = tokens_of(out_ref) // HALF
    per = CHUNK // segment_len
    for index in range(tokens_of(out_ref) // CHUNK):
        place, start = slice(index * per, (index + 1) * per), index * CHUNK
        for slot in range(2):
            for kind in range(2):
                if index % 2 == 0:
                    need(ins.direct, slot, kind, start)
                marks = ins.near[kind, slot, place] + ins.got_far[
                    kind, 1 - slot, place
                ].astype(jnp.float32)
                spread = jnp.broadcast_to(marks[:, None], (per, segment_len, HD))
                total = ins.direct[slot, kind, start : start + CHUNK] + spread.reshape(CHUNK, HD)
                store_chunk(out_ref, (kind, slot), index, total.astype(jnp.bfloat16))
        put(out_ref, index * group)


def exchange(packed):
    return lax.all_to_all(packed, "cube", split_axis=0, concat_axis=0, tiled=True)


def partner(array):
    return lax.ppermute(array, "half", SWAP)


def body(queries, keys, values, out_grad):
    half = lax.axis_index("half").reshape(1)
    qk, vg_packed = lax.optimization_barrier(
        (exchange(pack(half, queries, keys)), pack(half, values, out_grad))
    )
    tokens = qk.shape[0] * qk.shape[3]
    mine = landmarks_of(qk)
    theirs = partner(mine)
    vg_packed, mine = lax.optimization_barrier((vg_packed, mine))
    vg = exchange(vg_packed)
    kept = staged_call(
        probability_compute,
        dict(qk=qk, mine=mine, theirs=theirs),
        dict(
            marks=low(2, 2, M, HD),
            token_prob=wide(2, tokens, M),
            token_low=low(2, tokens, M),
            key_exp=wide(2, tokens, M),
            key_low=low(2, tokens, M),
            turned=low(2, 2, HD, tokens),
            stats=wide(8, M),
            mark_prob=wide(M, M),
            factor=wide(8, HD),
            pair_a=(low(EARLY_SWEEPS, 2, 2 * M, M), LEAD),
            weight_a=(low(EARLY_SWEEPS, 2, M, M), LEAD),
            growth_a=(low(EARLY_SWEEPS, 2, M, M), LEAD),
            pair_b=(low(PINV_ITERS - EARLY_SWEEPS, 2, 2 * M, M), LEAD),
            weight_b=(low(PINV_ITERS - EARLY_SWEEPS, 2, M, M), LEAD),
            growth_b=(low(PINV_ITERS - EARLY_SWEEPS, 2, M, M), LEAD),
            inverse=low(2, M, M),
            last_growth=low(2, M, M),
        ),
        LONG,
        extra=(pltpu.VMEM((M, M), jnp.float32), pltpu.VMEM((2 * M, M), jnp.float32)),
    )
    sums = staged_call(
        stats_partial_compute,
        dict(rows=(vg, SIDES[0]), lowered=(kept.key_low, LEAD), stats=kept.stats),
        dict(send=low(HD + 16, M), keep=wide(HD, M)),
        1,
    )
    got = partner(sums.send)
    grad_sums = staged_call(
        partial_compute,
        dict(rows=(vg, SIDES[1]), lowered=(kept.token_low, LEAD)),
        dict(send=low(HD, M), keep=wide(HD, M)),
        1,
        after=(sums.keep,),
    )
    share, mix = joined_sums(
        got, partner(grad_sums.send), sums.keep, grad_sums.keep, kept.stats, kept.inverse
    )
    got_share = partner(share)
    own = staged_call(
        own_gradient_compute,
        dict(
            mark_prob=kept.mark_prob,
            factor=kept.factor,
            mix=mix,
            token_low=(kept.token_low, SLOTS[0]),
            pair=(kept.pair_a, LEAD),
            weight=(kept.weight_a, LEAD),
            growth=(kept.growth_a, LEAD),
            key_exp=(kept.key_exp, SLOTS[0]),
        ),
        dict(
            out=low(qk.shape[0], 2, *qk.shape[3:]),
            state=wide(2, M, M),
            inverse_grad=low(2, M, M),
        ),
        8,
    )
    first_results = staged_call(
        other_out_compute,
        dict(
            got_share=got_share,
            mix=(mix, TOP),
            token_low=(kept.token_low, SLOTS[1]),
            key_exp=(kept.key_exp, SLOTS[1]),
            own_out=own.out,
        ),
        dict(out=(low(*qk.shape), GROUPS)),
        1,
    ).out
    attended, value_gradient_array = unpack(half, exchange(first_results))
    grads = staged_call(
        gradient_compute,
        dict(
            state=own.state,
            got_share=got_share,
            mix=(mix, TOP),
            marks=kept.marks,
            pair=(kept.pair_b, LEAD),
            weight=(kept.weight_b, LEAD),
            growth=(kept.growth_b, LEAD),
            vg=(vg, LATE),
            key_exp=(kept.key_exp, LEAD),
            turned=(kept.turned, LEAD),
            token_prob=(kept.token_prob, LEAD),
            inverse_grad=(own.inverse_grad, LAST),
            last_growth=(kept.last_growth, LAST),
            mark_prob=(kept.mark_prob, LAST),
            factor=(kept.factor, LAST),
        ),
        dict(
            far=low(2, 2, HALF, HD),
            near=wide(2, 2, HALF, HD),
            direct=(wide(2, 2, tokens, HD), LEAD),
        ),
        LONG,
        after=(first_results,),
    )
    results = staged_call(
        finish_compute,
        dict(got_far=partner(grads.far), near=grads.near, direct=(grads.direct, BLOCKS)),
        dict(out=(low(*qk.shape), GROUPS)),
        0.1,
    ).out
    query_grad, key_grad = unpack(half, exchange(results))
    return attended, query_grad, key_grad, value_gradient_array


def solution(mesh):
    whole_placement = P(("seq", "head"), None)
    halves_placement = P(("half", "cube"), None)

    def layer(queries, keys, values, out_grad):
        tokens, width = queries.shape
        own_head_each = width // HD == mesh.size and tokens == 8 * CHUNK
        if own_head_each:
            split = jax.sharding.Mesh(
                mesh.devices.reshape(2, mesh.size // 2), ("half", "cube")
            )
        return jax.shard_map(
            body if own_head_each else shared_body,
            mesh=split if own_head_each else mesh,
            in_specs=(halves_placement if own_head_each else whole_placement,) * 4,
            out_specs=(halves_placement if own_head_each else whole_placement,) * 4,
            check_vma=False,
        )(queries, keys, values, out_grad)

    return layer
```
